32 devices in a mesh: row: 4 (over x, core), col: 8 (over z, y).
Axes of the slice: x: 2, y: 2, z: 4, core: 2. Of those that a mesh axis runs over, the one named last changes fastest.
Arguments:
- features: bfloat16 [32, 256, 256], P('row', 'col'), may hold values from -16 to 16
- expand_weight: bfloat16 [2, 256, 1024], replicated, may hold values from -0.375 to 0.375
- expand_bias: float32 [2, 1024], replicated, may hold values from -3 to 3
- depth_weight: float32 [2, 3, 3, 1024], replicated, may hold values from -2 to 2
- depth_bias: float32 [2, 1024], replicated, may hold values from -3 to 3
- project_weight: bfloat16 [2, 1024, 256], replicated, may hold values from -0.1875 to 0.1875
- project_bias: float32 [2, 256], replicated, may hold values from -3 to 3
- qkv_weight: bfloat16 [2, 256, 768], replicated, may hold values from -0.375 to 0.375
- aggregate_depth: float32 [2, 5, 5, 768], replicated, may hold values from -1.25 to 1.25
- aggregate_group: bfloat16 [2, 24, 32, 32], replicated, may hold values from -1 to 1
- output_weight: bfloat16 [2, 512, 256], replicated, may hold values from -0.25 to 0.25
- output_bias: float32 [2, 256], replicated, may hold values from -3 to 3
- head_weight: bfloat16 [3, 3, 4, 256], replicated, may hold values from -0.125 to 0.125
- head_bias: float32 [4], replicated, may hold values from -3 to 3
Outputs:
- final_map: bfloat16 [32, 256, 256], P('row', 'col')
- boxes: float32 [4, 32, 256], P(None, 'row', 'col')
The draws below stay inside these ranges and needn't reach their ends.
All inputs are finite; a program needn't handle non-finite values.
Results may differ from the reference program's by a relative error of at most 0.009.
Values may be sent and summed in bfloat16 or wider, within the bound.
No kernel may reach another device: no remote copies, remote signals or barrier semaphores. Data moves between devices by JAX's collectives and lax.ppermute only.
A program may use at most 64 MiB of HBM per device.

```python
import jax
import jax.numpy as jnp
from jax import lax

C = 256
HD = 32
HEADS = 8
E = 1024
SECTIONS = 2
TH = 8
TW = 32
NH = 32
NW = 256
N_ROW = 4


def draw_features(key, part):
    key_base, key_rows, key_cols, key_tile_scale, key_tile_offset = jax.random.split(key, 5)
    tile_rows = NH // TH
    tile_cols = NW // TW
    row_scale = jnp.exp(jax.random.uniform(key_rows, (NH, 1, 1), jnp.float32, -0.57, 0.57))
    col_scale = jnp.exp(jax.random.uniform(key_cols, (1, NW, 1), jnp.float32, -0.57, 0.57))
    tile_scale = jnp.exp(jax.random.uniform(key_tile_scale, (tile_rows, tile_cols, 1), jnp.float32, -1.2, 1.2))
    tile_offset = jnp.clip(jax.random.normal(key_tile_offset, (tile_rows, tile_cols, C), jnp.float32), -2.5, 2.5)
    scale_map = jnp.repeat(jnp.repeat(tile_scale, TH, axis=0), TW, axis=1)
    offset_map = jnp.repeat(jnp.repeat(tile_offset, TH, axis=0), TW, axis=1)
    base = jnp.clip(jax.random.normal(key_base, (NH, NW, C), jnp.float32), -4.0, 4.0)
    value = (base * row_scale * col_scale + offset_map) * scale_map
    return jnp.clip(value, -16.0, 16.0).astype(jnp.bfloat16)


def centred(rng, shape, deviation, most, kind=jnp.bfloat16):
    return jnp.clip(deviation * jax.random.normal(rng, shape, jnp.float32), -most, most).astype(kind)


def setup_inputs(seed: int = 0) -> dict:
    splits = jax.random.split(jax.random.key(seed), 15)
    features = draw_features(jax.random.fold_in(splits[14], 71), 0)
    expand_weight = centred(splits[1], (SECTIONS, C, E), C ** -0.5, 0.375)
    expand_bias = centred(splits[2], (SECTIONS, E), 0.5, 3.0, jnp.float32)
    depth_weight = centred(splits[3], (SECTIONS, 3, 3, E), 9 ** -0.5, 2.0, jnp.float32)
    depth_bias = centred(splits[4], (SECTIONS, E), 0.5, 3.0, jnp.float32)
    project_weight = centred(splits[5], (SECTIONS, E, C), E ** -0.5, 0.1875)
    project_bias = centred(splits[6], (SECTIONS, C), 0.5, 3.0, jnp.float32)
    qkv_weight = centred(splits[7], (SECTIONS, C, 3 * C), C ** -0.5, 0.375)
    aggregate_depth = centred(splits[8], (SECTIONS, 5, 5, 3 * C), 25 ** -0.5, 1.25, jnp.float32)
    aggregate_group = centred(splits[9], (SECTIONS, 3 * HEADS, HD, HD), HD ** -0.5, 1.0)
    output_weight = centred(splits[10], (SECTIONS, 2 * C, C), (2 * C) ** -0.5, 0.25)
    output_bias = centred(splits[11], (SECTIONS, C), 0.5, 3.0, jnp.float32)
    head_weight = centred(splits[12], (3, 3, 4, C), (9 * C) ** -0.5, 0.125)
    head_bias = centred(splits[13], (4,), 1.0, 3.0, jnp.float32)
    return {"features": features, "expand_weight": expand_weight, "expand_bias": expand_bias, "depth_weight": depth_weight, "depth_bias": depth_bias, "project_weight": project_weight, "project_bias": project_bias, "qkv_weight": qkv_weight, "aggregate_depth": aggregate_depth, "aggregate_group": aggregate_group, "output_weight": output_weight, "output_bias": output_bias, "head_weight": head_weight, "head_bias": head_bias}


def hard_swish(value):
    return value * jnp.minimum(jnp.maximum(value + 3.0, 0.0), 6.0) / 6.0


def depthwise(padded, weight, rows, cols):
    ksize = weight.shape[0]
    total = jnp.zeros((rows, cols, padded.shape[2]), jnp.float32)
    for offset_r in range(ksize):
        for offset_c in range(ksize):
            total = total + padded[offset_r:offset_r + rows, offset_c:offset_c + cols, :].astype(jnp.float32) * weight[offset_r, offset_c]
    return total


def dense(values, weight):
    flat = values.reshape(-1, values.shape[-1])
    result = jnp.dot(flat, weight, preferred_element_type=jnp.float32)
    return result.reshape(values.shape[:-1] + (weight.shape[1],))


def heads_of(padded_qkv, agg_depth, agg_group, rows, cols, heads, head_dim):
    center = padded_qkv[2:2 + rows, 2:2 + cols, :]
    spread = depthwise(padded_qkv, agg_depth, rows, cols).astype(jnp.bfloat16)
    grouped = jnp.einsum("rcgd,gde->rcge", spread.reshape(rows, cols, 3 * heads, head_dim).astype(jnp.float32), agg_group.astype(jnp.float32), precision=lax.Precision.HIGHEST).astype(jnp.bfloat16)
    return jnp.concatenate([center.reshape(rows, cols, heads, 3, head_dim), grouped.reshape(rows, cols, heads, 3, head_dim)], axis=2)


def reference(features, expand_weight, expand_bias, depth_weight, depth_bias, project_weight, project_bias, qkv_weight, aggregate_depth, aggregate_group, output_weight, output_bias, head_weight, head_bias):
    current = features
    block_ids = jnp.arange(N_ROW, dtype=jnp.int32)
    col_at = jnp.arange(NW + 2, dtype=jnp.int32)
    col_ok = ((col_at >= 1) & (col_at <= NW)).astype(jnp.bfloat16)
    for section in range(SECTIONS):
        padded = jnp.pad(current, ((1, 1), (1, 1), (0, 0)))

        def mb_block(index, current=current, padded=padded, section=section):
            start = index * TH
            piece = lax.dynamic_slice_in_dim(padded, start, TH + 2, 0)
            hidden = hard_swish(dense(piece, expand_weight[section]) + expand_bias[section]).astype(jnp.bfloat16)
            row_at = start + jnp.arange(TH + 2, dtype=jnp.int32)
            row_ok = ((row_at >= 1) & (row_at <= NH)).astype(jnp.bfloat16)
            hidden = hidden * row_ok[:, None, None] * col_ok[None, :, None]
            spread = hard_swish(depthwise(hidden, depth_weight[section], TH, NW) + depth_bias[section]).astype(jnp.bfloat16)
            base = lax.dynamic_slice_in_dim(current, start, TH, 0)
            return (base + dense(spread, project_weight[section]) + project_bias[section]).astype(jnp.bfloat16)

        mixed = lax.map(mb_block, block_ids).reshape(NH, NW, C)
        padded_mixed = jnp.pad(mixed, ((2, 2), (2, 2), (0, 0)))

        def heads_block(index, padded_mixed=padded_mixed, section=section):
            piece = lax.dynamic_slice_in_dim(padded_mixed, index * TH, TH + 4, 0)
            qkv = dense(piece, qkv_weight[section]).astype(jnp.bfloat16)
            return heads_of(qkv, aggregate_depth[section], aggregate_group[section], TH, NW, HEADS, HD)

        def summary_block(index):
            both = heads_block(index)
            keys = jax.nn.relu(both[:, :, :, 1, :]).astype(jnp.float32)
            values = both[:, :, :, 2, :].astype(jnp.float32)
            kv = jnp.einsum("rchd,rche->hde", keys, values, precision=lax.Precision.HIGHEST)
            return kv, jnp.sum(keys, axis=(0, 1))

        kv_parts, key_parts = lax.map(summary_block, block_ids)
        kv_all = jnp.sum(kv_parts, axis=0)
        key_all = jnp.sum(key_parts, axis=0)

        def apply_block(index, mixed=mixed, section=section, kv_all=kv_all, key_all=key_all):
            both = heads_block(index)
            queries = jax.nn.relu(both[:, :, :, 0, :]).astype(jnp.float32)
            numer = jnp.einsum("rchd,hde->rche", queries, kv_all, precision=lax.Precision.HIGHEST)
            denom = jnp.einsum("rchd,hd->rch", queries, key_all, precision=lax.Precision.HIGHEST)
            attended = (numer / (denom[..., None] + 1e-6)).astype(jnp.bfloat16).reshape(TH, NW, 2 * C)
            base = lax.dynamic_slice_in_dim(mixed, index * TH, TH, 0)
            return (base + dense(attended, output_weight[section]) + output_bias[section]).astype(jnp.bfloat16)

        current = lax.map(apply_block, block_ids).reshape(NH, NW, C)
    padded = jnp.pad(current, ((1, 1), (1, 1), (0, 0)))
    total = jnp.zeros((NH * NW, 4), jnp.float32)
    for offset_r in range(3):
        for offset_c in range(3):
            window = padded[offset_r:offset_r + NH, offset_c:offset_c + NW, :].reshape(NH * NW, C)
            total = total + jnp.dot(window, head_weight[offset_r, offset_c].T, preferred_element_type=jnp.float32)
    boxes = total.T.reshape(4, NH, NW) + head_bias[:, None, None]
    return current, boxes
```

```python
import jax
import jax.numpy as jnp
from jax import lax
from jax.sharding import PartitionSpec as P

SECTIONS = 2


def with_halo(cells, sides, width):
    for axis, dim in sides:
        count = lax.axis_size(axis)
        ends = count - 1
        head = lax.slice_in_dim(cells, 0, width, axis=dim)
        tail = lax.slice_in_dim(cells, cells.shape[dim] - width, cells.shape[dim], axis=dim)
        cells = jnp.concatenate(
            [
                lax.ppermute(tail, axis, [(i, (i + 1) % count) for i in range(ends)]),
                cells,
                lax.ppermute(head, axis, [((i + 1) % count, i) for i in range(ends)]),
            ],
            axis=dim,
        )
    return cells


def digits(size, most):
    radices = []
    while size > 1:
        radix = next((r for r in range(min(most, size), 1, -1) if size % r == 0), size)
        radices.append(radix)
        size //= radix
    return radices


def sum_by_permutes(value):
    for axis in ("row", "col"):
        count = lax.axis_size(axis)
        stride = 1
        for radix in digits(count, 4):
            total = value
            for step in range(1, radix):
                pairs = []
                for i in range(count):
                    digit = (i // stride) % radix
                    pairs.append((i, i + ((digit + step) % radix - digit) * stride))
                total = total + lax.ppermute(value, axis, pairs)
            value = total
            stride *= radix
    return value


def sum_by_all_to_all(value):
    axes = ("row", "col")
    count = lax.axis_size("row") * lax.axis_size("col")
    rows = value.shape[0]
    share = -(-rows // count)
    value = jnp.pad(value, ((0, share * count - rows), (0, 0)))
    pieces = lax.all_to_all(value.reshape(count, share, -1), axes, 0, 0, tiled=True)
    total = jnp.sum(pieces, axis=0, keepdims=True)
    spread = jnp.broadcast_to(total, pieces.shape)
    return lax.all_to_all(spread, axes, 0, 0, tiled=True).reshape(share * count, -1)[:rows]


def hard_swish(value):
    return value * jnp.minimum(jnp.maximum(value + 3.0, 0.0), 6.0) / 6.0


def depthwise(padded, weight, rows, cols):
    ksize = weight.shape[0]
    total = jnp.zeros((rows, cols, padded.shape[2]), jnp.float32)
    for offset_r in range(ksize):
        for offset_c in range(ksize):
            total = (
                total
                + padded[offset_r : offset_r + rows, offset_c : offset_c + cols, :].astype(
                    jnp.float32
                )
                * weight[offset_r, offset_c]
            )
    return total


def dense(values, weight):
    return lax.dot_general(
        values, weight, (((values.ndim - 1,), (0,)), ((), ())), preferred_element_type=jnp.float32
    )


def heads_of(padded_qkv, agg_depth, agg_group, rows, cols, heads, head_dim):
    center = padded_qkv[2 : 2 + rows, 2 : 2 + cols, :]
    spread = depthwise(padded_qkv, agg_depth, rows, cols).astype(jnp.bfloat16)
    grouped = jnp.einsum(
        "rcgd,gde->rcge",
        spread.reshape(rows, cols, 3 * heads, head_dim),
        agg_group,
        preferred_element_type=jnp.float32,
    ).astype(jnp.bfloat16)
    return jnp.concatenate(
        [
            center.reshape(rows, cols, heads, 3, head_dim),
            grouped.reshape(rows, cols, heads, 3, head_dim),
        ],
        axis=2,
    )


def local(
    features,
    expand_weight,
    expand_bias,
    depth_weight,
    depth_bias,
    project_weight,
    project_bias,
    qkv_weight,
    aggregate_depth,
    aggregate_group,
    output_weight,
    output_bias,
    head_weight,
    head_bias,
):
    rows, cols, width = features.shape
    head_dim = aggregate_group.shape[2]
    heads = width // head_dim
    current = features
    for section in range(SECTIONS):
        hidden = hard_swish(dense(current, expand_weight[section]) + expand_bias[section]).astype(
            jnp.bfloat16
        )
        hidden = with_halo(hidden, (("row", 0), ("col", 1)), 1)
        spread = hard_swish(
            depthwise(hidden, depth_weight[section], rows, cols) + depth_bias[section]
        ).astype(jnp.bfloat16)
        mixed = (current + dense(spread, project_weight[section]) + project_bias[section]).astype(
            jnp.bfloat16
        )
        local_qkv = dense(mixed, qkv_weight[section]).astype(jnp.bfloat16)
        padded_qkv = with_halo(local_qkv, (("row", 0), ("col", 1)), 2)
        both = heads_of(
            padded_qkv,
            aggregate_depth[section],
            aggregate_group[section],
            rows,
            cols,
            heads,
            head_dim,
        )
        queries = jax.nn.relu(both[:, :, :, 0, :]).astype(jnp.float32)
        keys = jax.nn.relu(both[:, :, :, 1, :]).astype(jnp.float32)
        values = both[:, :, :, 2, :].astype(jnp.float32)
        kv_local = jnp.einsum("rchd,rche->hde", keys, values, precision=lax.Precision.HIGHEST)
        key_local = jnp.sum(keys, axis=(0, 1))
        packed = jnp.concatenate([kv_local.reshape(-1, 128), key_local.reshape(-1, 128)], axis=0)
        packed = sum_by_permutes(packed) if section == 0 else sum_by_all_to_all(packed)
        cut = kv_local.size // 128
        kv_all = packed[:cut].reshape(kv_local.shape)
        key_all = packed[cut:].reshape(key_local.shape)
        numer = jnp.einsum("rchd,hde->rche", queries, kv_all, precision=lax.Precision.HIGHEST)
        denom = jnp.einsum("rchd,hd->rch", queries, key_all, precision=lax.Precision.HIGHEST)
        attended = (
            (numer / (denom[..., None] + 1e-06)).astype(jnp.bfloat16).reshape(rows, cols, 2 * width)
        )
        current = (mixed + dense(attended, output_weight[section]) + output_bias[section]).astype(
            jnp.bfloat16
        )
    padded = with_halo(current, (("row", 0), ("col", 1)), 1)
    boxes = jnp.zeros((4, rows, cols), jnp.float32)
    for offset_r in range(3):
        for offset_c in range(3):
            window = padded[offset_r : offset_r + rows, offset_c : offset_c + cols, :]
            boxes = boxes + lax.dot_general(
                head_weight[offset_r, offset_c],
                window,
                (((1,), (2,)), ((), ())),
                preferred_element_type=jnp.float32,
            )
    boxes = boxes + head_bias[:, None, None]
    return (current, boxes)


def solution(mesh):
    return jax.shard_map(
        local,
        mesh=mesh,
        in_specs=(
            P("row", "col", None),
            P(),
            P(),
            P(),
            P(),
            P(),
            P(),
            P(),
            P(),
            P(),
            P(),
            P(),
            P(),
            P(),
        ),
        out_specs=(P("row", "col", None), P(None, "row", "col")),
        check_vma=False,
    )
```

```python
import functools

import jax
import jax.numpy as jnp
from jax import lax
from jax.experimental import pallas as pl
from jax.experimental.pallas import tpu as pltpu
from jax.sharding import PartitionSpec as P

SECTIONS = 2
LANES = 128
SIDE = 8
REACH = 7
PAYLOAD_ROWS = 144
F32 = jnp.float32
BF16 = jnp.bfloat16


def hard_swish(value):
    return value * jnp.minimum(jnp.maximum(value * (1.0 / 6.0) + 0.5, 0.0), 1.0)


def clear_outside(ref, halo, cols):
    rows = ref.shape[0]
    row, col = lax.axis_index("row"), lax.axis_index("col")

    @pl.when(row == 0)
    def _():
        ref[0:halo] = jnp.zeros((halo,) + ref.shape[1:], ref.dtype)

    @pl.when(row == lax.axis_size("row") - 1)
    def _():
        ref[rows - halo : rows] = jnp.zeros((halo,) + ref.shape[1:], ref.dtype)

    @pl.when(col == 0)
    def _():
        ref[:, cols + SIDE : cols + 2 * SIDE, :] = jnp.zeros((rows, SIDE, ref.shape[2]), ref.dtype)

    @pl.when(col == lax.axis_size("col") - 1)
    def _():
        ref[:, cols : cols + SIDE, :] = jnp.zeros((rows, SIDE, ref.shape[2]), ref.dtype)


def flat(value):
    return value.reshape(-1, value.shape[-1])


def same_head(head_dim):
    across = lax.broadcasted_iota(jnp.int32, (LANES, LANES), 0) // head_dim
    along = lax.broadcasted_iota(jnp.int32, (LANES, LANES), 1) // head_dim
    return across == along


def front(x_ref, weights, outs, scratch, halo, tile, head_dim):
    expand, expand_bias, depth, depth_bias, project, project_bias, qkv_weight, agg, group = weights
    mixed_out, query_out, payload_out = outs
    hidden, spread, total, mixed, qkv, scaled = scratch
    rows, width, channels = x_ref.shape
    tile_rows, tile_cols = tile
    inner = rows - 2
    chunk = hidden.shape[2]
    x = flat(x_ref[...])

    def expanded(step, carry):
        at = pl.multiple_of(step * chunk, chunk)
        value = jnp.dot(x, expand[0, :, pl.ds(at, chunk)], preferred_element_type=F32)
        value = hard_swish(value + expand_bias[:, pl.ds(at, chunk)])
        hidden[...] = value.reshape(rows, width, chunk)
        clear_outside(hidden, halo, tile_cols)

        def one_row(r, carry):
            for lane in range(0, chunk, LANES):
                here = pl.ds(pl.multiple_of(at + lane, LANES), LANES)
                above, level, below = (hidden[r + a, :, lane : lane + LANES] for a in range(3))
                parts = [
                    above * depth[0, 0, b : b + 1, here]
                    + level * depth[0, 1, b : b + 1, here]
                    + below * depth[0, 2, b : b + 1, here]
                    for b in range(3)
                ]
                value = parts[1] + pltpu.roll(parts[0], 1, 0) + pltpu.roll(parts[2], width - 1, 0)
                value = hard_swish(value + depth_bias[:, here])
                spread[r, :, lane : lane + LANES] = value.astype(BF16)
            return carry

        lax.fori_loop(0, inner, one_row, 0)
        product = jnp.dot(
            flat(spread[...]), project[0, pl.ds(at, chunk), :], preferred_element_type=F32
        )

        @pl.when(step == 0)
        def _():
            total[...] = product

        @pl.when(step > 0)
        def _():
            total[...] += product

        return carry

    lax.fori_loop(0, expand.shape[2] // chunk, expanded, 0)
    value = total[...] + project_bias[...] + flat(x_ref[1 : rows - 1]).astype(F32)
    mixed[...] = value.astype(BF16).reshape(inner, width, channels)
    mixed_out[...] = mixed[2 : inner - 2]
    value = jnp.dot(flat(mixed[...]), qkv_weight[...], preferred_element_type=F32)
    qkv[...] = value.reshape(inner, width, 3 * channels)
    around = halo - 1
    clear_outside(qkv, around, tile_cols)

    def aggregated(kind, first, count):
        def one_row(r, carry):
            for lane in range(0, channels, LANES):
                here = slice(kind * channels + lane, kind * channels + lane + LANES)
                value = None
                for b in range(5):
                    part = None
                    for a in range(5):
                        term = qkv[first + r + a, :, here] * agg[5 * a + b : 5 * a + b + 1, here]
                        part = term if part is None else part + term
                    if b != 2:
                        part = pltpu.roll(part, (2 - b) % width, 0)
                    value = part if value is None else value + part
                scaled[r, :, lane : lane + LANES] = value.astype(BF16)
            return carry

        lax.fori_loop(0, count, one_row, 0)
        value = jnp.dot(flat(scaled[0:count]), group[kind], preferred_element_type=F32)
        return value.reshape(count, width, channels)

    outer = inner - 4
    query_out[:, :, 0:channels] = jnp.maximum(qkv[2 : inner - 2, :, 0:channels], 0.0).astype(BF16)
    query_out[:, :, channels : 2 * channels] = jnp.maximum(
        aggregated(0, 0, outer), 0.0
    ).astype(BF16)

    def own(value):
        return flat(value[:, 0:tile_cols, :])

    mine = slice(around, around + tile_rows)
    keys = [own(qkv[mine, :, channels : 2 * channels]), own(aggregated(1, around - 2, tile_rows))]
    values = [
        own(qkv[mine, :, 2 * channels : 3 * channels]),
        own(aggregated(2, around - 2, tile_rows)),
    ]
    same = same_head(head_dim)
    summary = jnp.zeros((LANES, LANES), F32)
    payload_out[LANES:PAYLOAD_ROWS, :] = jnp.zeros((PAYLOAD_ROWS - LANES, LANES), F32)
    index = 0
    for key, value in zip(keys, values):
        key = jnp.maximum(key, 0.0)
        sums = jnp.sum(key, axis=0, keepdims=True)
        key, value = key.astype(BF16), value.astype(BF16)
        for lane in range(0, channels, LANES):
            here = slice(lane, lane + LANES)
            product = lax.dot_general(
                key[:, here], value[:, here], (((0,), (0,)), ((), ())), preferred_element_type=F32
            )
            product = jnp.where(same, product, 0.0)
            if index:
                product = pltpu.roll(product, index * head_dim, 1)
            summary = summary + product
            payload_out[LANES + index : LANES + index + 1, :] = sums[:, here]
            index += 1
    payload_out[0:LANES, :] = summary


def attend(mixed_ref, query_ref, payload_ref, weight, bias, head_dim):
    query = flat(query_ref[...])
    same = same_head(head_dim)
    square = (LANES, LANES)
    diagonal = lax.broadcasted_iota(jnp.int32, square, 0) == lax.broadcasted_iota(
        jnp.int32, square, 1
    )
    ones = jnp.where(same, 1.0, 0.0).astype(BF16)
    packed = payload_ref[0:LANES, :]
    total = flat(mixed_ref[...]).astype(F32) + bias[...]
    for index in range(query.shape[1] // LANES):
        summary = packed if index == 0 else pltpu.roll(packed, LANES - index * head_dim, 1)
        summary = jnp.where(same, summary, 0.0).astype(BF16)
        sums = payload_ref[LANES + index : LANES + index + 1, :]
        sums = jnp.where(diagonal, sums, 0.0).astype(BF16)
        sums = jnp.dot(sums, ones, preferred_element_type=F32).astype(BF16)
        part = query[:, index * LANES : (index + 1) * LANES]
        numer = jnp.dot(part, summary, preferred_element_type=F32)
        denom = jnp.dot(part, sums, preferred_element_type=F32)
        attended = (numer / (denom + 1e-6)).astype(BF16)
        total = total + jnp.dot(
            attended, weight[0, index * LANES : (index + 1) * LANES, :], preferred_element_type=F32
        )
    return total


def first_kernel(tile, head_dim, own, top, bottom, right, left, *refs):
    weights, outs, scratch = refs[:9], refs[9:12], refs[12:]
    x_ref = scratch[0]
    rows, cols = tile
    x_ref[0:REACH, 0:cols, :] = top[...]
    x_ref[REACH : REACH + rows, 0:cols, :] = own[...]
    x_ref[REACH + rows :, 0:cols, :] = bottom[...]
    x_ref[:, cols : cols + 2 * SIDE, :] = jnp.concatenate([right[...], left[...]], axis=1)
    front(x_ref, weights, outs, scratch[1:], REACH, tile, head_dim)


def second_kernel(tile, head_dim, mixed, query, payload, out_weight, out_bias, *refs):
    weights, outs, scratch = refs[:9], refs[9:12], refs[12:]
    x_ref = scratch[0]
    value = attend(mixed, query, payload, out_weight, out_bias, head_dim)
    x_ref[...] = value.astype(BF16).reshape(x_ref.shape)
    front(x_ref, weights, outs, scratch[1:], REACH - 3, tile, head_dim)


def last_kernel(
    tile, head_dim, mixed, query, payload, out_weight, out_bias, head_weight, head_bias,
    map_out, boxes_out, x_ref,
):
    rows, cols = tile
    width = cols + 2 * SIDE
    value = attend(mixed, query, payload, out_weight, out_bias, head_dim)
    x_ref[...] = value.astype(BF16).reshape(x_ref.shape)
    clear_outside(x_ref, 1, cols)
    map_out[...] = x_ref[1 : 1 + rows, 0:cols, :]
    total = None
    for a in range(3):
        part = lax.dot_general(
            flat(x_ref[a : a + rows]), head_weight[a], (((1,), (1,)), ((), ())),
            preferred_element_type=F32,
        )
        total = part if total is None else total + part
    total = total.reshape(rows, width, LANES)
    lane = lax.broadcasted_iota(jnp.int32, (width, LANES), 1) // 4
    shifted = [
        jnp.where(
            lane == 0,
            pltpu.roll(total[r], 1, 0),
            jnp.where(lane == 2, pltpu.roll(total[r], width - 1, 0), total[r]),
        )
        for r in range(rows)
    ]
    shifted = jnp.concatenate(shifted, axis=0)
    across = lax.broadcasted_iota(jnp.int32, (8, LANES), 0)
    along = lax.broadcasted_iota(jnp.int32, (8, LANES), 1)
    fold = jnp.where((along % 4 == across) & (along < 12), 1.0, 0.0)
    boxes = lax.dot_general(
        fold, shifted, (((1,), (1,)), ((), ())), precision=lax.Precision.HIGHEST,
        preferred_element_type=F32,
    )
    boxes = boxes[0:4] + head_bias[...]
    for r in range(rows):
        boxes_out[:, r, :] = boxes[:, r * width : r * width + cols]


def section_spec(array, section):
    block = (1,) + array.shape[1:]
    return pl.BlockSpec(block, lambda step: (section,) + (0,) * (array.ndim - 1))


def whole_spec():
    return pl.BlockSpec(memory_space=pltpu.VMEM)


def digits(size, most):
    radices = []
    while size > 1:
        radix = next((r for r in range(min(most, size), 1, -1) if size % r == 0), size)
        radices.append(radix)
        size //= radix
    return radices


def sum_by_permutes(value):
    for axis in ("row", "col"):
        count = lax.axis_size(axis)
        stride = 1
        for radix in digits(count, 4):
            total = value
            sent = value.astype(BF16)
            for step in range(1, radix):
                pairs = []
                for i in range(count):
                    digit = (i // stride) % radix
                    pairs.append((i, i + ((digit + step) % radix - digit) * stride))
                total = total + lax.ppermute(sent, axis, pairs).astype(F32)
            value = total
            stride *= radix
    return value


def shift(value, axis, step):
    count = lax.axis_size(axis)
    pairs = [(i, i + step) for i in range(count) if 0 <= i + step < count]
    return lax.ppermute(value, axis, pairs)


def local(
    features,
    expand_weight,
    expand_bias,
    depth_weight,
    depth_bias,
    project_weight,
    project_bias,
    qkv_weight,
    aggregate_depth,
    aggregate_group,
    output_weight,
    output_bias,
    head_weight,
    head_bias,
):
    rows, cols, channels = features.shape
    head_dim = aggregate_group.shape[2]
    heads = channels // head_dim
    width = cols + 2 * SIDE
    tile = (rows, cols)
    wide = expand_weight.shape[2]

    top = shift(features[rows - REACH :], "row", 1)
    bottom = shift(features[:REACH], "row", -1)
    column = jnp.concatenate([top[:, -SIDE:], features[:, -SIDE:], bottom[:, -SIDE:]], axis=0)
    left = shift(column, "col", 1)
    column = jnp.concatenate([top[:, :SIDE], features[:, :SIDE], bottom[:, :SIDE]], axis=0)
    right = shift(column, "col", -1)

    def by_kind(array, axis):
        shape = array.shape[:axis] + (heads, 3, head_dim) + array.shape[axis + 1 :]
        return jnp.swapaxes(array.reshape(shape), axis, axis + 1).reshape(array.shape)

    qkv_weight = by_kind(qkv_weight, 2)
    aggregate_depth = by_kind(aggregate_depth, 3).reshape(SECTIONS, 25, 3 * channels)
    group = aggregate_group.reshape(SECTIONS, heads, 3, head_dim, head_dim).swapaxes(1, 2)
    group = (
        group[:, :, :, :, None, :] * jnp.eye(heads, dtype=BF16)[None, None, :, None, :, None]
    ).reshape(SECTIONS, 3, channels, channels)
    head_weight = jnp.pad(
        head_weight.reshape(3, 12, channels), ((0, 0), (0, LANES - 12), (0, 0))
    )

    def weights_of(section):
        arrays = [
            expand_weight, expand_bias[section : section + 1], depth_weight,
            depth_bias[section : section + 1], project_weight, project_bias[section : section + 1],
            qkv_weight[section], aggregate_depth[section], group[section],
        ]
        specs = [whole_spec()] * 9
        for index in (0, 2, 4):
            specs[index] = section_spec(arrays[index], section)
        return arrays, specs

    def outs_of(count):
        return [
            jax.ShapeDtypeStruct((count, width, channels), BF16),
            jax.ShapeDtypeStruct((count, width, 2 * channels), BF16),
            jax.ShapeDtypeStruct((PAYLOAD_ROWS, LANES), F32),
        ]

    def scratch_of(count):
        return [
            pltpu.VMEM((count, width, channels), BF16),
            pltpu.VMEM((count, width, 256), F32),
            pltpu.VMEM((count - 2, width, 256), BF16),
            pltpu.VMEM(((count - 2) * width, channels), F32),
            pltpu.VMEM((count - 2, width, channels), BF16),
            pltpu.VMEM((count - 2, width, 3 * channels), F32),
            pltpu.VMEM((count - 6, width, channels), BF16),
        ]

    params = pltpu.CompilerParams(vmem_limit_bytes=40 * 2**20)
    first_rows = rows + 2 * REACH
    arrays, specs = weights_of(0)
    mixed, query, payload = pl.pallas_call(
        functools.partial(first_kernel, tile, head_dim),
        out_shape=outs_of(first_rows - 6),
        grid=(1,),
        in_specs=[whole_spec()] * 5 + specs,
        out_specs=[whole_spec()] * 3,
        scratch_shapes=scratch_of(first_rows),
        compiler_params=params,
        name="first",
    )(features, top, bottom, right, left, *arrays)
    payload = sum_by_permutes(payload)

    second_rows = first_rows - 6
    arrays, specs = weights_of(1)
    mixed, query, payload = pl.pallas_call(
        functools.partial(second_kernel, tile, head_dim),
        out_shape=outs_of(second_rows - 6),
        grid=(1,),
        in_specs=[whole_spec()] * 3 + [section_spec(output_weight, 0), whole_spec()] + specs,
        out_specs=[whole_spec()] * 3,
        scratch_shapes=scratch_of(second_rows),
        compiler_params=params,
        name="second",
    )(mixed, query, payload, output_weight, output_bias[0:1], *arrays)
    payload = sum_by_permutes(payload)

    return pl.pallas_call(
        functools.partial(last_kernel, tile, head_dim),
        out_shape=[
            jax.ShapeDtypeStruct((rows, cols, channels), BF16),
            jax.ShapeDtypeStruct((4, rows, cols), F32),
        ],
        grid=(1,),
        in_specs=[whole_spec()] * 3 + [section_spec(output_weight, 1)] + [whole_spec()] * 3,
        out_specs=[whole_spec()] * 2,
        scratch_shapes=[pltpu.VMEM((rows + 2, width, channels), BF16)],
        compiler_params=params,
        name="last",
    )(
        mixed, query, payload, output_weight, output_bias[1:2], head_weight, head_bias.reshape(4, 1)
    )


def solution(mesh):
    return jax.shard_map(
        local,
        mesh=mesh,
        in_specs=(P("row", "col", None),) + (P(),) * 13,
        out_specs=(P("row", "col", None), P(None, "row", "col")),
        check_vma=False,
    )
```

```python
import functools

import jax
import jax.numpy as jnp
from jax import lax
from jax.experimental import pallas as pl
from jax.experimental.pallas import tpu as pltpu
from jax.sharding import PartitionSpec as P

SECTIONS = 2
LANES = 128
SIDE = 8
REACH = 7
KEY_ROWS = 16
F32 = jnp.float32
BF16 = jnp.bfloat16


def hard_swish(value):
    return value * jnp.minimum(jnp.maximum(value * (1.0 / 6.0) + 0.5, 0.0), 1.0)


def clear_outside(ref, halo, cols):
    rows = ref.shape[0]
    row, col = lax.axis_index("row"), lax.axis_index("col")

    @pl.when(row == 0)
    def _():
        ref[0:halo] = jnp.zeros((halo,) + ref.shape[1:], ref.dtype)

    @pl.when(row == lax.axis_size("row") - 1)
    def _():
        ref[rows - halo : rows] = jnp.zeros((halo,) + ref.shape[1:], ref.dtype)

    @pl.when(col == 0)
    def _():
        ref[:, cols + SIDE : cols + 2 * SIDE, :] = jnp.zeros((rows, SIDE, ref.shape[2]), ref.dtype)

    @pl.when(col == lax.axis_size("col") - 1)
    def _():
        ref[:, cols : cols + SIDE, :] = jnp.zeros((rows, SIDE, ref.shape[2]), ref.dtype)


def flat(value):
    return value.reshape(-1, value.shape[-1])


def same_head(head_dim):
    across = lax.broadcasted_iota(jnp.int32, (LANES, LANES), 0) // head_dim
    along = lax.broadcasted_iota(jnp.int32, (LANES, LANES), 1) // head_dim
    return across == along


def front(x_ref, weights, outs, scratch, halo, tile, head_dim, section):
    expand, expand_bias, depth, depth_bias, project, project_bias, qkv_weight, agg, group = weights
    mixed_out, query_out, payload_out = outs
    hidden, spread, total, mixed, qkv, scaled = scratch
    rows, width, channels = x_ref.shape
    tile_rows, tile_cols = tile
    inner = rows - 2
    chunk = hidden.shape[2]
    x = flat(x_ref[...])

    def expanded(step, carry):
        at = pl.multiple_of(step * chunk, chunk)
        value = jnp.dot(x, expand[0, :, pl.ds(at, chunk)], preferred_element_type=F32)
        value = hard_swish(value + expand_bias[section : section + 1, pl.ds(at, chunk)])
        hidden[...] = value.reshape(rows, width, chunk)
        clear_outside(hidden, halo, tile_cols)

        def one_row(r, carry):
            for lane in range(0, chunk, LANES):
                here = pl.ds(pl.multiple_of(at + lane, LANES), LANES)
                above, level, below = (hidden[r + a, :, lane : lane + LANES] for a in range(3))
                parts = [
                    above * depth[0, b, section : section + 1, here]
                    + level * depth[1, b, section : section + 1, here]
                    + below * depth[2, b, section : section + 1, here]
                    for b in range(3)
                ]
                value = parts[1] + pltpu.roll(parts[0], 1, 0) + pltpu.roll(parts[2], width - 1, 0)
                value = hard_swish(value + depth_bias[section : section + 1, here])
                spread[r, :, lane : lane + LANES] = value.astype(BF16)
            return carry

        lax.fori_loop(0, inner, one_row, 0)
        product = jnp.dot(
            flat(spread[...]), project[0, pl.ds(at, chunk), :], preferred_element_type=F32
        )

        @pl.when(step == 0)
        def _():
            total[...] = product

        @pl.when(step > 0)
        def _():
            total[...] += product

        return carry

    lax.fori_loop(0, expand.shape[2] // chunk, expanded, 0)
    value = total[...] + project_bias[section : section + 1, :] + flat(x_ref[1 : rows - 1]).astype(F32)
    mixed[...] = value.astype(BF16).reshape(inner, width, channels)
    mixed_out[...] = mixed[2 : inner - 2]
    value = jnp.dot(flat(mixed[...]), qkv_weight[section], preferred_element_type=F32)
    qkv[...] = value.reshape(inner, width, 3 * channels)
    around = halo - 1
    clear_outside(qkv, around, tile_cols)

    def aggregated(kind, first, count):
        def one_row(r, carry):
            for lane in range(0, channels, LANES):
                here = slice(kind * channels + lane, kind * channels + lane + LANES)
                value = None
                for b in range(5):
                    part = None
                    for a in range(5):
                        term = qkv[first + r + a, :, here] * agg[tap(section, a, b), here]
                        part = term if part is None else part + term
                    if b != 2:
                        part = pltpu.roll(part, (2 - b) % width, 0)
                    value = part if value is None else value + part
                scaled[r, :, lane : lane + LANES] = value.astype(BF16)
            return carry

        lax.fori_loop(0, count, one_row, 0)
        value = jnp.dot(flat(scaled[0:count]), group[section, kind], preferred_element_type=F32)
        return value.reshape(count, width, channels)

    outer = inner - 4
    query_out[:, :, 0:channels] = jnp.maximum(qkv[2 : inner - 2, :, 0:channels], 0.0).astype(BF16)
    query_out[:, :, channels : 2 * channels] = jnp.maximum(
        aggregated(0, 0, outer), 0.0
    ).astype(BF16)

    def own(value):
        return flat(value[:, 0:tile_cols, :])

    mine = slice(around, around + tile_rows)
    keys = [own(qkv[mine, :, channels : 2 * channels]), own(aggregated(1, around - 2, tile_rows))]
    values = [
        own(qkv[mine, :, 2 * channels : 3 * channels]),
        own(aggregated(2, around - 2, tile_rows)),
    ]
    same = same_head(head_dim)
    summary = jnp.zeros((LANES, LANES), F32)
    key_sums = []
    index = 0
    for key, value in zip(keys, values):
        key = jnp.maximum(key, 0.0)
        sums = jnp.sum(key, axis=0, keepdims=True)
        key, value = key.astype(BF16), value.astype(BF16)
        for lane in range(0, channels, LANES):
            here = slice(lane, lane + LANES)
            product = lax.dot_general(
                key[:, here], value[:, here], (((0,), (0,)), ((), ())), preferred_element_type=F32
            )
            product = jnp.where(same, product, 0.0)
            if index:
                product = pltpu.roll(product, index * head_dim, 1)
            summary = summary + product
            key_sums.append(sums[:, here])
            index += 1
    key_sums = jnp.concatenate(
        key_sums + [jnp.zeros((KEY_ROWS - index, LANES), F32)], axis=0
    )
    payload_out[0:LANES, :] = summary.astype(BF16)
    payload_out[LANES : LANES + KEY_ROWS, :] = key_sums.astype(BF16)
    rest = payload_out.shape[0] - LANES - KEY_ROWS
    if rest:
        payload_out[LANES + KEY_ROWS :, :] = jnp.zeros((rest, LANES), BF16)


def attend(mixed_ref, query_ref, payload_ref, weight, bias, head_dim, section):
    query = flat(query_ref[...])
    same = same_head(head_dim)
    square = (LANES, LANES)
    diagonal = lax.broadcasted_iota(jnp.int32, square, 0) == lax.broadcasted_iota(
        jnp.int32, square, 1
    )
    ones = jnp.where(same, 1.0, 0.0).astype(BF16)
    payload = payload_ref[0].astype(F32)
    for part in range(1, payload_ref.shape[0]):
        payload = payload + payload_ref[part].astype(F32)
    packed = payload[0:LANES]
    total = flat(mixed_ref[...]).astype(F32) + bias[section : section + 1, :]
    for index in range(query.shape[1] // LANES):
        summary = packed if index == 0 else pltpu.roll(packed, LANES - index * head_dim, 1)
        summary = jnp.where(same, summary, 0.0).astype(BF16)
        sums = payload[LANES + index : LANES + index + 1]
        sums = jnp.where(diagonal, sums, 0.0).astype(BF16)
        sums = jnp.dot(sums, ones, preferred_element_type=F32).astype(BF16)
        part = query[:, index * LANES : (index + 1) * LANES]
        numer = jnp.dot(part, summary, preferred_element_type=F32)
        denom = jnp.dot(part, sums, preferred_element_type=F32)
        attended = (numer / (denom + 1e-6)).astype(BF16)
        total = total + jnp.dot(
            attended, weight[0, index * LANES : (index + 1) * LANES, :], preferred_element_type=F32
        )
    return total


def tap(section, a, b):
    at = 32 * section + 5 * a + b
    return slice(at, at + 1)


def prepare_kernel(head_dim, qkv, agg, group, head, qkv_out, agg_out, group_out, head_out, taps):
    sections, channels, wide = qkv.shape
    half = 3 * LANES
    heads = LANES // head_dim
    src = lax.broadcasted_iota(jnp.int32, (half, LANES), 0)
    dst = lax.broadcasted_iota(jnp.int32, (half, LANES), 1)
    first = (dst // head_dim) * 3 * head_dim + dst % head_dim
    picks = [jnp.where(src == first + k * head_dim, 1.0, 0.0).astype(BF16) for k in range(3)]
    taps[...] = jnp.zeros(taps.shape, F32)
    for section in range(sections):
        for a in range(5):
            for b in range(5):
                taps[tap(section, a, b), :] = agg[a, b, section : section + 1, :]
    rest = taps[...]
    high = rest.astype(BF16)
    rest = rest - high.astype(F32)
    middle = rest.astype(BF16)
    low = (rest - middle.astype(F32)).astype(BF16)
    split = jnp.concatenate([high, middle, low], axis=0)
    count = taps.shape[0]
    weights = qkv[...].reshape(sections * channels, wide)
    for part in range(wide // half):
        here = slice(part * half, (part + 1) * half)
        for kind in range(3):
            to = kind * channels + part * LANES
            there = slice(to, to + LANES)
            value = jnp.dot(weights[:, here], picks[kind], preferred_element_type=F32)
            qkv_out[:, :, there] = value.astype(BF16).reshape(sections, channels, LANES)
            value = jnp.dot(split[:, here], picks[kind], preferred_element_type=F32)
            agg_out[:, there] = value[:count] + value[count : 2 * count] + value[2 * count :]
    row = lax.broadcasted_iota(jnp.int32, (head_dim, channels), 0)
    lane = lax.broadcasted_iota(jnp.int32, (head_dim, channels), 1)
    spread = jnp.where(lane % head_dim == row, 1.0, 0.0).astype(BF16)
    across = lax.broadcasted_iota(jnp.int32, (channels, channels), 0) // head_dim
    along = lax.broadcasted_iota(jnp.int32, (channels, channels), 1) // head_dim
    for section in range(sections):
        for kind in range(3):
            tall = [group[section, 3 * h + kind] for h in range(channels // head_dim)]
            value = jnp.dot(jnp.concatenate(tall, axis=0), spread, preferred_element_type=F32)
            group_out[section, kind] = jnp.where(across == along, value, 0.0).astype(BF16)
    head_out[...] = jnp.zeros(head_out.shape, BF16)
    for a in range(3):
        rows = [head[a, b] for b in range(3)] + [jnp.zeros((4, channels), BF16)]
        head_out[a, 0:16, :] = jnp.concatenate(rows, axis=0)


def first_kernel(tile, head_dim, own, top, bottom, right, left, *refs):
    weights, outs, scratch = refs[:9], refs[9:12], refs[12:]
    x_ref = scratch[0]
    rows, cols = tile
    x_ref[0:REACH, 0:cols, :] = top[...]
    x_ref[REACH : REACH + rows, 0:cols, :] = own[...]
    x_ref[REACH + rows :, 0:cols, :] = bottom[...]
    x_ref[:, cols : cols + 2 * SIDE, :] = jnp.concatenate([right[...], left[...]], axis=1)
    front(x_ref, weights, outs, scratch[1:], REACH, tile, head_dim, 0)


def second_kernel(tile, head_dim, mixed, query, payload, out_weight, out_bias, *refs):
    weights, outs, scratch = refs[:9], refs[9:12], refs[12:]
    x_ref = scratch[0]
    value = attend(mixed, query, payload, out_weight, out_bias, head_dim, 0)
    x_ref[...] = value.astype(BF16).reshape(x_ref.shape)
    front(x_ref, weights, outs, scratch[1:], REACH - 3, tile, head_dim, 1)


def last_kernel(
    tile, head_dim, mixed, query, payload, out_weight, out_bias, head_weight, head_bias,
    map_out, boxes_out, x_ref,
):
    rows, cols = tile
    width = cols + 2 * SIDE
    value = attend(mixed, query, payload, out_weight, out_bias, head_dim, 1)
    x_ref[...] = value.astype(BF16).reshape(x_ref.shape)
    clear_outside(x_ref, 1, cols)
    map_out[...] = x_ref[1 : 1 + rows, 0:cols, :]
    total = None
    for a in range(3):
        part = lax.dot_general(
            flat(x_ref[a : a + rows]), head_weight[a], (((1,), (1,)), ((), ())),
            preferred_element_type=F32,
        )
        total = part if total is None else total + part
    total = total.reshape(rows, width, LANES)
    lane = lax.broadcasted_iota(jnp.int32, (width, LANES), 1) // 4
    shifted = [
        jnp.where(
            lane == 0,
            pltpu.roll(total[r], 1, 0),
            jnp.where(lane == 2, pltpu.roll(total[r], width - 1, 0), total[r]),
        )
        for r in range(rows)
    ]
    shifted = jnp.concatenate(shifted, axis=0)
    across = lax.broadcasted_iota(jnp.int32, (8, LANES), 0)
    along = lax.broadcasted_iota(jnp.int32, (8, LANES), 1)
    fold = jnp.where((along % 4 == across) & (along < 12), 1.0, 0.0)
    boxes = lax.dot_general(
        fold, shifted, (((1,), (1,)), ((), ())), precision=lax.Precision.HIGHEST,
        preferred_element_type=F32,
    )
    boxes = boxes[0:4] + head_bias[...]
    for r in range(rows):
        boxes_out[:, r, :] = boxes[:, r * width : r * width + cols]


def section_spec(array, section):
    block = (1,) + array.shape[1:]
    return pl.BlockSpec(block, lambda step: (section,) + (0,) * (array.ndim - 1))


def whole_spec():
    return pl.BlockSpec(memory_space=pltpu.VMEM)


def digits(size, most):
    radices = []
    while size > 1:
        radix = next((r for r in range(min(most, size), 1, -1) if size % r == 0), size)
        radices.append(radix)
        size //= radix
    return radices


def exchanged(pieces, axis):
    return lax.all_to_all(pieces, axis, 0, 0, tiled=True)


def copies(value, axis):
    return jnp.broadcast_to(value[None], (lax.axis_size(axis),) + value.shape)


def added(pieces):
    return jnp.sum(pieces.astype(F32), axis=0).astype(BF16)


def sum_whole(payload):
    payload = added(exchanged(copies(payload, "row"), "row"))
    return exchanged(copies(payload, "col"), "col")


def sum_in_shares(payload):
    count = lax.axis_size("row")
    pieces = exchanged(payload.reshape(count, -1, LANES), "row")
    pieces = exchanged(copies(added(pieces), "col"), "col")
    pieces = exchanged(copies(added(pieces), "row"), "row")
    return pieces.reshape(1, -1, LANES)


def shift(value, axis, step):
    count = lax.axis_size(axis)
    pairs = [(i, i + step) for i in range(count) if 0 <= i + step < count]
    return lax.ppermute(value, axis, pairs)


def local(
    features,
    expand_weight,
    expand_bias,
    depth_weight,
    depth_bias,
    project_weight,
    project_bias,
    qkv_weight,
    aggregate_depth,
    aggregate_group,
    output_weight,
    output_bias,
    head_weight,
    head_bias,
):
    rows, cols, channels = features.shape
    head_dim = aggregate_group.shape[2]
    heads = channels // head_dim
    width = cols + 2 * SIDE
    tile = (rows, cols)
    wide = expand_weight.shape[2]

    top = shift(features[rows - REACH :], "row", 1)
    bottom = shift(features[:REACH], "row", -1)
    column = jnp.concatenate([top[:, -SIDE:], features[:, -SIDE:], bottom[:, -SIDE:]], axis=0)
    left = shift(column, "col", 1)
    column = jnp.concatenate([top[:, :SIDE], features[:, :SIDE], bottom[:, :SIDE]], axis=0)
    right = shift(column, "col", -1)

    aggregate_depth = aggregate_depth.transpose(1, 2, 0, 3)
    depth_weight = depth_weight.transpose(1, 2, 0, 3)
    params = pltpu.CompilerParams(vmem_limit_bytes=24 * 2**20)
    qkv_weight, taps, group, head_weight = pl.pallas_call(
        functools.partial(prepare_kernel, head_dim),
        out_shape=[
            jax.ShapeDtypeStruct(qkv_weight.shape, BF16),
            jax.ShapeDtypeStruct((32 * SECTIONS, 3 * channels), F32),
            jax.ShapeDtypeStruct((SECTIONS, 3, channels, channels), BF16),
            jax.ShapeDtypeStruct((3, LANES, channels), BF16),
        ],
        grid=(1,),
        in_specs=[whole_spec()] * 4,
        out_specs=[whole_spec()] * 4,
        scratch_shapes=[pltpu.VMEM((32 * SECTIONS, 3 * channels), F32)],
        compiler_params=params,
        cost_estimate=pl.CostEstimate(
            flops=2 * 10**9, bytes_accessed=4 * 10**6, transcendentals=0
        ),
        name="prepare",
    )(qkv_weight, aggregate_depth, aggregate_group, head_weight)

    def weights_of(section):
        arrays = [
            expand_weight, expand_bias, depth_weight, depth_bias, project_weight, project_bias,
            qkv_weight, taps, group,
        ]
        specs = [whole_spec()] * 9
        for index in (0, 4):
            specs[index] = section_spec(arrays[index], section)
        return arrays, specs

    def outs_of(count, payload_rows):
        return [
            jax.ShapeDtypeStruct((count, width, channels), BF16),
            jax.ShapeDtypeStruct((count, width, 2 * channels), BF16),
            jax.ShapeDtypeStruct((payload_rows, LANES), BF16),
        ]

    def scratch_of(count):
        return [
            pltpu.VMEM((count, width, channels), BF16),
            pltpu.VMEM((count, width, 256), F32),
            pltpu.VMEM((count - 2, width, 256), BF16),
            pltpu.VMEM(((count - 2) * width, channels), F32),
            pltpu.VMEM((count - 2, width, channels), BF16),
            pltpu.VMEM((count - 2, width, 3 * channels), F32),
            pltpu.VMEM((count - 6, width, channels), BF16),
        ]

    shares = lax.axis_size("row")
    share_rows = -(-(LANES + KEY_ROWS) // (16 * shares)) * 16
    first_rows = rows + 2 * REACH
    arrays, specs = weights_of(0)
    mixed, query, payload = pl.pallas_call(
        functools.partial(first_kernel, tile, head_dim),
        out_shape=outs_of(first_rows - 6, LANES + KEY_ROWS),
        grid=(1,),
        in_specs=[whole_spec()] * 5 + specs,
        out_specs=[whole_spec()] * 3,
        scratch_shapes=scratch_of(first_rows),
        compiler_params=params,
        name="first",
    )(features, top, bottom, right, left, *arrays)
    payload = sum_whole(payload)

    second_rows = first_rows - 6
    arrays, specs = weights_of(1)
    mixed, query, payload = pl.pallas_call(
        functools.partial(second_kernel, tile, head_dim),
        out_shape=outs_of(second_rows - 6, share_rows * shares),
        grid=(1,),
        in_specs=[whole_spec()] * 3 + [section_spec(output_weight, 0), whole_spec()] + specs,
        out_specs=[whole_spec()] * 3,
        scratch_shapes=scratch_of(second_rows),
        compiler_params=params,
        name="second",
    )(mixed, query, payload, output_weight, output_bias, *arrays)
    payload = sum_in_shares(payload)

    return pl.pallas_call(
        functools.partial(last_kernel, tile, head_dim),
        out_shape=[
            jax.ShapeDtypeStruct((rows, cols, channels), BF16),
            jax.ShapeDtypeStruct((4, rows, cols), F32),
        ],
        grid=(1,),
        in_specs=[whole_spec()] * 3 + [section_spec(output_weight, 1)] + [whole_spec()] * 3,
        out_specs=[whole_spec()] * 2,
        scratch_shapes=[pltpu.VMEM((rows + 2, width, channels), BF16)],
        compiler_params=params,
        name="last",
    )(
        mixed, query, payload, output_weight, output_bias, head_weight, head_bias.reshape(4, 1)
    )


def solution(mesh):
    return jax.shard_map(
        local,
        mesh=mesh,
        in_specs=(P("row", "col", None),) + (P(),) * 13,
        out_specs=(P("row", "col", None), P(None, "row", "col")),
        check_vma=False,
    )
```

```python
import functools

import jax
import jax.numpy as jnp
from jax import lax
from jax.experimental import pallas as pl
from jax.experimental.pallas import tpu as pltpu
from jax.sharding import PartitionSpec as P

SECTIONS = 2
LANES = 128
SIDE = 8
REACH = 7
KEY_ROWS = 16
F32 = jnp.float32
BF16 = jnp.bfloat16


def hard_swish(value):
    return value * jnp.minimum(jnp.maximum(value * (1.0 / 6.0) + 0.5, 0.0), 1.0)


def clear_outside(ref, halo, cols):
    rows = ref.shape[0]
    row, col = lax.axis_index("row"), lax.axis_index("col")

    @pl.when(row == 0)
    def _():
        ref[0:halo] = jnp.zeros((halo,) + ref.shape[1:], ref.dtype)

    @pl.when(row == lax.axis_size("row") - 1)
    def _():
        ref[rows - halo : rows] = jnp.zeros((halo,) + ref.shape[1:], ref.dtype)

    @pl.when(col == 0)
    def _():
        ref[:, cols + SIDE : cols + 2 * SIDE, :] = jnp.zeros((rows, SIDE, ref.shape[2]), ref.dtype)

    @pl.when(col == lax.axis_size("col") - 1)
    def _():
        ref[:, cols : cols + SIDE, :] = jnp.zeros((rows, SIDE, ref.shape[2]), ref.dtype)


def grouped_loop(count, most, body):
    size = next(n for n in range(min(most, count), 0, -1) if count % n == 0)

    def group(index, carry):
        for r in range(size):
            body(index * size + r)
        return carry

    lax.fori_loop(0, count // size, group, 0)


def flat(value):
    return value.reshape(-1, value.shape[-1])


def same_head(head_dim):
    across = lax.broadcasted_iota(jnp.int32, (LANES, LANES), 0) // head_dim
    along = lax.broadcasted_iota(jnp.int32, (LANES, LANES), 1) // head_dim
    return across == along


def front(x_ref, weights, outs, scratch, halo, tile, head_dim, section):
    expand, expand_bias, depth, depth_bias, project, project_bias = weights[:6]
    mixed_out, query_out, payload_out = outs
    hidden, spread, total, mixed, qkv, scaled, query, qkv_weight, agg, group, sems = scratch
    loads = [
        pltpu.make_async_copy(weights[6].at[section], qkv_weight, sems.at[0]),
        pltpu.make_async_copy(weights[7].at[section], agg, sems.at[1]),
        pltpu.make_async_copy(weights[8].at[section], group, sems.at[2]),
    ]
    for load in loads:
        load.start()
    rows, width, channels = x_ref.shape
    tile_rows, tile_cols = tile
    inner = rows - 2
    chunk = hidden.shape[2]
    x = flat(x_ref[...])

    def expanded(step, carry):
        at = pl.multiple_of(step * chunk, chunk)
        value = jnp.dot(x, expand[section, :, pl.ds(at, chunk)], preferred_element_type=F32)
        value = hard_swish(value + expand_bias[section : section + 1, pl.ds(at, chunk)])
        hidden[...] = value.reshape(rows, width, chunk)
        clear_outside(hidden, halo, tile_cols)

        def one_row(r):
            for lane in range(0, chunk, LANES):
                here = pl.ds(pl.multiple_of(at + lane, LANES), LANES)
                above, level, below = (hidden[r + a, :, lane : lane + LANES] for a in range(3))
                parts = [
                    above * depth[0, b, section : section + 1, here]
                    + level * depth[1, b, section : section + 1, here]
                    + below * depth[2, b, section : section + 1, here]
                    for b in range(3)
                ]
                value = parts[1] + pltpu.roll(parts[0], 1, 0) + pltpu.roll(parts[2], width - 1, 0)
                value = hard_swish(value + depth_bias[section : section + 1, here])
                spread[r, :, lane : lane + LANES] = value.astype(BF16)

        grouped_loop(inner, 7, one_row)
        product = jnp.dot(
            flat(spread[...]), project[section, pl.ds(at, chunk), :], preferred_element_type=F32
        )

        @pl.when(step == 0)
        def _():
            total[...] = product

        @pl.when(step > 0)
        def _():
            total[...] += product

        return carry

    lax.fori_loop(0, expand.shape[2] // chunk, expanded, 0)
    value = total[...] + project_bias[section : section + 1, :] + flat(x_ref[1 : rows - 1]).astype(F32)
    mixed[...] = value.astype(BF16).reshape(inner, width, channels)
    outer = inner - 4
    stores = [
        pltpu.make_async_copy(mixed.at[pl.ds(2, outer)], mixed_out, sems.at[3]),
        pltpu.make_async_copy(query, query_out, sems.at[4]),
    ]
    stores[0].start()
    for load in loads:
        load.wait()
    value = jnp.dot(flat(mixed[...]), qkv_weight[...], preferred_element_type=F32)
    qkv[...] = value.reshape(inner, width, 3 * channels)
    around = halo - 1
    clear_outside(qkv, around, tile_cols)

    def aggregated(kind, first, count):
        def one_row(r):
            for lane in range(0, channels, LANES):
                here = slice(kind * channels + lane, kind * channels + lane + LANES)
                value = None
                for b in range(5):
                    part = None
                    for a in range(5):
                        term = qkv[first + r + a, :, here] * agg[5 * a + b : 5 * a + b + 1, here]
                        part = term if part is None else part + term
                    if b != 2:
                        part = pltpu.roll(part, (2 - b) % width, 0)
                    value = part if value is None else value + part
                scaled[r, :, lane : lane + LANES] = value.astype(BF16)

        grouped_loop(count, 5, one_row)
        value = jnp.dot(flat(scaled[0:count]), group[kind], preferred_element_type=F32)
        return value.reshape(count, width, channels)

    query[:, :, 0:channels] = jnp.maximum(qkv[2 : inner - 2, :, 0:channels], 0.0).astype(BF16)
    query[:, :, channels : 2 * channels] = jnp.maximum(
        aggregated(0, 0, outer), 0.0
    ).astype(BF16)

    stores[1].start()

    def own(value):
        return flat(value[:, 0:tile_cols, :])

    mine = slice(around, around + tile_rows)
    keys = [own(qkv[mine, :, channels : 2 * channels]), own(aggregated(1, around - 2, tile_rows))]
    values = [
        own(qkv[mine, :, 2 * channels : 3 * channels]),
        own(aggregated(2, around - 2, tile_rows)),
    ]
    same = same_head(head_dim)
    summary = jnp.zeros((LANES, LANES), F32)
    key_sums = []
    index = 0
    for key, value in zip(keys, values):
        key = jnp.maximum(key, 0.0)
        sums = jnp.sum(key, axis=0, keepdims=True)
        key, value = key.astype(BF16), value.astype(BF16)
        for lane in range(0, channels, LANES):
            here = slice(lane, lane + LANES)
            product = lax.dot_general(
                key[:, here], value[:, here], (((0,), (0,)), ((), ())), preferred_element_type=F32
            )
            product = jnp.where(same, product, 0.0)
            if index:
                product = pltpu.roll(product, index * head_dim, 1)
            summary = summary + product
            key_sums.append(sums[:, here])
            index += 1
    key_sums = jnp.concatenate(
        key_sums + [jnp.zeros((KEY_ROWS - index, LANES), F32)], axis=0
    )
    payload_out[0:LANES, :] = summary.astype(BF16)
    payload_out[LANES : LANES + KEY_ROWS, :] = key_sums.astype(BF16)
    for store in stores:
        store.wait()


def attend(
    mixed_in, query_in, payloads, weight, bias, mixed_ref, query_ref, sems, head_dim, section
):
    loads = [
        pltpu.make_async_copy(query_in, query_ref, sems.at[0]),
        pltpu.make_async_copy(mixed_in, mixed_ref, sems.at[1]),
    ]
    for load in loads:
        load.start()
    same = same_head(head_dim)
    square = (LANES, LANES)
    diagonal = lax.broadcasted_iota(jnp.int32, square, 0) == lax.broadcasted_iota(
        jnp.int32, square, 1
    )
    ones = jnp.where(same, 1.0, 0.0).astype(BF16)
    payload = payloads[0][...].astype(F32)
    for part in payloads[1:]:
        payload = payload + part[...].astype(F32)
    packed = payload[0:LANES]
    for load in loads:
        load.wait()
    query = flat(query_ref[...])
    total = flat(mixed_ref[...]).astype(F32) + bias[section : section + 1, :]
    for index in range(query.shape[1] // LANES):
        summary = packed if index == 0 else pltpu.roll(packed, LANES - index * head_dim, 1)
        summary = jnp.where(same, summary, 0.0).astype(BF16)
        sums = payload[LANES + index : LANES + index + 1]
        sums = jnp.where(diagonal, sums, 0.0).astype(BF16)
        sums = jnp.dot(sums, ones, preferred_element_type=F32).astype(BF16)
        part = query[:, index * LANES : (index + 1) * LANES]
        numer = jnp.dot(part, summary, preferred_element_type=F32)
        denom = jnp.dot(part, sums, preferred_element_type=F32)
        attended = (numer / (denom + 1e-6)).astype(BF16)
        total = total + jnp.dot(
            attended, weight[section, index * LANES : (index + 1) * LANES, :], preferred_element_type=F32
        )
    return total


def tap(section, a, b):
    at = 32 * section + 5 * a + b
    return slice(at, at + 1)


def prepare_kernel(head_dim, qkv, agg, group, head, *refs):
    outs, made, taps, sems = refs[:4], refs[4:8], refs[8], refs[9]
    qkv_out, agg_out, group_out, head_out = made
    sections, channels, wide = qkv.shape
    half = 3 * LANES
    heads = LANES // head_dim
    src = lax.broadcasted_iota(jnp.int32, (half, LANES), 0)
    dst = lax.broadcasted_iota(jnp.int32, (half, LANES), 1)
    first = (dst // head_dim) * 3 * head_dim + dst % head_dim
    picks = [jnp.where(src == first + k * head_dim, 1.0, 0.0).astype(BF16) for k in range(3)]
    taps[...] = jnp.zeros(taps.shape, F32)
    for section in range(sections):
        for a in range(5):
            for b in range(5):
                taps[tap(section, a, b), :] = agg[a, b, section : section + 1, :]
    rest = taps[...]
    high = rest.astype(BF16)
    rest = rest - high.astype(F32)
    middle = rest.astype(BF16)
    low = (rest - middle.astype(F32)).astype(BF16)
    split = jnp.concatenate([high, middle, low], axis=0)
    count = taps.shape[0]
    weights = qkv[...].reshape(sections * channels, wide)
    for part in range(wide // half):
        here = slice(part * half, (part + 1) * half)
        for kind in range(3):
            to = kind * channels + part * LANES
            there = slice(to, to + LANES)
            value = jnp.dot(weights[:, here], picks[kind], preferred_element_type=F32)
            qkv_out[:, :, there] = value.astype(BF16).reshape(sections, channels, LANES)
            value = jnp.dot(split[:, here], picks[kind], preferred_element_type=F32)
            value = value[:count] + value[count : 2 * count] + value[2 * count :]
            agg_out[:, :, there] = value.reshape(sections, -1, LANES)
    row = lax.broadcasted_iota(jnp.int32, (head_dim, channels), 0)
    lane = lax.broadcasted_iota(jnp.int32, (head_dim, channels), 1)
    spread = jnp.where(lane % head_dim == row, 1.0, 0.0).astype(BF16)
    across = lax.broadcasted_iota(jnp.int32, (channels, channels), 0) // head_dim
    along = lax.broadcasted_iota(jnp.int32, (channels, channels), 1) // head_dim
    for section in range(sections):
        for kind in range(3):
            tall = [group[section, 3 * h + kind] for h in range(channels // head_dim)]
            value = jnp.dot(jnp.concatenate(tall, axis=0), spread, preferred_element_type=F32)
            group_out[section, kind] = jnp.where(across == along, value, 0.0).astype(BF16)
    head_out[...] = jnp.zeros(head_out.shape, BF16)
    for a in range(3):
        rows = [head[a, b] for b in range(3)] + [jnp.zeros((4, channels), BF16)]
        head_out[a, 0:16, :] = jnp.concatenate(rows, axis=0)
    stores = [pltpu.make_async_copy(made[i], outs[i], sems.at[i]) for i in range(4)]
    for store in stores:
        store.start()
    for store in stores:
        store.wait()


def first_kernel(tile, head_dim, own, halos, *refs):
    weights, outs, scratch = refs[:9], refs[9:12], refs[12:]
    x_ref = scratch[0]
    rows, cols = tile
    x_ref[REACH : REACH + rows, 0:cols, :] = own[...]
    for step, at, count in ((-1, 0, REACH), (0, REACH, rows), (1, REACH + rows, REACH)):
        if step:
            x_ref[at : at + count, 0:cols, :] = halos[step, 0][...]
        sides = [halos[step, 1][...], halos[step, -1][...]]
        x_ref[at : at + count, cols : cols + 2 * SIDE, :] = jnp.concatenate(sides, axis=1)
    front(x_ref, weights, outs, scratch[1:], REACH, tile, head_dim, 0)


def second_kernel(tile, head_dim, mixed, query, payload, other, out_weight, out_bias, *refs):
    weights, outs, scratch = refs[:9], refs[9:12], refs[12:]
    x_ref, mixed_ref, query_ref, sems = scratch[:4]
    value = attend(
        mixed, query, (payload, other), out_weight, out_bias, mixed_ref, query_ref, sems, head_dim, 0
    )
    x_ref[...] = value.astype(BF16).reshape(x_ref.shape)
    front(x_ref, weights, outs, scratch[4:], REACH - 3, tile, head_dim, 1)


def last_kernel(
    tile, head_dim, mixed, query, payload, other, out_weight, out_bias, head_weight, head_bias,
    map_out, boxes_out, x_ref, mixed_ref, query_ref, sems,
):
    rows, cols = tile
    width = cols + 2 * SIDE
    value = attend(
        mixed, query, (payload, other), out_weight, out_bias, mixed_ref, query_ref, sems, head_dim, 1
    )
    x_ref[...] = value.astype(BF16).reshape(x_ref.shape)
    clear_outside(x_ref, 1, cols)
    map_out[...] = x_ref[1 : 1 + rows, 0:cols, :]
    total = None
    for a in range(3):
        part = lax.dot_general(
            flat(x_ref[a : a + rows]), head_weight[a], (((1,), (1,)), ((), ())),
            preferred_element_type=F32,
        )
        total = part if total is None else total + part
    total = total.reshape(rows, width, LANES)
    lane = lax.broadcasted_iota(jnp.int32, (width, LANES), 1) // 4
    shifted = [
        jnp.where(
            lane == 0,
            pltpu.roll(total[r], 1, 0),
            jnp.where(lane == 2, pltpu.roll(total[r], width - 1, 0), total[r]),
        )
        for r in range(rows)
    ]
    shifted = jnp.concatenate(shifted, axis=0)
    across = lax.broadcasted_iota(jnp.int32, (8, LANES), 0)
    along = lax.broadcasted_iota(jnp.int32, (8, LANES), 1)
    fold = jnp.where((along % 4 == across) & (along < 12), 1.0, 0.0)
    boxes = lax.dot_general(
        fold, shifted, (((1,), (1,)), ((), ())), precision=lax.Precision.HIGHEST,
        preferred_element_type=F32,
    )
    boxes = boxes[0:4] + head_bias[...]
    for r in range(rows):
        boxes_out[:, r, :] = boxes[:, r * width : r * width + cols]


def near():
    return pl.BlockSpec(memory_space=pltpu.VMEM)


def far():
    return pl.BlockSpec(memory_space=pltpu.HBM)


def digits(size, most):
    radices = []
    while size > 1:
        radix = next((r for r in range(min(most, size), 1, -1) if size % r == 0), size)
        radices.append(radix)
        size //= radix
    return radices


def partner(i, stride, radix, step):
    digit = (i // stride) % radix
    other = digit ^ step if radix & (radix - 1) == 0 else (digit + step) % radix
    return i + (other - digit) * stride


def sum_by_permutes(value):
    rounds = []
    for axis in ("row", "col"):
        stride = 1
        for radix in digits(lax.axis_size(axis), 4):
            rounds.append((axis, stride, radix))
            stride *= radix
    for axis, stride, radix in rounds:
        count = lax.axis_size(axis)
        others = [
            lax.ppermute(value, axis, [(i, partner(i, stride, radix, k)) for i in range(count)])
            for k in range(1, radix)
        ]
        if (axis, stride, radix) == rounds[-1] and radix == 2:
            return value, others[0]
        total = value.astype(F32)
        for other in others:
            total = total + other.astype(F32)
        value = total.astype(BF16)
    return value, jnp.zeros_like(value)


def digits(size, most):
    radices = []
    while size > 1:
        radix = next((r for r in range(min(most, size), 1, -1) if size % r == 0), size)
        radices.append(radix)
        size //= radix
    return radices


def from_neighbour(value, row_step, col_step):
    rows, cols = lax.axis_size("row"), lax.axis_size("col")
    pairs = [
        ((r + row_step) * cols + c + col_step, r * cols + c)
        for r in range(rows)
        for c in range(cols)
        if 0 <= r + row_step < rows and 0 <= c + col_step < cols
    ]
    return lax.ppermute(value, ("row", "col"), pairs)


def local(
    features,
    expand_weight,
    expand_bias,
    depth_weight,
    depth_bias,
    project_weight,
    project_bias,
    qkv_weight,
    aggregate_depth,
    aggregate_group,
    output_weight,
    output_bias,
    head_weight,
    head_bias,
):
    rows, cols, channels = features.shape
    head_dim = aggregate_group.shape[2]
    heads = channels // head_dim
    width = cols + 2 * SIDE
    tile = (rows, cols)
    wide = expand_weight.shape[2]

    row_part = {-1: slice(rows - REACH, rows), 0: slice(0, rows), 1: slice(0, REACH)}
    col_part = {-1: slice(cols - SIDE, cols), 0: slice(0, cols), 1: slice(0, SIDE)}
    halos = {
        (r, c): from_neighbour(features[row_part[r], col_part[c]], r, c)
        for r in (-1, 0, 1)
        for c in (-1, 0, 1)
        if r or c
    }

    aggregate_depth = aggregate_depth.transpose(1, 2, 0, 3)
    depth_weight = depth_weight.transpose(1, 2, 0, 3)
    params = pltpu.CompilerParams(vmem_limit_bytes=24 * 2**20)
    made = [
        jax.ShapeDtypeStruct(qkv_weight.shape, BF16),
        jax.ShapeDtypeStruct((SECTIONS, 32, 3 * channels), F32),
        jax.ShapeDtypeStruct((SECTIONS, 3, channels, channels), BF16),
        jax.ShapeDtypeStruct((3, LANES, channels), BF16),
    ]
    qkv_weight, taps, group, head_weight = pl.pallas_call(
        functools.partial(prepare_kernel, head_dim),
        out_shape=made,
        grid=(1,),
        in_specs=[near()] * 4,
        out_specs=[far()] * 4,
        scratch_shapes=[pltpu.VMEM(array.shape, array.dtype) for array in made]
        + [pltpu.VMEM((32 * SECTIONS, 3 * channels), F32), pltpu.SemaphoreType.DMA((4,))],
        compiler_params=params,
        cost_estimate=pl.CostEstimate(
            flops=2 * 10**9, bytes_accessed=4 * 10**6, transcendentals=0
        ),
        name="prepare",
    )(qkv_weight, aggregate_depth, aggregate_group, head_weight)

    weights = [
        expand_weight, expand_bias, depth_weight, depth_bias, project_weight, project_bias,
        qkv_weight, taps, group,
    ]
    weight_specs = [near()] * 6 + [far()] * 3

    def outs_of(count):
        return [
            jax.ShapeDtypeStruct((count, width, channels), BF16),
            jax.ShapeDtypeStruct((count, width, 2 * channels), BF16),
            jax.ShapeDtypeStruct((LANES + KEY_ROWS, LANES), BF16),
        ]

    def front_scratch(count):
        return [
            pltpu.VMEM((count, width, 256), F32),
            pltpu.VMEM((count - 2, width, 256), BF16),
            pltpu.VMEM(((count - 2) * width, channels), F32),
            pltpu.VMEM((count - 2, width, channels), BF16),
            pltpu.VMEM((count - 2, width, 3 * channels), F32),
            pltpu.VMEM((count - 6, width, channels), BF16),
            pltpu.VMEM((count - 6, width, 2 * channels), BF16),
            pltpu.VMEM(qkv_weight.shape[1:], BF16),
            pltpu.VMEM(taps.shape[1:], F32),
            pltpu.VMEM(group.shape[1:], BF16),
            pltpu.SemaphoreType.DMA((5,)),
        ]

    def attend_scratch(count):
        return [
            pltpu.VMEM((count, width, channels), BF16),
            pltpu.VMEM((count, width, channels), BF16),
            pltpu.VMEM((count, width, 2 * channels), BF16),
            pltpu.SemaphoreType.DMA((2,)),
        ]

    first_rows = rows + 2 * REACH
    names = list(halos)

    def first_body(own, *refs):
        parts = dict(zip(names, refs[: len(names)]))
        first_kernel(tile, head_dim, own, parts, *refs[len(names) :])

    mixed, query, payload = pl.pallas_call(
        first_body,
        out_shape=outs_of(first_rows - 6),
        grid=(1,),
        in_specs=[near()] * (1 + len(names)) + weight_specs,
        out_specs=[far(), far(), near()],
        scratch_shapes=[pltpu.VMEM((first_rows, width, channels), BF16)]
        + front_scratch(first_rows),
        compiler_params=params,
        name="first",
    )(features, *halos.values(), *weights)
    payload, other = sum_by_permutes(payload)

    second_rows = first_rows - 6
    mixed, query, payload = pl.pallas_call(
        functools.partial(second_kernel, tile, head_dim),
        out_shape=outs_of(second_rows - 6),
        grid=(1,),
        in_specs=[far()] * 2 + [near()] * 4 + weight_specs,
        out_specs=[far(), far(), near()],
        scratch_shapes=attend_scratch(second_rows) + front_scratch(second_rows),
        compiler_params=params,
        name="second",
    )(mixed, query, payload, other, output_weight, output_bias, *weights)
    payload, other = sum_by_permutes(payload)

    return pl.pallas_call(
        functools.partial(last_kernel, tile, head_dim),
        out_shape=[
            jax.ShapeDtypeStruct((rows, cols, channels), BF16),
            jax.ShapeDtypeStruct((4, rows, cols), F32),
        ],
        grid=(1,),
        in_specs=[far()] * 2 + [near()] * 6,
        out_specs=[near()] * 2,
        scratch_shapes=attend_scratch(rows + 2),
        compiler_params=params,
        name="last",
    )(
        mixed, query, payload, other, output_weight, output_bias, head_weight,
        head_bias.reshape(4, 1),
    )


def solution(mesh):
    return jax.shard_map(
        local,
        mesh=mesh,
        in_specs=(P("row", "col", None),) + (P(),) * 13,
        out_specs=(P("row", "col", None), P(None, "row", "col")),
        check_vma=False,
    )
```

```python
import functools

import jax
import jax.numpy as jnp
from jax import lax
from jax.experimental import pallas as pl
from jax.experimental.pallas import tpu as pltpu
from jax.sharding import PartitionSpec as P

SECTIONS = 2
LANES = 128
SIDE = 8
REACH = 7
KEY_ROWS = 16
F32 = jnp.float32
BF16 = jnp.bfloat16


def hard_swish(value):
    return value * jnp.minimum(jnp.maximum(value * (1.0 / 6.0) + 0.5, 0.0), 1.0)


def clear_outside(ref, halo, cols):
    rows = ref.shape[0]
    row, col = lax.axis_index("row"), lax.axis_index("col")

    @pl.when(row == 0)
    def _():
        ref[0:halo] = jnp.zeros((halo,) + ref.shape[1:], ref.dtype)

    @pl.when(row == lax.axis_size("row") - 1)
    def _():
        ref[rows - halo : rows] = jnp.zeros((halo,) + ref.shape[1:], ref.dtype)

    @pl.when(col == 0)
    def _():
        ref[:, cols + SIDE : cols + 2 * SIDE, :] = jnp.zeros((rows, SIDE, ref.shape[2]), ref.dtype)

    @pl.when(col == lax.axis_size("col") - 1)
    def _():
        ref[:, cols : cols + SIDE, :] = jnp.zeros((rows, SIDE, ref.shape[2]), ref.dtype)


def grouped_loop(count, most, body):
    size = next(n for n in range(min(most, count), 0, -1) if count % n == 0)

    def group(index, carry):
        for r in range(size):
            body(index * size + r)
        return carry

    lax.fori_loop(0, count // size, group, 0)


def flat(value):
    return value.reshape(-1, value.shape[-1])


def same_head(head_dim):
    across = lax.broadcasted_iota(jnp.int32, (LANES, LANES), 0) // head_dim
    along = lax.broadcasted_iota(jnp.int32, (LANES, LANES), 1) // head_dim
    return across == along


def front(x_ref, weights, outs, scratch, halo, tile, head_dim, section):
    expand, expand_bias, depth, depth_bias, project, project_bias = weights[:6]
    mixed_out, query_out, payload_out = outs
    hidden, spread, total, mixed, qkv, scaled, query, qkv_weight, agg, group, sems = scratch
    loads = [
        pltpu.make_async_copy(weights[6].at[section], qkv_weight, sems.at[0]),
        pltpu.make_async_copy(weights[7].at[section], agg, sems.at[1]),
        pltpu.make_async_copy(weights[8].at[section], group, sems.at[2]),
    ]
    for load in loads:
        load.start()
    rows, width, channels = x_ref.shape
    tile_rows, tile_cols = tile
    inner = rows - 2
    chunk = hidden.shape[2]
    x = flat(x_ref[...])

    def expanded(step, carry):
        at = pl.multiple_of(step * chunk, chunk)
        value = jnp.dot(x, expand[section, :, pl.ds(at, chunk)], preferred_element_type=F32)
        value = hard_swish(value + expand_bias[section : section + 1, pl.ds(at, chunk)])
        hidden[...] = value.reshape(rows, width, chunk)
        clear_outside(hidden, halo, tile_cols)

        def one_row(r):
            for lane in range(0, chunk, LANES):
                here = pl.ds(pl.multiple_of(at + lane, LANES), LANES)
                above, level, below = (hidden[r + a, :, lane : lane + LANES] for a in range(3))
                parts = [
                    above * depth[0, b, section : section + 1, here]
                    + level * depth[1, b, section : section + 1, here]
                    + below * depth[2, b, section : section + 1, here]
                    for b in range(3)
                ]
                value = parts[1] + pltpu.roll(parts[0], 1, 0) + pltpu.roll(parts[2], width - 1, 0)
                value = hard_swish(value + depth_bias[section : section + 1, here])
                spread[r, :, lane : lane + LANES] = value.astype(BF16)

        grouped_loop(inner, 7, one_row)
        product = jnp.dot(
            flat(spread[...]), project[section, pl.ds(at, chunk), :], preferred_element_type=F32
        )

        @pl.when(step == 0)
        def _():
            total[...] = product

        @pl.when(step > 0)
        def _():
            total[...] += product

        return carry

    lax.fori_loop(0, expand.shape[2] // chunk, expanded, 0)
    value = total[...] + project_bias[section : section + 1, :] + flat(x_ref[1 : rows - 1]).astype(F32)
    mixed[...] = value.astype(BF16).reshape(inner, width, channels)
    outer = inner - 4
    stores = [
        pltpu.make_async_copy(mixed.at[pl.ds(2, outer)], mixed_out, sems.at[3]),
        pltpu.make_async_copy(query, query_out, sems.at[4]),
    ]
    stores[0].start()
    for load in loads:
        load.wait()
    value = jnp.dot(flat(mixed[...]), qkv_weight[...], preferred_element_type=F32)
    qkv[...] = value.reshape(inner, width, 3 * channels)
    around = halo - 1
    clear_outside(qkv, around, tile_cols)

    def aggregated(kind, first, count):
        def one_row(r):
            for lane in range(0, channels, LANES):
                here = slice(kind * channels + lane, kind * channels + lane + LANES)
                value = None
                for b in range(5):
                    part = None
                    for a in range(5):
                        term = qkv[first + r + a, :, here] * agg[5 * a + b : 5 * a + b + 1, here]
                        part = term if part is None else part + term
                    if b != 2:
                        part = pltpu.roll(part, (2 - b) % width, 0)
                    value = part if value is None else value + part
                scaled[r, :, lane : lane + LANES] = value.astype(BF16)

        grouped_loop(count, 5, one_row)
        value = jnp.dot(flat(scaled[0:count]), group[kind], preferred_element_type=F32)
        return value.reshape(count, width, channels)

    query[:, :, 0:channels] = jnp.maximum(qkv[2 : inner - 2, :, 0:channels], 0.0).astype(BF16)
    query[:, :, channels : 2 * channels] = jnp.maximum(
        aggregated(0, 0, outer), 0.0
    ).astype(BF16)

    stores[1].start()

    def own(value):
        return flat(value[:, 0:tile_cols, :])

    mine = slice(around, around + tile_rows)
    keys = [own(qkv[mine, :, channels : 2 * channels]), own(aggregated(1, around - 2, tile_rows))]
    values = [
        own(qkv[mine, :, 2 * channels : 3 * channels]),
        own(aggregated(2, around - 2, tile_rows)),
    ]
    same = same_head(head_dim)
    summary = jnp.zeros((LANES, LANES), F32)
    key_sums = []
    index = 0
    for key, value in zip(keys, values):
        key = jnp.maximum(key, 0.0)
        sums = jnp.sum(key, axis=0, keepdims=True)
        key, value = key.astype(BF16), value.astype(BF16)
        for lane in range(0, channels, LANES):
            here = slice(lane, lane + LANES)
            product = lax.dot_general(
                key[:, here], value[:, here], (((0,), (0,)), ((), ())), preferred_element_type=F32
            )
            product = jnp.where(same, product, 0.0)
            if index:
                product = pltpu.roll(product, index * head_dim, 1)
            summary = summary + product
            key_sums.append(sums[:, here])
            index += 1
    key_sums = jnp.concatenate(
        key_sums + [jnp.zeros((KEY_ROWS - index, LANES), F32)], axis=0
    )
    payload_out[0:LANES, :] = summary.astype(BF16)
    payload_out[LANES : LANES + KEY_ROWS, :] = key_sums.astype(BF16)
    for store in stores:
        store.wait()


def attend(
    mixed_in, query_in, payloads, weight, bias, mixed_ref, query_ref, sems, head_dim, section
):
    loads = [
        pltpu.make_async_copy(query_in, query_ref, sems.at[0]),
        pltpu.make_async_copy(mixed_in, mixed_ref, sems.at[1]),
    ]
    for load in loads:
        load.start()
    same = same_head(head_dim)
    square = (LANES, LANES)
    diagonal = lax.broadcasted_iota(jnp.int32, square, 0) == lax.broadcasted_iota(
        jnp.int32, square, 1
    )
    ones = jnp.where(same, 1.0, 0.0).astype(BF16)
    payload = payloads[0][...].astype(F32)
    for part in payloads[1:]:
        payload = payload + part[...].astype(F32)
    packed = payload[0:LANES]
    for load in loads:
        load.wait()
    query = flat(query_ref[...])
    total = flat(mixed_ref[...]).astype(F32) + bias[section : section + 1, :]
    for index in range(query.shape[1] // LANES):
        summary = packed if index == 0 else pltpu.roll(packed, LANES - index * head_dim, 1)
        summary = jnp.where(same, summary, 0.0).astype(BF16)
        sums = payload[LANES + index : LANES + index + 1]
        sums = jnp.where(diagonal, sums, 0.0).astype(BF16)
        sums = jnp.dot(sums, ones, preferred_element_type=F32).astype(BF16)
        part = query[:, index * LANES : (index + 1) * LANES]
        numer = jnp.dot(part, summary, preferred_element_type=F32)
        denom = jnp.dot(part, sums, preferred_element_type=F32)
        attended = (numer / (denom + 1e-6)).astype(BF16)
        total = total + jnp.dot(
            attended, weight[section, index * LANES : (index + 1) * LANES, :], preferred_element_type=F32
        )
    return total


def tap(section, a, b):
    at = 32 * section + 5 * a + b
    return slice(at, at + 1)


def prepare_kernel(head_dim, qkv, agg, group, head, *refs):
    outs, made, taps, sems = refs[:4], refs[4:8], refs[8], refs[9]
    qkv_out, agg_out, group_out, head_out = made
    sections, channels, wide = qkv.shape
    half = 3 * LANES
    heads = LANES // head_dim
    src = lax.broadcasted_iota(jnp.int32, (half, LANES), 0)
    dst = lax.broadcasted_iota(jnp.int32, (half, LANES), 1)
    first = (dst // head_dim) * 3 * head_dim + dst % head_dim
    picks = [jnp.where(src == first + k * head_dim, 1.0, 0.0).astype(BF16) for k in range(3)]
    taps[...] = jnp.zeros(taps.shape, F32)
    for section in range(sections):
        for a in range(5):
            for b in range(5):
                taps[tap(section, a, b), :] = agg[a, b, section : section + 1, :]
    rest = taps[...]
    high = rest.astype(BF16)
    rest = rest - high.astype(F32)
    middle = rest.astype(BF16)
    low = (rest - middle.astype(F32)).astype(BF16)
    split = jnp.concatenate([high, middle, low], axis=0)
    count = taps.shape[0]
    weights = qkv[...].reshape(sections * channels, wide)
    for part in range(wide // half):
        here = slice(part * half, (part + 1) * half)
        for kind in range(3):
            to = kind * channels + part * LANES
            there = slice(to, to + LANES)
            value = jnp.dot(weights[:, here], picks[kind], preferred_element_type=F32)
            qkv_out[:, :, there] = value.astype(BF16).reshape(sections, channels, LANES)
            value = jnp.dot(split[:, here], picks[kind], preferred_element_type=F32)
            value = value[:count] + value[count : 2 * count] + value[2 * count :]
            agg_out[:, :, there] = value.reshape(sections, -1, LANES)
    row = lax.broadcasted_iota(jnp.int32, (head_dim, channels), 0)
    lane = lax.broadcasted_iota(jnp.int32, (head_dim, channels), 1)
    spread = jnp.where(lane % head_dim == row, 1.0, 0.0).astype(BF16)
    across = lax.broadcasted_iota(jnp.int32, (channels, channels), 0) // head_dim
    along = lax.broadcasted_iota(jnp.int32, (channels, channels), 1) // head_dim
    for section in range(sections):
        for kind in range(3):
            tall = [group[section, 3 * h + kind] for h in range(channels // head_dim)]
            value = jnp.dot(jnp.concatenate(tall, axis=0), spread, preferred_element_type=F32)
            group_out[section, kind] = jnp.where(across == along, value, 0.0).astype(BF16)
    head_out[...] = jnp.zeros(head_out.shape, BF16)
    for a in range(3):
        rows = [head[a, b] for b in range(3)] + [jnp.zeros((4, channels), BF16)]
        head_out[a, 0:16, :] = jnp.concatenate(rows, axis=0)
    stores = [pltpu.make_async_copy(made[i], outs[i], sems.at[i]) for i in range(4)]
    for store in stores:
        store.start()
    for store in stores:
        store.wait()


def first_kernel(tile, head_dim, own, row_0, row_1, col_0, col_1, *refs):
    weights, outs, scratch = refs[:9], refs[9:12], refs[12:]
    x_ref = scratch[0]
    rows, cols = tile
    x_ref[REACH : REACH + rows, 0:cols, :] = own[...]
    below = REACH + rows
    even = lax.axis_index("row") % 2 == 0
    x_ref[pl.ds(jnp.where(even, below, 0), REACH), 0:cols, :] = row_0[...]
    x_ref[pl.ds(jnp.where(even, 0, below), REACH), 0:cols, :] = row_1[...]
    even = lax.axis_index("col") % 2 == 0

    @pl.when(even)
    def _():
        x_ref[:, cols : cols + 2 * SIDE, :] = jnp.concatenate([col_0[...], col_1[...]], axis=1)

    @pl.when(jnp.logical_not(even))
    def _():
        x_ref[:, cols : cols + 2 * SIDE, :] = jnp.concatenate([col_1[...], col_0[...]], axis=1)

    front(x_ref, weights, outs, scratch[1:], REACH, tile, head_dim, 0)


def second_kernel(tile, head_dim, mixed, query, payload, other, out_weight, out_bias, *refs):
    weights, outs, scratch = refs[:9], refs[9:12], refs[12:]
    x_ref, mixed_ref, query_ref, sems = scratch[:4]
    value = attend(
        mixed, query, (payload, other), out_weight, out_bias, mixed_ref, query_ref, sems, head_dim, 0
    )
    x_ref[...] = value.astype(BF16).reshape(x_ref.shape)
    front(x_ref, weights, outs, scratch[4:], REACH - 3, tile, head_dim, 1)


def last_kernel(
    tile, head_dim, mixed, query, payload, other, out_weight, out_bias, head_weight, head_bias,
    map_out, boxes_out, x_ref, mixed_ref, query_ref, sems,
):
    rows, cols = tile
    width = cols + 2 * SIDE
    value = attend(
        mixed, query, (payload, other), out_weight, out_bias, mixed_ref, query_ref, sems, head_dim, 1
    )
    x_ref[...] = value.astype(BF16).reshape(x_ref.shape)
    clear_outside(x_ref, 1, cols)
    map_out[...] = x_ref[1 : 1 + rows, 0:cols, :]
    total = None
    for a in range(3):
        part = lax.dot_general(
            flat(x_ref[a : a + rows]), head_weight[a], (((1,), (1,)), ((), ())),
            preferred_element_type=F32,
        )
        total = part if total is None else total + part
    total = total.reshape(rows, width, LANES)
    lane = lax.broadcasted_iota(jnp.int32, (width, LANES), 1) // 4
    shifted = [
        jnp.where(
            lane == 0,
            pltpu.roll(total[r], 1, 0),
            jnp.where(lane == 2, pltpu.roll(total[r], width - 1, 0), total[r]),
        )
        for r in range(rows)
    ]
    shifted = jnp.concatenate(shifted, axis=0)
    across = lax.broadcasted_iota(jnp.int32, (8, LANES), 0)
    along = lax.broadcasted_iota(jnp.int32, (8, LANES), 1)
    fold = jnp.where((along % 4 == across) & (along < 12), 1.0, 0.0)
    boxes = lax.dot_general(
        fold, shifted, (((1,), (1,)), ((), ())), precision=lax.Precision.HIGHEST,
        preferred_element_type=F32,
    )
    boxes = boxes[0:4] + head_bias[...]
    for r in range(rows):
        boxes_out[:, r, :] = boxes[:, r * width : r * width + cols]


def near():
    return pl.BlockSpec(memory_space=pltpu.VMEM)


def far():
    return pl.BlockSpec(memory_space=pltpu.HBM)


def digits(size, most):
    radices = []
    while size > 1:
        radix = next((r for r in range(min(most, size), 1, -1) if size % r == 0), size)
        radices.append(radix)
        size //= radix
    return radices


def partner(i, stride, radix, step):
    digit = (i // stride) % radix
    other = digit ^ step if radix & (radix - 1) == 0 else (digit + step) % radix
    return i + (other - digit) * stride


def sum_by_permutes(value):
    rounds = []
    for axis in ("row", "col"):
        stride = 1
        for radix in digits(lax.axis_size(axis), 4):
            rounds.append((axis, stride, radix))
            stride *= radix
    for axis, stride, radix in rounds:
        count = lax.axis_size(axis)
        others = [
            lax.ppermute(value, axis, [(i, partner(i, stride, radix, k)) for i in range(count)])
            for k in range(1, radix)
        ]
        if (axis, stride, radix) == rounds[-1] and radix == 2:
            return value, others[0]
        total = value.astype(F32)
        for other in others:
            total = total + other.astype(F32)
        value = total.astype(BF16)
    return value, jnp.zeros_like(value)


def digits(size, most):
    radices = []
    while size > 1:
        radix = next((r for r in range(min(most, size), 1, -1) if size % r == 0), size)
        radices.append(radix)
        size //= radix
    return radices


def pair_exchange(value, axis, first):
    count = lax.axis_size(axis)
    pairs = []
    for i in range(first, count - 1, 2):
        pairs += [(i, i + 1), (i + 1, i)]
    return lax.ppermute(value, axis, pairs)


def local(
    features,
    expand_weight,
    expand_bias,
    depth_weight,
    depth_bias,
    project_weight,
    project_bias,
    qkv_weight,
    aggregate_depth,
    aggregate_group,
    output_weight,
    output_bias,
    head_weight,
    head_bias,
):
    rows, cols, channels = features.shape
    head_dim = aggregate_group.shape[2]
    heads = channels // head_dim
    width = cols + 2 * SIDE
    tile = (rows, cols)
    wide = expand_weight.shape[2]

    def edges(value, dim, size, odd):
        far = value.shape[dim] - size
        return [
            lax.dynamic_slice_in_dim(value, jnp.where(odd == at, far, 0), size, dim) for at in (0, 1)
        ]

    odd_row = lax.axis_index("row") % 2
    odd_col = lax.axis_index("col") % 2
    low, high = edges(features, 0, REACH, odd_row)
    row_halos = [pair_exchange(low, "row", 0), pair_exchange(high, "row", 1)]
    below = jnp.where(odd_row == 0, row_halos[0], row_halos[1])
    above = jnp.where(odd_row == 0, row_halos[1], row_halos[0])
    tall = jnp.concatenate([above, features, below], axis=0)
    low, high = edges(tall, 1, SIDE, odd_col)
    col_halos = [pair_exchange(low, "col", 0), pair_exchange(high, "col", 1)]

    aggregate_depth = aggregate_depth.transpose(1, 2, 0, 3)
    depth_weight = depth_weight.transpose(1, 2, 0, 3)
    params = pltpu.CompilerParams(vmem_limit_bytes=24 * 2**20)
    made = [
        jax.ShapeDtypeStruct(qkv_weight.shape, BF16),
        jax.ShapeDtypeStruct((SECTIONS, 32, 3 * channels), F32),
        jax.ShapeDtypeStruct((SECTIONS, 3, channels, channels), BF16),
        jax.ShapeDtypeStruct((3, LANES, channels), BF16),
    ]
    qkv_weight, taps, group, head_weight = pl.pallas_call(
        functools.partial(prepare_kernel, head_dim),
        out_shape=made,
        grid=(1,),
        in_specs=[near()] * 4,
        out_specs=[far()] * 4,
        scratch_shapes=[pltpu.VMEM(array.shape, array.dtype) for array in made]
        + [pltpu.VMEM((32 * SECTIONS, 3 * channels), F32), pltpu.SemaphoreType.DMA((4,))],
        compiler_params=params,
        cost_estimate=pl.CostEstimate(
            flops=2 * 10**9, bytes_accessed=4 * 10**6, transcendentals=0
        ),
        name="prepare",
    )(qkv_weight, aggregate_depth, aggregate_group, head_weight)

    weights = [
        expand_weight, expand_bias, depth_weight, depth_bias, project_weight, project_bias,
        qkv_weight, taps, group,
    ]
    weight_specs = [near()] * 6 + [far()] * 3

    def outs_of(count):
        return [
            jax.ShapeDtypeStruct((count, width, channels), BF16),
            jax.ShapeDtypeStruct((count, width, 2 * channels), BF16),
            jax.ShapeDtypeStruct((LANES + KEY_ROWS, LANES), BF16),
        ]

    def front_scratch(count):
        return [
            pltpu.VMEM((count, width, 256), F32),
            pltpu.VMEM((count - 2, width, 256), BF16),
            pltpu.VMEM(((count - 2) * width, channels), F32),
            pltpu.VMEM((count - 2, width, channels), BF16),
            pltpu.VMEM((count - 2, width, 3 * channels), F32),
            pltpu.VMEM((count - 6, width, channels), BF16),
            pltpu.VMEM((count - 6, width, 2 * channels), BF16),
            pltpu.VMEM(qkv_weight.shape[1:], BF16),
            pltpu.VMEM(taps.shape[1:], F32),
            pltpu.VMEM(group.shape[1:], BF16),
            pltpu.SemaphoreType.DMA((5,)),
        ]

    def attend_scratch(count):
        return [
            pltpu.VMEM((count, width, channels), BF16),
            pltpu.VMEM((count, width, channels), BF16),
            pltpu.VMEM((count, width, 2 * channels), BF16),
            pltpu.SemaphoreType.DMA((2,)),
        ]

    first_rows = rows + 2 * REACH
    mixed, query, payload = pl.pallas_call(
        functools.partial(first_kernel, tile, head_dim),
        out_shape=outs_of(first_rows - 6),
        grid=(1,),
        in_specs=[near()] * 5 + weight_specs,
        out_specs=[far(), far(), near()],
        scratch_shapes=[pltpu.VMEM((first_rows, width, channels), BF16)]
        + front_scratch(first_rows),
        compiler_params=params,
        name="first",
    )(features, *row_halos, *col_halos, *weights)
    payload, other = sum_by_permutes(payload)

    second_rows = first_rows - 6
    mixed, query, payload = pl.pallas_call(
        functools.partial(second_kernel, tile, head_dim),
        out_shape=outs_of(second_rows - 6),
        grid=(1,),
        in_specs=[far()] * 2 + [near()] * 4 + weight_specs,
        out_specs=[far(), far(), near()],
        scratch_shapes=attend_scratch(second_rows) + front_scratch(second_rows),
        compiler_params=params,
        name="second",
    )(mixed, query, payload, other, output_weight, output_bias, *weights)
    payload, other = sum_by_permutes(payload)

    return pl.pallas_call(
        functools.partial(last_kernel, tile, head_dim),
        out_shape=[
            jax.ShapeDtypeStruct((rows, cols, channels), BF16),
            jax.ShapeDtypeStruct((4, rows, cols), F32),
        ],
        grid=(1,),
        in_specs=[far()] * 2 + [near()] * 6,
        out_specs=[near()] * 2,
        scratch_shapes=attend_scratch(rows + 2),
        compiler_params=params,
        name="last",
    )(
        mixed, query, payload, other, output_weight, output_bias, head_weight,
        head_bias.reshape(4, 1),
    )


def solution(mesh):
    return jax.shard_map(
        local,
        mesh=mesh,
        in_specs=(P("row", "col", None),) + (P(),) * 13,
        out_specs=(P("row", "col", None), P(None, "row", "col")),
        check_vma=False,
    )
```

```python
import functools

import jax
import jax.numpy as jnp
from jax import lax
from jax.experimental import pallas as pl
from jax.experimental.pallas import tpu as pltpu
from jax.sharding import PartitionSpec as P

SECTIONS = 2
LANES = 128
SIDE = 8
REACH = 7
KEY_ROWS = 16
TILE = 16
PARTS = 4
F32 = jnp.float32
BF16 = jnp.bfloat16


def six_hard_swish(value):
    return value * jnp.minimum(jnp.maximum(value + 3.0, 0.0), 6.0)


def parted(count, parts):
    cuts = [count * k // parts for k in range(parts + 1)]
    return [(a, b - a) for a, b in zip(cuts, cuts[1:]) if b > a]


def clear_outside(ref, halo, cols):
    rows = ref.shape[0]
    row, col = lax.axis_index("row"), lax.axis_index("col")

    @pl.when(row == 0)
    def _():
        ref[0:halo] = jnp.zeros((halo,) + ref.shape[1:], ref.dtype)

    @pl.when(row == lax.axis_size("row") - 1)
    def _():
        ref[rows - halo : rows] = jnp.zeros((halo,) + ref.shape[1:], ref.dtype)

    @pl.when(col == 0)
    def _():
        ref[:, cols + SIDE : cols + 2 * SIDE, :] = jnp.zeros((rows, SIDE, ref.shape[2]), ref.dtype)

    @pl.when(col == lax.axis_size("col") - 1)
    def _():
        ref[:, cols : cols + SIDE, :] = jnp.zeros((rows, SIDE, ref.shape[2]), ref.dtype)


def flat(value):
    return value.reshape(-1, value.shape[-1])


def same_head(head_dim):
    across = lax.broadcasted_iota(jnp.int32, (LANES, LANES), 0) // head_dim
    along = lax.broadcasted_iota(jnp.int32, (LANES, LANES), 1) // head_dim
    return across == along


def depthwise_row(rows, taps, size, width):
    rows = [row.reshape(width // TILE, TILE, LANES) for row in rows]
    total = None
    for b in range(size):
        part = None
        for a in range(size):
            term = rows[a] * taps(a, b)[None]
            part = term if part is None else part + term
        part = part.reshape(width, LANES).astype(F32)
        if b != size // 2:
            part = pltpu.roll(part, (size // 2 - b) % width, 0)
        total = part if total is None else total + part
    return total


def front(x_ref, weights, outs, scratch, halo, tile, head_dim, section):
    expand, expand_bias, depth, depth_bias, project, project_bias = weights[:6]
    mixed_out, query_out, payload_out = outs
    (
        hidden_0, hidden_1, total, mixed, qkv, query, wide_depth, wide_agg,
        qkv_weight, agg, group, sems,
    ) = scratch
    loads = [
        pltpu.make_async_copy(weights[6].at[section], qkv_weight, sems.at[0]),
        pltpu.make_async_copy(weights[7].at[section], agg, sems.at[1]),
        pltpu.make_async_copy(weights[8].at[section], group, sems.at[2]),
    ]
    for load in loads:
        load.start()
    rows, width, channels = x_ref.shape
    tile_rows, tile_cols = tile
    inner = rows - 2
    chunk = hidden_0.shape[2]
    chunks = expand.shape[2] // chunk
    for index in range(9):
        taps = depth[index // 3, index % 3, section : section + 1, :] * (1.0 / 6.0)
        wide_depth[index] = jnp.broadcast_to(taps, (TILE, taps.shape[1])).astype(BF16)
    total[...] = 6.0 * (flat(x_ref[1 : rows - 1]).astype(F32) + project_bias[section : section + 1, :])

    def expand_rows(out, at, first, size):
        value = jnp.dot(
            flat(x_ref[first : first + size]), expand[section, :, pl.ds(at, chunk)],
            preferred_element_type=F32,
        )
        value = (value + expand_bias[section : section + 1, pl.ds(at, chunk)]).astype(BF16)
        out[first : first + size] = six_hard_swish(value).reshape(size, width, chunk)

    def spread_rows(hidden, at, first, size):
        spread = []
        for r in range(first, first + size):
            lanes = []
            for lane in range(0, chunk, LANES):
                here = pl.ds(pl.multiple_of(at + lane, LANES), LANES)
                value = depthwise_row(
                    [hidden[r + a, :, lane : lane + LANES] for a in range(3)],
                    lambda a, b: wide_depth[3 * a + b, :, here], 3, width,
                )
                value = (value + depth_bias[section : section + 1, here]).astype(BF16)
                lanes.append(six_hard_swish(value))
            spread.append(jnp.concatenate(lanes, axis=1))
        pixels = slice(first * width, (first + size) * width)
        total[pixels] += jnp.dot(
            jnp.concatenate(spread, axis=0), project[section, pl.ds(at, chunk), :],
            preferred_element_type=F32,
        )

    def stage(index, current, following):
        at = pl.multiple_of(index * chunk, chunk)
        ahead = pl.multiple_of(jnp.minimum(index + 1, chunks - 1) * chunk, chunk)
        for (first, size), (from_row, count) in zip(parted(inner, PARTS), parted(rows, PARTS)):
            expand_rows(following, ahead, from_row, count)
            spread_rows(current, at, first, size)
        clear_outside(following, halo, tile_cols)

    for first, size in parted(rows, PARTS):
        expand_rows(hidden_0, 0, first, size)
    clear_outside(hidden_0, halo, tile_cols)

    def two_stages(index, carry):
        stage(2 * index, hidden_0, hidden_1)
        stage(2 * index + 1, hidden_1, hidden_0)
        return carry

    lax.fori_loop(0, chunks // 2, two_stages, 0)
    mixed[...] = (total[...] * (1.0 / 6.0)).astype(BF16).reshape(inner, width, channels)
    outer = inner - 4
    stores = [
        pltpu.make_async_copy(mixed.at[pl.ds(2, outer)], mixed_out, sems.at[3]),
        pltpu.make_async_copy(query, query_out, sems.at[4]),
    ]
    stores[0].start()
    for load in loads:
        load.wait()
    for index in range(25):
        taps = agg[index : index + 1, :]
        wide_agg[index] = jnp.broadcast_to(taps, (TILE, taps.shape[1])).astype(BF16)
    for first, size in parted(inner, PARTS):
        value = jnp.dot(
            flat(mixed[first : first + size]), qkv_weight[...], preferred_element_type=F32
        )
        qkv[first : first + size] = value.astype(BF16).reshape(size, width, 3 * channels)
    around = halo - 1
    clear_outside(qkv, around, tile_cols)

    def aggregated(kind, first, size):
        scaled = []
        for r in range(size):
            lanes = []
            for lane in range(kind * channels, (kind + 1) * channels, LANES):
                here = slice(lane, lane + LANES)
                value = depthwise_row(
                    [qkv[first + r + a, :, here] for a in range(5)],
                    lambda a, b: wide_agg[5 * a + b, :, here], 5, width,
                )
                lanes.append(value.astype(BF16))
            scaled.append(jnp.concatenate(lanes, axis=1))
        value = jnp.dot(
            jnp.concatenate(scaled, axis=0), group[kind], preferred_element_type=F32
        )
        return value.astype(BF16).reshape(size, width, channels)

    query[:, :, 0:channels] = jnp.maximum(qkv[2 : inner - 2, :, 0:channels], 0.0)
    size = next(n for n in range(5, 0, -1) if outer % n == 0)

    def query_rows(index, carry):
        at = index * size
        query[pl.ds(at, size), :, channels : 2 * channels] = jnp.maximum(
            aggregated(0, at, size), 0.0
        )
        return carry

    lax.fori_loop(0, outer // size, query_rows, 0)
    stores[1].start()
    size = next(n for n in range(4, 0, -1) if tile_rows % n == 0)

    def summed(key, value):
        key = jnp.maximum(flat(key[:, 0:tile_cols]), 0.0)
        value = flat(value[:, 0:tile_cols])
        products = [
            lax.dot_general(
                key[:, lane : lane + LANES], value[:, lane : lane + LANES],
                (((0,), (0,)), ((), ())), preferred_element_type=F32,
            )
            for lane in range(0, channels, LANES)
        ]
        return products, jnp.sum(key.astype(F32), axis=0, keepdims=True)

    mine = slice(around, around + tile_rows)
    products, sums = summed(
        qkv[mine, :, channels : 2 * channels], qkv[mine, :, 2 * channels : 3 * channels]
    )

    def grouped_rows(index, carry):
        at = around - 2 + index * size
        more, sums = summed(aggregated(1, at, size), aggregated(2, at, size))
        return [a + b for a, b in zip(carry[0], more)], carry[1] + sums

    more, more_sums = lax.fori_loop(
        0, tile_rows // size, grouped_rows,
        ([jnp.zeros((LANES, LANES), F32) for _ in products], jnp.zeros_like(sums)),
    )
    products = products + more
    sums = jnp.concatenate([sums, more_sums], axis=1)
    same = same_head(head_dim)
    summary = jnp.zeros((LANES, LANES), F32)
    key_sums = []
    for index, product in enumerate(products):
        product = jnp.where(same, product, 0.0)
        if index:
            product = pltpu.roll(product, index * head_dim, 1)
        summary = summary + product
        key_sums.append(sums[:, index * LANES : (index + 1) * LANES])
    key_sums.append(jnp.zeros((KEY_ROWS - len(products), LANES), F32))
    payload_out[0:LANES, :] = summary.astype(BF16)
    payload_out[LANES : LANES + KEY_ROWS, :] = jnp.concatenate(key_sums, axis=0).astype(BF16)
    for store in stores:
        store.wait()


def attend(
    mixed_in, query_in, payloads, weight, bias, mixed_ref, query_ref, sems, head_dim, section, x_ref
):
    rows, width, channels = x_ref.shape
    groups = parted(rows, PARTS)
    loads = []
    for index, (first, size) in enumerate(groups):
        here = pl.ds(first, size)
        for at, (source, target) in enumerate(((query_in, query_ref), (mixed_in, mixed_ref))):
            load = pltpu.make_async_copy(source.at[here], target.at[here], sems.at[at, index])
            load.start()
            loads.append(load)
    same = same_head(head_dim)
    square = (LANES, LANES)
    diagonal = lax.broadcasted_iota(jnp.int32, square, 0) == lax.broadcasted_iota(
        jnp.int32, square, 1
    )
    ones = jnp.where(same, 1.0, 0.0).astype(BF16)
    nothing = jnp.zeros(square, BF16)
    payload = payloads[0][...].astype(F32)
    for part in payloads[1:]:
        payload = payload + part[...].astype(F32)
    packed = payload[0:LANES]
    count = 2 * channels // LANES
    summaries, sums = [], []
    for index in range(count):
        summary = packed if index == 0 else pltpu.roll(packed, LANES - index * head_dim, 1)
        summaries.append(jnp.where(same, summary, 0.0).astype(BF16))
        keys = payload[LANES + index : LANES + index + 1]
        keys = jnp.where(diagonal, keys, 0.0).astype(BF16)
        sums.append(jnp.dot(keys, ones, preferred_element_type=F32).astype(BF16))

    def paired(blocks, index):
        return jnp.concatenate(
            [
                jnp.concatenate([blocks[index], nothing], axis=1),
                jnp.concatenate([nothing, blocks[index + 1]], axis=1),
            ],
            axis=0,
        )

    summaries = [paired(summaries, index) for index in range(0, count, 2)]
    sums = [paired(sums, index) for index in range(0, count, 2)]
    step = 2 * LANES
    for index, (first, size) in enumerate(groups):
        for load in loads[2 * index : 2 * index + 2]:
            load.wait()
        query = flat(query_ref[first : first + size])
        parts = []
        for branch in range(count // 2):
            part = query[:, branch * step : (branch + 1) * step]
            numer = jnp.dot(part, summaries[branch], preferred_element_type=F32)
            denom = jnp.dot(part, sums[branch], preferred_element_type=F32) + 1e-6
            inverse = pl.reciprocal(denom, approx=True)
            inverse = inverse * (2.0 - denom * inverse)
            parts.append((numer * inverse).astype(BF16))
        value = jnp.dot(
            jnp.concatenate(parts, axis=1), weight[section], preferred_element_type=F32
        )
        value = value + bias[section : section + 1, :]
        value = value + flat(mixed_ref[first : first + size]).astype(F32)
        x_ref[first : first + size] = value.astype(BF16).reshape(size, width, channels)


def tap(section, a, b):
    at = 32 * section + 5 * a + b
    return slice(at, at + 1)


def prepare_kernel(head_dim, qkv, agg, group, head, *refs):
    outs, made, taps, sems = refs[:4], refs[4:8], refs[8], refs[9]
    qkv_out, agg_out, group_out, head_out = made
    sections, channels, wide = qkv.shape
    half = 3 * LANES
    heads = LANES // head_dim
    src = lax.broadcasted_iota(jnp.int32, (half, LANES), 0)
    dst = lax.broadcasted_iota(jnp.int32, (half, LANES), 1)
    first = (dst // head_dim) * 3 * head_dim + dst % head_dim
    picks = [jnp.where(src == first + k * head_dim, 1.0, 0.0).astype(BF16) for k in range(3)]
    taps[...] = jnp.zeros(taps.shape, F32)
    for section in range(sections):
        for a in range(5):
            for b in range(5):
                taps[tap(section, a, b), :] = agg[a, b, section : section + 1, :]
    rest = taps[...]
    high = rest.astype(BF16)
    rest = rest - high.astype(F32)
    middle = rest.astype(BF16)
    low = (rest - middle.astype(F32)).astype(BF16)
    split = jnp.concatenate([high, middle, low], axis=0)
    count = taps.shape[0]
    weights = qkv[...].reshape(sections * channels, wide)
    for part in range(wide // half):
        here = slice(part * half, (part + 1) * half)
        for kind in range(3):
            to = kind * channels + part * LANES
            there = slice(to, to + LANES)
            value = jnp.dot(weights[:, here], picks[kind], preferred_element_type=F32)
            qkv_out[:, :, there] = value.astype(BF16).reshape(sections, channels, LANES)
            value = jnp.dot(split[:, here], picks[kind], preferred_element_type=F32)
            value = value[:count] + value[count : 2 * count] + value[2 * count :]
            agg_out[:, :, there] = value.reshape(sections, -1, LANES)
    row = lax.broadcasted_iota(jnp.int32, (head_dim, channels), 0)
    lane = lax.broadcasted_iota(jnp.int32, (head_dim, channels), 1)
    spread = jnp.where(lane % head_dim == row, 1.0, 0.0).astype(BF16)
    across = lax.broadcasted_iota(jnp.int32, (channels, channels), 0) // head_dim
    along = lax.broadcasted_iota(jnp.int32, (channels, channels), 1) // head_dim
    for section in range(sections):
        for kind in range(3):
            tall = [group[section, 3 * h + kind] for h in range(channels // head_dim)]
            value = jnp.dot(jnp.concatenate(tall, axis=0), spread, preferred_element_type=F32)
            group_out[section, kind] = jnp.where(across == along, value, 0.0).astype(BF16)
    head_out[...] = jnp.zeros(head_out.shape, BF16)
    for a in range(3):
        rows = [head[a, b] for b in range(3)] + [jnp.zeros((4, channels), BF16)]
        head_out[a, 0:16, :] = jnp.concatenate(rows, axis=0)
    stores = [pltpu.make_async_copy(made[i], outs[i], sems.at[i]) for i in range(4)]
    for store in stores:
        store.start()
    for store in stores:
        store.wait()


def first_kernel(tile, head_dim, own, row_0, row_1, col_0, col_1, *refs):
    weights, outs, scratch = refs[:9], refs[9:12], refs[12:]
    x_ref = scratch[0]
    rows, cols = tile
    x_ref[REACH : REACH + rows, 0:cols, :] = own[...]
    below = REACH + rows
    even = lax.axis_index("row") % 2 == 0
    x_ref[pl.ds(jnp.where(even, below, 0), REACH), 0:cols, :] = row_0[...]
    x_ref[pl.ds(jnp.where(even, 0, below), REACH), 0:cols, :] = row_1[...]
    even = lax.axis_index("col") % 2 == 0

    @pl.when(even)
    def _():
        x_ref[:, cols : cols + 2 * SIDE, :] = jnp.concatenate([col_0[...], col_1[...]], axis=1)

    @pl.when(jnp.logical_not(even))
    def _():
        x_ref[:, cols : cols + 2 * SIDE, :] = jnp.concatenate([col_1[...], col_0[...]], axis=1)

    front(x_ref, weights, outs, scratch[1:], REACH, tile, head_dim, 0)


def second_kernel(tile, head_dim, mixed, query, payload, other, out_weight, out_bias, *refs):
    weights, outs, scratch = refs[:9], refs[9:12], refs[12:]
    x_ref, mixed_ref, query_ref, sems = scratch[:4]
    attend(
        mixed, query, (payload, other), out_weight, out_bias, mixed_ref, query_ref, sems, head_dim,
        0, x_ref,
    )
    front(x_ref, weights, outs, scratch[4:], REACH - 3, tile, head_dim, 1)


def last_kernel(
    tile, head_dim, mixed, query, payload, other, out_weight, out_bias, head_weight, head_bias,
    map_out, boxes_out, x_ref, mixed_ref, query_ref, sems,
):
    rows, cols = tile
    width = cols + 2 * SIDE
    attend(
        mixed, query, (payload, other), out_weight, out_bias, mixed_ref, query_ref, sems, head_dim,
        1, x_ref,
    )
    clear_outside(x_ref, 1, cols)
    map_out[...] = x_ref[1 : 1 + rows, 0:cols, :]
    total = None
    for a in range(3):
        part = lax.dot_general(
            flat(x_ref[a : a + rows]), head_weight[a], (((1,), (1,)), ((), ())),
            preferred_element_type=F32,
        )
        total = part if total is None else total + part
    total = total.reshape(rows, width, LANES)
    lane = lax.broadcasted_iota(jnp.int32, (width, LANES), 1) // 4
    shifted = [
        jnp.where(
            lane == 0,
            pltpu.roll(total[r], 1, 0),
            jnp.where(lane == 2, pltpu.roll(total[r], width - 1, 0), total[r]),
        )
        for r in range(rows)
    ]
    shifted = jnp.concatenate(shifted, axis=0)
    across = lax.broadcasted_iota(jnp.int32, (8, LANES), 0)
    along = lax.broadcasted_iota(jnp.int32, (8, LANES), 1)
    fold = jnp.where((along % 4 == across) & (along < 12), 1.0, 0.0)
    boxes = lax.dot_general(
        fold, shifted, (((1,), (1,)), ((), ())), precision=lax.Precision.HIGHEST,
        preferred_element_type=F32,
    )
    boxes = boxes[0:4] + head_bias[...]
    for r in range(rows):
        boxes_out[:, r, :] = boxes[:, r * width : r * width + cols]


def near():
    return pl.BlockSpec(memory_space=pltpu.VMEM)


def far():
    return pl.BlockSpec(memory_space=pltpu.HBM)


def digits(size, most):
    radices = []
    while size > 1:
        radix = next((r for r in range(min(most, size), 1, -1) if size % r == 0), size)
        radices.append(radix)
        size //= radix
    return radices


def partner(i, stride, radix, step):
    digit = (i // stride) % radix
    other = digit ^ step if radix & (radix - 1) == 0 else (digit + step) % radix
    return i + (other - digit) * stride


def sum_by_permutes(value):
    rounds = []
    for axis in ("row", "col"):
        stride = 1
        for radix in digits(lax.axis_size(axis), 4):
            rounds.append((axis, stride, radix))
            stride *= radix
    for axis, stride, radix in rounds:
        count = lax.axis_size(axis)
        others = [
            lax.ppermute(value, axis, [(i, partner(i, stride, radix, k)) for i in range(count)])
            for k in range(1, radix)
        ]
        if (axis, stride, radix) == rounds[-1] and radix == 2:
            return value, others[0]
        total = value.astype(F32)
        for other in others:
            total = total + other.astype(F32)
        value = total.astype(BF16)
    return value, jnp.zeros_like(value)


def digits(size, most):
    radices = []
    while size > 1:
        radix = next((r for r in range(min(most, size), 1, -1) if size % r == 0), size)
        radices.append(radix)
        size //= radix
    return radices


def pair_exchange(value, axis, first):
    count = lax.axis_size(axis)
    pairs = []
    for i in range(first, count - 1, 2):
        pairs += [(i, i + 1), (i + 1, i)]
    return lax.ppermute(value, axis, pairs)


def local(
    features,
    expand_weight,
    expand_bias,
    depth_weight,
    depth_bias,
    project_weight,
    project_bias,
    qkv_weight,
    aggregate_depth,
    aggregate_group,
    output_weight,
    output_bias,
    head_weight,
    head_bias,
):
    rows, cols, channels = features.shape
    head_dim = aggregate_group.shape[2]
    heads = channels // head_dim
    width = cols + 2 * SIDE
    tile = (rows, cols)
    wide = expand_weight.shape[2]

    def edges(value, dim, size, odd):
        far = value.shape[dim] - size
        return [
            lax.dynamic_slice_in_dim(value, jnp.where(odd == at, far, 0), size, dim) for at in (0, 1)
        ]

    odd_row = lax.axis_index("row") % 2
    odd_col = lax.axis_index("col") % 2
    low, high = edges(features, 0, REACH, odd_row)
    row_halos = [pair_exchange(low, "row", 0), pair_exchange(high, "row", 1)]
    below = jnp.where(odd_row == 0, row_halos[0], row_halos[1])
    above = jnp.where(odd_row == 0, row_halos[1], row_halos[0])
    tall = jnp.concatenate([above, features, below], axis=0)
    low, high = edges(tall, 1, SIDE, odd_col)
    col_halos = [pair_exchange(low, "col", 0), pair_exchange(high, "col", 1)]

    aggregate_depth = aggregate_depth.transpose(1, 2, 0, 3)
    depth_weight = depth_weight.transpose(1, 2, 0, 3)
    params = pltpu.CompilerParams(vmem_limit_bytes=24 * 2**20)
    made = [
        jax.ShapeDtypeStruct(qkv_weight.shape, BF16),
        jax.ShapeDtypeStruct((SECTIONS, 32, 3 * channels), F32),
        jax.ShapeDtypeStruct((SECTIONS, 3, channels, channels), BF16),
        jax.ShapeDtypeStruct((3, LANES, channels), BF16),
    ]
    qkv_weight, taps, group, head_weight = pl.pallas_call(
        functools.partial(prepare_kernel, head_dim),
        out_shape=made,
        grid=(1,),
        in_specs=[near()] * 4,
        out_specs=[far()] * 4,
        scratch_shapes=[pltpu.VMEM(array.shape, array.dtype) for array in made]
        + [pltpu.VMEM((32 * SECTIONS, 3 * channels), F32), pltpu.SemaphoreType.DMA((4,))],
        compiler_params=params,
        cost_estimate=pl.CostEstimate(
            flops=2 * 10**9, bytes_accessed=4 * 10**6, transcendentals=0
        ),
        name="prepare",
    )(qkv_weight, aggregate_depth, aggregate_group, head_weight)

    weights = [
        expand_weight, expand_bias, depth_weight, depth_bias, project_weight, project_bias,
        qkv_weight, taps, group,
    ]
    weight_specs = [near()] * 6 + [far()] * 3

    def outs_of(count):
        return [
            jax.ShapeDtypeStruct((count, width, channels), BF16),
            jax.ShapeDtypeStruct((count, width, 2 * channels), BF16),
            jax.ShapeDtypeStruct((LANES + KEY_ROWS, LANES), BF16),
        ]

    def front_scratch(count):
        return [
            pltpu.VMEM((count, width, 256), BF16),
            pltpu.VMEM((count, width, 256), BF16),
            pltpu.VMEM(((count - 2) * width, channels), F32),
            pltpu.VMEM((count - 2, width, channels), BF16),
            pltpu.VMEM((count - 2, width, 3 * channels), BF16),
            pltpu.VMEM((count - 6, width, 2 * channels), BF16),
            pltpu.VMEM((9, TILE, expand_weight.shape[2]), BF16),
            pltpu.VMEM((25, TILE, 3 * channels), BF16),
            pltpu.VMEM(qkv_weight.shape[1:], BF16),
            pltpu.VMEM(taps.shape[1:], F32),
            pltpu.VMEM(group.shape[1:], BF16),
            pltpu.SemaphoreType.DMA((5,)),
        ]

    def attend_scratch(count):
        return [
            pltpu.VMEM((count, width, channels), BF16),
            pltpu.VMEM((count, width, channels), BF16),
            pltpu.VMEM((count, width, 2 * channels), BF16),
            pltpu.SemaphoreType.DMA((2, PARTS)),
        ]

    first_rows = rows + 2 * REACH
    mixed, query, payload = pl.pallas_call(
        functools.partial(first_kernel, tile, head_dim),
        out_shape=outs_of(first_rows - 6),
        grid=(1,),
        in_specs=[near()] * 5 + weight_specs,
        out_specs=[far(), far(), near()],
        scratch_shapes=[pltpu.VMEM((first_rows, width, channels), BF16)]
        + front_scratch(first_rows),
        compiler_params=params,
        name="first",
    )(features, *row_halos, *col_halos, *weights)
    payload, other = sum_by_permutes(payload)

    second_rows = first_rows - 6
    mixed, query, payload = pl.pallas_call(
        functools.partial(second_kernel, tile, head_dim),
        out_shape=outs_of(second_rows - 6),
        grid=(1,),
        in_specs=[far()] * 2 + [near()] * 4 + weight_specs,
        out_specs=[far(), far(), near()],
        scratch_shapes=attend_scratch(second_rows) + front_scratch(second_rows),
        compiler_params=params,
        name="second",
    )(mixed, query, payload, other, output_weight, output_bias, *weights)
    payload, other = sum_by_permutes(payload)

    return pl.pallas_call(
        functools.partial(last_kernel, tile, head_dim),
        out_shape=[
            jax.ShapeDtypeStruct((rows, cols, channels), BF16),
            jax.ShapeDtypeStruct((4, rows, cols), F32),
        ],
        grid=(1,),
        in_specs=[far()] * 2 + [near()] * 6,
        out_specs=[near()] * 2,
        scratch_shapes=attend_scratch(rows + 2),
        compiler_params=params,
        name="last",
    )(
        mixed, query, payload, other, output_weight, output_bias, head_weight,
        head_bias.reshape(4, 1),
    )


def solution(mesh):
    return jax.shard_map(
        local,
        mesh=mesh,
        in_specs=(P("row", "col", None),) + (P(),) * 13,
        out_specs=(P("row", "col", None), P(None, "row", "col")),
        check_vma=False,
    )
```

```python
import functools

import jax
import jax.numpy as jnp
from jax import lax
from jax.experimental import pallas as pl
from jax.experimental.pallas import tpu as pltpu
from jax.sharding import PartitionSpec as P

SECTIONS = 2
LANES = 128
SIDE = 8
REACH = 7
KEY_ROWS = 16
TILE = 16
F32 = jnp.float32
BF16 = jnp.bfloat16


def six_hard_swish(value):
    return value * jnp.minimum(jnp.maximum(value + 3.0, 0.0), 6.0)


def group_size(count, most):
    return next(n for n in range(min(most, count), 0, -1) if count % n == 0)


def by_groups(count, most, body):
    size = group_size(count, most)

    def group(index, carry):
        body(index * size, size)
        return carry

    lax.fori_loop(0, count // size, group, 0)


def clear_outside(ref, halo, cols):
    rows = ref.shape[0]
    row, col = lax.axis_index("row"), lax.axis_index("col")

    @pl.when(row == 0)
    def _():
        ref[0:halo] = jnp.zeros((halo,) + ref.shape[1:], ref.dtype)

    @pl.when(row == lax.axis_size("row") - 1)
    def _():
        ref[rows - halo : rows] = jnp.zeros((halo,) + ref.shape[1:], ref.dtype)

    @pl.when(col == 0)
    def _():
        ref[:, cols + SIDE : cols + 2 * SIDE, :] = jnp.zeros((rows, SIDE, ref.shape[2]), ref.dtype)

    @pl.when(col == lax.axis_size("col") - 1)
    def _():
        ref[:, cols : cols + SIDE, :] = jnp.zeros((rows, SIDE, ref.shape[2]), ref.dtype)


def flat(value):
    return value.reshape(-1, value.shape[-1])


def same_head(head_dim):
    across = lax.broadcasted_iota(jnp.int32, (LANES, LANES), 0) // head_dim
    along = lax.broadcasted_iota(jnp.int32, (LANES, LANES), 1) // head_dim
    return across == along


def depthwise_row(rows, taps, size, width):
    rows = [row.reshape(width // TILE, TILE, LANES) for row in rows]
    total = None
    for b in range(size):
        part = None
        for a in range(size):
            term = rows[a] * taps(a, b)[None]
            part = term if part is None else part + term
        part = part.reshape(width, LANES).astype(F32)
        if b != size // 2:
            part = pltpu.roll(part, (size // 2 - b) % width, 0)
        total = part if total is None else total + part
    return total


def front(x_ref, weights, outs, scratch, halo, tile, head_dim, section):
    expand, expand_bias, depth, depth_bias, project, project_bias = weights[:6]
    mixed_out, query_out, payload_out = outs
    (
        hidden, total, mixed, qkv, query, wide_depth, wide_agg,
        qkv_weight, agg, group, sems,
    ) = scratch
    loads = [
        pltpu.make_async_copy(weights[6].at[section], qkv_weight, sems.at[0]),
        pltpu.make_async_copy(weights[7].at[section], agg, sems.at[1]),
        pltpu.make_async_copy(weights[8].at[section], group, sems.at[2]),
    ]
    for load in loads:
        load.start()
    rows, width, channels = x_ref.shape
    tile_rows, tile_cols = tile
    inner = rows - 2
    chunk = hidden.shape[3]
    chunks = expand.shape[2] // chunk
    for index in range(9):
        taps = depth[index // 3, index % 3, section : section + 1, :] * (1.0 / 6.0)
        wide_depth[index] = jnp.broadcast_to(taps, (TILE, taps.shape[1])).astype(BF16)

    def start_rows(first, size):
        value = x_ref[pl.ds(first + 1, size)].astype(F32) + project_bias[section : section + 1, :]
        total[pl.ds(first, size)] = 6.0 * value

    by_groups(inner, 2, start_rows)

    def expand_rows(slot, at, first, size):
        value = jnp.dot(
            flat(x_ref[pl.ds(first, size)]), expand[section, :, pl.ds(at, chunk)],
            preferred_element_type=F32,
        )
        value = (value + expand_bias[section : section + 1, pl.ds(at, chunk)]).astype(BF16)
        hidden[slot, pl.ds(first, size)] = six_hard_swish(value).reshape(size, width, chunk)

    def spread_rows(slot, at, first, size):
        spread = []
        for r in range(size):
            lanes = []
            for lane in range(0, chunk, LANES):
                here = pl.ds(pl.multiple_of(at + lane, LANES), LANES)
                value = depthwise_row(
                    [hidden[slot, first + r + a, :, lane : lane + LANES] for a in range(3)],
                    lambda a, b: wide_depth[3 * a + b, :, here], 3, width,
                )
                value = (value + depth_bias[section : section + 1, here]).astype(BF16)
                lanes.append(six_hard_swish(value))
            spread.append(jnp.concatenate(lanes, axis=1))
        value = jnp.dot(
            jnp.concatenate(spread, axis=0), project[section, pl.ds(at, chunk), :],
            preferred_element_type=F32,
        )
        total[pl.ds(first, size)] += value.reshape(size, width, channels)

    size = group_size(inner, 7)
    groups = inner // size
    ahead = -(-rows // groups)

    def ahead_rows(slot, at, group):
        expand_rows(slot, at, jnp.minimum(group * ahead, rows - ahead), ahead)

    def first_rows(group, carry):
        ahead_rows(0, 0, group)
        return carry

    lax.fori_loop(0, groups, first_rows, 0)
    clear_outside(hidden.at[0], halo, tile_cols)

    def stage(index, carry):
        slot = index % 2
        at = pl.multiple_of(index * chunk, chunk)
        following = pl.multiple_of(jnp.minimum(index + 1, chunks - 1) * chunk, chunk)

        def group_rows(group, carry):
            spread_rows(slot, at, group * size, size)
            ahead_rows(1 - slot, following, group)
            return carry

        lax.fori_loop(0, groups, group_rows, 0)
        clear_outside(hidden.at[1 - slot], halo, tile_cols)
        return carry

    lax.fori_loop(0, chunks, stage, 0)

    def mixed_rows(first, size):
        mixed[pl.ds(first, size)] = (total[pl.ds(first, size)] * (1.0 / 6.0)).astype(BF16)

    by_groups(inner, 2, mixed_rows)
    outer = inner - 4
    stores = [
        pltpu.make_async_copy(mixed.at[pl.ds(2, outer)], mixed_out, sems.at[3]),
        pltpu.make_async_copy(query, query_out, sems.at[4]),
    ]
    stores[0].start()
    for load in loads:
        load.wait()
    for index in range(25):
        taps = agg[index : index + 1, :]
        wide_agg[index] = jnp.broadcast_to(taps, (TILE, taps.shape[1])).astype(BF16)

    def qkv_rows(first, size):
        value = jnp.dot(
            flat(mixed[pl.ds(first, size)]), qkv_weight[...], preferred_element_type=F32
        )
        qkv[pl.ds(first, size)] = value.astype(BF16).reshape(size, width, 3 * channels)

    by_groups(inner, 7, qkv_rows)
    around = halo - 1
    clear_outside(qkv, around, tile_cols)

    def aggregated(kind, first, size):
        scaled = []
        for r in range(size):
            lanes = []
            for lane in range(kind * channels, (kind + 1) * channels, LANES):
                here = slice(lane, lane + LANES)
                value = depthwise_row(
                    [qkv[first + r + a, :, here] for a in range(5)],
                    lambda a, b: wide_agg[5 * a + b, :, here], 5, width,
                )
                lanes.append(value.astype(BF16))
            scaled.append(jnp.concatenate(lanes, axis=1))
        value = jnp.dot(
            jnp.concatenate(scaled, axis=0), group[kind], preferred_element_type=F32
        )
        return value.astype(BF16).reshape(size, width, channels)

    def query_rows(first, size):
        here = pl.ds(first, size)
        query[here, :, 0:channels] = jnp.maximum(qkv[pl.ds(first + 2, size), :, 0:channels], 0.0)
        query[here, :, channels : 2 * channels] = jnp.maximum(aggregated(0, first, size), 0.0)

    by_groups(outer, 5, query_rows)
    stores[1].start()
    size = group_size(tile_rows, 4)

    def summed(key, value):
        key = jnp.maximum(flat(key[:, 0:tile_cols]), 0.0)
        value = flat(value[:, 0:tile_cols])
        products = [
            lax.dot_general(
                key[:, lane : lane + LANES], value[:, lane : lane + LANES],
                (((0,), (0,)), ((), ())), preferred_element_type=F32,
            )
            for lane in range(0, channels, LANES)
        ]
        return products, jnp.sum(key.astype(F32), axis=0, keepdims=True)

    mine = slice(around, around + tile_rows)
    products, sums = summed(
        qkv[mine, :, channels : 2 * channels], qkv[mine, :, 2 * channels : 3 * channels]
    )

    def grouped_rows(index, carry):
        at = around - 2 + index * size
        more, sums = summed(aggregated(1, at, size), aggregated(2, at, size))
        return [a + b for a, b in zip(carry[0], more)], carry[1] + sums

    more, more_sums = lax.fori_loop(
        0, tile_rows // size, grouped_rows,
        ([jnp.zeros((LANES, LANES), F32) for _ in products], jnp.zeros_like(sums)),
    )
    products = products + more
    sums = jnp.concatenate([sums, more_sums], axis=1)
    same = same_head(head_dim)
    summary = jnp.zeros((LANES, LANES), F32)
    key_sums = []
    for index, product in enumerate(products):
        product = jnp.where(same, product, 0.0)
        if index:
            product = pltpu.roll(product, index * head_dim, 1)
        summary = summary + product
        key_sums.append(sums[:, index * LANES : (index + 1) * LANES])
    key_sums.append(jnp.zeros((KEY_ROWS - len(products), LANES), F32))
    payload_out[0:LANES, :] = summary.astype(BF16)
    payload_out[LANES : LANES + KEY_ROWS, :] = jnp.concatenate(key_sums, axis=0).astype(BF16)
    for store in stores:
        store.wait()


def attend(
    mixed_in, query_in, payloads, weight, bias, mixed_ref, query_ref, sems, head_dim, section, x_ref
):
    rows, width, channels = x_ref.shape
    halves = [(query_in, query_ref), (mixed_in, mixed_ref)]
    loads = [pltpu.make_async_copy(a, b, sems.at[k]) for k, (a, b) in enumerate(halves)]
    for load in loads:
        load.start()
    same = same_head(head_dim)
    square = (LANES, LANES)
    diagonal = lax.broadcasted_iota(jnp.int32, square, 0) == lax.broadcasted_iota(
        jnp.int32, square, 1
    )
    ones = jnp.where(same, 1.0, 0.0).astype(BF16)
    nothing = jnp.zeros(square, BF16)
    payload = payloads[0][...].astype(F32)
    for part in payloads[1:]:
        payload = payload + part[...].astype(F32)
    packed = payload[0:LANES]
    count = 2 * channels // LANES
    summaries, sums = [], []
    for index in range(count):
        summary = packed if index == 0 else pltpu.roll(packed, LANES - index * head_dim, 1)
        summaries.append(jnp.where(same, summary, 0.0).astype(BF16))
        keys = payload[LANES + index : LANES + index + 1]
        keys = jnp.where(diagonal, keys, 0.0).astype(BF16)
        sums.append(jnp.dot(keys, ones, preferred_element_type=F32).astype(BF16))

    def paired(blocks, index):
        return jnp.concatenate(
            [
                jnp.concatenate([blocks[index], nothing], axis=1),
                jnp.concatenate([nothing, blocks[index + 1]], axis=1),
            ],
            axis=0,
        )

    summaries = [paired(summaries, index) for index in range(0, count, 2)]
    sums = [paired(sums, index) for index in range(0, count, 2)]
    step = 2 * LANES
    for load in loads:
        load.wait()

    def attend_rows(first, size):
        query = flat(query_ref[pl.ds(first, size)])
        parts = []
        for branch in range(count // 2):
            part = query[:, branch * step : (branch + 1) * step]
            numer = jnp.dot(part, summaries[branch], preferred_element_type=F32)
            denom = jnp.dot(part, sums[branch], preferred_element_type=F32) + 1e-6
            inverse = pl.reciprocal(denom, approx=True)
            inverse = inverse * (2.0 - denom * inverse)
            parts.append((numer * inverse).astype(BF16))
        value = jnp.dot(
            jnp.concatenate(parts, axis=1), weight[section], preferred_element_type=F32
        )
        value = value + bias[section : section + 1, :]
        value = value + flat(mixed_ref[pl.ds(first, size)]).astype(F32)
        x_ref[pl.ds(first, size)] = value.astype(BF16).reshape(size, width, channels)

    by_groups(rows, 5, attend_rows)


def tap(section, a, b):
    at = 32 * section + 5 * a + b
    return slice(at, at + 1)


def prepare_kernel(head_dim, qkv, agg, group, head, *refs):
    outs, made, taps, sems = refs[:4], refs[4:8], refs[8], refs[9]
    qkv_out, agg_out, group_out, head_out = made
    sections, channels, wide = qkv.shape
    half = 3 * LANES
    heads = LANES // head_dim
    src = lax.broadcasted_iota(jnp.int32, (half, LANES), 0)
    dst = lax.broadcasted_iota(jnp.int32, (half, LANES), 1)
    first = (dst // head_dim) * 3 * head_dim + dst % head_dim
    picks = [jnp.where(src == first + k * head_dim, 1.0, 0.0).astype(BF16) for k in range(3)]
    taps[...] = jnp.zeros(taps.shape, F32)
    for section in range(sections):
        for a in range(5):
            for b in range(5):
                taps[tap(section, a, b), :] = agg[a, b, section : section + 1, :]
    rest = taps[...]
    high = rest.astype(BF16)
    rest = rest - high.astype(F32)
    middle = rest.astype(BF16)
    low = (rest - middle.astype(F32)).astype(BF16)
    split = jnp.concatenate([high, middle, low], axis=0)
    count = taps.shape[0]
    weights = qkv[...].reshape(sections * channels, wide)
    for part in range(wide // half):
        here = slice(part * half, (part + 1) * half)
        for kind in range(3):
            to = kind * channels + part * LANES
            there = slice(to, to + LANES)
            value = jnp.dot(weights[:, here], picks[kind], preferred_element_type=F32)
            qkv_out[:, :, there] = value.astype(BF16).reshape(sections, channels, LANES)
            value = jnp.dot(split[:, here], picks[kind], preferred_element_type=F32)
            value = value[:count] + value[count : 2 * count] + value[2 * count :]
            agg_out[:, :, there] = value.reshape(sections, -1, LANES)
    row = lax.broadcasted_iota(jnp.int32, (head_dim, channels), 0)
    lane = lax.broadcasted_iota(jnp.int32, (head_dim, channels), 1)
    spread = jnp.where(lane % head_dim == row, 1.0, 0.0).astype(BF16)
    across = lax.broadcasted_iota(jnp.int32, (channels, channels), 0) // head_dim
    along = lax.broadcasted_iota(jnp.int32, (channels, channels), 1) // head_dim
    for section in range(sections):
        for kind in range(3):
            tall = [group[section, 3 * h + kind] for h in range(channels // head_dim)]
            value = jnp.dot(jnp.concatenate(tall, axis=0), spread, preferred_element_type=F32)
            group_out[section, kind] = jnp.where(across == along, value, 0.0).astype(BF16)
    head_out[...] = jnp.zeros(head_out.shape, BF16)
    for a in range(3):
        rows = [head[a, b] for b in range(3)] + [jnp.zeros((4, channels), BF16)]
        head_out[a, 0:16, :] = jnp.concatenate(rows, axis=0)
    stores = [pltpu.make_async_copy(made[i], outs[i], sems.at[i]) for i in range(4)]
    for store in stores:
        store.start()
    for store in stores:
        store.wait()


def first_kernel(tile, head_dim, own, row_0, row_1, col_0, col_1, *refs):
    weights, outs, scratch = refs[:9], refs[9:12], refs[12:]
    x_ref = scratch[0]
    rows, cols = tile
    x_ref[REACH : REACH + rows, 0:cols, :] = own[...]
    below = REACH + rows
    even = lax.axis_index("row") % 2 == 0
    x_ref[pl.ds(jnp.where(even, below, 0), REACH), 0:cols, :] = row_0[...]
    x_ref[pl.ds(jnp.where(even, 0, below), REACH), 0:cols, :] = row_1[...]
    even = lax.axis_index("col") % 2 == 0

    @pl.when(even)
    def _():
        x_ref[:, cols : cols + 2 * SIDE, :] = jnp.concatenate([col_0[...], col_1[...]], axis=1)

    @pl.when(jnp.logical_not(even))
    def _():
        x_ref[:, cols : cols + 2 * SIDE, :] = jnp.concatenate([col_1[...], col_0[...]], axis=1)

    front(x_ref, weights, outs, scratch[1:], REACH, tile, head_dim, 0)


def second_kernel(tile, head_dim, mixed, query, payload, other, out_weight, out_bias, *refs):
    weights, outs, scratch = refs[:9], refs[9:12], refs[12:]
    x_ref, mixed_ref, query_ref, sems = scratch[:4]
    attend(
        mixed, query, (payload, other), out_weight, out_bias, mixed_ref, query_ref, sems, head_dim,
        0, x_ref,
    )
    front(x_ref, weights, outs, scratch[4:], REACH - 3, tile, head_dim, 1)


def last_kernel(
    tile, head_dim, mixed, query, payload, other, out_weight, out_bias, head_weight, head_bias,
    map_out, boxes_out, x_ref, mixed_ref, query_ref, sems,
):
    rows, cols = tile
    width = cols + 2 * SIDE
    attend(
        mixed, query, (payload, other), out_weight, out_bias, mixed_ref, query_ref, sems, head_dim,
        1, x_ref,
    )
    clear_outside(x_ref, 1, cols)
    map_out[...] = x_ref[1 : 1 + rows, 0:cols, :]
    total = None
    for a in range(3):
        part = lax.dot_general(
            flat(x_ref[a : a + rows]), head_weight[a], (((1,), (1,)), ((), ())),
            preferred_element_type=F32,
        )
        total = part if total is None else total + part
    total = total.reshape(rows, width, LANES)
    lane = lax.broadcasted_iota(jnp.int32, (width, LANES), 1) // 4
    shifted = [
        jnp.where(
            lane == 0,
            pltpu.roll(total[r], 1, 0),
            jnp.where(lane == 2, pltpu.roll(total[r], width - 1, 0), total[r]),
        )
        for r in range(rows)
    ]
    shifted = jnp.concatenate(shifted, axis=0)
    across = lax.broadcasted_iota(jnp.int32, (8, LANES), 0)
    along = lax.broadcasted_iota(jnp.int32, (8, LANES), 1)
    fold = jnp.where((along % 4 == across) & (along < 12), 1.0, 0.0)
    boxes = lax.dot_general(
        fold, shifted, (((1,), (1,)), ((), ())), precision=lax.Precision.HIGHEST,
        preferred_element_type=F32,
    )
    boxes = boxes[0:4] + head_bias[...]
    for r in range(rows):
        boxes_out[:, r, :] = boxes[:, r * width : r * width + cols]


def near():
    return pl.BlockSpec(memory_space=pltpu.VMEM)


def far():
    return pl.BlockSpec(memory_space=pltpu.HBM)


def digits(size, most):
    radices = []
    while size > 1:
        radix = next((r for r in range(min(most, size), 1, -1) if size % r == 0), size)
        radices.append(radix)
        size //= radix
    return radices


def partner(i, stride, radix, step):
    digit = (i // stride) % radix
    other = digit ^ step if radix & (radix - 1) == 0 else (digit + step) % radix
    return i + (other - digit) * stride


def sum_by_permutes(value):
    rounds = []
    for axis in ("row", "col"):
        stride = 1
        for radix in digits(lax.axis_size(axis), 4):
            rounds.append((axis, stride, radix))
            stride *= radix
    for axis, stride, radix in rounds:
        count = lax.axis_size(axis)
        others = [
            lax.ppermute(value, axis, [(i, partner(i, stride, radix, k)) for i in range(count)])
            for k in range(1, radix)
        ]
        if (axis, stride, radix) == rounds[-1] and radix == 2:
            return value, others[0]
        total = value.astype(F32)
        for other in others:
            total = total + other.astype(F32)
        value = total.astype(BF16)
    return value, jnp.zeros_like(value)


def digits(size, most):
    radices = []
    while size > 1:
        radix = next((r for r in range(min(most, size), 1, -1) if size % r == 0), size)
        radices.append(radix)
        size //= radix
    return radices


def pair_exchange(value, axis, first):
    count = lax.axis_size(axis)
    pairs = []
    for i in range(first, count - 1, 2):
        pairs += [(i, i + 1), (i + 1, i)]
    return lax.ppermute(value, axis, pairs)


def local(
    features,
    expand_weight,
    expand_bias,
    depth_weight,
    depth_bias,
    project_weight,
    project_bias,
    qkv_weight,
    aggregate_depth,
    aggregate_group,
    output_weight,
    output_bias,
    head_weight,
    head_bias,
):
    rows, cols, channels = features.shape
    head_dim = aggregate_group.shape[2]
    heads = channels // head_dim
    width = cols + 2 * SIDE
    tile = (rows, cols)
    wide = expand_weight.shape[2]

    def edges(value, dim, size, odd):
        far = value.shape[dim] - size
        return [
            lax.dynamic_slice_in_dim(value, jnp.where(odd == at, far, 0), size, dim) for at in (0, 1)
        ]

    odd_row = lax.axis_index("row") % 2
    odd_col = lax.axis_index("col") % 2
    low, high = edges(features, 0, REACH, odd_row)
    row_halos = [pair_exchange(low, "row", 0), pair_exchange(high, "row", 1)]
    below = jnp.where(odd_row == 0, row_halos[0], row_halos[1])
    above = jnp.where(odd_row == 0, row_halos[1], row_halos[0])
    tall = jnp.concatenate([above, features, below], axis=0)
    low, high = edges(tall, 1, SIDE, odd_col)
    col_halos = [pair_exchange(low, "col", 0), pair_exchange(high, "col", 1)]

    aggregate_depth = aggregate_depth.transpose(1, 2, 0, 3)
    depth_weight = depth_weight.transpose(1, 2, 0, 3)
    params = pltpu.CompilerParams(vmem_limit_bytes=24 * 2**20)
    made = [
        jax.ShapeDtypeStruct(qkv_weight.shape, BF16),
        jax.ShapeDtypeStruct((SECTIONS, 32, 3 * channels), F32),
        jax.ShapeDtypeStruct((SECTIONS, 3, channels, channels), BF16),
        jax.ShapeDtypeStruct((3, LANES, channels), BF16),
    ]
    qkv_weight, taps, group, head_weight = pl.pallas_call(
        functools.partial(prepare_kernel, head_dim),
        out_shape=made,
        grid=(1,),
        in_specs=[near()] * 4,
        out_specs=[far()] * 4,
        scratch_shapes=[pltpu.VMEM(array.shape, array.dtype) for array in made]
        + [pltpu.VMEM((32 * SECTIONS, 3 * channels), F32), pltpu.SemaphoreType.DMA((4,))],
        compiler_params=params,
        cost_estimate=pl.CostEstimate(
            flops=2 * 10**9, bytes_accessed=4 * 10**6, transcendentals=0
        ),
        name="prepare",
    )(qkv_weight, aggregate_depth, aggregate_group, head_weight)

    weights = [
        expand_weight, expand_bias, depth_weight, depth_bias, project_weight, project_bias,
        qkv_weight, taps, group,
    ]
    weight_specs = [near()] * 6 + [far()] * 3

    def outs_of(count):
        return [
            jax.ShapeDtypeStruct((count, width, channels), BF16),
            jax.ShapeDtypeStruct((count, width, 2 * channels), BF16),
            jax.ShapeDtypeStruct((LANES + KEY_ROWS, LANES), BF16),
        ]

    def front_scratch(count):
        return [
            pltpu.VMEM((2, count, width, 256), BF16),
            pltpu.VMEM((count - 2, width, channels), F32),
            pltpu.VMEM((count - 2, width, channels), BF16),
            pltpu.VMEM((count - 2, width, 3 * channels), BF16),
            pltpu.VMEM((count - 6, width, 2 * channels), BF16),
            pltpu.VMEM((9, TILE, expand_weight.shape[2]), BF16),
            pltpu.VMEM((25, TILE, 3 * channels), BF16),
            pltpu.VMEM(qkv_weight.shape[1:], BF16),
            pltpu.VMEM(taps.shape[1:], F32),
            pltpu.VMEM(group.shape[1:], BF16),
            pltpu.SemaphoreType.DMA((5,)),
        ]

    def attend_scratch(count):
        return [
            pltpu.VMEM((count, width, channels), BF16),
            pltpu.VMEM((count, width, channels), BF16),
            pltpu.VMEM((count, width, 2 * channels), BF16),
            pltpu.SemaphoreType.DMA((2,)),
        ]

    first_rows = rows + 2 * REACH
    mixed, query, payload = pl.pallas_call(
        functools.partial(first_kernel, tile, head_dim),
        out_shape=outs_of(first_rows - 6),
        grid=(1,),
        in_specs=[near()] * 5 + weight_specs,
        out_specs=[far(), far(), near()],
        scratch_shapes=[pltpu.VMEM((first_rows, width, channels), BF16)]
        + front_scratch(first_rows),
        compiler_params=params,
        name="first",
    )(features, *row_halos, *col_halos, *weights)
    payload, other = sum_by_permutes(payload)

    second_rows = first_rows - 6
    mixed, query, payload = pl.pallas_call(
        functools.partial(second_kernel, tile, head_dim),
        out_shape=outs_of(second_rows - 6),
        grid=(1,),
        in_specs=[far()] * 2 + [near()] * 4 + weight_specs,
        out_specs=[far(), far(), near()],
        scratch_shapes=attend_scratch(second_rows) + front_scratch(second_rows),
        compiler_params=params,
        name="second",
    )(mixed, query, payload, other, output_weight, output_bias, *weights)
    payload, other = sum_by_permutes(payload)

    return pl.pallas_call(
        functools.partial(last_kernel, tile, head_dim),
        out_shape=[
            jax.ShapeDtypeStruct((rows, cols, channels), BF16),
            jax.ShapeDtypeStruct((4, rows, cols), F32),
        ],
        grid=(1,),
        in_specs=[far()] * 2 + [near()] * 6,
        out_specs=[near()] * 2,
        scratch_shapes=attend_scratch(rows + 2),
        compiler_params=params,
        name="last",
    )(
        mixed, query, payload, other, output_weight, output_bias, head_weight,
        head_bias.reshape(4, 1),
    )


def solution(mesh):
    return jax.shard_map(
        local,
        mesh=mesh,
        in_specs=(P("row", "col", None),) + (P(),) * 13,
        out_specs=(P("row", "col", None), P(None, "row", "col")),
        check_vma=False,
    )
```

```python
import functools

import jax
import jax.numpy as jnp
from jax import lax
from jax.experimental import pallas as pl
from jax.experimental.pallas import tpu as pltpu
from jax.sharding import PartitionSpec as P

SECTIONS = 2
LANES = 128
SIDE = 8
REACH = 7
KEY_ROWS = 16
TILE = 16
PARTS = 4
F32 = jnp.float32
BF16 = jnp.bfloat16


def six_hard_swish(value):
    return value * jnp.minimum(jnp.maximum(value + 3.0, 0.0), 6.0)


def parted(count, parts):
    cuts = [count * k // parts for k in range(parts + 1)]
    return [(a, b - a) for a, b in zip(cuts, cuts[1:]) if b > a]


def group_size(count, most):
    return next(n for n in range(min(most, count), 0, -1) if count % n == 0)


def by_groups(count, most, body):
    size = group_size(count, most)

    def group(index, carry):
        body(index * size, size)
        return carry

    lax.fori_loop(0, count // size, group, 0)


def clear_outside(ref, halo, cols):
    rows = ref.shape[0]
    row, col = lax.axis_index("row"), lax.axis_index("col")

    @pl.when(row == 0)
    def _():
        ref[0:halo] = jnp.zeros((halo,) + ref.shape[1:], ref.dtype)

    @pl.when(row == lax.axis_size("row") - 1)
    def _():
        ref[rows - halo : rows] = jnp.zeros((halo,) + ref.shape[1:], ref.dtype)

    @pl.when(col == 0)
    def _():
        ref[:, cols + SIDE : cols + 2 * SIDE, :] = jnp.zeros((rows, SIDE, ref.shape[2]), ref.dtype)

    @pl.when(col == lax.axis_size("col") - 1)
    def _():
        ref[:, cols : cols + SIDE, :] = jnp.zeros((rows, SIDE, ref.shape[2]), ref.dtype)


def flat(value):
    return value.reshape(-1, value.shape[-1])


def same_head(head_dim):
    across = lax.broadcasted_iota(jnp.int32, (LANES, LANES), 0) // head_dim
    along = lax.broadcasted_iota(jnp.int32, (LANES, LANES), 1) // head_dim
    return across == along


def depthwise_row(rows, taps, size, width):
    rows = [row.reshape(width // TILE, TILE, LANES) for row in rows]
    total = None
    for b in range(size):
        part = None
        for a in range(size):
            term = rows[a] * taps(a, b)[None]
            part = term if part is None else part + term
        part = part.reshape(width, LANES).astype(F32)
        if b != size // 2:
            part = pltpu.roll(part, (size // 2 - b) % width, 0)
        total = part if total is None else total + part
    return total


def front(x_ref, weights, outs, scratch, halo, tile, head_dim, section):
    expand, expand_bias, depth, depth_bias, project, project_bias = weights[:6]
    mixed_out, query_out, payload_out = outs
    (
        hidden_0, hidden_1, total, mixed, qkv, query, wide_depth, wide_agg,
        qkv_weight, agg, group, sems,
    ) = scratch
    loads = [
        pltpu.make_async_copy(weights[6].at[section], qkv_weight, sems.at[0]),
        pltpu.make_async_copy(weights[7].at[section], agg, sems.at[1]),
        pltpu.make_async_copy(weights[8].at[section], group, sems.at[2]),
    ]
    for load in loads:
        load.start()
    rows, width, channels = x_ref.shape
    tile_rows, tile_cols = tile
    inner = rows - 2
    chunk = hidden_0.shape[2]
    chunks = expand.shape[2] // chunk
    for index in range(9):
        taps = depth[index // 3, index % 3, section : section + 1, :] * (1.0 / 6.0)
        wide_depth[index] = jnp.broadcast_to(taps, (TILE, taps.shape[1])).astype(BF16)
    total[...] = 6.0 * (flat(x_ref[1 : rows - 1]).astype(F32) + project_bias[section : section + 1, :])

    def expand_rows(out, at, first, size):
        value = jnp.dot(
            flat(x_ref[first : first + size]), expand[section, :, pl.ds(at, chunk)],
            preferred_element_type=F32,
        )
        value = (value + expand_bias[section : section + 1, pl.ds(at, chunk)]).astype(BF16)
        out[first : first + size] = six_hard_swish(value).reshape(size, width, chunk)

    def spread_rows(hidden, at, first, size):
        spread = []
        for r in range(first, first + size):
            lanes = []
            for lane in range(0, chunk, LANES):
                here = pl.ds(pl.multiple_of(at + lane, LANES), LANES)
                value = depthwise_row(
                    [hidden[r + a, :, lane : lane + LANES] for a in range(3)],
                    lambda a, b: wide_depth[3 * a + b, :, here], 3, width,
                )
                value = (value + depth_bias[section : section + 1, here]).astype(BF16)
                lanes.append(six_hard_swish(value))
            spread.append(jnp.concatenate(lanes, axis=1))
        pixels = slice(first * width, (first + size) * width)
        total[pixels] += jnp.dot(
            jnp.concatenate(spread, axis=0), project[section, pl.ds(at, chunk), :],
            preferred_element_type=F32,
        )

    def stage(index, current, following):
        at = pl.multiple_of(index * chunk, chunk)
        ahead = pl.multiple_of(jnp.minimum(index + 1, chunks - 1) * chunk, chunk)
        for (first, size), (from_row, count) in zip(parted(inner, PARTS), parted(rows, PARTS)):
            expand_rows(following, ahead, from_row, count)
            spread_rows(current, at, first, size)
        clear_outside(following, halo, tile_cols)

    for first, size in parted(rows, PARTS):
        expand_rows(hidden_0, 0, first, size)
    clear_outside(hidden_0, halo, tile_cols)

    def two_stages(index, carry):
        stage(2 * index, hidden_0, hidden_1)
        stage(2 * index + 1, hidden_1, hidden_0)
        return carry

    lax.fori_loop(0, chunks // 2, two_stages, 0)
    mixed[...] = (total[...] * (1.0 / 6.0)).astype(BF16).reshape(inner, width, channels)
    outer = inner - 4
    stores = [
        pltpu.make_async_copy(mixed.at[pl.ds(2, outer)], mixed_out, sems.at[3]),
        pltpu.make_async_copy(query, query_out, sems.at[4]),
    ]
    stores[0].start()
    for load in loads:
        load.wait()
    for index in range(25):
        taps = agg[index : index + 1, :]
        wide_agg[index] = jnp.broadcast_to(taps, (TILE, taps.shape[1])).astype(BF16)
    for first, size in parted(inner, PARTS):
        value = jnp.dot(
            flat(mixed[first : first + size]), qkv_weight[...], preferred_element_type=F32
        )
        qkv[first : first + size] = value.astype(BF16).reshape(size, width, 3 * channels)
    around = halo - 1
    clear_outside(qkv, around, tile_cols)

    def aggregated(kind, first, size):
        scaled = []
        for r in range(size):
            lanes = []
            for lane in range(kind * channels, (kind + 1) * channels, LANES):
                here = slice(lane, lane + LANES)
                value = depthwise_row(
                    [qkv[first + r + a, :, here] for a in range(5)],
                    lambda a, b: wide_agg[5 * a + b, :, here], 5, width,
                )
                lanes.append(value.astype(BF16))
            scaled.append(jnp.concatenate(lanes, axis=1))
        value = jnp.dot(
            jnp.concatenate(scaled, axis=0), group[kind], preferred_element_type=F32
        )
        return value.astype(BF16).reshape(size, width, channels)

    query[:, :, 0:channels] = jnp.maximum(qkv[2 : inner - 2, :, 0:channels], 0.0)
    size = next(n for n in range(5, 0, -1) if outer % n == 0)

    def query_rows(index, carry):
        at = index * size
        query[pl.ds(at, size), :, channels : 2 * channels] = jnp.maximum(
            aggregated(0, at, size), 0.0
        )
        return carry

    lax.fori_loop(0, outer // size, query_rows, 0)
    stores[1].start()
    size = next(n for n in range(4, 0, -1) if tile_rows % n == 0)

    def summed(key, value):
        key = jnp.maximum(flat(key[:, 0:tile_cols]), 0.0)
        value = flat(value[:, 0:tile_cols])
        products = [
            lax.dot_general(
                key[:, lane : lane + LANES], value[:, lane : lane + LANES],
                (((0,), (0,)), ((), ())), preferred_element_type=F32,
            )
            for lane in range(0, channels, LANES)
        ]
        return products, jnp.sum(key.astype(F32), axis=0, keepdims=True)

    mine = slice(around, around + tile_rows)
    products, sums = summed(
        qkv[mine, :, channels : 2 * channels], qkv[mine, :, 2 * channels : 3 * channels]
    )

    def grouped_rows(index, carry):
        at = around - 2 + index * size
        more, sums = summed(aggregated(1, at, size), aggregated(2, at, size))
        return [a + b for a, b in zip(carry[0], more)], carry[1] + sums

    more, more_sums = lax.fori_loop(
        0, tile_rows // size, grouped_rows,
        ([jnp.zeros((LANES, LANES), F32) for _ in products], jnp.zeros_like(sums)),
    )
    products = products + more
    sums = jnp.concatenate([sums, more_sums], axis=1)
    same = same_head(head_dim)
    summary = jnp.zeros((LANES, LANES), F32)
    key_sums = []
    for index, product in enumerate(products):
        product = jnp.where(same, product, 0.0)
        if index:
            product = pltpu.roll(product, index * head_dim, 1)
        summary = summary + product
        key_sums.append(sums[:, index * LANES : (index + 1) * LANES])
    key_sums.append(jnp.zeros((KEY_ROWS - len(products), LANES), F32))
    payload_out[0:LANES, :] = summary.astype(BF16)
    payload_out[LANES : LANES + KEY_ROWS, :] = jnp.concatenate(key_sums, axis=0).astype(BF16)
    for store in stores:
        store.wait()


def attend(
    mixed_in, query_in, payloads, weight, bias, mixed_ref, query_ref, sems, head_dim, section, x_ref
):
    rows, width, channels = x_ref.shape
    halves = [(query_in, query_ref), (mixed_in, mixed_ref)]
    loads = [pltpu.make_async_copy(a, b, sems.at[k]) for k, (a, b) in enumerate(halves)]
    for load in loads:
        load.start()
    same = same_head(head_dim)
    square = (LANES, LANES)
    diagonal = lax.broadcasted_iota(jnp.int32, square, 0) == lax.broadcasted_iota(
        jnp.int32, square, 1
    )
    ones = jnp.where(same, 1.0, 0.0).astype(BF16)
    nothing = jnp.zeros(square, BF16)
    payload = payloads[0][...].astype(F32)
    for part in payloads[1:]:
        payload = payload + part[...].astype(F32)
    packed = payload[0:LANES]
    count = 2 * channels // LANES
    summaries, sums = [], []
    for index in range(count):
        summary = packed if index == 0 else pltpu.roll(packed, LANES - index * head_dim, 1)
        summaries.append(jnp.where(same, summary, 0.0).astype(BF16))
        keys = payload[LANES + index : LANES + index + 1]
        keys = jnp.where(diagonal, keys, 0.0).astype(BF16)
        sums.append(jnp.dot(keys, ones, preferred_element_type=F32).astype(BF16))

    def paired(blocks, index):
        return jnp.concatenate(
            [
                jnp.concatenate([blocks[index], nothing], axis=1),
                jnp.concatenate([nothing, blocks[index + 1]], axis=1),
            ],
            axis=0,
        )

    summaries = [paired(summaries, index) for index in range(0, count, 2)]
    sums = [paired(sums, index) for index in range(0, count, 2)]
    step = 2 * LANES
    for load in loads:
        load.wait()

    def attend_rows(first, size):
        query = flat(query_ref[pl.ds(first, size)])
        parts = []
        for branch in range(count // 2):
            part = query[:, branch * step : (branch + 1) * step]
            numer = jnp.dot(part, summaries[branch], preferred_element_type=F32)
            denom = jnp.dot(part, sums[branch], preferred_element_type=F32) + 1e-6
            inverse = pl.reciprocal(denom, approx=True)
            inverse = inverse * (2.0 - denom * inverse)
            parts.append((numer * inverse).astype(BF16))
        value = jnp.dot(
            jnp.concatenate(parts, axis=1), weight[section], preferred_element_type=F32
        )
        value = value + bias[section : section + 1, :]
        value = value + flat(mixed_ref[pl.ds(first, size)]).astype(F32)
        x_ref[pl.ds(first, size)] = value.astype(BF16).reshape(size, width, channels)

    by_groups(rows, 5, attend_rows)


def tap(section, a, b):
    at = 32 * section + 5 * a + b
    return slice(at, at + 1)


def prepare_kernel(head_dim, qkv, agg, group, head, *refs):
    outs, made, taps, sems = refs[:4], refs[4:8], refs[8], refs[9]
    qkv_out, agg_out, group_out, head_out = made
    sections, channels, wide = qkv.shape
    half = 3 * LANES
    heads = LANES // head_dim
    src = lax.broadcasted_iota(jnp.int32, (half, LANES), 0)
    dst = lax.broadcasted_iota(jnp.int32, (half, LANES), 1)
    first = (dst // head_dim) * 3 * head_dim + dst % head_dim
    picks = [jnp.where(src == first + k * head_dim, 1.0, 0.0).astype(BF16) for k in range(3)]
    taps[...] = jnp.zeros(taps.shape, F32)
    for section in range(sections):
        for a in range(5):
            for b in range(5):
                taps[tap(section, a, b), :] = agg[a, b, section : section + 1, :]
    rest = taps[...]
    high = rest.astype(BF16)
    rest = rest - high.astype(F32)
    middle = rest.astype(BF16)
    low = (rest - middle.astype(F32)).astype(BF16)
    split = jnp.concatenate([high, middle, low], axis=0)
    count = taps.shape[0]
    weights = qkv[...].reshape(sections * channels, wide)
    for part in range(wide // half):
        here = slice(part * half, (part + 1) * half)
        for kind in range(3):
            to = kind * channels + part * LANES
            there = slice(to, to + LANES)
            value = jnp.dot(weights[:, here], picks[kind], preferred_element_type=F32)
            qkv_out[:, :, there] = value.astype(BF16).reshape(sections, channels, LANES)
            value = jnp.dot(split[:, here], picks[kind], preferred_element_type=F32)
            value = value[:count] + value[count : 2 * count] + value[2 * count :]
            agg_out[:, :, there] = value.reshape(sections, -1, LANES)
    row = lax.broadcasted_iota(jnp.int32, (head_dim, channels), 0)
    lane = lax.broadcasted_iota(jnp.int32, (head_dim, channels), 1)
    spread = jnp.where(lane % head_dim == row, 1.0, 0.0).astype(BF16)
    across = lax.broadcasted_iota(jnp.int32, (channels, channels), 0) // head_dim
    along = lax.broadcasted_iota(jnp.int32, (channels, channels), 1) // head_dim
    for section in range(sections):
        for kind in range(3):
            tall = [group[section, 3 * h + kind] for h in range(channels // head_dim)]
            value = jnp.dot(jnp.concatenate(tall, axis=0), spread, preferred_element_type=F32)
            group_out[section, kind] = jnp.where(across == along, value, 0.0).astype(BF16)
    head_out[...] = jnp.zeros(head_out.shape, BF16)
    for a in range(3):
        rows = [head[a, b] for b in range(3)] + [jnp.zeros((4, channels), BF16)]
        head_out[a, 0:16, :] = jnp.concatenate(rows, axis=0)
    stores = [pltpu.make_async_copy(made[i], outs[i], sems.at[i]) for i in range(4)]
    for store in stores:
        store.start()
    for store in stores:
        store.wait()


def first_kernel(tile, head_dim, own, row_0, row_1, *refs):
    weights, outs, scratch = refs[:9], refs[9:12], refs[12:]
    x_ref = scratch[0]
    rows, cols = tile
    below = REACH + rows
    even = lax.axis_index("row") & 1 == 0
    x_ref[REACH:below] = own[...]
    x_ref[pl.ds(jnp.where(even, below, 0), REACH)] = row_0[...]
    x_ref[pl.ds(jnp.where(even, 0, below), REACH)] = row_1[...]
    front(x_ref, weights, outs, scratch[1:], REACH, tile, head_dim, 0)


def second_kernel(tile, head_dim, mixed, query, payload, other, out_weight, out_bias, *refs):
    weights, outs, scratch = refs[:9], refs[9:12], refs[12:]
    x_ref, mixed_ref, query_ref, sems = scratch[:4]
    attend(
        mixed, query, (payload, other), out_weight, out_bias, mixed_ref, query_ref, sems, head_dim,
        0, x_ref,
    )
    front(x_ref, weights, outs, scratch[4:], REACH - 3, tile, head_dim, 1)


def last_kernel(
    tile, head_dim, mixed, query, payload, other, out_weight, out_bias, head_weight, head_bias,
    map_out, boxes_out, x_ref, mixed_ref, query_ref, sems,
):
    rows, cols = tile
    width = cols + 2 * SIDE
    attend(
        mixed, query, (payload, other), out_weight, out_bias, mixed_ref, query_ref, sems, head_dim,
        1, x_ref,
    )
    clear_outside(x_ref, 1, cols)
    map_out[...] = x_ref[1 : 1 + rows, 0:cols, :]
    total = None
    for a in range(3):
        part = lax.dot_general(
            flat(x_ref[a : a + rows]), head_weight[a], (((1,), (1,)), ((), ())),
            preferred_element_type=F32,
        )
        total = part if total is None else total + part
    total = total.reshape(rows, width, LANES)
    lane = lax.broadcasted_iota(jnp.int32, (width, LANES), 1) // 4
    shifted = [
        jnp.where(
            lane == 0,
            pltpu.roll(total[r], 1, 0),
            jnp.where(lane == 2, pltpu.roll(total[r], width - 1, 0), total[r]),
        )
        for r in range(rows)
    ]
    shifted = jnp.concatenate(shifted, axis=0)
    across = lax.broadcasted_iota(jnp.int32, (8, LANES), 0)
    along = lax.broadcasted_iota(jnp.int32, (8, LANES), 1)
    fold = jnp.where((along % 4 == across) & (along < 12), 1.0, 0.0)
    boxes = lax.dot_general(
        fold, shifted, (((1,), (1,)), ((), ())), precision=lax.Precision.HIGHEST,
        preferred_element_type=F32,
    )
    boxes = boxes[0:4] + head_bias[...]
    for r in range(rows):
        boxes_out[:, r, :] = boxes[:, r * width : r * width + cols]


def near():
    return pl.BlockSpec(memory_space=pltpu.VMEM)


def far():
    return pl.BlockSpec(memory_space=pltpu.HBM)


def digits(size, most):
    radices = []
    while size > 1:
        radix = next((r for r in range(min(most, size), 1, -1) if size % r == 0), size)
        radices.append(radix)
        size //= radix
    return radices


def partner(i, stride, radix, step):
    digit = (i // stride) % radix
    other = digit ^ step if radix & (radix - 1) == 0 else (digit + step) % radix
    return i + (other - digit) * stride


def sum_by_permutes(value):
    rounds = []
    for axis in ("row", "col"):
        stride = 1
        for radix in digits(lax.axis_size(axis), 4):
            rounds.append((axis, stride, radix))
            stride *= radix
    for axis, stride, radix in rounds:
        count = lax.axis_size(axis)
        others = [
            lax.ppermute(value, axis, [(i, partner(i, stride, radix, k)) for i in range(count)])
            for k in range(1, radix)
        ]
        if (axis, stride, radix) == rounds[-1] and radix == 2:
            return value, others[0]
        total = value.astype(F32)
        for other in others:
            total = total + other.astype(F32)
        value = total.astype(BF16)
    return value, jnp.zeros_like(value)


def digits(size, most):
    radices = []
    while size > 1:
        radix = next((r for r in range(min(most, size), 1, -1) if size % r == 0), size)
        radices.append(radix)
        size //= radix
    return radices


def pair_exchange(value, axis, first):
    count = lax.axis_size(axis)
    pairs = []
    for i in range(first, count - 1, 2):
        pairs += [(i, i + 1), (i + 1, i)]
    return lax.ppermute(value, axis, pairs)


def local(
    features,
    expand_weight,
    expand_bias,
    depth_weight,
    depth_bias,
    project_weight,
    project_bias,
    qkv_weight,
    aggregate_depth,
    aggregate_group,
    output_weight,
    output_bias,
    head_weight,
    head_bias,
):
    rows, cols, channels = features.shape
    head_dim = aggregate_group.shape[2]
    heads = channels // head_dim
    width = cols + 2 * SIDE
    tile = (rows, cols)
    wide = expand_weight.shape[2]

    def edges(value, dim, size, odd):
        far = value.shape[dim] - size
        return [
            lax.dynamic_slice_in_dim(value, jnp.where(odd == at, far, 0), size, dim) for at in (0, 1)
        ]

    odd_row = lax.axis_index("row") & 1
    odd_col = lax.axis_index("col") & 1
    low, high = edges(features, 1, SIDE, odd_col)
    col_1 = pair_exchange(high, "col", 1)
    col_0 = pair_exchange(low, "col", 0)
    right = jnp.where(odd_col == 0, col_0, col_1)
    left = jnp.where(odd_col == 0, col_1, col_0)
    wide_rows = jnp.concatenate([features, right, left], axis=1)
    low, high = edges(wide_rows, 0, REACH, odd_row)
    row_1 = pair_exchange(high, "row", 1)
    row_0 = pair_exchange(low, "row", 0)

    aggregate_depth = aggregate_depth.transpose(1, 2, 0, 3)
    depth_weight = depth_weight.transpose(1, 2, 0, 3)
    params = pltpu.CompilerParams(vmem_limit_bytes=24 * 2**20)
    made = [
        jax.ShapeDtypeStruct(qkv_weight.shape, BF16),
        jax.ShapeDtypeStruct((SECTIONS, 32, 3 * channels), F32),
        jax.ShapeDtypeStruct((SECTIONS, 3, channels, channels), BF16),
        jax.ShapeDtypeStruct((3, LANES, channels), BF16),
    ]
    qkv_weight, taps, group, head_weight = pl.pallas_call(
        functools.partial(prepare_kernel, head_dim),
        out_shape=made,
        grid=(1,),
        in_specs=[near()] * 4,
        out_specs=[far()] * 4,
        scratch_shapes=[pltpu.VMEM(array.shape, array.dtype) for array in made]
        + [pltpu.VMEM((32 * SECTIONS, 3 * channels), F32), pltpu.SemaphoreType.DMA((4,))],
        compiler_params=params,
        cost_estimate=pl.CostEstimate(
            flops=2 * 10**9, bytes_accessed=4 * 10**6, transcendentals=0
        ),
        name="prepare",
    )(qkv_weight, aggregate_depth, aggregate_group, head_weight)

    weights = [
        expand_weight, expand_bias, depth_weight, depth_bias, project_weight, project_bias,
        qkv_weight, taps, group,
    ]
    weight_specs = [near()] * 6 + [far()] * 3

    def outs_of(count):
        return [
            jax.ShapeDtypeStruct((count, width, channels), BF16),
            jax.ShapeDtypeStruct((count, width, 2 * channels), BF16),
            jax.ShapeDtypeStruct((LANES + KEY_ROWS, LANES), BF16),
        ]

    def front_scratch(count):
        return [
            pltpu.VMEM((count, width, 256), BF16),
            pltpu.VMEM((count, width, 256), BF16),
            pltpu.VMEM(((count - 2) * width, channels), F32),
            pltpu.VMEM((count - 2, width, channels), BF16),
            pltpu.VMEM((count - 2, width, 3 * channels), BF16),
            pltpu.VMEM((count - 6, width, 2 * channels), BF16),
            pltpu.VMEM((9, TILE, expand_weight.shape[2]), BF16),
            pltpu.VMEM((25, TILE, 3 * channels), BF16),
            pltpu.VMEM(qkv_weight.shape[1:], BF16),
            pltpu.VMEM(taps.shape[1:], F32),
            pltpu.VMEM(group.shape[1:], BF16),
            pltpu.SemaphoreType.DMA((5,)),
        ]

    def attend_scratch(count):
        return [
            pltpu.VMEM((count, width, channels), BF16),
            pltpu.VMEM((count, width, channels), BF16),
            pltpu.VMEM((count, width, 2 * channels), BF16),
            pltpu.SemaphoreType.DMA((2,)),
        ]

    first_rows = rows + 2 * REACH
    mixed, query, payload = pl.pallas_call(
        functools.partial(first_kernel, tile, head_dim),
        out_shape=outs_of(first_rows - 6),
        grid=(1,),
        in_specs=[near()] * 3 + weight_specs,
        out_specs=[far(), far(), near()],
        scratch_shapes=[pltpu.VMEM((first_rows, width, channels), BF16)]
        + front_scratch(first_rows),
        compiler_params=params,
        name="first",
    )(wide_rows, row_0, row_1, *weights)
    payload, other = sum_by_permutes(payload)

    second_rows = first_rows - 6
    mixed, query, payload = pl.pallas_call(
        functools.partial(second_kernel, tile, head_dim),
        out_shape=outs_of(second_rows - 6),
        grid=(1,),
        in_specs=[far()] * 2 + [near()] * 4 + weight_specs,
        out_specs=[far(), far(), near()],
        scratch_shapes=attend_scratch(second_rows) + front_scratch(second_rows),
        compiler_params=params,
        name="second",
    )(mixed, query, payload, other, output_weight, output_bias, *weights)
    payload, other = sum_by_permutes(payload)

    return pl.pallas_call(
        functools.partial(last_kernel, tile, head_dim),
        out_shape=[
            jax.ShapeDtypeStruct((rows, cols, channels), BF16),
            jax.ShapeDtypeStruct((4, rows, cols), F32),
        ],
        grid=(1,),
        in_specs=[far()] * 2 + [near()] * 6,
        out_specs=[near()] * 2,
        scratch_shapes=attend_scratch(rows + 2),
        compiler_params=params,
        name="last",
    )(
        mixed, query, payload, other, output_weight, output_bias, head_weight,
        head_bias.reshape(4, 1),
    )


def solution(mesh):
    return jax.shard_map(
        local,
        mesh=mesh,
        in_specs=(P("row", "col", None),) + (P(),) * 13,
        out_specs=(P("row", "col", None), P(None, "row", "col")),
        check_vma=False,
    )
```

```python
import functools

import jax
import jax.numpy as jnp
from jax import lax
from jax.experimental import pallas as pl
from jax.experimental.pallas import tpu as pltpu
from jax.sharding import PartitionSpec as P

SECTIONS = 2
LANES = 128
SIDE = 8
TILE = 16
REACH = 7
KEY_ROWS = 16
PARTS = 4
F32 = jnp.float32
BF16 = jnp.bfloat16


def six_hard_swish(value, bound=6.0):
    return value * jnp.minimum(jnp.maximum(value + 3.0, 0.0), bound)


def parted(count, parts):
    cuts = [count * k // parts for k in range(parts + 1)]
    return [(a, b - a) for a, b in zip(cuts, cuts[1:]) if b > a]


def group_size(count, most):
    return next(n for n in range(min(most, count), 0, -1) if count % n == 0)


def by_groups(count, most, body):
    size = group_size(count, most)

    def group(index, carry):
        body(index * size, size)
        return carry

    lax.fori_loop(0, count // size, group, 0)


def clear_rows(ref, halo):
    rows = ref.shape[0]
    row = lax.axis_index("row")

    @pl.when(row == 0)
    def _():
        ref[0:halo] = jnp.zeros((halo,) + ref.shape[1:], ref.dtype)

    @pl.when(row == lax.axis_size("row") - 1)
    def _():
        ref[rows - halo : rows] = jnp.zeros((halo,) + ref.shape[1:], ref.dtype)


def column_of(low, count, total, lanes):
    shape = (count, TILE, lanes)
    number = lax.broadcasted_iota(jnp.int32, shape, 0) + low
    column = lax.broadcasted_iota(jnp.int32, shape, 1) * total + number
    width = total * TILE
    return jnp.where(column < 0, column + width, jnp.where(column >= width, column - width, column))


def inside(low, count, total, cols, lanes):
    column = column_of(low, count, total, lanes)
    col = lax.axis_index("col")
    last = col == lax.axis_size("col") - 1
    start = jnp.where(last, cols, cols + SIDE)
    stop = jnp.where(col == 0, total * TILE, cols + SIDE)
    return jnp.where((column >= start) & (column < stop), 0.0, 1.0)


def class_of(value, number):
    total = value.shape[0]
    steps = number // total
    part = value[number - steps * total]
    return pltpu.roll(part, -steps % TILE, 0) if steps else part


def flat(value):
    return value.reshape(-1, value.shape[-1])


def wide(value):
    return jnp.broadcast_to(value, (TILE, value.shape[1])).astype(BF16)


def same_head(head_dim):
    across = lax.broadcasted_iota(jnp.int32, (LANES, LANES), 0) // head_dim
    along = lax.broadcasted_iota(jnp.int32, (LANES, LANES), 1) // head_dim
    return across == along


def depthwise_row(rows, taps, size, total):
    value = None
    for b in range(size):
        part = None
        for a in range(size):
            term = rows[a][b : b + total] * taps(a, b)[None]
            part = term if part is None else part + term
        value = part if value is None else value + part
    return value


def front(x_ref, weights, outs, scratch, halo, tile, head_dim, section):
    expand, expand_bias, depth, depth_bias, project = weights[:5]
    mixed_out, query_out, payload_out = outs
    (
        hidden_0, hidden_1, total, mixed, around_mixed, qkv, query, wide_depth, wide_agg, bound,
        project_bias, qkv_weight, agg, group, sems,
    ) = scratch
    loads = [
        pltpu.make_async_copy(weights[5], project_bias, sems.at[0]),
        pltpu.make_async_copy(weights[6].at[section], qkv_weight, sems.at[1]),
        pltpu.make_async_copy(weights[7].at[section], agg, sems.at[2]),
        pltpu.make_async_copy(weights[8].at[section], group, sems.at[3]),
    ]
    for load in loads:
        load.start()
    rows, channels = x_ref.shape[0], x_ref.shape[3]
    classes = x_ref.shape[1] - 2
    width = classes * TILE
    tile_rows, tile_cols = tile
    inner = rows - 2
    chunk = hidden_0.shape[3]
    chunks = expand.shape[2] // chunk
    this = slice(section, section + 1)
    for index in range(9):
        wide_depth[index] = wide(depth[index // 3, index % 3, this, :] * (1.0 / 6.0))
    wide_depth[9] = wide(depth_bias[this, :])
    bound[...] = (6.0 * inside(-1, classes + 2, classes, tile_cols, chunk)).astype(BF16)

    def start_rows(first, size):
        value = x_ref[pl.ds(first + 1, size), 1 : 1 + classes].astype(F32)
        total[pl.ds(first, size)] = 6.0 * value

    by_groups(inner, 2, start_rows)

    def expand_rows(out, at, first, size):
        value = jnp.dot(
            flat(x_ref[first : first + size]), expand[section, :, pl.ds(at, chunk)],
            preferred_element_type=F32,
        )
        value = (value + expand_bias[this, pl.ds(at, chunk)]).astype(BF16)
        value = value.reshape(size, classes + 2, TILE, chunk)
        out[first : first + size] = six_hard_swish(value, bound[...][None])

    def spread_rows(hidden, at, first, size):
        spread = []
        for r in range(first, first + size):
            lanes = []
            for lane in range(0, chunk, LANES):
                here = pl.ds(pl.multiple_of(at + lane, LANES), LANES)
                value = depthwise_row(
                    [hidden[r + a, :, :, lane : lane + LANES] for a in range(3)],
                    lambda a, b: wide_depth[3 * a + b, :, here], 3, classes,
                )
                lanes.append(six_hard_swish(value + wide_depth[9, :, here][None]))
            spread.append(jnp.concatenate(lanes, axis=2))
        value = jnp.dot(
            flat(jnp.concatenate(spread, axis=0)), project[section, pl.ds(at, chunk), :],
            preferred_element_type=F32,
        )
        total[first : first + size] += value.reshape(size, classes, TILE, channels)

    def stage(index, current, following):
        at = pl.multiple_of(index * chunk, chunk)
        ahead = pl.multiple_of(jnp.minimum(index + 1, chunks - 1) * chunk, chunk)
        for (first, size), (from_row, count) in zip(parted(inner, PARTS), parted(rows, PARTS)):
            expand_rows(following, ahead, from_row, count)
            spread_rows(current, at, first, size)
        clear_rows(following, halo)

    for first, size in parted(rows, PARTS):
        expand_rows(hidden_0, 0, first, size)
    clear_rows(hidden_0, halo)

    def two_stages(index, carry):
        stage(2 * index, hidden_0, hidden_1)
        stage(2 * index + 1, hidden_1, hidden_0)
        return carry

    lax.fori_loop(0, chunks // 2, two_stages, 0)
    loads[0].wait()

    def mixed_rows(index, carry):
        value = total[index] * (1.0 / 6.0) + project_bias[this, :]
        mixed[index] = value.astype(BF16)
        for number in range(-2, classes + 2):
            around_mixed[index, number + 2] = class_of(value, number).astype(BF16)
        return carry

    lax.fori_loop(0, inner, mixed_rows, 0)
    outer = inner - 4
    stores = [
        pltpu.make_async_copy(mixed.at[pl.ds(2, outer)], mixed_out, sems.at[4]),
        pltpu.make_async_copy(query, query_out, sems.at[5]),
    ]
    stores[0].start()
    for load in loads[1:]:
        load.wait()
    for index in range(25):
        wide_agg[index] = wide(agg[index : index + 1, :])
    around = halo - 1
    in_map = inside(-2, classes + 4, classes, tile_cols, channels).astype(BF16)

    def qkv_rows(first, size, low, high):
        value = jnp.dot(
            flat(around_mixed[first : first + size]), qkv_weight[:, low:high],
            preferred_element_type=F32,
        )
        value = value.astype(BF16).reshape(size, classes + 4, TILE, high - low)
        for lane in range(low, high, channels):
            part = value[..., lane - low : lane - low + channels]
            qkv[first : first + size, :, :, lane : lane + channels] = part * in_map[None]

    for first, size in parted(inner, PARTS):
        qkv_rows(first, size, 0, channels)
    for first, size in parted(tile_rows + 4, PARTS - 1):
        qkv_rows(around - 2 + first, size, channels, 3 * channels)
    clear_rows(qkv, around)

    def aggregated(kind, first, size):
        scaled = []
        for r in range(size):
            lanes = []
            for lane in range(kind * channels, (kind + 1) * channels, LANES):
                here = slice(lane, lane + LANES)
                value = depthwise_row(
                    [qkv[first + r + a, :, :, here] for a in range(5)],
                    lambda a, b: wide_agg[5 * a + b, :, here], 5, classes,
                )
                lanes.append(value)
            scaled.append(jnp.concatenate(lanes, axis=2))
        value = jnp.dot(
            flat(jnp.concatenate(scaled, axis=0)), group[kind], preferred_element_type=F32
        )
        return value.astype(BF16).reshape(size, classes, TILE, channels)

    def query_rows(first, size):
        here = pl.ds(first, size)
        centre = qkv[pl.ds(first + 2, size), 2 : 2 + classes, :, 0:channels]
        query[here, :, :, 0:channels] = jnp.maximum(centre, 0.0)
        query[here, :, :, channels : 2 * channels] = jnp.maximum(aggregated(0, first, size), 0.0)

    by_groups(outer, 5, query_rows)
    stores[1].start()
    size = group_size(tile_rows, 4)
    own = jnp.where(column_of(0, classes, classes, channels) < tile_cols, 1.0, 0.0).astype(BF16)

    def summed(key, value):
        key = flat(jnp.maximum(key, 0.0) * own[None])
        value = flat(value)
        products = [
            lax.dot_general(
                key[:, lane : lane + LANES], value[:, lane : lane + LANES],
                (((0,), (0,)), ((), ())), preferred_element_type=F32,
            )
            for lane in range(0, channels, LANES)
        ]
        return products, jnp.sum(key.astype(F32), axis=0, keepdims=True)

    mine = qkv[around : around + tile_rows, 2 : 2 + classes, :, channels : 3 * channels]
    products, sums = summed(mine[..., 0:channels], mine[..., channels : 2 * channels])

    def grouped_rows(index, carry):
        at = around - 2 + index * size
        more, sums = summed(aggregated(1, at, size), aggregated(2, at, size))
        return [a + b for a, b in zip(carry[0], more)], carry[1] + sums

    more, more_sums = lax.fori_loop(
        0, tile_rows // size, grouped_rows,
        ([jnp.zeros((LANES, LANES), F32) for _ in products], jnp.zeros_like(sums)),
    )
    products = products + more
    sums = jnp.concatenate([sums, more_sums], axis=1)
    same = same_head(head_dim)
    summary = jnp.zeros((LANES, LANES), F32)
    key_sums = []
    for index, product in enumerate(products):
        product = jnp.where(same, product, 0.0)
        if index:
            product = pltpu.roll(product, index * head_dim, 1)
        summary = summary + product
        key_sums.append(sums[:, index * LANES : (index + 1) * LANES])
    key_sums.append(jnp.zeros((KEY_ROWS - len(products), LANES), F32))
    payload_out[0:LANES, :] = summary.astype(BF16)
    payload_out[LANES : LANES + KEY_ROWS, :] = jnp.concatenate(key_sums, axis=0).astype(BF16)
    for store in stores:
        store.wait()


def attend(
    mixed_in, query_in, payloads, weight, bias_in, held, head_dim, section, x_ref, beyond
):
    mixed_ref, query_ref, bias, sems = held
    rows, channels = x_ref.shape[0], x_ref.shape[3]
    classes = x_ref.shape[1] - 2 * beyond
    halves = [(query_in, query_ref), (mixed_in, mixed_ref), (bias_in, bias)]
    loads = [pltpu.make_async_copy(a, b, sems.at[k]) for k, (a, b) in enumerate(halves)]
    for load in loads:
        load.start()
    same = same_head(head_dim)
    square = (LANES, LANES)
    diagonal = lax.broadcasted_iota(jnp.int32, square, 0) == lax.broadcasted_iota(
        jnp.int32, square, 1
    )
    ones = jnp.where(same, 1.0, 0.0).astype(BF16)
    nothing = jnp.zeros(square, BF16)
    payload = payloads[0][...].astype(F32)
    for part in payloads[1:]:
        payload = payload + part[...].astype(F32)
    packed = payload[0:LANES]
    count = 2 * channels // LANES
    summaries, sums = [], []
    for index in range(count):
        summary = packed if index == 0 else pltpu.roll(packed, LANES - index * head_dim, 1)
        summaries.append(jnp.where(same, summary, 0.0).astype(BF16))
        keys = payload[LANES + index : LANES + index + 1]
        keys = jnp.where(diagonal, keys, 0.0).astype(BF16)
        sums.append(jnp.dot(keys, ones, preferred_element_type=F32).astype(BF16))

    def paired(blocks, index):
        return jnp.concatenate(
            [
                jnp.concatenate([blocks[index], nothing], axis=1),
                jnp.concatenate([nothing, blocks[index + 1]], axis=1),
            ],
            axis=0,
        )

    summaries = [paired(summaries, index) for index in range(0, count, 2)]
    sums = [paired(sums, index) for index in range(0, count, 2)]
    step = 2 * LANES
    for load in loads:
        load.wait()

    def attend_rows(first, size):
        query = flat(query_ref[pl.ds(first, size)])
        parts = []
        for branch in range(count // 2):
            part = query[:, branch * step : (branch + 1) * step]
            numer = jnp.dot(part, summaries[branch], preferred_element_type=F32)
            denom = jnp.dot(part, sums[branch], preferred_element_type=F32) + 1e-6
            inverse = pl.reciprocal(denom, approx=True)
            inverse = inverse * (2.0 - denom * inverse)
            parts.append((numer * inverse).astype(BF16))
        value = jnp.dot(
            jnp.concatenate(parts, axis=1), weight[section], preferred_element_type=F32
        )
        value = value + bias[section : section + 1, :]
        value = value + flat(mixed_ref[pl.ds(first, size)]).astype(F32)
        value = value.reshape(size, classes, TILE, channels)
        x_ref[pl.ds(first, size), beyond : beyond + classes] = value.astype(BF16)
        for number in [*range(-beyond, 0), *range(classes, classes + beyond)]:
            for r in range(size):
                x_ref[first + r, number + beyond] = class_of(value[r], number).astype(BF16)

    by_groups(rows, 5, attend_rows)


def tap(section, a, b):
    at = 32 * section + 5 * a + b
    return slice(at, at + 1)


def prepare_kernel(head_dim, qkv, agg, group, head, *refs):
    outs, made, taps, sems = refs[:4], refs[4:8], refs[8], refs[9]
    qkv_out, agg_out, group_out, head_out = made
    sections, channels, wide = qkv.shape
    half = 3 * LANES
    heads = LANES // head_dim
    src = lax.broadcasted_iota(jnp.int32, (half, LANES), 0)
    dst = lax.broadcasted_iota(jnp.int32, (half, LANES), 1)
    first = (dst // head_dim) * 3 * head_dim + dst % head_dim
    picks = [jnp.where(src == first + k * head_dim, 1.0, 0.0).astype(BF16) for k in range(3)]
    taps[...] = jnp.zeros(taps.shape, F32)
    for section in range(sections):
        for a in range(5):
            for b in range(5):
                taps[tap(section, a, b), :] = agg[a, b, section : section + 1, :]
    rest = taps[...]
    high = rest.astype(BF16)
    rest = rest - high.astype(F32)
    middle = rest.astype(BF16)
    low = (rest - middle.astype(F32)).astype(BF16)
    split = jnp.concatenate([high, middle, low], axis=0)
    count = taps.shape[0]
    weights = qkv[...].reshape(sections * channels, wide)
    for part in range(wide // half):
        here = slice(part * half, (part + 1) * half)
        for kind in range(3):
            to = kind * channels + part * LANES
            there = slice(to, to + LANES)
            value = jnp.dot(weights[:, here], picks[kind], preferred_element_type=F32)
            qkv_out[:, :, there] = value.astype(BF16).reshape(sections, channels, LANES)
            value = jnp.dot(split[:, here], picks[kind], preferred_element_type=F32)
            value = value[:count] + value[count : 2 * count] + value[2 * count :]
            agg_out[:, :, there] = value.reshape(sections, -1, LANES)
    row = lax.broadcasted_iota(jnp.int32, (head_dim, channels), 0)
    lane = lax.broadcasted_iota(jnp.int32, (head_dim, channels), 1)
    spread = jnp.where(lane % head_dim == row, 1.0, 0.0).astype(BF16)
    across = lax.broadcasted_iota(jnp.int32, (channels, channels), 0) // head_dim
    along = lax.broadcasted_iota(jnp.int32, (channels, channels), 1) // head_dim
    for section in range(sections):
        for kind in range(3):
            tall = [group[section, 3 * h + kind] for h in range(channels // head_dim)]
            value = jnp.dot(jnp.concatenate(tall, axis=0), spread, preferred_element_type=F32)
            group_out[section, kind] = jnp.where(across == along, value, 0.0).astype(BF16)
    head_out[...] = jnp.zeros(head_out.shape, BF16)
    for a in range(3):
        rows = [head[a, b] for b in range(3)] + [jnp.zeros((4, channels), BF16)]
        head_out[a, 0:16, :] = jnp.concatenate(rows, axis=0)
    stores = [pltpu.make_async_copy(made[i], outs[i], sems.at[i]) for i in range(4)]
    for store in stores:
        store.start()
    for store in stores:
        store.wait()


def first_kernel(tile, head_dim, own, row_0, row_1, *refs):
    weights, outs, scratch = refs[:9], refs[9:12], refs[12:]
    natural, x_ref = scratch[:2]
    rows, width = own.shape[:2]
    classes = x_ref.shape[1] - 2
    even = lax.axis_index("row") & 1 == 0
    below = REACH + rows
    pieces = [
        (own, REACH, rows),
        (row_0, jnp.where(even, below, 0), REACH),
        (row_1, jnp.where(even, 0, below), REACH),
    ]
    for piece, start, count in pieces:

        def one_row(index, carry, piece=piece, start=start):
            value = piece[index].astype(F32)
            for lane in range(0, value.shape[1], LANES):
                half = lane // LANES
                part = value[:, lane : lane + LANES]
                natural[half, 8 : 8 + width, :] = part
                natural[half, 7:8, :] = part[width - 1 : width]
                natural[half, 8 + width : 9 + width, :] = part[0:1]
                for number in range(-1, classes + 1):
                    part = natural[half, pl.ds(8 + number, TILE, stride=classes), :]
                    x_ref[start + index, number + 1, :, lane : lane + LANES] = part.astype(BF16)
            return carry

        lax.fori_loop(0, count, one_row, 0)
    front(x_ref, weights, outs, scratch[2:], REACH, tile, head_dim, 0)


def second_kernel(tile, head_dim, mixed, query, payload, other, out_weight, out_bias, *refs):
    weights, outs, scratch = refs[:9], refs[9:12], refs[12:]
    x_ref = scratch[0]
    attend(
        mixed, query, (payload, other), out_weight, out_bias, scratch[1:5], head_dim, 0, x_ref, 1
    )
    front(x_ref, weights, outs, scratch[5:], REACH - 3, tile, head_dim, 1)


def last_kernel(
    tile, head_dim, mixed, query, payload, other, out_weight, out_bias, head_weight, head_bias,
    map_out, boxes_out, x_ref, mixed_ref, query_ref, bias, natural, sems,
):
    rows, cols = tile
    classes, channels = x_ref.shape[1], x_ref.shape[3]
    width = classes * TILE
    attend(
        mixed, query, (payload, other), out_weight, out_bias, (mixed_ref, query_ref, bias, sems),
        head_dim, 1, x_ref, 0,
    )
    in_map = inside(0, classes, classes, cols, channels).astype(BF16)
    x_ref[...] = x_ref[...] * in_map[None]
    clear_rows(x_ref, 1)

    def natural_row(value, r):
        for number in range(classes):
            natural[r, pl.ds(number, TILE, stride=classes), :] = value[number]

    for lane in range(0, channels, LANES):
        for r in range(rows):
            natural_row(x_ref[1 + r, :, :, lane : lane + LANES].astype(F32), r)
        map_out[:, :, lane : lane + LANES] = natural[:, 0:cols, :].astype(BF16)
    total = None
    for a in range(3):
        part = lax.dot_general(
            flat(x_ref[a : a + rows]), head_weight[a], (((1,), (1,)), ((), ())),
            preferred_element_type=F32,
        )
        total = part if total is None else total + part
    total = total.reshape(rows, classes, TILE, LANES)
    tap = lax.broadcasted_iota(jnp.int32, (TILE, LANES), 1) // 4
    for r in range(rows):
        numbers = [class_of(total[r], number) for number in range(-1, classes + 1)]
        natural_row(
            [
                jnp.where(tap == 0, numbers[k], jnp.where(tap == 2, numbers[k + 2], numbers[k + 1]))
                for k in range(classes)
            ],
            r,
        )
    across = lax.broadcasted_iota(jnp.int32, (8, LANES), 0)
    along = lax.broadcasted_iota(jnp.int32, (8, LANES), 1)
    fold = jnp.where((along % 4 == across) & (along < 12), 1.0, 0.0)
    boxes = lax.dot_general(
        fold, flat(natural[...]), (((1,), (1,)), ((), ())), precision=lax.Precision.HIGHEST,
        preferred_element_type=F32,
    )
    boxes = boxes[0:4] + head_bias[...]
    for r in range(rows):
        boxes_out[:, r, :] = boxes[:, r * width : r * width + cols]


def near():
    return pl.BlockSpec(memory_space=pltpu.VMEM)


def far():
    return pl.BlockSpec(memory_space=pltpu.HBM)


def digits(size, most):
    radices = []
    while size > 1:
        radix = next((r for r in range(min(most, size), 1, -1) if size % r == 0), size)
        radices.append(radix)
        size //= radix
    return radices


def partner(i, stride, radix, step):
    digit = (i // stride) % radix
    other = digit ^ step if radix & (radix - 1) == 0 else (digit + step) % radix
    return i + (other - digit) * stride


def sum_by_permutes(value):
    rounds = []
    for axis in ("row", "col"):
        stride = 1
        for radix in digits(lax.axis_size(axis), 4):
            rounds.append((axis, stride, radix))
            stride *= radix
    for axis, stride, radix in rounds:
        count = lax.axis_size(axis)
        others = [
            lax.ppermute(value, axis, [(i, partner(i, stride, radix, k)) for i in range(count)])
            for k in range(1, radix)
        ]
        if (axis, stride, radix) == rounds[-1] and radix == 2:
            return value, others[0]
        total = value.astype(F32)
        for other in others:
            total = total + other.astype(F32)
        value = total.astype(BF16)
    return value, jnp.zeros_like(value)


def digits(size, most):
    radices = []
    while size > 1:
        radix = next((r for r in range(min(most, size), 1, -1) if size % r == 0), size)
        radices.append(radix)
        size //= radix
    return radices


def pair_exchange(value, axis, first):
    count = lax.axis_size(axis)
    pairs = []
    for i in range(first, count - 1, 2):
        pairs += [(i, i + 1), (i + 1, i)]
    return lax.ppermute(value, axis, pairs)


def local(
    features,
    expand_weight,
    expand_bias,
    depth_weight,
    depth_bias,
    project_weight,
    project_bias,
    qkv_weight,
    aggregate_depth,
    aggregate_group,
    output_weight,
    output_bias,
    head_weight,
    head_bias,
):
    rows, cols, channels = features.shape
    head_dim = aggregate_group.shape[2]
    heads = channels // head_dim
    width = cols + 2 * SIDE
    classes = width // TILE
    tile = (rows, cols)
    hidden = expand_weight.shape[2]

    def edges(value, dim, size, odd):
        far = value.shape[dim] - size
        return [
            lax.dynamic_slice_in_dim(value, jnp.where(odd == at, far, 0), size, dim) for at in (0, 1)
        ]

    odd_row = lax.axis_index("row") & 1
    odd_col = lax.axis_index("col") & 1
    low, high = edges(features, 1, SIDE, odd_col)
    col_1 = pair_exchange(high, "col", 1)
    col_0 = pair_exchange(low, "col", 0)
    right = jnp.where(odd_col == 1, col_1, col_0)
    left = jnp.where(odd_col == 1, col_0, col_1)
    wide_rows = jnp.concatenate([features, right, left], axis=1)
    low, high = edges(wide_rows, 0, REACH, odd_row)
    row_1 = pair_exchange(high, "row", 1)
    row_0 = pair_exchange(low, "row", 0)

    aggregate_depth = aggregate_depth.transpose(1, 2, 0, 3)
    depth_weight = depth_weight.transpose(1, 2, 0, 3)
    params = pltpu.CompilerParams(vmem_limit_bytes=24 * 2**20)
    made = [
        jax.ShapeDtypeStruct(qkv_weight.shape, BF16),
        jax.ShapeDtypeStruct((SECTIONS, 32, 3 * channels), F32),
        jax.ShapeDtypeStruct((SECTIONS, 3, channels, channels), BF16),
        jax.ShapeDtypeStruct((3, LANES, channels), BF16),
    ]
    qkv_weight, taps, group, head_weight = pl.pallas_call(
        functools.partial(prepare_kernel, head_dim),
        out_shape=made,
        grid=(1,),
        in_specs=[near()] * 4,
        out_specs=[far()] * 4,
        scratch_shapes=[pltpu.VMEM(array.shape, array.dtype) for array in made]
        + [pltpu.VMEM((32 * SECTIONS, 3 * channels), F32), pltpu.SemaphoreType.DMA((4,))],
        compiler_params=params,
        cost_estimate=pl.CostEstimate(
            flops=2 * 10**9, bytes_accessed=4 * 10**6, transcendentals=0
        ),
        name="prepare",
    )(qkv_weight, aggregate_depth, aggregate_group, head_weight)

    weights = [
        expand_weight, expand_bias, depth_weight, depth_bias, project_weight, project_bias,
        qkv_weight, taps, group,
    ]
    weight_specs = [near()] * 5 + [far()] * 4

    def held(count, beyond, kinds=1):
        return pltpu.VMEM((count, classes + 2 * beyond, TILE, kinds * channels), BF16)

    def outs_of(count):
        return [
            jax.ShapeDtypeStruct((count, classes, TILE, channels), BF16),
            jax.ShapeDtypeStruct((count, classes, TILE, 2 * channels), BF16),
            jax.ShapeDtypeStruct((LANES + KEY_ROWS, LANES), BF16),
        ]

    def front_scratch(count):
        return [
            held(count, 1),
            held(count, 1),
            pltpu.VMEM((count - 2, classes, TILE, channels), F32),
            held(count - 2, 0),
            held(count - 2, 2),
            held(count - 2, 2, 3),
            held(count - 6, 0, 2),
            pltpu.VMEM((10, TILE, hidden), BF16),
            pltpu.VMEM((25, TILE, 3 * channels), BF16),
            pltpu.VMEM((classes + 2, TILE, channels), BF16),
            pltpu.VMEM(project_bias.shape, F32),
            pltpu.VMEM(qkv_weight.shape[1:], BF16),
            pltpu.VMEM(taps.shape[1:], F32),
            pltpu.VMEM(group.shape[1:], BF16),
            pltpu.SemaphoreType.DMA((6,)),
        ]

    def attend_scratch(count, beyond):
        return [
            held(count, beyond),
            held(count, 0),
            held(count, 0, 2),
            pltpu.VMEM(output_bias.shape, F32),
        ]

    first_rows = rows + 2 * REACH
    mixed, query, payload = pl.pallas_call(
        functools.partial(first_kernel, tile, head_dim),
        out_shape=outs_of(first_rows - 6),
        grid=(1,),
        in_specs=[near()] * 3 + weight_specs,
        out_specs=[far(), far(), near()],
        scratch_shapes=[pltpu.VMEM((channels // LANES, width + 16, LANES), F32), held(first_rows, 1)]
        + front_scratch(first_rows),
        compiler_params=params,
        name="first",
    )(wide_rows, row_0, row_1, *weights)
    payload, other = sum_by_permutes(payload)

    second_rows = first_rows - 6
    mixed, query, payload = pl.pallas_call(
        functools.partial(second_kernel, tile, head_dim),
        out_shape=outs_of(second_rows - 6),
        grid=(1,),
        in_specs=[far()] * 2 + [near()] * 3 + [far()] + weight_specs,
        out_specs=[far(), far(), near()],
        scratch_shapes=attend_scratch(second_rows, 1)
        + [pltpu.SemaphoreType.DMA((3,))]
        + front_scratch(second_rows),
        compiler_params=params,
        name="second",
    )(mixed, query, payload, other, output_weight, output_bias, *weights)
    payload, other = sum_by_permutes(payload)

    return pl.pallas_call(
        functools.partial(last_kernel, tile, head_dim),
        out_shape=[
            jax.ShapeDtypeStruct((rows, cols, channels), BF16),
            jax.ShapeDtypeStruct((4, rows, cols), F32),
        ],
        grid=(1,),
        in_specs=[far()] * 2 + [near()] * 3 + [far()] + [near()] * 2,
        out_specs=[near()] * 2,
        scratch_shapes=attend_scratch(rows + 2, 0)
        + [pltpu.VMEM((rows, width, LANES), F32), pltpu.SemaphoreType.DMA((3,))],
        compiler_params=params,
        name="last",
    )(
        mixed, query, payload, other, output_weight, output_bias, head_weight,
        head_bias.reshape(4, 1),
    )


def solution(mesh):
    return jax.shard_map(
        local,
        mesh=mesh,
        in_specs=(P("row", "col", None),) + (P(),) * 13,
        out_specs=(P("row", "col", None), P(None, "row", "col")),
        check_vma=False,
    )
```

```python
import functools

import jax
import jax.numpy as jnp
from jax import lax
from jax.experimental import pallas as pl
from jax.experimental.pallas import tpu as pltpu
from jax.sharding import PartitionSpec as P

SECTIONS = 2
LANES = 128
SIDE = 8
REACH = 7
KEY_ROWS = 16
TILE = 16
PARTS = 4
F32 = jnp.float32
BF16 = jnp.bfloat16


def six_hard_swish(value):
    return value * jnp.minimum(jnp.maximum(value + 3.0, 0.0), 6.0)


def parted(count, parts):
    cuts = [count * k // parts for k in range(parts + 1)]
    return [(a, b - a) for a, b in zip(cuts, cuts[1:]) if b > a]


def group_size(count, most):
    return next(n for n in range(min(most, count), 0, -1) if count % n == 0)


def by_groups(count, most, body):
    size = group_size(count, most)

    def group(index, carry):
        body(index * size, size)
        return carry

    lax.fori_loop(0, count // size, group, 0)


def clear_outside(ref, halo, cols):
    rows = ref.shape[0]
    row, col = lax.axis_index("row"), lax.axis_index("col")

    @pl.when(row == 0)
    def _():
        ref[0:halo] = jnp.zeros((halo,) + ref.shape[1:], ref.dtype)

    @pl.when(row == lax.axis_size("row") - 1)
    def _():
        ref[rows - halo : rows] = jnp.zeros((halo,) + ref.shape[1:], ref.dtype)

    @pl.when(col == 0)
    def _():
        ref[:, cols + SIDE : cols + 2 * SIDE, :] = jnp.zeros((rows, SIDE, ref.shape[2]), ref.dtype)

    @pl.when(col == lax.axis_size("col") - 1)
    def _():
        ref[:, cols : cols + SIDE, :] = jnp.zeros((rows, SIDE, ref.shape[2]), ref.dtype)


def flat(value):
    return value.reshape(-1, value.shape[-1])


def same_head(head_dim):
    across = lax.broadcasted_iota(jnp.int32, (LANES, LANES), 0) // head_dim
    along = lax.broadcasted_iota(jnp.int32, (LANES, LANES), 1) // head_dim
    return across == along


def depthwise_row(rows, taps, size, width):
    rows = [row.reshape(width // TILE, TILE, LANES) for row in rows]
    total = None
    for b in range(size):
        part = None
        for a in range(size):
            term = rows[a] * taps(a, b)[None]
            part = term if part is None else part + term
        part = part.reshape(width, LANES).astype(F32)
        if b != size // 2:
            part = pltpu.roll(part, (size // 2 - b) % width, 0)
        total = part if total is None else total + part
    return total


def spread_taps(agg, wide_agg):
    for index in range(25):
        taps = agg[index : index + 1, :]
        wide_agg[index] = jnp.broadcast_to(taps, (TILE, taps.shape[1])).astype(BF16)


def aggregated(source, wide_agg, group, low, first, size, channels):
    width = source.shape[1]
    scaled = []
    for r in range(size):
        lanes = []
        for lane in range(low, low + channels, LANES):
            here = slice(lane, lane + LANES)
            value = depthwise_row(
                [source[first + r + a, :, here] for a in range(5)],
                lambda a, b: wide_agg[5 * a + b, :, here], 5, width,
            )
            lanes.append(value.astype(BF16))
        scaled.append(jnp.concatenate(lanes, axis=1))
    value = jnp.dot(jnp.concatenate(scaled, axis=0), group, preferred_element_type=F32)
    return value.astype(BF16).reshape(size, width, channels)


def front(x_ref, weights, outs, scratch, halo, tile, head_dim, section):
    expand, expand_bias, depth, depth_bias, project = weights[:5]
    mixed_out, payload_out = outs
    (
        hidden_0, hidden_1, total, mixed, pairs, wide_depth, wide_agg,
        project_bias, pair_weight, agg, group, sems,
    ) = scratch
    channels = x_ref.shape[2]
    tail = pl.ds(channels, 2 * channels)
    loads = [
        pltpu.make_async_copy(weights[5], project_bias, sems.at[0]),
        pltpu.make_async_copy(weights[6].at[section, :, tail], pair_weight, sems.at[1]),
        pltpu.make_async_copy(weights[7].at[section, :, tail], agg, sems.at[2]),
        pltpu.make_async_copy(weights[8].at[section, pl.ds(1, 2)], group, sems.at[3]),
    ]
    for load in loads:
        load.start()
    rows, width, channels = x_ref.shape
    tile_rows, tile_cols = tile
    inner = rows - 2
    chunk = hidden_0.shape[2]
    chunks = expand.shape[2] // chunk
    for index in range(9):
        taps = depth[index // 3, index % 3, section : section + 1, :] * (1.0 / 6.0)
        wide_depth[index] = jnp.broadcast_to(taps, (TILE, taps.shape[1])).astype(BF16)
    total[...] = 6.0 * flat(x_ref[1 : rows - 1]).astype(F32)

    def expand_rows(out, at, first, size):
        value = jnp.dot(
            flat(x_ref[first : first + size]), expand[section, :, pl.ds(at, chunk)],
            preferred_element_type=F32,
        )
        value = (value + expand_bias[section : section + 1, pl.ds(at, chunk)]).astype(BF16)
        out[first : first + size] = six_hard_swish(value).reshape(size, width, chunk)

    def spread_rows(hidden, at, first, size):
        spread = []
        for r in range(first, first + size):
            lanes = []
            for lane in range(0, chunk, LANES):
                here = pl.ds(pl.multiple_of(at + lane, LANES), LANES)
                value = depthwise_row(
                    [hidden[r + a, :, lane : lane + LANES] for a in range(3)],
                    lambda a, b: wide_depth[3 * a + b, :, here], 3, width,
                )
                value = (value + depth_bias[section : section + 1, here]).astype(BF16)
                lanes.append(six_hard_swish(value))
            spread.append(jnp.concatenate(lanes, axis=1))
        pixels = slice(first * width, (first + size) * width)
        total[pixels] += jnp.dot(
            jnp.concatenate(spread, axis=0), project[section, pl.ds(at, chunk), :],
            preferred_element_type=F32,
        )

    def stage(index, current, following):
        at = pl.multiple_of(index * chunk, chunk)
        ahead = pl.multiple_of(jnp.minimum(index + 1, chunks - 1) * chunk, chunk)
        for (first, size), (from_row, count) in zip(parted(inner, PARTS), parted(rows, PARTS)):
            expand_rows(following, ahead, from_row, count)
            spread_rows(current, at, first, size)
        clear_outside(following, halo, tile_cols)

    for first, size in parted(rows, PARTS):
        expand_rows(hidden_0, 0, first, size)
    clear_outside(hidden_0, halo, tile_cols)

    def two_stages(index, carry):
        stage(2 * index, hidden_0, hidden_1)
        stage(2 * index + 1, hidden_1, hidden_0)
        return carry

    lax.fori_loop(0, chunks // 2, two_stages, 0)
    loads[0].wait()
    value = total[...] * (1.0 / 6.0) + project_bias[section : section + 1, :]
    mixed[...] = value.astype(BF16).reshape(inner, width, channels)
    store = pltpu.make_async_copy(mixed, mixed_out, sems.at[4])
    store.start()
    for load in loads[1:]:
        load.wait()
    spread_taps(agg, wide_agg)
    around = halo - 1
    first_pair = around - 2
    count = tile_rows + 4
    for first, size in parted(count, PARTS - 1):
        at = first_pair + first
        value = jnp.dot(
            flat(mixed[at : at + size]), pair_weight[...], preferred_element_type=F32
        )
        pairs[first : first + size] = value.astype(BF16).reshape(size, width, 2 * channels)
    clear_outside(pairs, 2, tile_cols)
    size = group_size(tile_rows, 4)

    def summed(key, value):
        key = jnp.maximum(flat(key[:, 0:tile_cols]), 0.0)
        value = flat(value[:, 0:tile_cols])
        products = [
            lax.dot_general(
                key[:, lane : lane + LANES], value[:, lane : lane + LANES],
                (((0,), (0,)), ((), ())), preferred_element_type=F32,
            )
            for lane in range(0, channels, LANES)
        ]
        return products, jnp.sum(key.astype(F32), axis=0, keepdims=True)

    mine = slice(2, 2 + tile_rows)
    products, sums = summed(
        pairs[mine, :, 0:channels], pairs[mine, :, channels : 2 * channels]
    )

    def grouped_rows(index, carry):
        at = index * size
        more, sums = summed(
            aggregated(pairs, wide_agg, group[0], 0, at, size, channels),
            aggregated(pairs, wide_agg, group[1], channels, at, size, channels),
        )
        return [a + b for a, b in zip(carry[0], more)], carry[1] + sums

    more, more_sums = lax.fori_loop(
        0, tile_rows // size, grouped_rows,
        ([jnp.zeros((LANES, LANES), F32) for _ in products], jnp.zeros_like(sums)),
    )
    products = products + more
    sums = jnp.concatenate([sums, more_sums], axis=1)
    same = same_head(head_dim)
    summary = jnp.zeros((LANES, LANES), F32)
    key_sums = []
    for index, product in enumerate(products):
        product = jnp.where(same, product, 0.0)
        if index:
            product = pltpu.roll(product, index * head_dim, 1)
        summary = summary + product
        key_sums.append(sums[:, index * LANES : (index + 1) * LANES])
    key_sums.append(jnp.zeros((KEY_ROWS - len(products), LANES), F32))
    payload_out[0:LANES, :] = summary.astype(BF16)
    payload_out[LANES : LANES + KEY_ROWS, :] = jnp.concatenate(key_sums, axis=0).astype(BF16)
    store.wait()


def query_kernel(
    tile, section, mixed_in, qkv_weight, taps, groups, query_out,
    mixed, centre, query, weight, agg, group, wide_agg, sems,
):
    rows, width, channels = mixed.shape
    head = pl.ds(0, channels)
    loads = [
        pltpu.make_async_copy(mixed_in, mixed, sems.at[0]),
        pltpu.make_async_copy(qkv_weight.at[section, :, head], weight, sems.at[1]),
        pltpu.make_async_copy(taps.at[section, :, head], agg, sems.at[2]),
        pltpu.make_async_copy(groups.at[section, 0], group, sems.at[3]),
    ]
    for load in loads:
        load.start()
    for load in loads:
        load.wait()
    spread_taps(agg, wide_agg)
    for first, size in parted(rows, PARTS):
        value = jnp.dot(
            flat(mixed[first : first + size]), weight[...], preferred_element_type=F32
        )
        centre[first : first + size] = value.astype(BF16).reshape(size, width, channels)
    clear_outside(centre, (rows - tile[0]) // 2, tile[1])

    def query_rows(first, size):
        here = pl.ds(first, size)
        query[here, :, 0:channels] = jnp.maximum(centre[pl.ds(first + 2, size)], 0.0)
        grouped = aggregated(centre, wide_agg, group[...], 0, first, size, channels)
        query[here, :, channels : 2 * channels] = jnp.maximum(grouped, 0.0)

    by_groups(rows - 4, 5, query_rows)
    store = pltpu.make_async_copy(query, query_out, sems.at[4])
    store.start()
    store.wait()


def attend(
    mixed_in, query_in, payloads, weight, bias_in, held, head_dim, section, x_ref
):
    rows, width, channels = x_ref.shape
    mixed_ref, query_ref, bias, sems = held
    inner = mixed_in.at[pl.ds(2, rows)]
    halves = [(query_in, query_ref), (inner, mixed_ref), (bias_in, bias)]
    loads = [pltpu.make_async_copy(a, b, sems.at[k]) for k, (a, b) in enumerate(halves)]
    for load in loads:
        load.start()
    same = same_head(head_dim)
    square = (LANES, LANES)
    diagonal = lax.broadcasted_iota(jnp.int32, square, 0) == lax.broadcasted_iota(
        jnp.int32, square, 1
    )
    ones = jnp.where(same, 1.0, 0.0).astype(BF16)
    nothing = jnp.zeros(square, BF16)
    payload = payloads[0][...].astype(F32)
    for part in payloads[1:]:
        payload = payload + part[...].astype(F32)
    packed = payload[0:LANES]
    count = 2 * channels // LANES
    summaries, sums = [], []
    for index in range(count):
        summary = packed if index == 0 else pltpu.roll(packed, LANES - index * head_dim, 1)
        summaries.append(jnp.where(same, summary, 0.0).astype(BF16))
        keys = payload[LANES + index : LANES + index + 1]
        keys = jnp.where(diagonal, keys, 0.0).astype(BF16)
        sums.append(jnp.dot(keys, ones, preferred_element_type=F32).astype(BF16))

    def paired(blocks, index):
        return jnp.concatenate(
            [
                jnp.concatenate([blocks[index], nothing], axis=1),
                jnp.concatenate([nothing, blocks[index + 1]], axis=1),
            ],
            axis=0,
        )

    summaries = [paired(summaries, index) for index in range(0, count, 2)]
    sums = [paired(sums, index) for index in range(0, count, 2)]
    step = 2 * LANES
    for load in loads:
        load.wait()

    def attend_rows(first, size):
        query = flat(query_ref[pl.ds(first, size)])
        parts = []
        for branch in range(count // 2):
            part = query[:, branch * step : (branch + 1) * step]
            numer = jnp.dot(part, summaries[branch], preferred_element_type=F32)
            denom = jnp.dot(part, sums[branch], preferred_element_type=F32) + 1e-6
            inverse = pl.reciprocal(denom, approx=True)
            inverse = inverse * (2.0 - denom * inverse)
            parts.append((numer * inverse).astype(BF16))
        value = jnp.dot(
            jnp.concatenate(parts, axis=1), weight[section], preferred_element_type=F32
        )
        value = value + bias[section : section + 1, :]
        value = value + flat(mixed_ref[pl.ds(first, size)]).astype(F32)
        x_ref[pl.ds(first, size)] = value.astype(BF16).reshape(size, width, channels)

    by_groups(rows, 5, attend_rows)


def tap(section, a, b):
    at = 32 * section + 5 * a + b
    return slice(at, at + 1)


def prepare_kernel(head_dim, qkv, agg, group, head, *refs):
    outs, made, taps, sems = refs[:4], refs[4:8], refs[8], refs[9]
    qkv_out, agg_out, group_out, head_out = made
    sections, channels, wide = qkv.shape
    half = 3 * LANES
    heads = LANES // head_dim
    src = lax.broadcasted_iota(jnp.int32, (half, LANES), 0)
    dst = lax.broadcasted_iota(jnp.int32, (half, LANES), 1)
    first = (dst // head_dim) * 3 * head_dim + dst % head_dim
    picks = [jnp.where(src == first + k * head_dim, 1.0, 0.0).astype(BF16) for k in range(3)]
    taps[...] = jnp.zeros(taps.shape, F32)
    for section in range(sections):
        for a in range(5):
            for b in range(5):
                taps[tap(section, a, b), :] = agg[a, b, section : section + 1, :]
    rest = taps[...]
    high = rest.astype(BF16)
    rest = rest - high.astype(F32)
    middle = rest.astype(BF16)
    low = (rest - middle.astype(F32)).astype(BF16)
    split = jnp.concatenate([high, middle, low], axis=0)
    count = taps.shape[0]
    weights = qkv[...].reshape(sections * channels, wide)
    for part in range(wide // half):
        here = slice(part * half, (part + 1) * half)
        for kind in range(3):
            to = kind * channels + part * LANES
            there = slice(to, to + LANES)
            value = jnp.dot(weights[:, here], picks[kind], preferred_element_type=F32)
            qkv_out[:, :, there] = value.astype(BF16).reshape(sections, channels, LANES)
            value = jnp.dot(split[:, here], picks[kind], preferred_element_type=F32)
            value = value[:count] + value[count : 2 * count] + value[2 * count :]
            agg_out[:, :, there] = value.reshape(sections, -1, LANES)
    row = lax.broadcasted_iota(jnp.int32, (head_dim, channels), 0)
    lane = lax.broadcasted_iota(jnp.int32, (head_dim, channels), 1)
    spread = jnp.where(lane % head_dim == row, 1.0, 0.0).astype(BF16)
    across = lax.broadcasted_iota(jnp.int32, (channels, channels), 0) // head_dim
    along = lax.broadcasted_iota(jnp.int32, (channels, channels), 1) // head_dim
    for section in range(sections):
        for kind in range(3):
            tall = [group[section, 3 * h + kind] for h in range(channels // head_dim)]
            value = jnp.dot(jnp.concatenate(tall, axis=0), spread, preferred_element_type=F32)
            group_out[section, kind] = jnp.where(across == along, value, 0.0).astype(BF16)
    head_out[...] = jnp.zeros(head_out.shape, BF16)
    for a in range(3):
        rows = [head[a, b] for b in range(3)] + [jnp.zeros((4, channels), BF16)]
        head_out[a, 0:16, :] = jnp.concatenate(rows, axis=0)
    stores = [pltpu.make_async_copy(made[i], outs[i], sems.at[i]) for i in range(4)]
    for store in stores:
        store.start()
    for store in stores:
        store.wait()


def first_kernel(tile, head_dim, own, row_0, row_1, *refs):
    weights, outs, scratch = refs[:9], refs[9:11], refs[11:]
    x_ref = scratch[0]
    rows, cols = tile
    below = REACH + rows
    even = lax.axis_index("row") & 1 == 0
    x_ref[REACH:below] = own[...]
    x_ref[pl.ds(jnp.where(even, below, 0), REACH)] = row_0[...]
    x_ref[pl.ds(jnp.where(even, 0, below), REACH)] = row_1[...]
    front(x_ref, weights, outs, scratch[1:], REACH, tile, head_dim, 0)


def second_kernel(tile, head_dim, mixed, query, payload, other, out_weight, out_bias, *refs):
    weights, outs, scratch = refs[:9], refs[9:11], refs[11:]
    x_ref = scratch[0]
    attend(
        mixed, query, (payload, other), out_weight, out_bias, scratch[1:5], head_dim, 0, x_ref
    )
    front(x_ref, weights, outs, scratch[5:], REACH - 3, tile, head_dim, 1)


def last_kernel(
    tile, head_dim, mixed, query, payload, other, out_weight, out_bias, head_weight, head_bias,
    map_out, boxes_out, x_ref, *held,
):
    rows, cols = tile
    width = cols + 2 * SIDE
    attend(
        mixed, query, (payload, other), out_weight, out_bias, held, head_dim, 1, x_ref
    )
    clear_outside(x_ref, 1, cols)
    map_out[...] = x_ref[1 : 1 + rows, 0:cols, :]
    total = None
    for a in range(3):
        part = lax.dot_general(
            flat(x_ref[a : a + rows]), head_weight[a], (((1,), (1,)), ((), ())),
            preferred_element_type=F32,
        )
        total = part if total is None else total + part
    total = total.reshape(rows, width, LANES)
    lane = lax.broadcasted_iota(jnp.int32, (width, LANES), 1) // 4
    shifted = [
        jnp.where(
            lane == 0,
            pltpu.roll(total[r], 1, 0),
            jnp.where(lane == 2, pltpu.roll(total[r], width - 1, 0), total[r]),
        )
        for r in range(rows)
    ]
    shifted = jnp.concatenate(shifted, axis=0)
    across = lax.broadcasted_iota(jnp.int32, (8, LANES), 0)
    along = lax.broadcasted_iota(jnp.int32, (8, LANES), 1)
    fold = jnp.where((along % 4 == across) & (along < 12), 1.0, 0.0)
    boxes = lax.dot_general(
        fold, shifted, (((1,), (1,)), ((), ())), precision=lax.Precision.HIGHEST,
        preferred_element_type=F32,
    )
    boxes = boxes[0:4] + head_bias[...]
    for r in range(rows):
        boxes_out[:, r, :] = boxes[:, r * width : r * width + cols]


def near():
    return pl.BlockSpec(memory_space=pltpu.VMEM)


def far():
    return pl.BlockSpec(memory_space=pltpu.HBM)


def digits(size, most):
    radices = []
    while size > 1:
        radix = next((r for r in range(min(most, size), 1, -1) if size % r == 0), size)
        radices.append(radix)
        size //= radix
    return radices


def partner(i, stride, radix, step):
    digit = (i // stride) % radix
    other = digit ^ step if radix & (radix - 1) == 0 else (digit + step) % radix
    return i + (other - digit) * stride


def sum_by_permutes(value):
    rounds = []
    for axis in ("row", "col"):
        stride = 1
        for radix in digits(lax.axis_size(axis), 4):
            rounds.append((axis, stride, radix))
            stride *= radix
    for axis, stride, radix in rounds:
        count = lax.axis_size(axis)
        others = [
            lax.ppermute(value, axis, [(i, partner(i, stride, radix, k)) for i in range(count)])
            for k in range(1, radix)
        ]
        if (axis, stride, radix) == rounds[-1] and radix == 2:
            return value, others[0]
        total = value.astype(F32)
        for other in others:
            total = total + other.astype(F32)
        value = total.astype(BF16)
    return value, jnp.zeros_like(value)


def digits(size, most):
    radices = []
    while size > 1:
        radix = next((r for r in range(min(most, size), 1, -1) if size % r == 0), size)
        radices.append(radix)
        size //= radix
    return radices


def pair_exchange(value, axis, first):
    count = lax.axis_size(axis)
    pairs = []
    for i in range(first, count - 1, 2):
        pairs += [(i, i + 1), (i + 1, i)]
    return lax.ppermute(value, axis, pairs)


def local(
    features,
    expand_weight,
    expand_bias,
    depth_weight,
    depth_bias,
    project_weight,
    project_bias,
    qkv_weight,
    aggregate_depth,
    aggregate_group,
    output_weight,
    output_bias,
    head_weight,
    head_bias,
):
    rows, cols, channels = features.shape
    head_dim = aggregate_group.shape[2]
    heads = channels // head_dim
    width = cols + 2 * SIDE
    tile = (rows, cols)
    wide = expand_weight.shape[2]

    def edges(value, dim, size, odd):
        far = value.shape[dim] - size
        return [
            lax.dynamic_slice_in_dim(value, jnp.where(odd == at, far, 0), size, dim) for at in (0, 1)
        ]

    odd_row = lax.axis_index("row") & 1
    odd_col = lax.axis_index("col") & 1
    low, high = edges(features, 1, SIDE, odd_col)
    col_1 = pair_exchange(high, "col", 1)
    col_0 = pair_exchange(low, "col", 0)
    right = jnp.where(odd_col == 1, col_1, col_0)
    left = jnp.where(odd_col == 1, col_0, col_1)
    wide_rows = jnp.concatenate([features, right, left], axis=1)
    low, high = edges(wide_rows, 0, REACH, odd_row)
    row_1 = pair_exchange(high, "row", 1)
    row_0 = pair_exchange(low, "row", 0)

    aggregate_depth = aggregate_depth.transpose(1, 2, 0, 3)
    depth_weight = depth_weight.transpose(1, 2, 0, 3)
    params = pltpu.CompilerParams(vmem_limit_bytes=24 * 2**20)
    made = [
        jax.ShapeDtypeStruct(qkv_weight.shape, BF16),
        jax.ShapeDtypeStruct((SECTIONS, 32, 3 * channels), F32),
        jax.ShapeDtypeStruct((SECTIONS, 3, channels, channels), BF16),
        jax.ShapeDtypeStruct((3, LANES, channels), BF16),
    ]
    qkv_weight, taps, group, head_weight = pl.pallas_call(
        functools.partial(prepare_kernel, head_dim),
        out_shape=made,
        grid=(1,),
        in_specs=[near()] * 4,
        out_specs=[far()] * 4,
        scratch_shapes=[pltpu.VMEM(array.shape, array.dtype) for array in made]
        + [pltpu.VMEM((32 * SECTIONS, 3 * channels), F32), pltpu.SemaphoreType.DMA((4,))],
        compiler_params=params,
        cost_estimate=pl.CostEstimate(
            flops=2 * 10**9, bytes_accessed=4 * 10**6, transcendentals=0
        ),
        name="prepare",
    )(qkv_weight, aggregate_depth, aggregate_group, head_weight)

    weights = [
        expand_weight, expand_bias, depth_weight, depth_bias, project_weight, project_bias,
        qkv_weight, taps, group,
    ]
    weight_specs = [near()] * 5 + [far()] * 4

    def outs_of(count):
        return [
            jax.ShapeDtypeStruct((count, width, channels), BF16),
            jax.ShapeDtypeStruct((LANES + KEY_ROWS, LANES), BF16),
        ]

    def front_scratch(count):
        return [
            pltpu.VMEM((count, width, 256), BF16),
            pltpu.VMEM((count, width, 256), BF16),
            pltpu.VMEM(((count - 2) * width, channels), F32),
            pltpu.VMEM((count - 2, width, channels), BF16),
            pltpu.VMEM((rows + 4, width, 2 * channels), BF16),
            pltpu.VMEM((9, TILE, expand_weight.shape[2]), BF16),
            pltpu.VMEM((25, TILE, 2 * channels), BF16),
            pltpu.VMEM(project_bias.shape, F32),
            pltpu.VMEM((channels, 2 * channels), BF16),
            pltpu.VMEM((32, 2 * channels), F32),
            pltpu.VMEM((2, channels, channels), BF16),
            pltpu.SemaphoreType.DMA((5,)),
        ]

    def attend_scratch(count):
        return [
            pltpu.VMEM((count, width, channels), BF16),
            pltpu.VMEM((count, width, channels), BF16),
            pltpu.VMEM((count, width, 2 * channels), BF16),
            pltpu.VMEM(output_bias.shape, F32),
            pltpu.SemaphoreType.DMA((3,)),
        ]

    def queries(mixed, section):
        count = mixed.shape[0]
        units = (count - 4) * width * channels
        return pl.pallas_call(
            functools.partial(query_kernel, tile, section),
            out_shape=jax.ShapeDtypeStruct((count - 4, width, 2 * channels), BF16),
            grid=(1,),
            in_specs=[far()] * 4,
            out_specs=far(),
            scratch_shapes=[
                pltpu.VMEM((count, width, channels), BF16),
                pltpu.VMEM((count, width, channels), BF16),
                pltpu.VMEM((count - 4, width, 2 * channels), BF16),
                pltpu.VMEM((channels, channels), BF16),
                pltpu.VMEM((32, channels), F32),
                pltpu.VMEM((channels, channels), BF16),
                pltpu.VMEM((25, TILE, channels), BF16),
                pltpu.SemaphoreType.DMA((5,)),
            ],
            compiler_params=params,
            cost_estimate=pl.CostEstimate(
                flops=8 * units * channels, bytes_accessed=8 * units, transcendentals=0
            ),
            name="queries",
        )(mixed, qkv_weight, taps, group)

    first_rows = rows + 2 * REACH
    mixed, payload = pl.pallas_call(
        functools.partial(first_kernel, tile, head_dim),
        out_shape=outs_of(first_rows - 2),
        grid=(1,),
        in_specs=[near()] * 3 + weight_specs,
        out_specs=[far(), near()],
        scratch_shapes=[pltpu.VMEM((first_rows, width, channels), BF16)]
        + front_scratch(first_rows),
        compiler_params=params,
        name="first",
    )(wide_rows, row_0, row_1, *weights)
    query = queries(mixed, 0)
    payload, other = sum_by_permutes(payload)

    second_rows = first_rows - 6
    mixed, payload = pl.pallas_call(
        functools.partial(second_kernel, tile, head_dim),
        out_shape=outs_of(second_rows - 2),
        grid=(1,),
        in_specs=[far()] * 2 + [near()] * 3 + [far()] + weight_specs,
        out_specs=[far(), near()],
        scratch_shapes=attend_scratch(second_rows) + front_scratch(second_rows),
        compiler_params=params,
        name="second",
    )(mixed, query, payload, other, output_weight, output_bias, *weights)
    query = queries(mixed, 1)
    payload, other = sum_by_permutes(payload)

    return pl.pallas_call(
        functools.partial(last_kernel, tile, head_dim),
        out_shape=[
            jax.ShapeDtypeStruct((rows, cols, channels), BF16),
            jax.ShapeDtypeStruct((4, rows, cols), F32),
        ],
        grid=(1,),
        in_specs=[far()] * 2 + [near()] * 3 + [far()] + [near()] * 2,
        out_specs=[near()] * 2,
        scratch_shapes=attend_scratch(rows + 2),
        compiler_params=params,
        name="last",
    )(
        mixed, query, payload, other, output_weight, output_bias, head_weight,
        head_bias.reshape(4, 1),
    )


def solution(mesh):
    return jax.shard_map(
        local,
        mesh=mesh,
        in_specs=(P("row", "col", None),) + (P(),) * 13,
        out_specs=(P("row", "col", None), P(None, "row", "col")),
        check_vma=False,
    )
```

```python
import functools

import jax
import jax.numpy as jnp
from jax import lax
from jax.experimental import pallas as pl
from jax.experimental.pallas import tpu as pltpu
from jax.sharding import PartitionSpec as P

SECTIONS = 2
LANES = 128
SIDE = 8
REACH = 7
KEY_ROWS = 16
TILE = 16
PARTS = 2
F32 = jnp.float32
BF16 = jnp.bfloat16


def six_hard_swish(value):
    return value * jnp.minimum(jnp.maximum(value + 3.0, 0.0), 6.0)


def parted(count, parts):
    cuts = [count * k // parts for k in range(parts + 1)]
    return [(a, b - a) for a, b in zip(cuts, cuts[1:]) if b > a]


def group_size(count, most):
    return next(n for n in range(min(most, count), 0, -1) if count % n == 0)


def by_groups(count, most, body):
    size = group_size(count, most)

    def group(index, carry):
        body(index * size, size)
        return carry

    lax.fori_loop(0, count // size, group, 0)


def clear_outside(ref, halo, cols):
    rows = ref.shape[0]
    row, col = lax.axis_index("row"), lax.axis_index("col")

    @pl.when(row == 0)
    def _():
        ref[0:halo] = jnp.zeros((halo,) + ref.shape[1:], ref.dtype)

    @pl.when(row == lax.axis_size("row") - 1)
    def _():
        ref[rows - halo : rows] = jnp.zeros((halo,) + ref.shape[1:], ref.dtype)

    @pl.when(col == 0)
    def _():
        ref[:, cols + SIDE : cols + 2 * SIDE, :] = jnp.zeros((rows, SIDE, ref.shape[2]), ref.dtype)

    @pl.when(col == lax.axis_size("col") - 1)
    def _():
        ref[:, cols : cols + SIDE, :] = jnp.zeros((rows, SIDE, ref.shape[2]), ref.dtype)


def flat(value):
    return value.reshape(-1, value.shape[-1])


def same_head(head_dim):
    across = lax.broadcasted_iota(jnp.int32, (LANES, LANES), 0) // head_dim
    along = lax.broadcasted_iota(jnp.int32, (LANES, LANES), 1) // head_dim
    return across == along


def depthwise_row(rows, taps, size, width):
    rows = [row.reshape(width // TILE, TILE, LANES) for row in rows]
    total = None
    for b in range(size):
        part = None
        for a in range(size):
            term = rows[a] * taps(a, b)[None]
            part = term if part is None else part + term
        part = part.reshape(width, LANES).astype(F32)
        if b != size // 2:
            part = pltpu.roll(part, (size // 2 - b) % width, 0)
        total = part if total is None else total + part
    return total


def spread_taps(agg, wide_agg):
    for index in range(25):
        taps = agg[index : index + 1, :]
        wide_agg[index] = jnp.broadcast_to(taps, (TILE, taps.shape[1])).astype(BF16)


def aggregated(source, wide_agg, group, low, first, size, channels):
    width = source.shape[1]
    scaled = []
    for r in range(size):
        lanes = []
        for lane in range(low, low + channels, LANES):
            here = slice(lane, lane + LANES)
            value = depthwise_row(
                [source[first + r + a, :, here] for a in range(5)],
                lambda a, b: wide_agg[5 * a + b, :, here], 5, width,
            )
            lanes.append(value.astype(BF16))
        scaled.append(jnp.concatenate(lanes, axis=1))
    value = jnp.dot(jnp.concatenate(scaled, axis=0), group, preferred_element_type=F32)
    return value.astype(BF16).reshape(size, width, channels)


def front(x_ref, weights, outs, scratch, halo, tile, head_dim, section):
    expand, expand_bias, depth, depth_bias, project = weights[:5]
    mixed_out, payload_out = outs
    (
        hidden_0, hidden_1, total, mixed, pairs, wide_depth, wide_agg,
        project_bias, pair_weight, agg, group, sems,
    ) = scratch
    channels = x_ref.shape[2]
    tail = pl.ds(channels, 2 * channels)
    loads = [
        pltpu.make_async_copy(weights[5], project_bias, sems.at[0]),
        pltpu.make_async_copy(weights[6].at[section, :, tail], pair_weight, sems.at[1]),
        pltpu.make_async_copy(weights[7].at[section, :, tail], agg, sems.at[2]),
        pltpu.make_async_copy(weights[8].at[section, pl.ds(1, 2)], group, sems.at[3]),
    ]
    for load in loads:
        load.start()
    rows, width, channels = x_ref.shape
    tile_rows, tile_cols = tile
    inner = rows - 2
    chunk = hidden_0.shape[2]
    chunks = expand.shape[2] // chunk
    for index in range(9):
        taps = depth[index // 3, index % 3, section : section + 1, :] * (1.0 / 6.0)
        wide_depth[index] = jnp.broadcast_to(taps, (TILE, taps.shape[1])).astype(BF16)
    total[...] = 6.0 * flat(x_ref[1 : rows - 1]).astype(F32)

    def expand_rows(out, at, first, size):
        value = jnp.dot(
            flat(x_ref[first : first + size]), expand[section, :, pl.ds(at, chunk)],
            preferred_element_type=F32,
        )
        value = (value + expand_bias[section : section + 1, pl.ds(at, chunk)]).astype(BF16)
        out[first : first + size] = six_hard_swish(value).reshape(size, width, chunk)

    def spread_rows(hidden, at, first, size):
        spread = []
        for r in range(first, first + size):
            lanes = []
            for lane in range(0, chunk, LANES):
                here = pl.ds(pl.multiple_of(at + lane, LANES), LANES)
                value = depthwise_row(
                    [hidden[r + a, :, lane : lane + LANES] for a in range(3)],
                    lambda a, b: wide_depth[3 * a + b, :, here], 3, width,
                )
                value = (value + depth_bias[section : section + 1, here]).astype(BF16)
                lanes.append(six_hard_swish(value))
            spread.append(jnp.concatenate(lanes, axis=1))
        pixels = slice(first * width, (first + size) * width)
        total[pixels] += jnp.dot(
            jnp.concatenate(spread, axis=0), project[section, pl.ds(at, chunk), :],
            preferred_element_type=F32,
        )

    def stage(index, current, following):
        at = pl.multiple_of(index * chunk, chunk)
        ahead = pl.multiple_of(jnp.minimum(index + 1, chunks - 1) * chunk, chunk)
        for (first, size), (from_row, count) in zip(parted(inner, PARTS), parted(rows, PARTS)):
            expand_rows(following, ahead, from_row, count)
            spread_rows(current, at, first, size)
        clear_outside(following, halo, tile_cols)

    for first, size in parted(rows, PARTS):
        expand_rows(hidden_0, 0, first, size)
    clear_outside(hidden_0, halo, tile_cols)

    def two_stages(index, carry):
        stage(2 * index, hidden_0, hidden_1)
        stage(2 * index + 1, hidden_1, hidden_0)
        return carry

    lax.fori_loop(0, chunks // 2, two_stages, 0)
    loads[0].wait()
    value = total[...] * (1.0 / 6.0) + project_bias[section : section + 1, :]
    mixed[...] = value.astype(BF16).reshape(inner, width, channels)
    store = pltpu.make_async_copy(mixed, mixed_out, sems.at[4])
    store.start()
    for load in loads[1:]:
        load.wait()
    spread_taps(agg, wide_agg)
    around = halo - 1
    first_pair = around - 2
    count = tile_rows + 4
    for first, size in parted(count, PARTS - 1):
        at = first_pair + first
        value = jnp.dot(
            flat(mixed[at : at + size]), pair_weight[...], preferred_element_type=F32
        )
        pairs[first : first + size] = value.astype(BF16).reshape(size, width, 2 * channels)
    clear_outside(pairs, 2, tile_cols)
    size = group_size(tile_rows, 4)

    def summed(key, value):
        key = jnp.maximum(flat(key[:, 0:tile_cols]), 0.0)
        value = flat(value[:, 0:tile_cols])
        products = [
            lax.dot_general(
                key[:, lane : lane + LANES], value[:, lane : lane + LANES],
                (((0,), (0,)), ((), ())), preferred_element_type=F32,
            )
            for lane in range(0, channels, LANES)
        ]
        return products, jnp.sum(key.astype(F32), axis=0, keepdims=True)

    mine = slice(2, 2 + tile_rows)
    products, sums = summed(
        pairs[mine, :, 0:channels], pairs[mine, :, channels : 2 * channels]
    )

    def grouped_rows(index, carry):
        at = index * size
        more, sums = summed(
            aggregated(pairs, wide_agg, group[0], 0, at, size, channels),
            aggregated(pairs, wide_agg, group[1], channels, at, size, channels),
        )
        return [a + b for a, b in zip(carry[0], more)], carry[1] + sums

    more, more_sums = lax.fori_loop(
        0, tile_rows // size, grouped_rows,
        ([jnp.zeros((LANES, LANES), F32) for _ in products], jnp.zeros_like(sums)),
    )
    products = products + more
    sums = jnp.concatenate([sums, more_sums], axis=1)
    same = same_head(head_dim)
    summary = jnp.zeros((LANES, LANES), F32)
    key_sums = []
    for index, product in enumerate(products):
        product = jnp.where(same, product, 0.0)
        if index:
            product = pltpu.roll(product, index * head_dim, 1)
        summary = summary + product
        key_sums.append(sums[:, index * LANES : (index + 1) * LANES])
    key_sums.append(jnp.zeros((KEY_ROWS - len(products), LANES), F32))
    payload_out[0:LANES, :] = summary.astype(BF16)
    payload_out[LANES : LANES + KEY_ROWS, :] = jnp.concatenate(key_sums, axis=0).astype(BF16)
    store.wait()


def query_kernel(
    tile, section, mixed_in, qkv_weight, taps, groups, query, mixed_out,
    mixed, centre, weight, agg, group, wide_agg, sems,
):
    rows, width, channels = mixed.shape
    head = pl.ds(0, channels)
    loads = [
        pltpu.make_async_copy(mixed_in, mixed, sems.at[0]),
        pltpu.make_async_copy(qkv_weight.at[section, :, head], weight, sems.at[1]),
        pltpu.make_async_copy(taps.at[section, :, head], agg, sems.at[2]),
        pltpu.make_async_copy(groups.at[section, 0], group, sems.at[3]),
    ]
    for load in loads:
        load.start()
    for load in loads:
        load.wait()
    mixed_out[...] = mixed[2 : rows - 2]
    spread_taps(agg, wide_agg)
    for first, size in parted(rows, PARTS):
        value = jnp.dot(
            flat(mixed[first : first + size]), weight[...], preferred_element_type=F32
        )
        centre[first : first + size] = value.astype(BF16).reshape(size, width, channels)
    clear_outside(centre, (rows - tile[0]) // 2, tile[1])

    def query_rows(first, size):
        here = pl.ds(first, size)
        query[here, :, 0:channels] = jnp.maximum(centre[pl.ds(first + 2, size)], 0.0)
        grouped = aggregated(centre, wide_agg, group[...], 0, first, size, channels)
        query[here, :, channels : 2 * channels] = jnp.maximum(grouped, 0.0)

    by_groups(rows - 4, 5, query_rows)


def attend(
    mixed_ref, query_ref, payloads, weight, bias_in, held, head_dim, section, x_ref
):
    rows, width, channels = x_ref.shape
    bias, sem = held
    load = pltpu.make_async_copy(bias_in, bias, sem)
    load.start()
    same = same_head(head_dim)
    square = (LANES, LANES)
    diagonal = lax.broadcasted_iota(jnp.int32, square, 0) == lax.broadcasted_iota(
        jnp.int32, square, 1
    )
    ones = jnp.where(same, 1.0, 0.0).astype(BF16)
    nothing = jnp.zeros(square, BF16)
    payload = payloads[0][...].astype(F32)
    for part in payloads[1:]:
        payload = payload + part[...].astype(F32)
    packed = payload[0:LANES]
    count = 2 * channels // LANES
    summaries, sums = [], []
    for index in range(count):
        summary = packed if index == 0 else pltpu.roll(packed, LANES - index * head_dim, 1)
        summaries.append(jnp.where(same, summary, 0.0).astype(BF16))
        keys = payload[LANES + index : LANES + index + 1]
        keys = jnp.where(diagonal, keys, 0.0).astype(BF16)
        sums.append(jnp.dot(keys, ones, preferred_element_type=F32).astype(BF16))

    def paired(blocks, index):
        return jnp.concatenate(
            [
                jnp.concatenate([blocks[index], nothing], axis=1),
                jnp.concatenate([nothing, blocks[index + 1]], axis=1),
            ],
            axis=0,
        )

    summaries = [paired(summaries, index) for index in range(0, count, 2)]
    sums = [paired(sums, index) for index in range(0, count, 2)]
    step = 2 * LANES
    load.wait()

    def attend_rows(first, size):
        query = flat(query_ref[pl.ds(first, size)])
        parts = []
        for branch in range(count // 2):
            part = query[:, branch * step : (branch + 1) * step]
            numer = jnp.dot(part, summaries[branch], preferred_element_type=F32)
            denom = jnp.dot(part, sums[branch], preferred_element_type=F32) + 1e-6
            inverse = pl.reciprocal(denom, approx=True)
            inverse = inverse * (2.0 - denom * inverse)
            parts.append((numer * inverse).astype(BF16))
        value = jnp.dot(
            jnp.concatenate(parts, axis=1), weight[section], preferred_element_type=F32
        )
        value = value + bias[section : section + 1, :]
        value = value + flat(mixed_ref[pl.ds(first, size)]).astype(F32)
        x_ref[pl.ds(first, size)] = value.astype(BF16).reshape(size, width, channels)

    by_groups(rows, 5, attend_rows)


def tap(section, a, b):
    at = 32 * section + 5 * a + b
    return slice(at, at + 1)


def prepare_kernel(head_dim, qkv, agg, group, head, project_bias, output_bias, *refs):
    outs, made, taps, sems = refs[:6], refs[6:10], refs[10], refs[11]
    qkv_out, agg_out, group_out, head_out = made
    made = [*made, project_bias, output_bias]
    sections, channels, wide = qkv.shape
    half = 3 * LANES
    heads = LANES // head_dim
    src = lax.broadcasted_iota(jnp.int32, (half, LANES), 0)
    dst = lax.broadcasted_iota(jnp.int32, (half, LANES), 1)
    first = (dst // head_dim) * 3 * head_dim + dst % head_dim
    picks = [jnp.where(src == first + k * head_dim, 1.0, 0.0).astype(BF16) for k in range(3)]
    taps[...] = jnp.zeros(taps.shape, F32)
    for section in range(sections):
        for a in range(5):
            for b in range(5):
                taps[tap(section, a, b), :] = agg[a, b, section : section + 1, :]
    rest = taps[...]
    high = rest.astype(BF16)
    rest = rest - high.astype(F32)
    middle = rest.astype(BF16)
    low = (rest - middle.astype(F32)).astype(BF16)
    split = jnp.concatenate([high, middle, low], axis=0)
    count = taps.shape[0]
    weights = qkv[...].reshape(sections * channels, wide)
    for part in range(wide // half):
        here = slice(part * half, (part + 1) * half)
        for kind in range(3):
            to = kind * channels + part * LANES
            there = slice(to, to + LANES)
            value = jnp.dot(weights[:, here], picks[kind], preferred_element_type=F32)
            qkv_out[:, :, there] = value.astype(BF16).reshape(sections, channels, LANES)
            value = jnp.dot(split[:, here], picks[kind], preferred_element_type=F32)
            value = value[:count] + value[count : 2 * count] + value[2 * count :]
            agg_out[:, :, there] = value.reshape(sections, -1, LANES)
    row = lax.broadcasted_iota(jnp.int32, (head_dim, channels), 0)
    lane = lax.broadcasted_iota(jnp.int32, (head_dim, channels), 1)
    spread = jnp.where(lane % head_dim == row, 1.0, 0.0).astype(BF16)
    across = lax.broadcasted_iota(jnp.int32, (channels, channels), 0) // head_dim
    along = lax.broadcasted_iota(jnp.int32, (channels, channels), 1) // head_dim
    for section in range(sections):
        for kind in range(3):
            tall = [group[section, 3 * h + kind] for h in range(channels // head_dim)]
            value = jnp.dot(jnp.concatenate(tall, axis=0), spread, preferred_element_type=F32)
            group_out[section, kind] = jnp.where(across == along, value, 0.0).astype(BF16)
    head_out[...] = jnp.zeros(head_out.shape, BF16)
    for a in range(3):
        rows = [head[a, b] for b in range(3)] + [jnp.zeros((4, channels), BF16)]
        head_out[a, 0:16, :] = jnp.concatenate(rows, axis=0)
    stores = [pltpu.make_async_copy(made[i], outs[i], sems.at[i]) for i in range(6)]
    for store in stores:
        store.start()
    for store in stores:
        store.wait()


def first_kernel(tile, head_dim, own, row_0, row_1, *refs):
    weights, outs, scratch = refs[:9], refs[9:11], refs[11:]
    x_ref = scratch[0]
    rows, cols = tile
    below = REACH + rows
    even = lax.axis_index("row") & 1 == 0
    x_ref[REACH:below] = own[...]
    x_ref[pl.ds(jnp.where(even, below, 0), REACH)] = row_0[...]
    x_ref[pl.ds(jnp.where(even, 0, below), REACH)] = row_1[...]
    front(x_ref, weights, outs, scratch[1:], REACH, tile, head_dim, 0)


def second_kernel(tile, head_dim, mixed, query, payload, other, out_weight, out_bias, *refs):
    weights, outs, scratch = refs[:9], refs[9:11], refs[11:]
    x_ref = scratch[0]
    attend(
        mixed, query, (payload, other), out_weight, out_bias, scratch[1:3], head_dim, 0, x_ref
    )
    front(x_ref, weights, outs, scratch[3:], REACH - 3, tile, head_dim, 1)


def last_kernel(
    tile, head_dim, mixed, query, payload, other, out_weight, out_bias, head_weight, head_bias,
    map_out, boxes_out, x_ref, *held,
):
    rows, cols = tile
    width = cols + 2 * SIDE
    attend(
        mixed, query, (payload, other), out_weight, out_bias, held, head_dim, 1, x_ref
    )
    clear_outside(x_ref, 1, cols)
    map_out[...] = x_ref[1 : 1 + rows, 0:cols, :]
    total = None
    for a in range(3):
        part = lax.dot_general(
            flat(x_ref[a : a + rows]), head_weight[a], (((1,), (1,)), ((), ())),
            preferred_element_type=F32,
        )
        total = part if total is None else total + part
    total = total.reshape(rows, width, LANES)
    lane = lax.broadcasted_iota(jnp.int32, (width, LANES), 1) // 4
    shifted = [
        jnp.where(
            lane == 0,
            pltpu.roll(total[r], 1, 0),
            jnp.where(lane == 2, pltpu.roll(total[r], width - 1, 0), total[r]),
        )
        for r in range(rows)
    ]
    shifted = jnp.concatenate(shifted, axis=0)
    across = lax.broadcasted_iota(jnp.int32, (8, LANES), 0)
    along = lax.broadcasted_iota(jnp.int32, (8, LANES), 1)
    fold = jnp.where((along % 4 == across) & (along < 12), 1.0, 0.0)
    boxes = lax.dot_general(
        fold, shifted, (((1,), (1,)), ((), ())), precision=lax.Precision.HIGHEST,
        preferred_element_type=F32,
    )
    boxes = boxes[0:4] + head_bias[...]
    for r in range(rows):
        boxes_out[:, r, :] = boxes[:, r * width : r * width + cols]


def near():
    return pl.BlockSpec(memory_space=pltpu.VMEM)


def far():
    return pl.BlockSpec(memory_space=pltpu.HBM)


def digits(size, most):
    radices = []
    while size > 1:
        radix = next((r for r in range(min(most, size), 1, -1) if size % r == 0), size)
        radices.append(radix)
        size //= radix
    return radices


def partner(i, stride, radix, step):
    digit = (i // stride) % radix
    other = digit ^ step if radix & (radix - 1) == 0 else (digit + step) % radix
    return i + (other - digit) * stride


def sum_by_permutes(value, most):
    rounds = []
    for axis in ("row", "col"):
        stride = 1
        for radix in digits(lax.axis_size(axis), most[axis]):
            rounds.append((axis, stride, radix))
            stride *= radix
    for axis, stride, radix in rounds:
        count = lax.axis_size(axis)
        others = [
            lax.ppermute(value, axis, [(i, partner(i, stride, radix, k)) for i in range(count)])
            for k in range(1, radix)
        ]
        if (axis, stride, radix) == rounds[-1] and radix == 2:
            return value, others[0]
        total = value.astype(F32)
        for other in others:
            total = total + other.astype(F32)
        value = total.astype(BF16)
    return value, jnp.zeros_like(value)


def digits(size, most):
    radices = []
    while size > 1:
        radix = next((r for r in range(min(most, size), 1, -1) if size % r == 0), size)
        radices.append(radix)
        size //= radix
    return radices


def pair_exchange(value, axis, first):
    count = lax.axis_size(axis)
    pairs = []
    for i in range(first, count - 1, 2):
        pairs += [(i, i + 1), (i + 1, i)]
    return lax.ppermute(value, axis, pairs)


def local(
    features,
    expand_weight,
    expand_bias,
    depth_weight,
    depth_bias,
    project_weight,
    project_bias,
    qkv_weight,
    aggregate_depth,
    aggregate_group,
    output_weight,
    output_bias,
    head_weight,
    head_bias,
):
    rows, cols, channels = features.shape
    head_dim = aggregate_group.shape[2]
    heads = channels // head_dim
    width = cols + 2 * SIDE
    tile = (rows, cols)
    wide = expand_weight.shape[2]

    def edges(value, dim, size, odd):
        far = value.shape[dim] - size
        return [
            lax.dynamic_slice_in_dim(value, jnp.where(odd == at, far, 0), size, dim) for at in (0, 1)
        ]

    odd_row = lax.axis_index("row") & 1
    odd_col = lax.axis_index("col") & 1
    low, high = edges(features, 1, SIDE, odd_col)
    col_1 = pair_exchange(high, "col", 1)
    col_0 = pair_exchange(low, "col", 0)
    right = jnp.where(odd_col == 1, col_1, col_0)
    left = jnp.where(odd_col == 1, col_0, col_1)
    wide_rows = jnp.concatenate([features, right, left], axis=1)
    low, high = edges(wide_rows, 0, REACH, odd_row)
    row_1 = pair_exchange(high, "row", 1)
    row_0 = pair_exchange(low, "row", 0)

    aggregate_depth = aggregate_depth.transpose(1, 2, 0, 3)
    depth_weight = depth_weight.transpose(1, 2, 0, 3)
    params = pltpu.CompilerParams(vmem_limit_bytes=24 * 2**20)
    made = [
        jax.ShapeDtypeStruct(qkv_weight.shape, BF16),
        jax.ShapeDtypeStruct((SECTIONS, 32, 3 * channels), F32),
        jax.ShapeDtypeStruct((SECTIONS, 3, channels, channels), BF16),
        jax.ShapeDtypeStruct((3, LANES, channels), BF16),
    ]
    biases = [jax.ShapeDtypeStruct(array.shape, F32) for array in (project_bias, output_bias)]
    qkv_weight, taps, group, head_weight, project_bias, output_bias = pl.pallas_call(
        functools.partial(prepare_kernel, head_dim),
        out_shape=made + biases,
        grid=(1,),
        in_specs=[near()] * 6,
        out_specs=[far()] * 6,
        scratch_shapes=[pltpu.VMEM(array.shape, array.dtype) for array in made]
        + [pltpu.VMEM((32 * SECTIONS, 3 * channels), F32), pltpu.SemaphoreType.DMA((6,))],
        compiler_params=params,
        cost_estimate=pl.CostEstimate(
            flops=2 * 10**9, bytes_accessed=4 * 10**6, transcendentals=0
        ),
        name="prepare",
    )(qkv_weight, aggregate_depth, aggregate_group, head_weight, project_bias, output_bias)

    weights = [
        expand_weight, expand_bias, depth_weight, depth_bias, project_weight, project_bias,
        qkv_weight, taps, group,
    ]
    weight_specs = [near()] * 5 + [far()] * 4

    def outs_of(count):
        return [
            jax.ShapeDtypeStruct((count, width, channels), BF16),
            jax.ShapeDtypeStruct((LANES + KEY_ROWS, LANES), BF16),
        ]

    def front_scratch(count):
        return [
            pltpu.VMEM((count, width, 256), BF16),
            pltpu.VMEM((count, width, 256), BF16),
            pltpu.VMEM(((count - 2) * width, channels), F32),
            pltpu.VMEM((count - 2, width, channels), BF16),
            pltpu.VMEM((rows + 4, width, 2 * channels), BF16),
            pltpu.VMEM((9, TILE, expand_weight.shape[2]), BF16),
            pltpu.VMEM((25, TILE, 2 * channels), BF16),
            pltpu.VMEM(project_bias.shape, F32),
            pltpu.VMEM((channels, 2 * channels), BF16),
            pltpu.VMEM((32, 2 * channels), F32),
            pltpu.VMEM((2, channels, channels), BF16),
            pltpu.SemaphoreType.DMA((5,)),
        ]

    def attend_scratch(count):
        return [
            pltpu.VMEM((count, width, channels), BF16),
            pltpu.VMEM(output_bias.shape, F32),
            pltpu.SemaphoreType.DMA,
        ]

    def queries(mixed, section):
        count = mixed.shape[0]
        units = (count - 4) * width * channels
        return pl.pallas_call(
            functools.partial(query_kernel, tile, section),
            out_shape=[
                jax.ShapeDtypeStruct((count - 4, width, 2 * channels), BF16),
                jax.ShapeDtypeStruct((count - 4, width, channels), BF16),
            ],
            grid=(1,),
            in_specs=[far()] * 4,
            out_specs=[near()] * 2,
            scratch_shapes=[
                pltpu.VMEM((count, width, channels), BF16),
                pltpu.VMEM((count, width, channels), BF16),
                pltpu.VMEM((channels, channels), BF16),
                pltpu.VMEM((32, channels), F32),
                pltpu.VMEM((channels, channels), BF16),
                pltpu.VMEM((25, TILE, channels), BF16),
                pltpu.SemaphoreType.DMA((4,)),
            ],
            compiler_params=params,
            cost_estimate=pl.CostEstimate(
                flops=8 * units * channels, bytes_accessed=8 * units, transcendentals=0
            ),
            name="queries",
        )(mixed, qkv_weight, taps, group)

    first_rows = rows + 2 * REACH
    mixed, payload = pl.pallas_call(
        functools.partial(first_kernel, tile, head_dim),
        out_shape=outs_of(first_rows - 2),
        grid=(1,),
        in_specs=[near()] * 3 + weight_specs,
        out_specs=[far(), near()],
        scratch_shapes=[pltpu.VMEM((first_rows, width, channels), BF16)]
        + front_scratch(first_rows),
        compiler_params=params,
        name="first",
    )(wide_rows, row_0, row_1, *weights)
    query, mixed = queries(mixed, 0)
    payload, other = sum_by_permutes(payload, {"row": 4, "col": 2})

    second_rows = first_rows - 6
    mixed, payload = pl.pallas_call(
        functools.partial(second_kernel, tile, head_dim),
        out_shape=outs_of(second_rows - 2),
        grid=(1,),
        in_specs=[near()] * 5 + [far()] + weight_specs,
        out_specs=[far(), near()],
        scratch_shapes=attend_scratch(second_rows) + front_scratch(second_rows),
        compiler_params=params,
        name="second",
    )(mixed, query, payload, other, output_weight, output_bias, *weights)
    query, mixed = queries(mixed, 1)
    payload, other = sum_by_permutes(payload, {"row": 2, "col": 2})

    return pl.pallas_call(
        functools.partial(last_kernel, tile, head_dim),
        out_shape=[
            jax.ShapeDtypeStruct((rows, cols, channels), BF16),
            jax.ShapeDtypeStruct((4, rows, cols), F32),
        ],
        grid=(1,),
        in_specs=[near()] * 5 + [far()] + [near()] * 2,
        out_specs=[near()] * 2,
        scratch_shapes=attend_scratch(rows + 2),
        compiler_params=params,
        name="last",
    )(
        mixed, query, payload, other, output_weight, output_bias, head_weight,
        head_bias.reshape(4, 1),
    )


def solution(mesh):
    return jax.shard_map(
        local,
        mesh=mesh,
        in_specs=(P("row", "col", None),) + (P(),) * 13,
        out_specs=(P("row", "col", None), P(None, "row", "col")),
        check_vma=False,
    )
```

```python
import functools
import itertools

import jax
import jax.numpy as jnp
from jax import lax
from jax.experimental import pallas as pl
from jax.experimental.pallas import tpu as pltpu
from jax.sharding import PartitionSpec as P

SECTIONS = 2
LANES = 128
SIDE = 8
REACH = 7
KEY_ROWS = 16
TILE = 16
PARTS = 2
F32 = jnp.float32
BF16 = jnp.bfloat16


def six_hard_swish(value):
    return value * jnp.minimum(jnp.maximum(value + 3.0, 0.0), 6.0)


def parted(count, parts):
    cuts = [count * k // parts for k in range(parts + 1)]
    return [(a, b - a) for a, b in zip(cuts, cuts[1:]) if b > a]


def group_size(count, most):
    return next(n for n in range(min(most, count), 0, -1) if count % n == 0)


def by_groups(count, most, body):
    size = group_size(count, most)

    def group(index, carry):
        body(index * size, size)
        return carry

    lax.fori_loop(0, count // size, group, 0)


def clear_outside(ref, halo, cols):
    rows = ref.shape[0]
    row, col = lax.axis_index("row"), lax.axis_index("col")

    @pl.when(row == 0)
    def _():
        ref[0:halo] = jnp.zeros((halo,) + ref.shape[1:], ref.dtype)

    @pl.when(row == lax.axis_size("row") - 1)
    def _():
        ref[rows - halo : rows] = jnp.zeros((halo,) + ref.shape[1:], ref.dtype)

    @pl.when(col == 0)
    def _():
        ref[:, cols + SIDE : cols + 2 * SIDE, :] = jnp.zeros((rows, SIDE, ref.shape[2]), ref.dtype)

    @pl.when(col == lax.axis_size("col") - 1)
    def _():
        ref[:, cols : cols + SIDE, :] = jnp.zeros((rows, SIDE, ref.shape[2]), ref.dtype)


def flat(value):
    return value.reshape(-1, value.shape[-1])


def same_head(head_dim):
    across = lax.broadcasted_iota(jnp.int32, (LANES, LANES), 0) // head_dim
    along = lax.broadcasted_iota(jnp.int32, (LANES, LANES), 1) // head_dim
    return across == along


def depthwise_row(rows, taps, size, width):
    rows = [row.reshape(width // TILE, TILE, LANES) for row in rows]
    total = None
    for b in range(size):
        part = None
        for a in range(size):
            term = rows[a] * taps(a, b)[None]
            part = term if part is None else part + term
        part = part.reshape(width, LANES).astype(F32)
        if b != size // 2:
            part = pltpu.roll(part, (size // 2 - b) % width, 0)
        total = part if total is None else total + part
    return total


def spread_taps(agg, wide_agg):
    for index in range(25):
        taps = agg[index : index + 1, :]
        wide_agg[index] = jnp.broadcast_to(taps, (TILE, taps.shape[1])).astype(BF16)


def aggregated(source, wide_agg, group, low, first, size, channels):
    width = source.shape[1]
    scaled = []
    for r in range(size):
        lanes = []
        for lane in range(low, low + channels, LANES):
            here = slice(lane, lane + LANES)
            value = depthwise_row(
                [source[first + r + a, :, here] for a in range(5)],
                lambda a, b: wide_agg[5 * a + b, :, here], 5, width,
            )
            lanes.append(value.astype(BF16))
        scaled.append(jnp.concatenate(lanes, axis=1))
    value = jnp.dot(jnp.concatenate(scaled, axis=0), group, preferred_element_type=F32)
    return value.astype(BF16).reshape(size, width, channels)


def front(x_ref, weights, outs, scratch, halo, tile, head_dim, section):
    expand, expand_bias, depth, depth_bias, project = weights[:5]
    mixed_out, payload_out = outs
    (
        hidden_0, hidden_1, total, mixed, pairs, wide_depth, wide_agg,
        project_bias, pair_weight, agg, group, sems,
    ) = scratch
    channels = x_ref.shape[2]
    tail = pl.ds(channels, 2 * channels)
    loads = [
        pltpu.make_async_copy(weights[5], project_bias, sems.at[0]),
        pltpu.make_async_copy(weights[6].at[section, :, tail], pair_weight, sems.at[1]),
        pltpu.make_async_copy(weights[7].at[section, :, tail], agg, sems.at[2]),
        pltpu.make_async_copy(weights[8].at[section, pl.ds(1, 2)], group, sems.at[3]),
    ]
    for load in loads:
        load.start()
    rows, width, channels = x_ref.shape
    tile_rows, tile_cols = tile
    inner = rows - 2
    chunk = hidden_0.shape[2]
    chunks = expand.shape[2] // chunk
    for index in range(9):
        taps = depth[index // 3, index % 3, section : section + 1, :] * (1.0 / 6.0)
        wide_depth[index] = jnp.broadcast_to(taps, (TILE, taps.shape[1])).astype(BF16)
    total[...] = 6.0 * flat(x_ref[1 : rows - 1]).astype(F32)

    def expand_rows(out, at, first, size):
        value = jnp.dot(
            flat(x_ref[first : first + size]), expand[section, :, pl.ds(at, chunk)],
            preferred_element_type=F32,
        )
        value = (value + expand_bias[section : section + 1, pl.ds(at, chunk)]).astype(BF16)
        out[first : first + size] = six_hard_swish(value).reshape(size, width, chunk)

    def spread_rows(hidden, at, first, size):
        spread = []
        for r in range(first, first + size):
            lanes = []
            for lane in range(0, chunk, LANES):
                here = pl.ds(pl.multiple_of(at + lane, LANES), LANES)
                value = depthwise_row(
                    [hidden[r + a, :, lane : lane + LANES] for a in range(3)],
                    lambda a, b: wide_depth[3 * a + b, :, here], 3, width,
                )
                value = (value + depth_bias[section : section + 1, here]).astype(BF16)
                lanes.append(six_hard_swish(value))
            spread.append(jnp.concatenate(lanes, axis=1))
        pixels = slice(first * width, (first + size) * width)
        total[pixels] += jnp.dot(
            jnp.concatenate(spread, axis=0), project[section, pl.ds(at, chunk), :],
            preferred_element_type=F32,
        )

    def stage(index, current, following):
        at = pl.multiple_of(index * chunk, chunk)
        ahead = pl.multiple_of(jnp.minimum(index + 1, chunks - 1) * chunk, chunk)
        for (first, size), (from_row, count) in zip(parted(inner, PARTS), parted(rows, PARTS)):
            expand_rows(following, ahead, from_row, count)
            spread_rows(current, at, first, size)
        clear_outside(following, halo, tile_cols)

    for first, size in parted(rows, PARTS):
        expand_rows(hidden_0, 0, first, size)
    clear_outside(hidden_0, halo, tile_cols)

    def two_stages(index, carry):
        stage(2 * index, hidden_0, hidden_1)
        stage(2 * index + 1, hidden_1, hidden_0)
        return carry

    lax.fori_loop(0, chunks // 2, two_stages, 0)
    loads[0].wait()
    value = total[...] * (1.0 / 6.0) + project_bias[section : section + 1, :]
    mixed[...] = value.astype(BF16).reshape(inner, width, channels)
    store = pltpu.make_async_copy(mixed, mixed_out, sems.at[4])
    store.start()
    for load in loads[1:]:
        load.wait()
    spread_taps(agg, wide_agg)
    around = halo - 1
    first_pair = around - 2
    count = tile_rows + 4
    for first, size in parted(count, PARTS - 1):
        at = first_pair + first
        value = jnp.dot(
            flat(mixed[at : at + size]), pair_weight[...], preferred_element_type=F32
        )
        pairs[first : first + size] = value.astype(BF16).reshape(size, width, 2 * channels)
    clear_outside(pairs, 2, tile_cols)
    size = group_size(tile_rows, 4)

    def summed(key, value):
        key = jnp.maximum(flat(key[:, 0:tile_cols]), 0.0)
        value = flat(value[:, 0:tile_cols])
        products = [
            lax.dot_general(
                key[:, lane : lane + LANES], value[:, lane : lane + LANES],
                (((0,), (0,)), ((), ())), preferred_element_type=F32,
            )
            for lane in range(0, channels, LANES)
        ]
        return products, jnp.sum(key.astype(F32), axis=0, keepdims=True)

    mine = slice(2, 2 + tile_rows)
    products, sums = summed(
        pairs[mine, :, 0:channels], pairs[mine, :, channels : 2 * channels]
    )

    def grouped_rows(index, carry):
        at = index * size
        more, sums = summed(
            aggregated(pairs, wide_agg, group[0], 0, at, size, channels),
            aggregated(pairs, wide_agg, group[1], channels, at, size, channels),
        )
        return [a + b for a, b in zip(carry[0], more)], carry[1] + sums

    more, more_sums = lax.fori_loop(
        0, tile_rows // size, grouped_rows,
        ([jnp.zeros((LANES, LANES), F32) for _ in products], jnp.zeros_like(sums)),
    )
    products = products + more
    sums = jnp.concatenate([sums, more_sums], axis=1)
    same = same_head(head_dim)
    summary = jnp.zeros((LANES, LANES), F32)
    key_sums = []
    for index, product in enumerate(products):
        product = jnp.where(same, product, 0.0)
        if index:
            product = pltpu.roll(product, index * head_dim, 1)
        summary = summary + product
        key_sums.append(sums[:, index * LANES : (index + 1) * LANES])
    key_sums.append(jnp.zeros((KEY_ROWS - len(products), LANES), F32))
    payload_out[0:LANES, :] = summary.astype(BF16)
    payload_out[LANES : LANES + KEY_ROWS, :] = jnp.concatenate(key_sums, axis=0).astype(BF16)
    store.wait()


def query_kernel(
    tile, section, mixed_in, qkv_weight, taps, groups, query, mixed_out,
    mixed, centre, weight, agg, group, wide_agg, sems,
):
    rows, width, channels = mixed.shape
    head = pl.ds(0, channels)
    loads = [
        pltpu.make_async_copy(mixed_in, mixed, sems.at[0]),
        pltpu.make_async_copy(qkv_weight.at[section, :, head], weight, sems.at[1]),
        pltpu.make_async_copy(taps.at[section, :, head], agg, sems.at[2]),
        pltpu.make_async_copy(groups.at[section, 0], group, sems.at[3]),
    ]
    for load in loads:
        load.start()
    for load in loads:
        load.wait()
    mixed_out[...] = mixed[2 : rows - 2]
    spread_taps(agg, wide_agg)
    for first, size in parted(rows, PARTS):
        value = jnp.dot(
            flat(mixed[first : first + size]), weight[...], preferred_element_type=F32
        )
        centre[first : first + size] = value.astype(BF16).reshape(size, width, channels)
    clear_outside(centre, (rows - tile[0]) // 2, tile[1])

    def query_rows(first, size):
        here = pl.ds(first, size)
        query[here, :, 0:channels] = jnp.maximum(centre[pl.ds(first + 2, size)], 0.0)
        grouped = aggregated(centre, wide_agg, group[...], 0, first, size, channels)
        query[here, :, channels : 2 * channels] = jnp.maximum(grouped, 0.0)

    by_groups(rows - 4, 5, query_rows)


def attend(
    mixed_ref, query_ref, payloads, weight, bias_in, held, head_dim, section, x_ref
):
    rows, width, channels = x_ref.shape
    bias, sem = held
    load = pltpu.make_async_copy(bias_in, bias, sem)
    load.start()
    same = same_head(head_dim)
    square = (LANES, LANES)
    diagonal = lax.broadcasted_iota(jnp.int32, square, 0) == lax.broadcasted_iota(
        jnp.int32, square, 1
    )
    ones = jnp.where(same, 1.0, 0.0).astype(BF16)
    nothing = jnp.zeros(square, BF16)
    payload = payloads[0][...].astype(F32)
    for part in payloads[1:]:
        payload = payload + part[...].astype(F32)
    packed = payload[0:LANES]
    count = 2 * channels // LANES
    summaries, sums = [], []
    for index in range(count):
        summary = packed if index == 0 else pltpu.roll(packed, LANES - index * head_dim, 1)
        summaries.append(jnp.where(same, summary, 0.0).astype(BF16))
        keys = payload[LANES + index : LANES + index + 1]
        keys = jnp.where(diagonal, keys, 0.0).astype(BF16)
        sums.append(jnp.dot(keys, ones, preferred_element_type=F32).astype(BF16))

    def paired(blocks, index):
        return jnp.concatenate(
            [
                jnp.concatenate([blocks[index], nothing], axis=1),
                jnp.concatenate([nothing, blocks[index + 1]], axis=1),
            ],
            axis=0,
        )

    summaries = [paired(summaries, index) for index in range(0, count, 2)]
    sums = [paired(sums, index) for index in range(0, count, 2)]
    step = 2 * LANES
    load.wait()

    def attend_rows(first, size):
        query = flat(query_ref[pl.ds(first, size)])
        parts = []
        for branch in range(count // 2):
            part = query[:, branch * step : (branch + 1) * step]
            numer = jnp.dot(part, summaries[branch], preferred_element_type=F32)
            denom = jnp.dot(part, sums[branch], preferred_element_type=F32) + 1e-6
            inverse = pl.reciprocal(denom, approx=True)
            inverse = inverse * (2.0 - denom * inverse)
            parts.append((numer * inverse).astype(BF16))
        value = jnp.dot(
            jnp.concatenate(parts, axis=1), weight[section], preferred_element_type=F32
        )
        value = value + bias[section : section + 1, :]
        value = value + flat(mixed_ref[pl.ds(first, size)]).astype(F32)
        x_ref[pl.ds(first, size)] = value.astype(BF16).reshape(size, width, channels)

    by_groups(rows, 5, attend_rows)


def tap(section, a, b):
    at = 32 * section + 5 * a + b
    return slice(at, at + 1)


def prepare_kernel(head_dim, qkv, agg, group, head, project_bias, output_bias, *refs):
    outs, made, taps, sems = refs[:6], refs[6:10], refs[10], refs[11]
    qkv_out, agg_out, group_out, head_out = made
    made = [*made, project_bias, output_bias]
    sections, channels, wide = qkv.shape
    half = 3 * LANES
    heads = LANES // head_dim
    src = lax.broadcasted_iota(jnp.int32, (half, LANES), 0)
    dst = lax.broadcasted_iota(jnp.int32, (half, LANES), 1)
    first = (dst // head_dim) * 3 * head_dim + dst % head_dim
    picks = [jnp.where(src == first + k * head_dim, 1.0, 0.0).astype(BF16) for k in range(3)]
    taps[...] = jnp.zeros(taps.shape, F32)
    for section in range(sections):
        for a in range(5):
            for b in range(5):
                taps[tap(section, a, b), :] = agg[a, b, section : section + 1, :]
    rest = taps[...]
    high = rest.astype(BF16)
    rest = rest - high.astype(F32)
    middle = rest.astype(BF16)
    low = (rest - middle.astype(F32)).astype(BF16)
    split = jnp.concatenate([high, middle, low], axis=0)
    count = taps.shape[0]
    weights = qkv[...].reshape(sections * channels, wide)
    for part in range(wide // half):
        here = slice(part * half, (part + 1) * half)
        for kind in range(3):
            to = kind * channels + part * LANES
            there = slice(to, to + LANES)
            value = jnp.dot(weights[:, here], picks[kind], preferred_element_type=F32)
            qkv_out[:, :, there] = value.astype(BF16).reshape(sections, channels, LANES)
            value = jnp.dot(split[:, here], picks[kind], preferred_element_type=F32)
            value = value[:count] + value[count : 2 * count] + value[2 * count :]
            agg_out[:, :, there] = value.reshape(sections, -1, LANES)
    row = lax.broadcasted_iota(jnp.int32, (head_dim, channels), 0)
    lane = lax.broadcasted_iota(jnp.int32, (head_dim, channels), 1)
    spread = jnp.where(lane % head_dim == row, 1.0, 0.0).astype(BF16)
    across = lax.broadcasted_iota(jnp.int32, (channels, channels), 0) // head_dim
    along = lax.broadcasted_iota(jnp.int32, (channels, channels), 1) // head_dim
    for section in range(sections):
        for kind in range(3):
            tall = [group[section, 3 * h + kind] for h in range(channels // head_dim)]
            value = jnp.dot(jnp.concatenate(tall, axis=0), spread, preferred_element_type=F32)
            group_out[section, kind] = jnp.where(across == along, value, 0.0).astype(BF16)
    head_out[...] = jnp.zeros(head_out.shape, BF16)
    for a in range(3):
        rows = [head[a, b] for b in range(3)] + [jnp.zeros((4, channels), BF16)]
        head_out[a, 0:16, :] = jnp.concatenate(rows, axis=0)
    stores = [pltpu.make_async_copy(made[i], outs[i], sems.at[i]) for i in range(6)]
    for store in stores:
        store.start()
    for store in stores:
        store.wait()


def first_kernel(tile, head_dim, own, row_0, row_1, *refs):
    weights, outs, scratch = refs[:9], refs[9:11], refs[11:]
    x_ref = scratch[0]
    rows, cols = tile
    below = REACH + rows
    even = lax.axis_index("row") & 1 == 0
    x_ref[REACH:below] = own[...]
    x_ref[pl.ds(jnp.where(even, below, 0), REACH)] = row_0[...]
    x_ref[pl.ds(jnp.where(even, 0, below), REACH)] = row_1[...]
    front(x_ref, weights, outs, scratch[1:], REACH, tile, head_dim, 0)


def second_kernel(tile, head_dim, mixed, query, payload, other, out_weight, out_bias, *refs):
    weights, outs, scratch = refs[:9], refs[9:11], refs[11:]
    x_ref = scratch[0]
    attend(
        mixed, query, (payload, other), out_weight, out_bias, scratch[1:3], head_dim, 0, x_ref
    )
    front(x_ref, weights, outs, scratch[3:], REACH - 3, tile, head_dim, 1)


def last_kernel(
    tile, head_dim, mixed, query, payload, other, out_weight, out_bias, head_weight, head_bias,
    map_out, boxes_out, x_ref, *held,
):
    rows, cols = tile
    width = cols + 2 * SIDE
    attend(
        mixed, query, (payload, other), out_weight, out_bias, held, head_dim, 1, x_ref
    )
    clear_outside(x_ref, 1, cols)
    map_out[...] = x_ref[1 : 1 + rows, 0:cols, :]
    total = None
    for a in range(3):
        part = lax.dot_general(
            flat(x_ref[a : a + rows]), head_weight[a], (((1,), (1,)), ((), ())),
            preferred_element_type=F32,
        )
        total = part if total is None else total + part
    total = total.reshape(rows, width, LANES)
    lane = lax.broadcasted_iota(jnp.int32, (width, LANES), 1) // 4
    shifted = [
        jnp.where(
            lane == 0,
            pltpu.roll(total[r], 1, 0),
            jnp.where(lane == 2, pltpu.roll(total[r], width - 1, 0), total[r]),
        )
        for r in range(rows)
    ]
    shifted = jnp.concatenate(shifted, axis=0)
    across = lax.broadcasted_iota(jnp.int32, (8, LANES), 0)
    along = lax.broadcasted_iota(jnp.int32, (8, LANES), 1)
    fold = jnp.where((along % 4 == across) & (along < 12), 1.0, 0.0)
    boxes = lax.dot_general(
        fold, shifted, (((1,), (1,)), ((), ())), precision=lax.Precision.HIGHEST,
        preferred_element_type=F32,
    )
    boxes = boxes[0:4] + head_bias[...]
    for r in range(rows):
        boxes_out[:, r, :] = boxes[:, r * width : r * width + cols]


def near():
    return pl.BlockSpec(memory_space=pltpu.VMEM)


def far():
    return pl.BlockSpec(memory_space=pltpu.HBM)


def factors(size):
    found = []
    while size > 1:
        found.append(next(p for p in range(2, size + 1) if size % p == 0))
        size //= found[-1]
    return found


def rounds_of(rows, cols, most):
    rounds, places = [], most + 1
    for axis, stride, size in (("row", 2, rows // 2), ("col", 1, cols)):
        for radix in factors(size):
            if places * radix > most:
                rounds.append([])
                places = 1
            rounds[-1].append((axis, stride, radix))
            places *= radix
            stride *= radix
    return rounds


def moved(place, digits, steps):
    place = dict(place)
    for (axis, stride, radix), step in zip(digits, steps):
        digit = (place[axis] // stride) % radix
        other = digit ^ step if radix == 2 else (digit + step) % radix
        place[axis] += (other - digit) * stride
    return place


def sum_by_permutes(value):
    rows, cols = lax.axis_size("row"), lax.axis_size("col")
    odd = lax.axis_index("row") & 1 == 1
    value = value.astype(F32) + lax.ppermute(
        value, "row", [(r, r + 1) for r in range(0, rows, 2)]
    ).astype(F32)
    for digits in rounds_of(rows, cols, 4):
        sent = value.astype(BF16)
        value = sent.astype(F32)
        for steps in itertools.product(*(range(radix) for _, _, radix in digits)):
            if not any(steps):
                continue
            pairs = []
            for r in range(1, rows, 2):
                for c in range(cols):
                    to = moved({"row": r, "col": c}, digits, steps)
                    pairs.append((r * cols + c, to["row"] * cols + to["col"]))
            value = value + lax.ppermute(sent, ("row", "col"), pairs).astype(F32)
    value = jnp.where(odd, value, 0.0).astype(BF16)
    return value, lax.ppermute(value, "row", [(r + 1, r) for r in range(0, rows, 2)])


def pair_exchange(value, axis, first):
    count = lax.axis_size(axis)
    pairs = []
    for i in range(first, count - 1, 2):
        pairs += [(i, i + 1), (i + 1, i)]
    return lax.ppermute(value, axis, pairs)


def local(
    features,
    expand_weight,
    expand_bias,
    depth_weight,
    depth_bias,
    project_weight,
    project_bias,
    qkv_weight,
    aggregate_depth,
    aggregate_group,
    output_weight,
    output_bias,
    head_weight,
    head_bias,
):
    rows, cols, channels = features.shape
    head_dim = aggregate_group.shape[2]
    heads = channels // head_dim
    width = cols + 2 * SIDE
    tile = (rows, cols)
    wide = expand_weight.shape[2]

    def edges(value, dim, size, odd):
        far = value.shape[dim] - size
        return [
            lax.dynamic_slice_in_dim(value, jnp.where(odd == at, far, 0), size, dim) for at in (0, 1)
        ]

    odd_row = lax.axis_index("row") & 1
    odd_col = lax.axis_index("col") & 1
    low, high = edges(features, 1, SIDE, odd_col)
    col_1 = pair_exchange(high, "col", 1)
    col_0 = pair_exchange(low, "col", 0)
    right = jnp.where(odd_col == 1, col_1, col_0)
    left = jnp.where(odd_col == 1, col_0, col_1)
    wide_rows = jnp.concatenate([features, right, left], axis=1)
    low, high = edges(wide_rows, 0, REACH, odd_row)
    row_1 = pair_exchange(high, "row", 1)
    row_0 = pair_exchange(low, "row", 0)

    aggregate_depth = aggregate_depth.transpose(1, 2, 0, 3)
    depth_weight = depth_weight.transpose(1, 2, 0, 3)
    params = pltpu.CompilerParams(vmem_limit_bytes=24 * 2**20)
    made = [
        jax.ShapeDtypeStruct(qkv_weight.shape, BF16),
        jax.ShapeDtypeStruct((SECTIONS, 32, 3 * channels), F32),
        jax.ShapeDtypeStruct((SECTIONS, 3, channels, channels), BF16),
        jax.ShapeDtypeStruct((3, LANES, channels), BF16),
    ]
    biases = [jax.ShapeDtypeStruct(array.shape, F32) for array in (project_bias, output_bias)]
    qkv_weight, taps, group, head_weight, project_bias, output_bias = pl.pallas_call(
        functools.partial(prepare_kernel, head_dim),
        out_shape=made + biases,
        grid=(1,),
        in_specs=[near()] * 6,
        out_specs=[far()] * 6,
        scratch_shapes=[pltpu.VMEM(array.shape, array.dtype) for array in made]
        + [pltpu.VMEM((32 * SECTIONS, 3 * channels), F32), pltpu.SemaphoreType.DMA((6,))],
        compiler_params=params,
        cost_estimate=pl.CostEstimate(
            flops=2 * 10**9, bytes_accessed=4 * 10**6, transcendentals=0
        ),
        name="prepare",
    )(qkv_weight, aggregate_depth, aggregate_group, head_weight, project_bias, output_bias)

    weights = [
        expand_weight, expand_bias, depth_weight, depth_bias, project_weight, project_bias,
        qkv_weight, taps, group,
    ]
    weight_specs = [near()] * 5 + [far()] * 4

    def outs_of(count):
        return [
            jax.ShapeDtypeStruct((count, width, channels), BF16),
            jax.ShapeDtypeStruct((LANES + KEY_ROWS, LANES), BF16),
        ]

    def front_scratch(count):
        return [
            pltpu.VMEM((count, width, 256), BF16),
            pltpu.VMEM((count, width, 256), BF16),
            pltpu.VMEM(((count - 2) * width, channels), F32),
            pltpu.VMEM((count - 2, width, channels), BF16),
            pltpu.VMEM((rows + 4, width, 2 * channels), BF16),
            pltpu.VMEM((9, TILE, expand_weight.shape[2]), BF16),
            pltpu.VMEM((25, TILE, 2 * channels), BF16),
            pltpu.VMEM(project_bias.shape, F32),
            pltpu.VMEM((channels, 2 * channels), BF16),
            pltpu.VMEM((32, 2 * channels), F32),
            pltpu.VMEM((2, channels, channels), BF16),
            pltpu.SemaphoreType.DMA((5,)),
        ]

    def attend_scratch(count):
        return [
            pltpu.VMEM((count, width, channels), BF16),
            pltpu.VMEM(output_bias.shape, F32),
            pltpu.SemaphoreType.DMA,
        ]

    def queries(mixed, section):
        count = mixed.shape[0]
        units = (count - 4) * width * channels
        return pl.pallas_call(
            functools.partial(query_kernel, tile, section),
            out_shape=[
                jax.ShapeDtypeStruct((count - 4, width, 2 * channels), BF16),
                jax.ShapeDtypeStruct((count - 4, width, channels), BF16),
            ],
            grid=(1,),
            in_specs=[far()] * 4,
            out_specs=[near()] * 2,
            scratch_shapes=[
                pltpu.VMEM((count, width, channels), BF16),
                pltpu.VMEM((count, width, channels), BF16),
                pltpu.VMEM((channels, channels), BF16),
                pltpu.VMEM((32, channels), F32),
                pltpu.VMEM((channels, channels), BF16),
                pltpu.VMEM((25, TILE, channels), BF16),
                pltpu.SemaphoreType.DMA((4,)),
            ],
            compiler_params=params,
            cost_estimate=pl.CostEstimate(
                flops=8 * units * channels, bytes_accessed=8 * units, transcendentals=0
            ),
            name="queries",
        )(mixed, qkv_weight, taps, group)

    first_rows = rows + 2 * REACH
    mixed, payload = pl.pallas_call(
        functools.partial(first_kernel, tile, head_dim),
        out_shape=outs_of(first_rows - 2),
        grid=(1,),
        in_specs=[near()] * 3 + weight_specs,
        out_specs=[far(), near()],
        scratch_shapes=[pltpu.VMEM((first_rows, width, channels), BF16)]
        + front_scratch(first_rows),
        compiler_params=params,
        name="first",
    )(wide_rows, row_0, row_1, *weights)
    query, mixed = queries(mixed, 0)
    payload, other = sum_by_permutes(payload)

    second_rows = first_rows - 6
    mixed, payload = pl.pallas_call(
        functools.partial(second_kernel, tile, head_dim),
        out_shape=outs_of(second_rows - 2),
        grid=(1,),
        in_specs=[near()] * 5 + [far()] + weight_specs,
        out_specs=[far(), near()],
        scratch_shapes=attend_scratch(second_rows) + front_scratch(second_rows),
        compiler_params=params,
        name="second",
    )(mixed, query, payload, other, output_weight, output_bias, *weights)
    query, mixed = queries(mixed, 1)
    payload, other = sum_by_permutes(payload)

    return pl.pallas_call(
        functools.partial(last_kernel, tile, head_dim),
        out_shape=[
            jax.ShapeDtypeStruct((rows, cols, channels), BF16),
            jax.ShapeDtypeStruct((4, rows, cols), F32),
        ],
        grid=(1,),
        in_specs=[near()] * 5 + [far()] + [near()] * 2,
        out_specs=[near()] * 2,
        scratch_shapes=attend_scratch(rows + 2),
        compiler_params=params,
        name="last",
    )(
        mixed, query, payload, other, output_weight, output_bias, head_weight,
        head_bias.reshape(4, 1),
    )


def solution(mesh):
    return jax.shard_map(
        local,
        mesh=mesh,
        in_specs=(P("row", "col", None),) + (P(),) * 13,
        out_specs=(P("row", "col", None), P(None, "row", "col")),
        check_vma=False,
    )
```

```python
import functools

import jax
import jax.numpy as jnp
from jax import lax
from jax.experimental import pallas as pl
from jax.experimental.pallas import tpu as pltpu
from jax.sharding import PartitionSpec as P

SECTIONS = 2
LANES = 128
SIDE = 8
REACH = 7
KEY_ROWS = 16
TILE = 16
PARTS = 2
F32 = jnp.float32
BF16 = jnp.bfloat16


def six_hard_swish(value, bound=6.0):
    return value * jnp.minimum(jnp.maximum(value + 3.0, 0.0), bound)


def parted(count, parts):
    cuts = [count * k // parts for k in range(parts + 1)]
    return [(a, b - a) for a, b in zip(cuts, cuts[1:]) if b > a]


def group_size(count, most):
    return next(n for n in range(min(most, count), 0, -1) if count % n == 0)


def by_groups(count, most, body):
    size = group_size(count, most)

    def group(index, carry):
        body(index * size, size)
        return carry

    lax.fori_loop(0, count // size, group, 0)


def clear_outside(ref, halo, cols):
    rows = ref.shape[0]
    row, col = lax.axis_index("row"), lax.axis_index("col")

    @pl.when(row == 0)
    def _():
        ref[0:halo] = jnp.zeros((halo,) + ref.shape[1:], ref.dtype)

    @pl.when(row == lax.axis_size("row") - 1)
    def _():
        ref[rows - halo : rows] = jnp.zeros((halo,) + ref.shape[1:], ref.dtype)

    @pl.when(col == 0)
    def _():
        ref[:, cols + SIDE : cols + 2 * SIDE, :] = jnp.zeros((rows, SIDE, ref.shape[2]), ref.dtype)

    @pl.when(col == lax.axis_size("col") - 1)
    def _():
        ref[:, cols : cols + SIDE, :] = jnp.zeros((rows, SIDE, ref.shape[2]), ref.dtype)


def set_bounds(bounds, cols):
    shape = bounds.shape[1:]
    column = lax.broadcasted_iota(jnp.int32, shape, 0)
    row, col = lax.axis_index("row"), lax.axis_index("col")
    start = jnp.where(col == lax.axis_size("col") - 1, cols, cols + SIDE)
    stop = jnp.where(col == 0, cols + 2 * SIDE, cols + SIDE)
    level = jnp.where((column >= start) & (column < stop), 0.0, 6.0)
    bounds[0] = jnp.where(row == 0, 0.0, level).astype(BF16)
    bounds[1] = level.astype(BF16)
    bounds[2] = jnp.where(row == lax.axis_size("row") - 1, 0.0, level).astype(BF16)


def flat(value):
    return value.reshape(-1, value.shape[-1])


def same_head(head_dim):
    across = lax.broadcasted_iota(jnp.int32, (LANES, LANES), 0) // head_dim
    along = lax.broadcasted_iota(jnp.int32, (LANES, LANES), 1) // head_dim
    return across == along


def depthwise_row(rows, taps, size, width):
    rows = [row.reshape(width // TILE, TILE, LANES) for row in rows]
    total = None
    for b in range(size):
        part = None
        for a in range(size):
            term = rows[a] * taps(a, b)[None]
            part = term if part is None else part + term
        part = part.reshape(width, LANES).astype(F32)
        if b != size // 2:
            part = pltpu.roll(part, (size // 2 - b) % width, 0)
        total = part if total is None else total + part
    return total


def spread_taps(agg, wide_agg):
    for index in range(25):
        taps = agg[index : index + 1, :]
        wide_agg[index] = jnp.broadcast_to(taps, (TILE, taps.shape[1])).astype(BF16)


def aggregated(source, wide_agg, group, low, first, size, channels):
    width = source.shape[1]
    scaled = []
    for r in range(size):
        lanes = []
        for lane in range(low, low + channels, LANES):
            here = slice(lane, lane + LANES)
            value = depthwise_row(
                [source[first + r + a, :, here] for a in range(5)],
                lambda a, b: wide_agg[5 * a + b, :, here], 5, width,
            )
            lanes.append(value.astype(BF16))
        scaled.append(jnp.concatenate(lanes, axis=1))
    value = jnp.dot(jnp.concatenate(scaled, axis=0), group, preferred_element_type=F32)
    return value.astype(BF16).reshape(size, width, channels)


def front(x_ref, weights, outs, scratch, halo, tile, head_dim, section):
    expand, expand_bias, depth, depth_bias, project = weights[:5]
    mixed_out, payload_out = outs
    (
        hidden, spread, bounds, mixed, pairs, wide_depth, wide_agg,
        project_bias, pair_weight, agg, group, sems,
    ) = scratch
    channels = x_ref.shape[2]
    tail = pl.ds(channels, 2 * channels)
    loads = [
        pltpu.make_async_copy(weights[5], project_bias, sems.at[0]),
        pltpu.make_async_copy(weights[6].at[section, :, tail], pair_weight, sems.at[1]),
        pltpu.make_async_copy(weights[7].at[section, :, tail], agg, sems.at[2]),
        pltpu.make_async_copy(weights[8].at[section, pl.ds(1, 2)], group, sems.at[3]),
    ]
    for load in loads:
        load.start()
    rows, width, channels = x_ref.shape
    tile_rows, tile_cols = tile
    inner = rows - 2
    chunk = bounds.shape[2]
    chunks = hidden.shape[2] // chunk
    this = slice(section, section + 1)
    for index in range(9):
        taps = depth[index // 3, index % 3, section : section + 1, :] * (1.0 / 6.0)
        wide_depth[index] = jnp.broadcast_to(taps, (TILE, taps.shape[1])).astype(BF16)
    set_bounds(bounds, tile_cols)

    def expand_rows(at, first, size):
        value = jnp.dot(
            flat(x_ref[first : first + size]), expand[section, :, at : at + chunk],
            preferred_element_type=F32,
        )
        value = (value + expand_bias[this, at : at + chunk]).astype(BF16)
        for r in range(size):
            which = 0 if first + r < halo else 2 if first + r >= rows - halo else 1
            row = value[r * width : (r + 1) * width]
            hidden[first + r, :, at : at + chunk] = six_hard_swish(row, bounds[which])

    def spread_rows(at, first, size):
        for r in range(first, first + size):
            for lane in range(at, at + chunk, LANES):
                here = slice(lane, lane + LANES)
                value = depthwise_row(
                    [hidden[r + a, :, here] for a in range(3)],
                    lambda a, b: wide_depth[3 * a + b, :, here], 3, width,
                )
                value = (value + depth_bias[this, here]).astype(BF16)
                spread[r, :, here] = six_hard_swish(value)

    for first, size in parted(rows, PARTS):
        expand_rows(0, first, size)
    for at in range(0, chunks * chunk, chunk):
        for (first, size), (from_row, count) in zip(parted(inner, PARTS), parted(rows, PARTS)):
            if at + chunk < chunks * chunk:
                expand_rows(at + chunk, from_row, count)
            spread_rows(at, first, size)
    loads[0].wait()
    for first, size in parted(inner, PARTS):
        value = jnp.dot(
            flat(spread[first : first + size]), project[section], preferred_element_type=F32
        )
        value = value * (1.0 / 6.0) + project_bias[this, :]
        value = value + flat(x_ref[first + 1 : first + 1 + size]).astype(F32)
        mixed[first : first + size] = value.astype(BF16).reshape(size, width, channels)
    store = pltpu.make_async_copy(mixed, mixed_out, sems.at[4])
    store.start()
    for load in loads[1:]:
        load.wait()
    spread_taps(agg, wide_agg)
    around = halo - 1
    first_pair = around - 2
    count = tile_rows + 4
    for first, size in parted(count, PARTS - 1):
        at = first_pair + first
        value = jnp.dot(
            flat(mixed[at : at + size]), pair_weight[...], preferred_element_type=F32
        )
        pairs[first : first + size] = value.astype(BF16).reshape(size, width, 2 * channels)
    clear_outside(pairs, 2, tile_cols)
    size = group_size(tile_rows, 4)

    def summed(key, value):
        key = jnp.maximum(flat(key[:, 0:tile_cols]), 0.0)
        value = flat(value[:, 0:tile_cols])
        products = [
            lax.dot_general(
                key[:, lane : lane + LANES], value[:, lane : lane + LANES],
                (((0,), (0,)), ((), ())), preferred_element_type=F32,
            )
            for lane in range(0, channels, LANES)
        ]
        return products, jnp.sum(key.astype(F32), axis=0, keepdims=True)

    mine = slice(2, 2 + tile_rows)
    products, sums = summed(
        pairs[mine, :, 0:channels], pairs[mine, :, channels : 2 * channels]
    )

    def grouped_rows(index, carry):
        at = index * size
        more, sums = summed(
            aggregated(pairs, wide_agg, group[0], 0, at, size, channels),
            aggregated(pairs, wide_agg, group[1], channels, at, size, channels),
        )
        return [a + b for a, b in zip(carry[0], more)], carry[1] + sums

    more, more_sums = lax.fori_loop(
        0, tile_rows // size, grouped_rows,
        ([jnp.zeros((LANES, LANES), F32) for _ in products], jnp.zeros_like(sums)),
    )
    products = products + more
    sums = jnp.concatenate([sums, more_sums], axis=1)
    same = same_head(head_dim)
    summary = jnp.zeros((LANES, LANES), F32)
    key_sums = []
    for index, product in enumerate(products):
        product = jnp.where(same, product, 0.0)
        if index:
            product = pltpu.roll(product, index * head_dim, 1)
        summary = summary + product
        key_sums.append(sums[:, index * LANES : (index + 1) * LANES])
    key_sums.append(jnp.zeros((KEY_ROWS - len(products), LANES), F32))
    payload_out[0:LANES, :] = summary.astype(BF16)
    payload_out[LANES : LANES + KEY_ROWS, :] = jnp.concatenate(key_sums, axis=0).astype(BF16)
    store.wait()


def query_kernel(
    tile, section, mixed_in, qkv_weight, taps, groups, query, mixed_out,
    mixed, centre, weight, agg, group, wide_agg, sems,
):
    rows, width, channels = mixed.shape
    head = pl.ds(0, channels)
    loads = [
        pltpu.make_async_copy(mixed_in, mixed, sems.at[0]),
        pltpu.make_async_copy(qkv_weight.at[section, :, head], weight, sems.at[1]),
        pltpu.make_async_copy(taps.at[section, :, head], agg, sems.at[2]),
        pltpu.make_async_copy(groups.at[section, 0], group, sems.at[3]),
    ]
    for load in loads:
        load.start()
    for load in loads:
        load.wait()
    mixed_out[...] = mixed[2 : rows - 2]
    spread_taps(agg, wide_agg)
    for first, size in parted(rows, PARTS):
        value = jnp.dot(
            flat(mixed[first : first + size]), weight[...], preferred_element_type=F32
        )
        centre[first : first + size] = value.astype(BF16).reshape(size, width, channels)
    clear_outside(centre, (rows - tile[0]) // 2, tile[1])

    def query_rows(first, size):
        here = pl.ds(first, size)
        query[here, :, 0:channels] = jnp.maximum(centre[pl.ds(first + 2, size)], 0.0)
        grouped = aggregated(centre, wide_agg, group[...], 0, first, size, channels)
        query[here, :, channels : 2 * channels] = jnp.maximum(grouped, 0.0)

    by_groups(rows - 4, 5, query_rows)


def attend(
    mixed_ref, query_ref, payloads, weight, bias_in, held, head_dim, section, x_ref
):
    rows, width, channels = x_ref.shape
    bias, sem = held
    load = pltpu.make_async_copy(bias_in, bias, sem)
    load.start()
    same = same_head(head_dim)
    square = (LANES, LANES)
    diagonal = lax.broadcasted_iota(jnp.int32, square, 0) == lax.broadcasted_iota(
        jnp.int32, square, 1
    )
    ones = jnp.where(same, 1.0, 0.0).astype(BF16)
    nothing = jnp.zeros(square, BF16)
    payload = payloads[0][...].astype(F32)
    for part in payloads[1:]:
        payload = payload + part[...].astype(F32)
    packed = payload[0:LANES]
    count = 2 * channels // LANES
    summaries, sums = [], []
    for index in range(count):
        summary = packed if index == 0 else pltpu.roll(packed, LANES - index * head_dim, 1)
        summaries.append(jnp.where(same, summary, 0.0).astype(BF16))
        keys = payload[LANES + index : LANES + index + 1]
        keys = jnp.where(diagonal, keys, 0.0).astype(BF16)
        sums.append(jnp.dot(keys, ones, preferred_element_type=F32).astype(BF16))

    def paired(blocks, index):
        return jnp.concatenate(
            [
                jnp.concatenate([blocks[index], nothing], axis=1),
                jnp.concatenate([nothing, blocks[index + 1]], axis=1),
            ],
            axis=0,
        )

    summaries = [paired(summaries, index) for index in range(0, count, 2)]
    sums = [paired(sums, index) for index in range(0, count, 2)]
    step = 2 * LANES
    load.wait()

    def attend_rows(first, size):
        query = flat(query_ref[pl.ds(first, size)])
        parts = []
        for branch in range(count // 2):
            part = query[:, branch * step : (branch + 1) * step]
            numer = jnp.dot(part, summaries[branch], preferred_element_type=F32)
            denom = jnp.dot(part, sums[branch], preferred_element_type=F32) + 1e-6
            inverse = pl.reciprocal(denom, approx=True)
            inverse = inverse * (2.0 - denom * inverse)
            parts.append((numer * inverse).astype(BF16))
        value = jnp.dot(
            jnp.concatenate(parts, axis=1), weight[section], preferred_element_type=F32
        )
        value = value + bias[section : section + 1, :]
        value = value + flat(mixed_ref[pl.ds(first, size)]).astype(F32)
        x_ref[pl.ds(first, size)] = value.astype(BF16).reshape(size, width, channels)

    by_groups(rows, 5, attend_rows)


def tap(section, a, b):
    at = 32 * section + 5 * a + b
    return slice(at, at + 1)


def prepare_kernel(head_dim, qkv, agg, group, head, project_bias, output_bias, *refs):
    outs, made, taps, sems = refs[:6], refs[6:10], refs[10], refs[11]
    qkv_out, agg_out, group_out, head_out = made
    made = [*made, project_bias, output_bias]
    sections, channels, wide = qkv.shape
    half = 3 * LANES
    heads = LANES // head_dim
    src = lax.broadcasted_iota(jnp.int32, (half, LANES), 0)
    dst = lax.broadcasted_iota(jnp.int32, (half, LANES), 1)
    first = (dst // head_dim) * 3 * head_dim + dst % head_dim
    picks = [jnp.where(src == first + k * head_dim, 1.0, 0.0).astype(BF16) for k in range(3)]
    taps[...] = jnp.zeros(taps.shape, F32)
    for section in range(sections):
        for a in range(5):
            for b in range(5):
                taps[tap(section, a, b), :] = agg[a, b, section : section + 1, :]
    rest = taps[...]
    high = rest.astype(BF16)
    rest = rest - high.astype(F32)
    middle = rest.astype(BF16)
    low = (rest - middle.astype(F32)).astype(BF16)
    split = jnp.concatenate([high, middle, low], axis=0)
    count = taps.shape[0]
    weights = qkv[...].reshape(sections * channels, wide)
    for part in range(wide // half):
        here = slice(part * half, (part + 1) * half)
        for kind in range(3):
            to = kind * channels + part * LANES
            there = slice(to, to + LANES)
            value = jnp.dot(weights[:, here], picks[kind], preferred_element_type=F32)
            qkv_out[:, :, there] = value.astype(BF16).reshape(sections, channels, LANES)
            value = jnp.dot(split[:, here], picks[kind], preferred_element_type=F32)
            value = value[:count] + value[count : 2 * count] + value[2 * count :]
            agg_out[:, :, there] = value.reshape(sections, -1, LANES)
    row = lax.broadcasted_iota(jnp.int32, (head_dim, channels), 0)
    lane = lax.broadcasted_iota(jnp.int32, (head_dim, channels), 1)
    spread = jnp.where(lane % head_dim == row, 1.0, 0.0).astype(BF16)
    across = lax.broadcasted_iota(jnp.int32, (channels, channels), 0) // head_dim
    along = lax.broadcasted_iota(jnp.int32, (channels, channels), 1) // head_dim
    for section in range(sections):
        for kind in range(3):
            tall = [group[section, 3 * h + kind] for h in range(channels // head_dim)]
            value = jnp.dot(jnp.concatenate(tall, axis=0), spread, preferred_element_type=F32)
            group_out[section, kind] = jnp.where(across == along, value, 0.0).astype(BF16)
    head_out[...] = jnp.zeros(head_out.shape, BF16)
    for a in range(3):
        rows = [head[a, b] for b in range(3)] + [jnp.zeros((4, channels), BF16)]
        head_out[a, 0:16, :] = jnp.concatenate(rows, axis=0)
    stores = [pltpu.make_async_copy(made[i], outs[i], sems.at[i]) for i in range(6)]
    for store in stores:
        store.start()
    for store in stores:
        store.wait()


def first_kernel(tile, head_dim, own, row_0, row_1, *refs):
    weights, outs, scratch = refs[:9], refs[9:11], refs[11:]
    x_ref = scratch[0]
    rows, cols = tile
    below = REACH + rows
    even = lax.axis_index("row") & 1 == 0
    x_ref[REACH:below] = own[...]
    x_ref[pl.ds(jnp.where(even, below, 0), REACH)] = row_0[...]
    x_ref[pl.ds(jnp.where(even, 0, below), REACH)] = row_1[...]
    front(x_ref, weights, outs, scratch[1:], REACH, tile, head_dim, 0)


def second_kernel(tile, head_dim, mixed, query, payload, other, out_weight, out_bias, *refs):
    weights, outs, scratch = refs[:9], refs[9:11], refs[11:]
    x_ref = scratch[0]
    attend(
        mixed, query, (payload, other), out_weight, out_bias, scratch[1:3], head_dim, 0, x_ref
    )
    front(x_ref, weights, outs, scratch[3:], REACH - 3, tile, head_dim, 1)


def last_kernel(
    tile, head_dim, mixed, query, payload, other, out_weight, out_bias, head_weight, head_bias,
    map_out, boxes_out, x_ref, *held,
):
    rows, cols = tile
    width = cols + 2 * SIDE
    attend(
        mixed, query, (payload, other), out_weight, out_bias, held, head_dim, 1, x_ref
    )
    clear_outside(x_ref, 1, cols)
    map_out[...] = x_ref[1 : 1 + rows, 0:cols, :]
    total = None
    for a in range(3):
        part = lax.dot_general(
            flat(x_ref[a : a + rows]), head_weight[a], (((1,), (1,)), ((), ())),
            preferred_element_type=F32,
        )
        total = part if total is None else total + part
    total = total.reshape(rows, width, LANES)
    lane = lax.broadcasted_iota(jnp.int32, (width, LANES), 1) // 4
    shifted = [
        jnp.where(
            lane == 0,
            pltpu.roll(total[r], 1, 0),
            jnp.where(lane == 2, pltpu.roll(total[r], width - 1, 0), total[r]),
        )
        for r in range(rows)
    ]
    shifted = jnp.concatenate(shifted, axis=0)
    across = lax.broadcasted_iota(jnp.int32, (8, LANES), 0)
    along = lax.broadcasted_iota(jnp.int32, (8, LANES), 1)
    fold = jnp.where((along % 4 == across) & (along < 12), 1.0, 0.0)
    boxes = lax.dot_general(
        fold, shifted, (((1,), (1,)), ((), ())), precision=lax.Precision.HIGHEST,
        preferred_element_type=F32,
    )
    boxes = boxes[0:4] + head_bias[...]
    for r in range(rows):
        boxes_out[:, r, :] = boxes[:, r * width : r * width + cols]


def near():
    return pl.BlockSpec(memory_space=pltpu.VMEM)


def far():
    return pl.BlockSpec(memory_space=pltpu.HBM)


def digits(size, most):
    radices = []
    while size > 1:
        radix = next((r for r in range(min(most, size), 1, -1) if size % r == 0), size)
        radices.append(radix)
        size //= radix
    return radices


def partner(i, stride, radix, step):
    digit = (i // stride) % radix
    other = digit ^ step if radix & (radix - 1) == 0 else (digit + step) % radix
    return i + (other - digit) * stride


def sum_by_permutes(value):
    rounds = []
    for axis in ("row", "col"):
        stride = 1
        for radix in digits(lax.axis_size(axis), 4):
            rounds.append((axis, stride, radix))
            stride *= radix
    for axis, stride, radix in rounds:
        count = lax.axis_size(axis)
        others = [
            lax.ppermute(value, axis, [(i, partner(i, stride, radix, k)) for i in range(count)])
            for k in range(1, radix)
        ]
        if (axis, stride, radix) == rounds[-1] and radix == 2:
            return value, others[0]
        total = value.astype(F32)
        for other in others:
            total = total + other.astype(F32)
        value = total.astype(BF16)
    return value, jnp.zeros_like(value)


def digits(size, most):
    radices = []
    while size > 1:
        radix = next((r for r in range(min(most, size), 1, -1) if size % r == 0), size)
        radices.append(radix)
        size //= radix
    return radices


def pair_exchange(value, axis, first):
    count = lax.axis_size(axis)
    pairs = []
    for i in range(first, count - 1, 2):
        pairs += [(i, i + 1), (i + 1, i)]
    return lax.ppermute(value, axis, pairs)


def local(
    features,
    expand_weight,
    expand_bias,
    depth_weight,
    depth_bias,
    project_weight,
    project_bias,
    qkv_weight,
    aggregate_depth,
    aggregate_group,
    output_weight,
    output_bias,
    head_weight,
    head_bias,
):
    rows, cols, channels = features.shape
    head_dim = aggregate_group.shape[2]
    heads = channels // head_dim
    width = cols + 2 * SIDE
    tile = (rows, cols)
    wide = expand_weight.shape[2]

    def edges(value, dim, size, odd):
        far = value.shape[dim] - size
        return [
            lax.dynamic_slice_in_dim(value, jnp.where(odd == at, far, 0), size, dim) for at in (0, 1)
        ]

    odd_row = lax.axis_index("row") & 1
    odd_col = lax.axis_index("col") & 1
    low, high = edges(features, 1, SIDE, odd_col)
    col_1 = pair_exchange(high, "col", 1)
    col_0 = pair_exchange(low, "col", 0)
    right = jnp.where(odd_col == 1, col_1, col_0)
    left = jnp.where(odd_col == 1, col_0, col_1)
    wide_rows = jnp.concatenate([features, right, left], axis=1)
    low, high = edges(wide_rows, 0, REACH, odd_row)
    row_1 = pair_exchange(high, "row", 1)
    row_0 = pair_exchange(low, "row", 0)

    aggregate_depth = aggregate_depth.transpose(1, 2, 0, 3)
    depth_weight = depth_weight.transpose(1, 2, 0, 3)
    params = pltpu.CompilerParams(vmem_limit_bytes=24 * 2**20)
    made = [
        jax.ShapeDtypeStruct(qkv_weight.shape, BF16),
        jax.ShapeDtypeStruct((SECTIONS, 32, 3 * channels), F32),
        jax.ShapeDtypeStruct((SECTIONS, 3, channels, channels), BF16),
        jax.ShapeDtypeStruct((3, LANES, channels), BF16),
    ]
    biases = [jax.ShapeDtypeStruct(array.shape, F32) for array in (project_bias, output_bias)]
    qkv_weight, taps, group, head_weight, project_bias, output_bias = pl.pallas_call(
        functools.partial(prepare_kernel, head_dim),
        out_shape=made + biases,
        grid=(1,),
        in_specs=[near()] * 6,
        out_specs=[far()] * 6,
        scratch_shapes=[pltpu.VMEM(array.shape, array.dtype) for array in made]
        + [pltpu.VMEM((32 * SECTIONS, 3 * channels), F32), pltpu.SemaphoreType.DMA((6,))],
        compiler_params=params,
        cost_estimate=pl.CostEstimate(
            flops=2 * 10**9, bytes_accessed=4 * 10**6, transcendentals=0
        ),
        name="prepare",
    )(qkv_weight, aggregate_depth, aggregate_group, head_weight, project_bias, output_bias)

    weights = [
        expand_weight, expand_bias, depth_weight, depth_bias, project_weight, project_bias,
        qkv_weight, taps, group,
    ]
    weight_specs = [near()] * 5 + [far()] * 4

    def outs_of(count):
        return [
            jax.ShapeDtypeStruct((count, width, channels), BF16),
            jax.ShapeDtypeStruct((LANES + KEY_ROWS, LANES), BF16),
        ]

    def front_scratch(count):
        return [
            pltpu.VMEM((count, width, expand_weight.shape[2]), BF16),
            pltpu.VMEM((count - 2, width, expand_weight.shape[2]), BF16),
            pltpu.VMEM((3, width, 256), BF16),
            pltpu.VMEM((count - 2, width, channels), BF16),
            pltpu.VMEM((rows + 4, width, 2 * channels), BF16),
            pltpu.VMEM((9, TILE, expand_weight.shape[2]), BF16),
            pltpu.VMEM((25, TILE, 2 * channels), BF16),
            pltpu.VMEM(project_bias.shape, F32),
            pltpu.VMEM((channels, 2 * channels), BF16),
            pltpu.VMEM((32, 2 * channels), F32),
            pltpu.VMEM((2, channels, channels), BF16),
            pltpu.SemaphoreType.DMA((5,)),
        ]

    def attend_scratch(count):
        return [
            pltpu.VMEM((count, width, channels), BF16),
            pltpu.VMEM(output_bias.shape, F32),
            pltpu.SemaphoreType.DMA,
        ]

    def queries(mixed, section):
        count = mixed.shape[0]
        units = (count - 4) * width * channels
        return pl.pallas_call(
            functools.partial(query_kernel, tile, section),
            out_shape=[
                jax.ShapeDtypeStruct((count - 4, width, 2 * channels), BF16),
                jax.ShapeDtypeStruct((count - 4, width, channels), BF16),
            ],
            grid=(1,),
            in_specs=[far()] * 4,
            out_specs=[near()] * 2,
            scratch_shapes=[
                pltpu.VMEM((count, width, channels), BF16),
                pltpu.VMEM((count, width, channels), BF16),
                pltpu.VMEM((channels, channels), BF16),
                pltpu.VMEM((32, channels), F32),
                pltpu.VMEM((channels, channels), BF16),
                pltpu.VMEM((25, TILE, channels), BF16),
                pltpu.SemaphoreType.DMA((4,)),
            ],
            compiler_params=params,
            cost_estimate=pl.CostEstimate(
                flops=8 * units * channels, bytes_accessed=8 * units, transcendentals=0
            ),
            name="queries",
        )(mixed, qkv_weight, taps, group)

    first_rows = rows + 2 * REACH
    mixed, payload = pl.pallas_call(
        functools.partial(first_kernel, tile, head_dim),
        out_shape=outs_of(first_rows - 2),
        grid=(1,),
        in_specs=[near()] * 3 + weight_specs,
        out_specs=[far(), near()],
        scratch_shapes=[pltpu.VMEM((first_rows, width, channels), BF16)]
        + front_scratch(first_rows),
        compiler_params=params,
        name="first",
    )(wide_rows, row_0, row_1, *weights)
    query, mixed = queries(mixed, 0)
    payload, other = sum_by_permutes(payload)

    second_rows = first_rows - 6
    mixed, payload = pl.pallas_call(
        functools.partial(second_kernel, tile, head_dim),
        out_shape=outs_of(second_rows - 2),
        grid=(1,),
        in_specs=[near()] * 5 + [far()] + weight_specs,
        out_specs=[far(), near()],
        scratch_shapes=attend_scratch(second_rows) + front_scratch(second_rows),
        compiler_params=params,
        name="second",
    )(mixed, query, payload, other, output_weight, output_bias, *weights)
    query, mixed = queries(mixed, 1)
    payload, other = sum_by_permutes(payload)

    return pl.pallas_call(
        functools.partial(last_kernel, tile, head_dim),
        out_shape=[
            jax.ShapeDtypeStruct((rows, cols, channels), BF16),
            jax.ShapeDtypeStruct((4, rows, cols), F32),
        ],
        grid=(1,),
        in_specs=[near()] * 5 + [far()] + [near()] * 2,
        out_specs=[near()] * 2,
        scratch_shapes=attend_scratch(rows + 2),
        compiler_params=params,
        name="last",
    )(
        mixed, query, payload, other, output_weight, output_bias, head_weight,
        head_bias.reshape(4, 1),
    )


def solution(mesh):
    return jax.shard_map(
        local,
        mesh=mesh,
        in_specs=(P("row", "col", None),) + (P(),) * 13,
        out_specs=(P("row", "col", None), P(None, "row", "col")),
        check_vma=False,
    )
```

```python
import functools

import jax
import jax.numpy as jnp
from jax import lax
from jax.experimental import pallas as pl
from jax.experimental.pallas import tpu as pltpu
from jax.sharding import PartitionSpec as P

SECTIONS = 2
LANES = 128
SIDE = 8
REACH = 7
KEY_ROWS = 16
TILE = 16
PARTS = 2
F32 = jnp.float32
BF16 = jnp.bfloat16


def six_hard_swish(value, bound=6.0):
    return value * jnp.minimum(jnp.maximum(value + 3.0, 0.0), bound)


def group_size(count, most):
    return next(n for n in range(min(most, count), 0, -1) if count % n == 0)


def by_groups(count, most, body):
    size = group_size(count, most)

    def group(index, carry):
        body(index * size, size)
        return carry

    lax.fori_loop(0, count // size, group, 0)


def clear_outside(ref, halo, cols):
    rows = ref.shape[0]
    row, col = lax.axis_index("row"), lax.axis_index("col")

    @pl.when(row == 0)
    def _():
        ref[0:halo] = jnp.zeros((halo,) + ref.shape[1:], ref.dtype)

    @pl.when(row == lax.axis_size("row") - 1)
    def _():
        ref[rows - halo : rows] = jnp.zeros((halo,) + ref.shape[1:], ref.dtype)

    @pl.when(col == 0)
    def _():
        ref[:, cols + SIDE : cols + 2 * SIDE, :] = jnp.zeros((rows, SIDE, ref.shape[2]), ref.dtype)

    @pl.when(col == lax.axis_size("col") - 1)
    def _():
        ref[:, cols : cols + SIDE, :] = jnp.zeros((rows, SIDE, ref.shape[2]), ref.dtype)


def set_bounds(bounds, cols):
    shape = bounds.shape[1:]
    column = lax.broadcasted_iota(jnp.int32, shape, 0)
    row, col = lax.axis_index("row"), lax.axis_index("col")
    start = jnp.where(col == lax.axis_size("col") - 1, cols, cols + SIDE)
    stop = jnp.where(col == 0, cols + 2 * SIDE, cols + SIDE)
    level = jnp.where((column >= start) & (column < stop), 0.0, 6.0)
    bounds[0] = jnp.where(row == 0, 0.0, level).astype(BF16)
    bounds[1] = level.astype(BF16)
    bounds[2] = jnp.where(row == lax.axis_size("row") - 1, 0.0, level).astype(BF16)


def flat(value):
    return value.reshape(-1, value.shape[-1])


def same_head(head_dim):
    across = lax.broadcasted_iota(jnp.int32, (LANES, LANES), 0) // head_dim
    along = lax.broadcasted_iota(jnp.int32, (LANES, LANES), 1) // head_dim
    return across == along


def depthwise_row(rows, taps, size, width):
    rows = [row.reshape(width // TILE, TILE, LANES) for row in rows]
    total = None
    for b in range(size):
        part = None
        for a in range(size):
            term = rows[a] * taps(a, b)[None]
            part = term if part is None else part + term
        part = part.reshape(width, LANES).astype(F32)
        if b != size // 2:
            part = pltpu.roll(part, (size // 2 - b) % width, 0)
        total = part if total is None else total + part
    return total


def spread_taps(agg, wide_agg, kind):
    channels = wide_agg.shape[3]
    for index in range(25):
        taps = agg[index : index + 1, kind * channels : (kind + 1) * channels]
        wide_agg[kind, index] = jnp.broadcast_to(taps, (TILE, channels)).astype(BF16)


def aggregated(source, wide_agg, group, first, size):
    width, channels = source.shape[1:]
    scaled = []
    for r in range(size):
        lanes = []
        for lane in range(0, channels, LANES):
            here = slice(lane, lane + LANES)
            value = depthwise_row(
                [source[first + r + a, :, here] for a in range(5)],
                lambda a, b: wide_agg[5 * a + b, :, here], 5, width,
            )
            lanes.append(value.astype(BF16))
        scaled.append(jnp.concatenate(lanes, axis=1))
    value = jnp.dot(jnp.concatenate(scaled, axis=0), group, preferred_element_type=F32)
    return value.astype(BF16).reshape(size, width, channels)


def front(x_ref, weights, outs, scratch, halo, tile, head_dim, section):
    expand, expand_bias, depth, depth_bias, project = weights[:5]
    mixed_out, payload_out = outs
    (
        hidden_0, hidden_1, spread, bounds, mixed, pairs, grouped, wide_depth, wide_agg,
        project_bias, pair_weight, agg, group, sems,
    ) = scratch
    channels = x_ref.shape[2]
    tail = pl.ds(channels, 2 * channels)
    loads = [
        pltpu.make_async_copy(weights[5], project_bias, sems.at[0]),
        pltpu.make_async_copy(weights[6].at[section, :, tail], pair_weight, sems.at[1]),
        pltpu.make_async_copy(weights[7].at[section, :, tail], agg, sems.at[2]),
        pltpu.make_async_copy(weights[8].at[section, pl.ds(1, 2)], group, sems.at[3]),
    ]
    for load in loads:
        load.start()
    rows, width, channels = x_ref.shape
    tile_rows, tile_cols = tile
    inner = rows - 2
    chunk = bounds.shape[2]
    chunks = spread.shape[0]
    this = slice(section, section + 1)
    for index in range(9):
        taps = depth[index // 3, index % 3, section : section + 1, :] * (1.0 / 6.0)
        wide_depth[index] = jnp.broadcast_to(taps, (TILE, taps.shape[1])).astype(BF16)
    set_bounds(bounds, tile_cols)

    def expand_rows(hidden, index, first, size):
        at = pl.ds(pl.multiple_of(index * chunk, chunk), chunk)
        value = jnp.dot(
            flat(x_ref[pl.ds(first, size)]), expand[section, :, at], preferred_element_type=F32
        )
        value = (value + expand_bias[this, at]).astype(BF16)
        for r in range(size):
            row = first + r
            which = jnp.where(row < halo, 0, jnp.where(row >= rows - halo, 2, 1))
            part = value[r * width : (r + 1) * width]
            hidden[row] = six_hard_swish(part, bounds[which])

    def spread_rows(hidden, index, first, size):
        for r in range(size):
            for lane in range(0, chunk, LANES):
                here = pl.ds(pl.multiple_of(index * chunk + lane, LANES), LANES)
                value = depthwise_row(
                    [hidden[first + r + a, :, lane : lane + LANES] for a in range(3)],
                    lambda a, b: wide_depth[3 * a + b, :, here], 3, width,
                )
                value = (value + depth_bias[this, here]).astype(BF16)
                spread[index, first + r, :, lane : lane + LANES] = six_hard_swish(value)

    size = inner // PARTS
    ahead = -(-rows // PARTS)

    def loop(count, body):
        lax.fori_loop(0, count, lambda index, carry: (body(index), carry)[1], 0)

    def ahead_rows(hidden, index, part):
        expand_rows(hidden, index, jnp.minimum(part * ahead, rows - ahead), ahead)

    loop(PARTS, lambda part: ahead_rows(hidden_0, 0, part))

    def two_chunks(pair):
        def even_rows(part):
            spread_rows(hidden_0, 2 * pair, part * size, size)
            ahead_rows(hidden_1, 2 * pair + 1, part)

        def odd_rows(part):
            spread_rows(hidden_1, 2 * pair + 1, part * size, size)
            ahead_rows(hidden_0, jnp.minimum(2 * pair + 2, chunks - 1), part)

        loop(PARTS, even_rows)
        loop(PARTS, odd_rows)

    loop(chunks // 2, two_chunks)
    loads[0].wait()
    weight = project[section]

    def project_rows(part):
        here = pl.ds(part * size, size)
        value = project_bias[this, :] + flat(x_ref[pl.ds(part * size + 1, size)]).astype(F32)
        lanes = [flat(spread[index, here]) for index in range(chunks)]
        product = jnp.dot(
            jnp.concatenate(lanes, axis=1), weight, preferred_element_type=F32
        )
        value = product * (1.0 / 6.0) + value
        mixed[here] = value.astype(BF16).reshape(size, width, channels)

    loop(PARTS, project_rows)
    store = pltpu.make_async_copy(mixed, mixed_out, sems.at[4])
    store.start()
    for load in loads[1:]:
        load.wait()
    for kind in range(2):
        spread_taps(agg, wide_agg, kind)
    around = halo - 1
    count = tile_rows + 4
    size = group_size(count, 6)

    def pair_rows(part):
        first = part * size
        value = jnp.dot(
            flat(mixed[pl.ds(around - 2 + first, size)]), pair_weight[...],
            preferred_element_type=F32,
        )
        value = value.astype(BF16).reshape(size, width, 2 * channels)
        for kind in range(2):
            here = slice(kind * channels, (kind + 1) * channels)
            pairs[kind, pl.ds(first, size)] = value[:, :, here]

    loop(count // size, pair_rows)
    for kind in range(2):
        clear_outside(pairs.at[kind], 2, tile_cols)
    step = group_size(tile_rows, 4)
    turns = tile_rows // step

    def grouped_rows(index):
        kind, first = index // turns, index % turns * step
        value = aggregated(pairs.at[kind], wide_agg.at[kind], group[kind], first, step)
        grouped[kind, pl.ds(first, step)] = value

    loop(2 * turns, grouped_rows)

    def summed(key, value):
        key = jnp.maximum(flat(key[:, 0:tile_cols]), 0.0)
        value = flat(value[:, 0:tile_cols])
        products = [
            lax.dot_general(
                key[:, lane : lane + LANES], value[:, lane : lane + LANES],
                (((0,), (0,)), ((), ())), preferred_element_type=F32,
            )
            for lane in range(0, channels, LANES)
        ]
        return products, jnp.sum(key.astype(F32), axis=0, keepdims=True)

    mine = slice(2, 2 + tile_rows)
    products, sums = summed(pairs[0, mine], pairs[1, mine])
    more, more_sums = summed(grouped[0], grouped[1])
    products = products + more
    sums = jnp.concatenate([sums, more_sums], axis=1)
    same = same_head(head_dim)
    summary = jnp.zeros((LANES, LANES), F32)
    key_sums = []
    for index, product in enumerate(products):
        product = jnp.where(same, product, 0.0)
        if index:
            product = pltpu.roll(product, index * head_dim, 1)
        summary = summary + product
        key_sums.append(sums[:, index * LANES : (index + 1) * LANES])
    key_sums.append(jnp.zeros((KEY_ROWS - len(products), LANES), F32))
    payload_out[0:LANES, :] = summary.astype(BF16)
    payload_out[LANES : LANES + KEY_ROWS, :] = jnp.concatenate(key_sums, axis=0).astype(BF16)
    store.wait()


def query_kernel(
    tile, section, mixed_in, qkv_weight, taps, groups, query, mixed_out,
    mixed, centre, weight, agg, group, wide_agg, sems,
):
    rows, width, channels = mixed.shape
    head = pl.ds(0, channels)
    loads = [
        pltpu.make_async_copy(mixed_in, mixed, sems.at[0]),
        pltpu.make_async_copy(qkv_weight.at[section, :, head], weight, sems.at[1]),
        pltpu.make_async_copy(taps.at[section, :, head], agg, sems.at[2]),
        pltpu.make_async_copy(groups.at[section, 0], group, sems.at[3]),
    ]
    for load in loads:
        load.start()
    for load in loads:
        load.wait()
    mixed_out[...] = mixed[2 : rows - 2]
    spread_taps(agg, wide_agg, 0)

    def centre_rows(first, size):
        here = pl.ds(first, size)
        value = jnp.dot(flat(mixed[here]), weight[...], preferred_element_type=F32)
        centre[here] = value.astype(BF16).reshape(size, width, channels)

    by_groups(rows, 10, centre_rows)
    clear_outside(centre, (rows - tile[0]) // 2, tile[1])

    def query_rows(first, size):
        here = pl.ds(first, size)
        query[here, :, 0:channels] = jnp.maximum(centre[pl.ds(first + 2, size)], 0.0)
        grouped = aggregated(centre, wide_agg.at[0], group[...], first, size)
        query[here, :, channels : 2 * channels] = jnp.maximum(grouped, 0.0)

    by_groups(rows - 4, 5, query_rows)


def attend(
    mixed_ref, query_ref, payloads, weight, bias_in, held, head_dim, section, x_ref
):
    rows, width, channels = x_ref.shape
    bias, sem = held
    load = pltpu.make_async_copy(bias_in, bias, sem)
    load.start()
    same = same_head(head_dim)
    square = (LANES, LANES)
    diagonal = lax.broadcasted_iota(jnp.int32, square, 0) == lax.broadcasted_iota(
        jnp.int32, square, 1
    )
    ones = jnp.where(same, 1.0, 0.0).astype(BF16)
    nothing = jnp.zeros(square, BF16)
    payload = payloads[0][...].astype(F32)
    for part in payloads[1:]:
        payload = payload + part[...].astype(F32)
    packed = payload[0:LANES]
    count = 2 * channels // LANES
    summaries, sums = [], []
    for index in range(count):
        summary = packed if index == 0 else pltpu.roll(packed, LANES - index * head_dim, 1)
        summaries.append(jnp.where(same, summary, 0.0).astype(BF16))
        keys = payload[LANES + index : LANES + index + 1]
        keys = jnp.where(diagonal, keys, 0.0).astype(BF16)
        sums.append(jnp.dot(keys, ones, preferred_element_type=F32).astype(BF16))

    def paired(blocks, index):
        return jnp.concatenate(
            [
                jnp.concatenate([blocks[index], nothing], axis=1),
                jnp.concatenate([nothing, blocks[index + 1]], axis=1),
            ],
            axis=0,
        )

    summaries = [paired(summaries, index) for index in range(0, count, 2)]
    sums = [paired(sums, index) for index in range(0, count, 2)]
    step = 2 * LANES
    load.wait()

    def attend_rows(first, size):
        query = flat(query_ref[pl.ds(first, size)])
        parts = []
        for branch in range(count // 2):
            part = query[:, branch * step : (branch + 1) * step]
            numer = jnp.dot(part, summaries[branch], preferred_element_type=F32)
            denom = jnp.dot(part, sums[branch], preferred_element_type=F32) + 1e-6
            inverse = pl.reciprocal(denom, approx=True)
            inverse = inverse * (2.0 - denom * inverse)
            parts.append((numer * inverse).astype(BF16))
        value = jnp.dot(
            jnp.concatenate(parts, axis=1), weight[section], preferred_element_type=F32
        )
        value = value + bias[section : section + 1, :]
        value = value + flat(mixed_ref[pl.ds(first, size)]).astype(F32)
        x_ref[pl.ds(first, size)] = value.astype(BF16).reshape(size, width, channels)

    by_groups(rows, 5, attend_rows)


def tap(section, a, b):
    at = 32 * section + 5 * a + b
    return slice(at, at + 1)


def prepare_kernel(head_dim, qkv, agg, group, head, project_bias, output_bias, *refs):
    outs, made, taps, sems = refs[:6], refs[6:10], refs[10], refs[11]
    qkv_out, agg_out, group_out, head_out = made
    made = [*made, project_bias, output_bias]
    sections, channels, wide = qkv.shape
    half = 3 * LANES
    heads = LANES // head_dim
    src = lax.broadcasted_iota(jnp.int32, (half, LANES), 0)
    dst = lax.broadcasted_iota(jnp.int32, (half, LANES), 1)
    first = (dst // head_dim) * 3 * head_dim + dst % head_dim
    picks = [jnp.where(src == first + k * head_dim, 1.0, 0.0).astype(BF16) for k in range(3)]
    taps[...] = jnp.zeros(taps.shape, F32)
    for section in range(sections):
        for a in range(5):
            for b in range(5):
                taps[tap(section, a, b), :] = agg[a, b, section : section + 1, :]
    rest = taps[...]
    high = rest.astype(BF16)
    rest = rest - high.astype(F32)
    middle = rest.astype(BF16)
    low = (rest - middle.astype(F32)).astype(BF16)
    split = jnp.concatenate([high, middle, low], axis=0)
    count = taps.shape[0]
    weights = qkv[...].reshape(sections * channels, wide)
    for part in range(wide // half):
        here = slice(part * half, (part + 1) * half)
        for kind in range(3):
            to = kind * channels + part * LANES
            there = slice(to, to + LANES)
            value = jnp.dot(weights[:, here], picks[kind], preferred_element_type=F32)
            qkv_out[:, :, there] = value.astype(BF16).reshape(sections, channels, LANES)
            value = jnp.dot(split[:, here], picks[kind], preferred_element_type=F32)
            value = value[:count] + value[count : 2 * count] + value[2 * count :]
            agg_out[:, :, there] = value.reshape(sections, -1, LANES)
    row = lax.broadcasted_iota(jnp.int32, (head_dim, channels), 0)
    lane = lax.broadcasted_iota(jnp.int32, (head_dim, channels), 1)
    spread = jnp.where(lane % head_dim == row, 1.0, 0.0).astype(BF16)
    across = lax.broadcasted_iota(jnp.int32, (channels, channels), 0) // head_dim
    along = lax.broadcasted_iota(jnp.int32, (channels, channels), 1) // head_dim
    for section in range(sections):
        for kind in range(3):
            tall = [group[section, 3 * h + kind] for h in range(channels // head_dim)]
            value = jnp.dot(jnp.concatenate(tall, axis=0), spread, preferred_element_type=F32)
            group_out[section, kind] = jnp.where(across == along, value, 0.0).astype(BF16)
    head_out[...] = jnp.zeros(head_out.shape, BF16)
    for a in range(3):
        rows = [head[a, b] for b in range(3)] + [jnp.zeros((4, channels), BF16)]
        head_out[a, 0:16, :] = jnp.concatenate(rows, axis=0)
    stores = [pltpu.make_async_copy(made[i], outs[i], sems.at[i]) for i in range(6)]
    for store in stores:
        store.start()
    for store in stores:
        store.wait()


def first_kernel(tile, head_dim, own, row_0, row_1, *refs):
    weights, outs, scratch = refs[:9], refs[9:11], refs[11:]
    x_ref = scratch[0]
    rows, cols = tile
    below = REACH + rows
    even = lax.axis_index("row") & 1 == 0
    x_ref[REACH:below] = own[...]
    x_ref[pl.ds(jnp.where(even, below, 0), REACH)] = row_0[...]
    x_ref[pl.ds(jnp.where(even, 0, below), REACH)] = row_1[...]
    front(x_ref, weights, outs, scratch[1:], REACH, tile, head_dim, 0)


def second_kernel(tile, head_dim, mixed, query, payload, other, out_weight, out_bias, *refs):
    weights, outs, scratch = refs[:9], refs[9:11], refs[11:]
    x_ref = scratch[0]
    attend(
        mixed, query, (payload, other), out_weight, out_bias, scratch[1:3], head_dim, 0, x_ref
    )
    front(x_ref, weights, outs, scratch[3:], REACH - 3, tile, head_dim, 1)


def last_kernel(
    tile, head_dim, mixed, query, payload, other, out_weight, out_bias, head_weight, head_bias,
    map_out, boxes_out, x_ref, *held,
):
    rows, cols = tile
    width = cols + 2 * SIDE
    attend(
        mixed, query, (payload, other), out_weight, out_bias, held, head_dim, 1, x_ref
    )
    clear_outside(x_ref, 1, cols)
    map_out[...] = x_ref[1 : 1 + rows, 0:cols, :]
    total = None
    for a in range(3):
        part = lax.dot_general(
            flat(x_ref[a : a + rows]), head_weight[a], (((1,), (1,)), ((), ())),
            preferred_element_type=F32,
        )
        total = part if total is None else total + part
    total = total.reshape(rows, width, LANES)
    lane = lax.broadcasted_iota(jnp.int32, (width, LANES), 1) // 4
    shifted = [
        jnp.where(
            lane == 0,
            pltpu.roll(total[r], 1, 0),
            jnp.where(lane == 2, pltpu.roll(total[r], width - 1, 0), total[r]),
        )
        for r in range(rows)
    ]
    shifted = jnp.concatenate(shifted, axis=0)
    across = lax.broadcasted_iota(jnp.int32, (8, LANES), 0)
    along = lax.broadcasted_iota(jnp.int32, (8, LANES), 1)
    fold = jnp.where((along % 4 == across) & (along < 12), 1.0, 0.0)
    boxes = lax.dot_general(
        fold, shifted, (((1,), (1,)), ((), ())), precision=lax.Precision.HIGHEST,
        preferred_element_type=F32,
    )
    boxes = boxes[0:4] + head_bias[...]
    for r in range(rows):
        boxes_out[:, r, :] = boxes[:, r * width : r * width + cols]


def near():
    return pl.BlockSpec(memory_space=pltpu.VMEM)


def far():
    return pl.BlockSpec(memory_space=pltpu.HBM)


def digits(size, most):
    radices = []
    while size > 1:
        radix = next((r for r in range(min(most, size), 1, -1) if size % r == 0), size)
        radices.append(radix)
        size //= radix
    return radices


def partner(i, stride, radix, step):
    digit = (i // stride) % radix
    other = digit ^ step if radix & (radix - 1) == 0 else (digit + step) % radix
    return i + (other - digit) * stride


def sum_by_permutes(value):
    rounds = []
    for axis in ("row", "col"):
        stride = 1
        for radix in digits(lax.axis_size(axis), 4):
            rounds.append((axis, stride, radix))
            stride *= radix
    for axis, stride, radix in rounds:
        count = lax.axis_size(axis)
        others = [
            lax.ppermute(value, axis, [(i, partner(i, stride, radix, k)) for i in range(count)])
            for k in range(1, radix)
        ]
        if (axis, stride, radix) == rounds[-1] and radix == 2:
            return value, others[0]
        total = value.astype(F32)
        for other in others:
            total = total + other.astype(F32)
        value = total.astype(BF16)
    return value, jnp.zeros_like(value)


def digits(size, most):
    radices = []
    while size > 1:
        radix = next((r for r in range(min(most, size), 1, -1) if size % r == 0), size)
        radices.append(radix)
        size //= radix
    return radices


def pair_exchange(value, axis, first):
    count = lax.axis_size(axis)
    pairs = []
    for i in range(first, count - 1, 2):
        pairs += [(i, i + 1), (i + 1, i)]
    return lax.ppermute(value, axis, pairs)


def local(
    features,
    expand_weight,
    expand_bias,
    depth_weight,
    depth_bias,
    project_weight,
    project_bias,
    qkv_weight,
    aggregate_depth,
    aggregate_group,
    output_weight,
    output_bias,
    head_weight,
    head_bias,
):
    rows, cols, channels = features.shape
    head_dim = aggregate_group.shape[2]
    heads = channels // head_dim
    width = cols + 2 * SIDE
    tile = (rows, cols)
    wide = expand_weight.shape[2]

    def edges(value, dim, size, odd):
        far = value.shape[dim] - size
        return [
            lax.dynamic_slice_in_dim(value, jnp.where(odd == at, far, 0), size, dim) for at in (0, 1)
        ]

    odd_row = lax.axis_index("row") & 1
    odd_col = lax.axis_index("col") & 1
    low, high = edges(features, 1, SIDE, odd_col)
    col_1 = pair_exchange(high, "col", 1)
    col_0 = pair_exchange(low, "col", 0)
    right = jnp.where(odd_col == 1, col_1, col_0)
    left = jnp.where(odd_col == 1, col_0, col_1)
    wide_rows = jnp.concatenate([features, right, left], axis=1)
    low, high = edges(wide_rows, 0, REACH, odd_row)
    row_1 = pair_exchange(high, "row", 1)
    row_0 = pair_exchange(low, "row", 0)

    aggregate_depth = aggregate_depth.transpose(1, 2, 0, 3)
    depth_weight = depth_weight.transpose(1, 2, 0, 3)
    params = pltpu.CompilerParams(vmem_limit_bytes=24 * 2**20)
    made = [
        jax.ShapeDtypeStruct(qkv_weight.shape, BF16),
        jax.ShapeDtypeStruct((SECTIONS, 32, 3 * channels), F32),
        jax.ShapeDtypeStruct((SECTIONS, 3, channels, channels), BF16),
        jax.ShapeDtypeStruct((3, LANES, channels), BF16),
    ]
    biases = [jax.ShapeDtypeStruct(array.shape, F32) for array in (project_bias, output_bias)]
    qkv_weight, taps, group, head_weight, project_bias, output_bias = pl.pallas_call(
        functools.partial(prepare_kernel, head_dim),
        out_shape=made + biases,
        grid=(1,),
        in_specs=[near()] * 6,
        out_specs=[far()] * 6,
        scratch_shapes=[pltpu.VMEM(array.shape, array.dtype) for array in made]
        + [pltpu.VMEM((32 * SECTIONS, 3 * channels), F32), pltpu.SemaphoreType.DMA((6,))],
        compiler_params=params,
        cost_estimate=pl.CostEstimate(
            flops=2 * 10**9, bytes_accessed=4 * 10**6, transcendentals=0
        ),
        name="prepare",
    )(qkv_weight, aggregate_depth, aggregate_group, head_weight, project_bias, output_bias)

    weights = [
        expand_weight, expand_bias, depth_weight, depth_bias, project_weight, project_bias,
        qkv_weight, taps, group,
    ]
    weight_specs = [near()] * 5 + [far()] * 4

    def outs_of(count):
        return [
            jax.ShapeDtypeStruct((count, width, channels), BF16),
            jax.ShapeDtypeStruct((LANES + KEY_ROWS, LANES), BF16),
        ]

    def front_scratch(count):
        return [
            pltpu.VMEM((count, width, 256), BF16),
            pltpu.VMEM((count, width, 256), BF16),
            pltpu.VMEM((expand_weight.shape[2] // 256, count - 2, width, 256), BF16),
            pltpu.VMEM((3, width, 256), BF16),
            pltpu.VMEM((count - 2, width, channels), BF16),
            pltpu.VMEM((2, rows + 4, width, channels), BF16),
            pltpu.VMEM((2, rows, width, channels), BF16),
            pltpu.VMEM((9, TILE, expand_weight.shape[2]), BF16),
            pltpu.VMEM((2, 25, TILE, channels), BF16),
            pltpu.VMEM(project_bias.shape, F32),
            pltpu.VMEM((channels, 2 * channels), BF16),
            pltpu.VMEM((32, 2 * channels), F32),
            pltpu.VMEM((2, channels, channels), BF16),
            pltpu.SemaphoreType.DMA((5,)),
        ]

    def attend_scratch(count):
        return [
            pltpu.VMEM((count, width, channels), BF16),
            pltpu.VMEM(output_bias.shape, F32),
            pltpu.SemaphoreType.DMA,
        ]

    def queries(mixed, section):
        count = mixed.shape[0]
        units = (count - 4) * width * channels
        return pl.pallas_call(
            functools.partial(query_kernel, tile, section),
            out_shape=[
                jax.ShapeDtypeStruct((count - 4, width, 2 * channels), BF16),
                jax.ShapeDtypeStruct((count - 4, width, channels), BF16),
            ],
            grid=(1,),
            in_specs=[far()] * 4,
            out_specs=[near()] * 2,
            scratch_shapes=[
                pltpu.VMEM((count, width, channels), BF16),
                pltpu.VMEM((count, width, channels), BF16),
                pltpu.VMEM((channels, channels), BF16),
                pltpu.VMEM((32, channels), F32),
                pltpu.VMEM((channels, channels), BF16),
                pltpu.VMEM((1, 25, TILE, channels), BF16),
                pltpu.SemaphoreType.DMA((4,)),
            ],
            compiler_params=params,
            cost_estimate=pl.CostEstimate(
                flops=8 * units * channels, bytes_accessed=8 * units, transcendentals=0
            ),
            name="queries",
        )(mixed, qkv_weight, taps, group)

    first_rows = rows + 2 * REACH
    mixed, payload = pl.pallas_call(
        functools.partial(first_kernel, tile, head_dim),
        out_shape=outs_of(first_rows - 2),
        grid=(1,),
        in_specs=[near()] * 3 + weight_specs,
        out_specs=[far(), near()],
        scratch_shapes=[pltpu.VMEM((first_rows, width, channels), BF16)]
        + front_scratch(first_rows),
        compiler_params=params,
        name="first",
    )(wide_rows, row_0, row_1, *weights)
    query, mixed = queries(mixed, 0)
    payload, other = sum_by_permutes(payload)

    second_rows = first_rows - 6
    mixed, payload = pl.pallas_call(
        functools.partial(second_kernel, tile, head_dim),
        out_shape=outs_of(second_rows - 2),
        grid=(1,),
        in_specs=[near()] * 5 + [far()] + weight_specs,
        out_specs=[far(), near()],
        scratch_shapes=attend_scratch(second_rows) + front_scratch(second_rows),
        compiler_params=params,
        name="second",
    )(mixed, query, payload, other, output_weight, output_bias, *weights)
    query, mixed = queries(mixed, 1)
    payload, other = sum_by_permutes(payload)

    return pl.pallas_call(
        functools.partial(last_kernel, tile, head_dim),
        out_shape=[
            jax.ShapeDtypeStruct((rows, cols, channels), BF16),
            jax.ShapeDtypeStruct((4, rows, cols), F32),
        ],
        grid=(1,),
        in_specs=[near()] * 5 + [far()] + [near()] * 2,
        out_specs=[near()] * 2,
        scratch_shapes=attend_scratch(rows + 2),
        compiler_params=params,
        name="last",
    )(
        mixed, query, payload, other, output_weight, output_bias, head_weight,
        head_bias.reshape(4, 1),
    )


def solution(mesh):
    return jax.shard_map(
        local,
        mesh=mesh,
        in_specs=(P("row", "col", None),) + (P(),) * 13,
        out_specs=(P("row", "col", None), P(None, "row", "col")),
        check_vma=False,
    )
```

```python
import functools

import jax
import jax.numpy as jnp
from jax import lax
from jax.experimental import pallas as pl
from jax.experimental.pallas import tpu as pltpu
from jax.sharding import PartitionSpec as P

SECTIONS = 2
LANES = 128
SIDE = 8
REACH = 7
KEY_ROWS = 16
TILE = 16
PARTS = 2
F32 = jnp.float32
BF16 = jnp.bfloat16


def six_hard_swish(value):
    return value * jnp.minimum(jnp.maximum(value + 3.0, 0.0), 6.0)


def parted(count, parts):
    cuts = [count * k // parts for k in range(parts + 1)]
    return [(a, b - a) for a, b in zip(cuts, cuts[1:]) if b > a]


def group_size(count, most):
    return next(n for n in range(min(most, count), 0, -1) if count % n == 0)


def by_groups(count, most, body):
    size = group_size(count, most)

    def group(index, carry):
        body(index * size, size)
        return carry

    lax.fori_loop(0, count // size, group, 0)


def clear_outside(ref, halo, cols):
    rows = ref.shape[0]
    row, col = lax.axis_index("row"), lax.axis_index("col")

    @pl.when(row == 0)
    def _():
        ref[0:halo] = jnp.zeros((halo,) + ref.shape[1:], ref.dtype)

    @pl.when(row == lax.axis_size("row") - 1)
    def _():
        ref[rows - halo : rows] = jnp.zeros((halo,) + ref.shape[1:], ref.dtype)

    @pl.when(col == 0)
    def _():
        ref[:, cols + SIDE : cols + 2 * SIDE, :] = jnp.zeros((rows, SIDE, ref.shape[2]), ref.dtype)

    @pl.when(col == lax.axis_size("col") - 1)
    def _():
        ref[:, cols : cols + SIDE, :] = jnp.zeros((rows, SIDE, ref.shape[2]), ref.dtype)


def flat(value):
    return value.reshape(-1, value.shape[-1])


def same_head(head_dim):
    across = lax.broadcasted_iota(jnp.int32, (LANES, LANES), 0) // head_dim
    along = lax.broadcasted_iota(jnp.int32, (LANES, LANES), 1) // head_dim
    return across == along


def depthwise_row(rows, taps, size, width):
    rows = [row.reshape(width // TILE, TILE, LANES) for row in rows]
    total = None
    for b in range(size):
        part = None
        for a in range(size):
            term = rows[a] * taps(a, b)[None]
            part = term if part is None else part + term
        part = part.reshape(width, LANES).astype(F32)
        if b != size // 2:
            part = pltpu.roll(part, (size // 2 - b) % width, 0)
        total = part if total is None else total + part
    return total


def spread_taps(agg, wide_agg):
    for index in range(25):
        taps = agg[index : index + 1, :]
        wide_agg[index] = jnp.broadcast_to(taps, (TILE, taps.shape[1])).astype(BF16)


def aggregated(source, wide_agg, group, low, first, size, channels):
    width = source.shape[1]
    scaled = []
    for r in range(size):
        lanes = []
        for lane in range(low, low + channels, LANES):
            here = slice(lane, lane + LANES)
            value = depthwise_row(
                [source[first + r + a, :, here] for a in range(5)],
                lambda a, b: wide_agg[5 * a + b, :, here], 5, width,
            )
            lanes.append(value.astype(BF16))
        scaled.append(jnp.concatenate(lanes, axis=1))
    value = jnp.dot(jnp.concatenate(scaled, axis=0), group, preferred_element_type=F32)
    return value.astype(BF16).reshape(size, width, channels)


def front(x_ref, weights, outs, scratch, halo, tile, head_dim, section):
    expand, expand_bias, depth, depth_bias, project = weights[:5]
    mixed_out, payload_out = outs
    (
        hidden_0, hidden_1, total, mixed, pairs, wide_depth, wide_agg,
        project_bias, pair_weight, agg, group, sems,
    ) = scratch
    channels = x_ref.shape[2]
    tail = pl.ds(channels, 2 * channels)
    loads = [
        pltpu.make_async_copy(weights[5], project_bias, sems.at[0]),
        pltpu.make_async_copy(weights[6].at[section, :, tail], pair_weight, sems.at[1]),
        pltpu.make_async_copy(weights[7].at[section, :, tail], agg, sems.at[2]),
        pltpu.make_async_copy(weights[8].at[section, pl.ds(1, 2)], group, sems.at[3]),
    ]
    for load in loads:
        load.start()
    rows, width, channels = x_ref.shape
    tile_rows, tile_cols = tile
    inner = rows - 2
    chunk = hidden_0.shape[2]
    chunks = expand.shape[2] // chunk
    for index in range(9):
        taps = depth[index // 3, index % 3, section : section + 1, :] * (1.0 / 6.0)
        wide_depth[index] = jnp.broadcast_to(taps, (TILE, taps.shape[1])).astype(BF16)
    total[...] = 6.0 * flat(x_ref[1 : rows - 1]).astype(F32)

    def expand_rows(out, at, first, size):
        value = jnp.dot(
            flat(x_ref[first : first + size]), expand[section, :, pl.ds(at, chunk)],
            preferred_element_type=F32,
        )
        value = (value + expand_bias[section : section + 1, pl.ds(at, chunk)]).astype(BF16)
        out[first : first + size] = six_hard_swish(value).reshape(size, width, chunk)

    def spread_rows(hidden, at, first, size):
        spread = []
        for r in range(first, first + size):
            lanes = []
            for lane in range(0, chunk, LANES):
                here = pl.ds(pl.multiple_of(at + lane, LANES), LANES)
                value = depthwise_row(
                    [hidden[r + a, :, lane : lane + LANES] for a in range(3)],
                    lambda a, b: wide_depth[3 * a + b, :, here], 3, width,
                )
                value = (value + depth_bias[section : section + 1, here]).astype(BF16)
                lanes.append(six_hard_swish(value))
            spread.append(jnp.concatenate(lanes, axis=1))
        pixels = slice(first * width, (first + size) * width)
        total[pixels] += jnp.dot(
            jnp.concatenate(spread, axis=0), project[section, pl.ds(at, chunk), :],
            preferred_element_type=F32,
        )

    def stage(index, current, following):
        at = pl.multiple_of(index * chunk, chunk)
        ahead = pl.multiple_of(jnp.minimum(index + 1, chunks - 1) * chunk, chunk)
        for (first, size), (from_row, count) in zip(parted(inner, PARTS), parted(rows, PARTS)):
            expand_rows(following, ahead, from_row, count)
            spread_rows(current, at, first, size)
        clear_outside(following, halo, tile_cols)

    for first, size in parted(rows, PARTS):
        expand_rows(hidden_0, 0, first, size)
    clear_outside(hidden_0, halo, tile_cols)

    def two_stages(index, carry):
        stage(2 * index, hidden_0, hidden_1)
        stage(2 * index + 1, hidden_1, hidden_0)
        return carry

    lax.fori_loop(0, chunks // 2, two_stages, 0)
    loads[0].wait()
    value = total[...] * (1.0 / 6.0) + project_bias[section : section + 1, :]
    mixed[...] = value.astype(BF16).reshape(inner, width, channels)
    store = pltpu.make_async_copy(mixed, mixed_out, sems.at[4])
    store.start()
    for load in loads[1:]:
        load.wait()
    spread_taps(agg, wide_agg)
    around = halo - 1
    first_pair = around - 2
    count = tile_rows + 4
    for first, size in parted(count, PARTS - 1):
        at = first_pair + first
        value = jnp.dot(
            flat(mixed[at : at + size]), pair_weight[...], preferred_element_type=F32
        )
        pairs[first : first + size] = value.astype(BF16).reshape(size, width, 2 * channels)
    clear_outside(pairs, 2, tile_cols)
    size = group_size(tile_rows, 4)

    def summed(key, value):
        key = jnp.maximum(flat(key[:, 0:tile_cols]), 0.0)
        value = flat(value[:, 0:tile_cols])
        products = [
            lax.dot_general(
                key[:, lane : lane + LANES], value[:, lane : lane + LANES],
                (((0,), (0,)), ((), ())), preferred_element_type=F32,
            )
            for lane in range(0, channels, LANES)
        ]
        return products, jnp.sum(key.astype(F32), axis=0, keepdims=True)

    mine = slice(2, 2 + tile_rows)
    products, sums = summed(
        pairs[mine, :, 0:channels], pairs[mine, :, channels : 2 * channels]
    )

    def grouped_rows(index, carry):
        at = index * size
        more, sums = summed(
            aggregated(pairs, wide_agg, group[0], 0, at, size, channels),
            aggregated(pairs, wide_agg, group[1], channels, at, size, channels),
        )
        return [a + b for a, b in zip(carry[0], more)], carry[1] + sums

    more, more_sums = lax.fori_loop(
        0, tile_rows // size, grouped_rows,
        ([jnp.zeros((LANES, LANES), F32) for _ in products], jnp.zeros_like(sums)),
    )
    products = products + more
    sums = jnp.concatenate([sums, more_sums], axis=1)
    same = same_head(head_dim)
    summary = jnp.zeros((LANES, LANES), F32)
    key_sums = []
    for index, product in enumerate(products):
        product = jnp.where(same, product, 0.0)
        if index:
            product = pltpu.roll(product, index * head_dim, 1)
        summary = summary + product
        key_sums.append(sums[:, index * LANES : (index + 1) * LANES])
    key_sums.append(jnp.zeros((KEY_ROWS - len(products), LANES), F32))
    payload_out[0:LANES, :] = summary.astype(BF16)
    payload_out[LANES : LANES + KEY_ROWS, :] = jnp.concatenate(key_sums, axis=0).astype(BF16)
    store.wait()


def query_kernel(
    tile, section, mixed_in, qkv_weight, taps, groups, query, mixed_out,
    mixed, centre, weight, agg, group, wide_agg, sems,
):
    rows, width, channels = mixed.shape
    head = pl.ds(0, channels)
    loads = [
        pltpu.make_async_copy(mixed_in, mixed, sems.at[0]),
        pltpu.make_async_copy(qkv_weight.at[section, :, head], weight, sems.at[1]),
        pltpu.make_async_copy(taps.at[section, :, head], agg, sems.at[2]),
        pltpu.make_async_copy(groups.at[section, 0], group, sems.at[3]),
    ]
    for load in loads:
        load.start()
    for load in loads:
        load.wait()
    mixed_out[...] = mixed[2 : rows - 2]
    spread_taps(agg, wide_agg)
    for first, size in parted(rows, PARTS):
        value = jnp.dot(
            flat(mixed[first : first + size]), weight[...], preferred_element_type=F32
        )
        centre[first : first + size] = value.astype(BF16).reshape(size, width, channels)
    clear_outside(centre, (rows - tile[0]) // 2, tile[1])

    def query_rows(first, size):
        here = pl.ds(first, size)
        query[here, :, 0:channels] = jnp.maximum(centre[pl.ds(first + 2, size)], 0.0)
        grouped = aggregated(centre, wide_agg, group[...], 0, first, size, channels)
        query[here, :, channels : 2 * channels] = jnp.maximum(grouped, 0.0)

    by_groups(rows - 4, 5, query_rows)


def attend(
    mixed_ref, query_ref, payloads, weight, bias_in, held, head_dim, section, x_ref
):
    rows, width, channels = x_ref.shape
    bias, sem = held
    load = pltpu.make_async_copy(bias_in, bias, sem)
    load.start()
    same = same_head(head_dim)
    square = (LANES, LANES)
    diagonal = lax.broadcasted_iota(jnp.int32, square, 0) == lax.broadcasted_iota(
        jnp.int32, square, 1
    )
    ones = jnp.where(same, 1.0, 0.0).astype(BF16)
    nothing = jnp.zeros(square, BF16)
    payload = payloads[0][...].astype(F32)
    for part in payloads[1:]:
        payload = payload + part[...].astype(F32)
    packed = payload[0:LANES]
    count = 2 * channels // LANES
    summaries, sums = [], []
    for index in range(count):
        summary = packed if index == 0 else pltpu.roll(packed, LANES - index * head_dim, 1)
        summaries.append(jnp.where(same, summary, 0.0).astype(BF16))
        keys = payload[LANES + index : LANES + index + 1]
        keys = jnp.where(diagonal, keys, 0.0).astype(BF16)
        sums.append(jnp.dot(keys, ones, preferred_element_type=F32).astype(BF16))

    def paired(blocks, index):
        return jnp.concatenate(
            [
                jnp.concatenate([blocks[index], nothing], axis=1),
                jnp.concatenate([nothing, blocks[index + 1]], axis=1),
            ],
            axis=0,
        )

    summaries = [paired(summaries, index) for index in range(0, count, 2)]
    sums = [paired(sums, index) for index in range(0, count, 2)]
    step = 2 * LANES
    load.wait()

    def attend_rows(first, size):
        query = flat(query_ref[pl.ds(first, size)])
        parts = []
        for branch in range(count // 2):
            part = query[:, branch * step : (branch + 1) * step]
            numer = jnp.dot(part, summaries[branch], preferred_element_type=F32)
            denom = jnp.dot(part, sums[branch], preferred_element_type=F32) + 1e-6
            inverse = pl.reciprocal(denom, approx=True)
            inverse = inverse * (2.0 - denom * inverse)
            parts.append((numer * inverse).astype(BF16))
        value = jnp.dot(
            jnp.concatenate(parts, axis=1), weight[section], preferred_element_type=F32
        )
        value = value + bias[section : section + 1, :]
        value = value + flat(mixed_ref[pl.ds(first, size)]).astype(F32)
        x_ref[pl.ds(first, size)] = value.astype(BF16).reshape(size, width, channels)

    by_groups(rows, 5, attend_rows)


def tap(section, a, b):
    at = 32 * section + 5 * a + b
    return slice(at, at + 1)


def prepare_kernel(head_dim, qkv, agg, group, head, project_bias, output_bias, *refs):
    outs, made, taps, sems = refs[:6], refs[6:10], refs[10], refs[11]
    qkv_out, agg_out, group_out, head_out = made
    made = [*made, project_bias, output_bias]
    sections, channels, wide = qkv.shape
    half = 3 * LANES
    heads = LANES // head_dim
    src = lax.broadcasted_iota(jnp.int32, (half, LANES), 0)
    dst = lax.broadcasted_iota(jnp.int32, (half, LANES), 1)
    first = (dst // head_dim) * 3 * head_dim + dst % head_dim
    picks = [jnp.where(src == first + k * head_dim, 1.0, 0.0).astype(BF16) for k in range(3)]
    taps[...] = jnp.zeros(taps.shape, F32)
    for section in range(sections):
        for a in range(5):
            for b in range(5):
                taps[tap(section, a, b), :] = agg[a, b, section : section + 1, :]
    rest = taps[...]
    high = rest.astype(BF16)
    rest = rest - high.astype(F32)
    middle = rest.astype(BF16)
    low = (rest - middle.astype(F32)).astype(BF16)
    split = jnp.concatenate([high, middle, low], axis=0)
    count = taps.shape[0]
    weights = qkv[...].reshape(sections * channels, wide)
    for part in range(wide // half):
        here = slice(part * half, (part + 1) * half)
        for kind in range(3):
            to = kind * channels + part * LANES
            there = slice(to, to + LANES)
            value = jnp.dot(weights[:, here], picks[kind], preferred_element_type=F32)
            qkv_out[:, :, there] = value.astype(BF16).reshape(sections, channels, LANES)
            value = jnp.dot(split[:, here], picks[kind], preferred_element_type=F32)
            value = value[:count] + value[count : 2 * count] + value[2 * count :]
            agg_out[:, :, there] = value.reshape(sections, -1, LANES)
    row = lax.broadcasted_iota(jnp.int32, (head_dim, channels), 0)
    lane = lax.broadcasted_iota(jnp.int32, (head_dim, channels), 1)
    spread = jnp.where(lane % head_dim == row, 1.0, 0.0).astype(BF16)
    across = lax.broadcasted_iota(jnp.int32, (channels, channels), 0) // head_dim
    along = lax.broadcasted_iota(jnp.int32, (channels, channels), 1) // head_dim
    for section in range(sections):
        for kind in range(3):
            tall = [group[section, 3 * h + kind] for h in range(channels // head_dim)]
            value = jnp.dot(jnp.concatenate(tall, axis=0), spread, preferred_element_type=F32)
            group_out[section, kind] = jnp.where(across == along, value, 0.0).astype(BF16)
    head_out[...] = jnp.zeros(head_out.shape, BF16)
    for a in range(3):
        rows = [head[a, b] for b in range(3)] + [jnp.zeros((4, channels), BF16)]
        head_out[a, 0:16, :] = jnp.concatenate(rows, axis=0)
    stores = [pltpu.make_async_copy(made[i], outs[i], sems.at[i]) for i in range(6)]
    for store in stores:
        store.start()
    for store in stores:
        store.wait()


def first_kernel(
    tile, head_dim, own, row_0, row_1, col_0, col_1, corner_0, corner_1, *refs
):
    weights, outs, scratch = refs[:9], refs[9:11], refs[11:]
    x_ref = scratch[0]
    rows, cols = tile
    below = REACH + rows
    even_row = lax.axis_index("row") & 1 == 0
    even_col = lax.axis_index("col") & 1 == 0

    def sides(part_0, part_1):
        right = jnp.where(even_col, part_0, part_1)
        left = jnp.where(even_col, part_1, part_0)
        return jnp.concatenate([right, left], axis=1)

    x_ref[REACH:below, 0:cols, :] = own[...]
    x_ref[REACH:below, cols : cols + 2 * SIDE, :] = sides(col_0[...], col_1[...])
    for row, corner, first in (
        (row_0, corner_0, jnp.where(even_row, below, 0)),
        (row_1, corner_1, jnp.where(even_row, 0, below)),
    ):
        here = pl.ds(first, REACH)
        x_ref[here, 0:cols, :] = row[...]
        x_ref[here, cols : cols + 2 * SIDE, :] = sides(corner[0:REACH], corner[REACH:])
    front(x_ref, weights, outs, scratch[1:], REACH, tile, head_dim, 0)


def second_kernel(tile, head_dim, mixed, query, payload, other, out_weight, out_bias, *refs):
    weights, outs, scratch = refs[:9], refs[9:11], refs[11:]
    x_ref = scratch[0]
    attend(
        mixed, query, (payload, other), out_weight, out_bias, scratch[1:3], head_dim, 0, x_ref
    )
    front(x_ref, weights, outs, scratch[3:], REACH - 3, tile, head_dim, 1)


def last_kernel(
    tile, head_dim, mixed, query, payload, other, out_weight, out_bias, head_weight, head_bias,
    map_out, boxes_out, x_ref, *held,
):
    rows, cols = tile
    width = cols + 2 * SIDE
    attend(
        mixed, query, (payload, other), out_weight, out_bias, held, head_dim, 1, x_ref
    )
    clear_outside(x_ref, 1, cols)
    map_out[...] = x_ref[1 : 1 + rows, 0:cols, :]
    total = None
    for a in range(3):
        part = lax.dot_general(
            flat(x_ref[a : a + rows]), head_weight[a], (((1,), (1,)), ((), ())),
            preferred_element_type=F32,
        )
        total = part if total is None else total + part
    total = total.reshape(rows, width, LANES)
    lane = lax.broadcasted_iota(jnp.int32, (width, LANES), 1) // 4
    shifted = [
        jnp.where(
            lane == 0,
            pltpu.roll(total[r], 1, 0),
            jnp.where(lane == 2, pltpu.roll(total[r], width - 1, 0), total[r]),
        )
        for r in range(rows)
    ]
    shifted = jnp.concatenate(shifted, axis=0)
    across = lax.broadcasted_iota(jnp.int32, (8, LANES), 0)
    along = lax.broadcasted_iota(jnp.int32, (8, LANES), 1)
    fold = jnp.where((along % 4 == across) & (along < 12), 1.0, 0.0)
    boxes = lax.dot_general(
        fold, shifted, (((1,), (1,)), ((), ())), precision=lax.Precision.HIGHEST,
        preferred_element_type=F32,
    )
    boxes = boxes[0:4] + head_bias[...]
    for r in range(rows):
        boxes_out[:, r, :] = boxes[:, r * width : r * width + cols]


def near():
    return pl.BlockSpec(memory_space=pltpu.VMEM)


def far():
    return pl.BlockSpec(memory_space=pltpu.HBM)


def digits(size, most):
    radices = []
    while size > 1:
        radix = next((r for r in range(min(most, size), 1, -1) if size % r == 0), size)
        radices.append(radix)
        size //= radix
    return radices


def partner(i, stride, radix, step):
    digit = (i // stride) % radix
    other = digit ^ step if radix & (radix - 1) == 0 else (digit + step) % radix
    return i + (other - digit) * stride


def sum_by_permutes(value):
    rounds = []
    for axis in ("row", "col"):
        stride = 1
        for radix in digits(lax.axis_size(axis), 4):
            rounds.append((axis, stride, radix))
            stride *= radix
    for axis, stride, radix in rounds:
        count = lax.axis_size(axis)
        others = [
            lax.ppermute(value, axis, [(i, partner(i, stride, radix, k)) for i in range(count)])
            for k in range(1, radix)
        ]
        if (axis, stride, radix) == rounds[-1] and radix == 2:
            return value, others[0]
        total = value.astype(F32)
        for other in others:
            total = total + other.astype(F32)
        value = total.astype(BF16)
    return value, jnp.zeros_like(value)


def digits(size, most):
    radices = []
    while size > 1:
        radix = next((r for r in range(min(most, size), 1, -1) if size % r == 0), size)
        radices.append(radix)
        size //= radix
    return radices


def pair_exchange(value, axis, first):
    count = lax.axis_size(axis)
    pairs = []
    for i in range(first, count - 1, 2):
        pairs += [(i, i + 1), (i + 1, i)]
    return lax.ppermute(value, axis, pairs)


def local(
    features,
    expand_weight,
    expand_bias,
    depth_weight,
    depth_bias,
    project_weight,
    project_bias,
    qkv_weight,
    aggregate_depth,
    aggregate_group,
    output_weight,
    output_bias,
    head_weight,
    head_bias,
):
    rows, cols, channels = features.shape
    head_dim = aggregate_group.shape[2]
    heads = channels // head_dim
    width = cols + 2 * SIDE
    tile = (rows, cols)
    wide = expand_weight.shape[2]

    def edges(value, dim, size, odd):
        far = value.shape[dim] - size
        return [
            lax.dynamic_slice_in_dim(value, jnp.where(odd == at, far, 0), size, dim) for at in (0, 1)
        ]

    odd_row = lax.axis_index("row") & 1
    odd_col = lax.axis_index("col") & 1
    low, high = edges(features, 1, SIDE, odd_col)
    col_1 = pair_exchange(high, "col", 1)
    col_0 = pair_exchange(low, "col", 0)
    low, high = edges(features, 0, REACH, odd_row)
    row_1 = pair_exchange(high, "row", 1)
    row_0 = pair_exchange(low, "row", 0)
    low, high = (
        jnp.concatenate(pieces, axis=0)
        for pieces in zip(edges(col_0, 0, REACH, odd_row), edges(col_1, 0, REACH, odd_row))
    )
    corner_1 = pair_exchange(high, "row", 1)
    corner_0 = pair_exchange(low, "row", 0)

    aggregate_depth = aggregate_depth.transpose(1, 2, 0, 3)
    depth_weight = depth_weight.transpose(1, 2, 0, 3)
    params = pltpu.CompilerParams(vmem_limit_bytes=24 * 2**20)
    made = [
        jax.ShapeDtypeStruct(qkv_weight.shape, BF16),
        jax.ShapeDtypeStruct((SECTIONS, 32, 3 * channels), F32),
        jax.ShapeDtypeStruct((SECTIONS, 3, channels, channels), BF16),
        jax.ShapeDtypeStruct((3, LANES, channels), BF16),
    ]
    biases = [jax.ShapeDtypeStruct(array.shape, F32) for array in (project_bias, output_bias)]
    qkv_weight, taps, group, head_weight, project_bias, output_bias = pl.pallas_call(
        functools.partial(prepare_kernel, head_dim),
        out_shape=made + biases,
        grid=(1,),
        in_specs=[near()] * 6,
        out_specs=[far()] * 6,
        scratch_shapes=[pltpu.VMEM(array.shape, array.dtype) for array in made]
        + [pltpu.VMEM((32 * SECTIONS, 3 * channels), F32), pltpu.SemaphoreType.DMA((6,))],
        compiler_params=params,
        cost_estimate=pl.CostEstimate(
            flops=2 * 10**9, bytes_accessed=4 * 10**6, transcendentals=0
        ),
        name="prepare",
    )(qkv_weight, aggregate_depth, aggregate_group, head_weight, project_bias, output_bias)

    weights = [
        expand_weight, expand_bias, depth_weight, depth_bias, project_weight, project_bias,
        qkv_weight, taps, group,
    ]
    weight_specs = [near()] * 5 + [far()] * 4

    def outs_of(count):
        return [
            jax.ShapeDtypeStruct((count, width, channels), BF16),
            jax.ShapeDtypeStruct((LANES + KEY_ROWS, LANES), BF16),
        ]

    def front_scratch(count):
        return [
            pltpu.VMEM((count, width, 256), BF16),
            pltpu.VMEM((count, width, 256), BF16),
            pltpu.VMEM(((count - 2) * width, channels), F32),
            pltpu.VMEM((count - 2, width, channels), BF16),
            pltpu.VMEM((rows + 4, width, 2 * channels), BF16),
            pltpu.VMEM((9, TILE, expand_weight.shape[2]), BF16),
            pltpu.VMEM((25, TILE, 2 * channels), BF16),
            pltpu.VMEM(project_bias.shape, F32),
            pltpu.VMEM((channels, 2 * channels), BF16),
            pltpu.VMEM((32, 2 * channels), F32),
            pltpu.VMEM((2, channels, channels), BF16),
            pltpu.SemaphoreType.DMA((5,)),
        ]

    def attend_scratch(count):
        return [
            pltpu.VMEM((count, width, channels), BF16),
            pltpu.VMEM(output_bias.shape, F32),
            pltpu.SemaphoreType.DMA,
        ]

    def queries(mixed, section):
        count = mixed.shape[0]
        units = (count - 4) * width * channels
        return pl.pallas_call(
            functools.partial(query_kernel, tile, section),
            out_shape=[
                jax.ShapeDtypeStruct((count - 4, width, 2 * channels), BF16),
                jax.ShapeDtypeStruct((count - 4, width, channels), BF16),
            ],
            grid=(1,),
            in_specs=[far()] * 4,
            out_specs=[near()] * 2,
            scratch_shapes=[
                pltpu.VMEM((count, width, channels), BF16),
                pltpu.VMEM((count, width, channels), BF16),
                pltpu.VMEM((channels, channels), BF16),
                pltpu.VMEM((32, channels), F32),
                pltpu.VMEM((channels, channels), BF16),
                pltpu.VMEM((25, TILE, channels), BF16),
                pltpu.SemaphoreType.DMA((4,)),
            ],
            compiler_params=params,
            cost_estimate=pl.CostEstimate(
                flops=8 * units * channels, bytes_accessed=8 * units, transcendentals=0
            ),
            name="queries",
        )(mixed, qkv_weight, taps, group)

    first_rows = rows + 2 * REACH
    mixed, payload = pl.pallas_call(
        functools.partial(first_kernel, tile, head_dim),
        out_shape=outs_of(first_rows - 2),
        grid=(1,),
        in_specs=[near()] * 7 + weight_specs,
        out_specs=[far(), near()],
        scratch_shapes=[pltpu.VMEM((first_rows, width, channels), BF16)]
        + front_scratch(first_rows),
        compiler_params=params,
        name="first",
    )(features, row_0, row_1, col_0, col_1, corner_0, corner_1, *weights)
    query, mixed = queries(mixed, 0)
    payload, other = sum_by_permutes(payload)

    second_rows = first_rows - 6
    mixed, payload = pl.pallas_call(
        functools.partial(second_kernel, tile, head_dim),
        out_shape=outs_of(second_rows - 2),
        grid=(1,),
        in_specs=[near()] * 5 + [far()] + weight_specs,
        out_specs=[far(), near()],
        scratch_shapes=attend_scratch(second_rows) + front_scratch(second_rows),
        compiler_params=params,
        name="second",
    )(mixed, query, payload, other, output_weight, output_bias, *weights)
    query, mixed = queries(mixed, 1)
    payload, other = sum_by_permutes(payload)

    return pl.pallas_call(
        functools.partial(last_kernel, tile, head_dim),
        out_shape=[
            jax.ShapeDtypeStruct((rows, cols, channels), BF16),
            jax.ShapeDtypeStruct((4, rows, cols), F32),
        ],
        grid=(1,),
        in_specs=[near()] * 5 + [far()] + [near()] * 2,
        out_specs=[near()] * 2,
        scratch_shapes=attend_scratch(rows + 2),
        compiler_params=params,
        name="last",
    )(
        mixed, query, payload, other, output_weight, output_bias, head_weight,
        head_bias.reshape(4, 1),
    )


def solution(mesh):
    return jax.shard_map(
        local,
        mesh=mesh,
        in_specs=(P("row", "col", None),) + (P(),) * 13,
        out_specs=(P("row", "col", None), P(None, "row", "col")),
        check_vma=False,
    )
```

```python
import functools

import jax
import jax.numpy as jnp
from jax import lax
from jax.experimental import pallas as pl
from jax.experimental.pallas import tpu as pltpu
from jax.sharding import PartitionSpec as P

SECTIONS = 2
LANES = 128
SIDE = 8
REACH = 7
KEY_ROWS = 16
TILE = 16
PARTS = 2
F32 = jnp.float32
BF16 = jnp.bfloat16


def six_hard_swish(value):
    return value * jnp.minimum(jnp.maximum(value + 3.0, 0.0), 6.0)


def parted(count, parts):
    cuts = [count * k // parts for k in range(parts + 1)]
    return [(a, b - a) for a, b in zip(cuts, cuts[1:]) if b > a]


def group_size(count, most):
    return next(n for n in range(min(most, count), 0, -1) if count % n == 0)


def by_groups(count, most, body):
    size = group_size(count, most)

    def group(index, carry):
        body(index * size, size)
        return carry

    lax.fori_loop(0, count // size, group, 0)


def clear_outside(ref, halo, cols):
    rows = ref.shape[0]
    row, col = lax.axis_index("row"), lax.axis_index("col")

    @pl.when(row == 0)
    def _():
        ref[0:halo] = jnp.zeros((halo,) + ref.shape[1:], ref.dtype)

    @pl.when(row == lax.axis_size("row") - 1)
    def _():
        ref[rows - halo : rows] = jnp.zeros((halo,) + ref.shape[1:], ref.dtype)

    @pl.when(col == 0)
    def _():
        ref[:, cols + SIDE : cols + 2 * SIDE, :] = jnp.zeros((rows, SIDE, ref.shape[2]), ref.dtype)

    @pl.when(col == lax.axis_size("col") - 1)
    def _():
        ref[:, cols : cols + SIDE, :] = jnp.zeros((rows, SIDE, ref.shape[2]), ref.dtype)


def flat(value):
    return value.reshape(-1, value.shape[-1])


def same_head(head_dim):
    across = lax.broadcasted_iota(jnp.int32, (LANES, LANES), 0) // head_dim
    along = lax.broadcasted_iota(jnp.int32, (LANES, LANES), 1) // head_dim
    return across == along


def depthwise_row(rows, taps, size, width):
    rows = [row.reshape(width // TILE, TILE, LANES) for row in rows]
    total = None
    for b in range(size):
        part = None
        for a in range(size):
            term = rows[a] * taps(a, b)[None]
            part = term if part is None else part + term
        part = part.reshape(width, LANES).astype(F32)
        if b != size // 2:
            part = pltpu.roll(part, (size // 2 - b) % width, 0)
        total = part if total is None else total + part
    return total


def spread_taps(agg, wide_agg):
    for index in range(25):
        taps = agg[index : index + 1, :]
        wide_agg[index] = jnp.broadcast_to(taps, (TILE, taps.shape[1])).astype(BF16)


def aggregated(source, wide_agg, group, low, first, size, channels):
    width = source.shape[1]
    scaled = []
    for r in range(size):
        lanes = []
        for lane in range(low, low + channels, LANES):
            here = slice(lane, lane + LANES)
            value = depthwise_row(
                [source[first + r + a, :, here] for a in range(5)],
                lambda a, b: wide_agg[5 * a + b, :, here], 5, width,
            )
            lanes.append(value.astype(BF16))
        scaled.append(jnp.concatenate(lanes, axis=1))
    value = jnp.dot(jnp.concatenate(scaled, axis=0), group, preferred_element_type=F32)
    return value.astype(BF16).reshape(size, width, channels)


def front(x_ref, weights, outs, scratch, halo, tile, head_dim, section):
    expand, expand_bias, depth, depth_bias, project = weights[:5]
    mixed_out, payload_out = outs
    (
        hidden_0, hidden_1, total, mixed, pairs, wide_depth, wide_agg,
        project_bias, pair_weight, agg, group, sems,
    ) = scratch
    channels = x_ref.shape[2]
    tail = pl.ds(channels, 2 * channels)
    loads = [
        pltpu.make_async_copy(weights[5], project_bias, sems.at[0]),
        pltpu.make_async_copy(weights[6].at[section, :, tail], pair_weight, sems.at[1]),
        pltpu.make_async_copy(weights[7].at[section, :, tail], agg, sems.at[2]),
        pltpu.make_async_copy(weights[8].at[section, pl.ds(1, 2)], group, sems.at[3]),
    ]
    for load in loads:
        load.start()
    rows, width, channels = x_ref.shape
    tile_rows, tile_cols = tile
    inner = rows - 2
    chunk = hidden_0.shape[2]
    chunks = expand.shape[2] // chunk
    for index in range(9):
        taps = depth[index // 3, index % 3, section : section + 1, :] * (1.0 / 6.0)
        wide_depth[index] = jnp.broadcast_to(taps, (TILE, taps.shape[1])).astype(BF16)
    total[...] = 6.0 * flat(x_ref[1 : rows - 1]).astype(F32)

    def expand_rows(out, at, first, size):
        value = jnp.dot(
            flat(x_ref[first : first + size]), expand[section, :, pl.ds(at, chunk)],
            preferred_element_type=F32,
        )
        value = (value + expand_bias[section : section + 1, pl.ds(at, chunk)]).astype(BF16)
        out[first : first + size] = six_hard_swish(value).reshape(size, width, chunk)

    def spread_rows(hidden, at, first, size):
        spread = []
        for r in range(first, first + size):
            lanes = []
            for lane in range(0, chunk, LANES):
                here = pl.ds(pl.multiple_of(at + lane, LANES), LANES)
                value = depthwise_row(
                    [hidden[r + a, :, lane : lane + LANES] for a in range(3)],
                    lambda a, b: wide_depth[3 * a + b, :, here], 3, width,
                )
                value = (value + depth_bias[section : section + 1, here]).astype(BF16)
                lanes.append(six_hard_swish(value))
            spread.append(jnp.concatenate(lanes, axis=1))
        pixels = slice(first * width, (first + size) * width)
        total[pixels] += jnp.dot(
            jnp.concatenate(spread, axis=0), project[section, pl.ds(at, chunk), :],
            preferred_element_type=F32,
        )

    def stage(index, current, following):
        at = pl.multiple_of(index * chunk, chunk)
        ahead = pl.multiple_of(jnp.minimum(index + 1, chunks - 1) * chunk, chunk)
        for (first, size), (from_row, count) in zip(parted(inner, PARTS), parted(rows, PARTS)):
            expand_rows(following, ahead, from_row, count)
            spread_rows(current, at, first, size)
        clear_outside(following, halo, tile_cols)

    for first, size in parted(rows, PARTS):
        expand_rows(hidden_0, 0, first, size)
    clear_outside(hidden_0, halo, tile_cols)

    def two_stages(index, carry):
        stage(2 * index, hidden_0, hidden_1)
        stage(2 * index + 1, hidden_1, hidden_0)
        return carry

    lax.fori_loop(0, chunks // 2, two_stages, 0)
    loads[0].wait()
    value = total[...] * (1.0 / 6.0) + project_bias[section : section + 1, :]
    mixed[...] = value.astype(BF16).reshape(inner, width, channels)
    store = pltpu.make_async_copy(mixed, mixed_out, sems.at[4])
    store.start()
    for load in loads[1:]:
        load.wait()
    spread_taps(agg, wide_agg)
    around = halo - 1
    first_pair = around - 2
    count = tile_rows + 4
    for first, size in parted(count, PARTS - 1):
        at = first_pair + first
        value = jnp.dot(
            flat(mixed[at : at + size]), pair_weight[...], preferred_element_type=F32
        )
        pairs[first : first + size] = value.astype(BF16).reshape(size, width, 2 * channels)
    clear_outside(pairs, 2, tile_cols)
    size = group_size(tile_rows, 4)

    def summed(key, value):
        key = jnp.maximum(flat(key[:, 0:tile_cols]), 0.0)
        value = flat(value[:, 0:tile_cols])
        products = [
            lax.dot_general(
                key[:, lane : lane + LANES], value[:, lane : lane + LANES],
                (((0,), (0,)), ((), ())), preferred_element_type=F32,
            )
            for lane in range(0, channels, LANES)
        ]
        return products, jnp.sum(key.astype(F32), axis=0, keepdims=True)

    mine = slice(2, 2 + tile_rows)
    products, sums = summed(
        pairs[mine, :, 0:channels], pairs[mine, :, channels : 2 * channels]
    )

    def grouped_rows(index, carry):
        at = index * size
        more, sums = summed(
            aggregated(pairs, wide_agg, group[0], 0, at, size, channels),
            aggregated(pairs, wide_agg, group[1], channels, at, size, channels),
        )
        return [a + b for a, b in zip(carry[0], more)], carry[1] + sums

    more, more_sums = lax.fori_loop(
        0, tile_rows // size, grouped_rows,
        ([jnp.zeros((LANES, LANES), F32) for _ in products], jnp.zeros_like(sums)),
    )
    products = products + more
    sums = jnp.concatenate([sums, more_sums], axis=1)
    same = same_head(head_dim)
    summary = jnp.zeros((LANES, LANES), F32)
    key_sums = []
    for index, product in enumerate(products):
        product = jnp.where(same, product, 0.0)
        if index:
            product = pltpu.roll(product, index * head_dim, 1)
        summary = summary + product
        key_sums.append(sums[:, index * LANES : (index + 1) * LANES])
    key_sums.append(jnp.zeros((KEY_ROWS - len(products), LANES), F32))
    payload_out[0:LANES, :] = summary.astype(BF16)
    payload_out[LANES : LANES + KEY_ROWS, :] = jnp.concatenate(key_sums, axis=0).astype(BF16)
    store.wait()


def query_kernel(
    tile, section, mixed_in, qkv_weight, taps, groups, query, mixed_out,
    mixed, centre, weight, agg, group, wide_agg, sems,
):
    rows, width, channels = mixed.shape
    head = pl.ds(0, channels)
    loads = [
        pltpu.make_async_copy(mixed_in, mixed, sems.at[0]),
        pltpu.make_async_copy(qkv_weight.at[section, :, head], weight, sems.at[1]),
        pltpu.make_async_copy(taps.at[section, :, head], agg, sems.at[2]),
        pltpu.make_async_copy(groups.at[section, 0], group, sems.at[3]),
    ]
    for load in loads:
        load.start()
    for load in loads:
        load.wait()
    mixed_out[...] = mixed[2 : rows - 2]
    spread_taps(agg, wide_agg)
    for first, size in parted(rows, PARTS):
        value = jnp.dot(
            flat(mixed[first : first + size]), weight[...], preferred_element_type=F32
        )
        centre[first : first + size] = value.astype(BF16).reshape(size, width, channels)
    clear_outside(centre, (rows - tile[0]) // 2, tile[1])

    def query_rows(first, size):
        here = pl.ds(first, size)
        query[here, :, 0:channels] = jnp.maximum(centre[pl.ds(first + 2, size)], 0.0)
        grouped = aggregated(centre, wide_agg, group[...], 0, first, size, channels)
        query[here, :, channels : 2 * channels] = jnp.maximum(grouped, 0.0)

    by_groups(rows - 4, 5, query_rows)


def attend(
    mixed_ref, query_ref, payloads, weight, bias_in, held, head_dim, section, x_ref
):
    rows, width, channels = x_ref.shape
    bias, sem = held
    load = pltpu.make_async_copy(bias_in, bias, sem)
    load.start()
    same = same_head(head_dim)
    square = (LANES, LANES)
    diagonal = lax.broadcasted_iota(jnp.int32, square, 0) == lax.broadcasted_iota(
        jnp.int32, square, 1
    )
    ones = jnp.where(same, 1.0, 0.0).astype(BF16)
    nothing = jnp.zeros(square, BF16)
    payload = payloads[0][...].astype(F32)
    for part in payloads[1:]:
        payload = payload + part[...].astype(F32)
    packed = payload[0:LANES]
    count = 2 * channels // LANES
    summaries, sums = [], []
    for index in range(count):
        summary = packed if index == 0 else pltpu.roll(packed, LANES - index * head_dim, 1)
        summaries.append(jnp.where(same, summary, 0.0).astype(BF16))
        keys = payload[LANES + index : LANES + index + 1]
        keys = jnp.where(diagonal, keys, 0.0).astype(BF16)
        sums.append(jnp.dot(keys, ones, preferred_element_type=F32).astype(BF16))

    def paired(blocks, index):
        return jnp.concatenate(
            [
                jnp.concatenate([blocks[index], nothing], axis=1),
                jnp.concatenate([nothing, blocks[index + 1]], axis=1),
            ],
            axis=0,
        )

    summaries = [paired(summaries, index) for index in range(0, count, 2)]
    sums = [paired(sums, index) for index in range(0, count, 2)]
    step = 2 * LANES
    load.wait()

    def attend_rows(first, size):
        query = flat(query_ref[pl.ds(first, size)])
        parts = []
        for branch in range(count // 2):
            part = query[:, branch * step : (branch + 1) * step]
            numer = jnp.dot(part, summaries[branch], preferred_element_type=F32)
            denom = jnp.dot(part, sums[branch], preferred_element_type=F32) + 1e-6
            inverse = pl.reciprocal(denom, approx=True)
            inverse = inverse * (2.0 - denom * inverse)
            parts.append((numer * inverse).astype(BF16))
        value = jnp.dot(
            jnp.concatenate(parts, axis=1), weight[section], preferred_element_type=F32
        )
        value = value + bias[section : section + 1, :]
        value = value + flat(mixed_ref[pl.ds(first, size)]).astype(F32)
        x_ref[pl.ds(first, size)] = value.astype(BF16).reshape(size, width, channels)

    by_groups(rows, 5, attend_rows)


def tap(section, a, b):
    at = 32 * section + 5 * a + b
    return slice(at, at + 1)


def prepare_kernel(head_dim, qkv, agg, group, head, project_bias, output_bias, *refs):
    outs, made, taps, sems = refs[:6], refs[6:10], refs[10], refs[11]
    qkv_out, agg_out, group_out, head_out = made
    made = [*made, project_bias, output_bias]
    sections, channels, wide = qkv.shape
    half = 3 * LANES
    heads = LANES // head_dim
    src = lax.broadcasted_iota(jnp.int32, (half, LANES), 0)
    dst = lax.broadcasted_iota(jnp.int32, (half, LANES), 1)
    first = (dst // head_dim) * 3 * head_dim + dst % head_dim
    picks = [jnp.where(src == first + k * head_dim, 1.0, 0.0).astype(BF16) for k in range(3)]
    taps[...] = jnp.zeros(taps.shape, F32)
    for section in range(sections):
        for a in range(5):
            for b in range(5):
                taps[tap(section, a, b), :] = agg[a, b, section : section + 1, :]
    rest = taps[...]
    high = rest.astype(BF16)
    rest = rest - high.astype(F32)
    middle = rest.astype(BF16)
    low = (rest - middle.astype(F32)).astype(BF16)
    split = jnp.concatenate([high, middle, low], axis=0)
    count = taps.shape[0]
    weights = qkv[...].reshape(sections * channels, wide)
    for part in range(wide // half):
        here = slice(part * half, (part + 1) * half)
        for kind in range(3):
            to = kind * channels + part * LANES
            there = slice(to, to + LANES)
            value = jnp.dot(weights[:, here], picks[kind], preferred_element_type=F32)
            qkv_out[:, :, there] = value.astype(BF16).reshape(sections, channels, LANES)
            value = jnp.dot(split[:, here], picks[kind], preferred_element_type=F32)
            value = value[:count] + value[count : 2 * count] + value[2 * count :]
            agg_out[:, :, there] = value.reshape(sections, -1, LANES)
    row = lax.broadcasted_iota(jnp.int32, (head_dim, channels), 0)
    lane = lax.broadcasted_iota(jnp.int32, (head_dim, channels), 1)
    spread = jnp.where(lane % head_dim == row, 1.0, 0.0).astype(BF16)
    across = lax.broadcasted_iota(jnp.int32, (channels, channels), 0) // head_dim
    along = lax.broadcasted_iota(jnp.int32, (channels, channels), 1) // head_dim
    for section in range(sections):
        for kind in range(3):
            tall = [group[section, 3 * h + kind] for h in range(channels // head_dim)]
            value = jnp.dot(jnp.concatenate(tall, axis=0), spread, preferred_element_type=F32)
            group_out[section, kind] = jnp.where(across == along, value, 0.0).astype(BF16)
    head_out[...] = jnp.zeros(head_out.shape, BF16)
    for a in range(3):
        rows = [head[a, b] for b in range(3)] + [jnp.zeros((4, channels), BF16)]
        head_out[a, 0:16, :] = jnp.concatenate(rows, axis=0)
    stores = [pltpu.make_async_copy(made[i], outs[i], sems.at[i]) for i in range(6)]
    for store in stores:
        store.start()
    for store in stores:
        store.wait()


def first_kernel(
    tile, head_dim, own, row_0, row_1, col_0, col_1, corner_0, corner_1, *refs
):
    weights, outs, scratch = refs[:9], refs[9:11], refs[11:]
    x_ref = scratch[0]
    rows, cols = tile
    below = REACH + rows
    even_row = lax.axis_index("row") & 1 == 0
    even_col = lax.axis_index("col") & 1 == 0

    def sides(part_0, part_1):
        right = jnp.where(even_col, part_0, part_1)
        left = jnp.where(even_col, part_1, part_0)
        return jnp.concatenate([right, left], axis=1)

    x_ref[REACH:below, 0:cols, :] = own[...]
    x_ref[REACH:below, cols : cols + 2 * SIDE, :] = sides(col_0[...], col_1[...])
    for row, corner, first in (
        (row_0, corner_0, jnp.where(even_row, below, 0)),
        (row_1, corner_1, jnp.where(even_row, 0, below)),
    ):
        here = pl.ds(first, REACH)
        x_ref[here, 0:cols, :] = row[...]
        x_ref[here, cols : cols + 2 * SIDE, :] = sides(corner[0:REACH], corner[REACH:])
    front(x_ref, weights, outs, scratch[1:], REACH, tile, head_dim, 0)


def second_kernel(tile, head_dim, mixed, query, payload, other, out_weight, out_bias, *refs):
    weights, outs, scratch = refs[:9], refs[9:11], refs[11:]
    x_ref = scratch[0]
    attend(
        mixed, query, (payload, other), out_weight, out_bias, scratch[1:3], head_dim, 0, x_ref
    )
    front(x_ref, weights, outs, scratch[3:], REACH - 3, tile, head_dim, 1)


def last_kernel(
    tile, head_dim, mixed, query, payload, other, out_weight, out_bias, head_weight, head_bias,
    map_out, boxes_out, x_ref, *held,
):
    rows, cols = tile
    width = cols + 2 * SIDE
    attend(
        mixed, query, (payload, other), out_weight, out_bias, held, head_dim, 1, x_ref
    )
    clear_outside(x_ref, 1, cols)
    map_out[...] = x_ref[1 : 1 + rows, 0:cols, :]
    total = None
    for a in range(3):
        part = lax.dot_general(
            flat(x_ref[a : a + rows]), head_weight[a], (((1,), (1,)), ((), ())),
            preferred_element_type=F32,
        )
        total = part if total is None else total + part
    total = total.reshape(rows, width, LANES)
    lane = lax.broadcasted_iota(jnp.int32, (width, LANES), 1) // 4
    shifted = [
        jnp.where(
            lane == 0,
            pltpu.roll(total[r], 1, 0),
            jnp.where(lane == 2, pltpu.roll(total[r], width - 1, 0), total[r]),
        )
        for r in range(rows)
    ]
    shifted = jnp.concatenate(shifted, axis=0)
    across = lax.broadcasted_iota(jnp.int32, (8, LANES), 0)
    along = lax.broadcasted_iota(jnp.int32, (8, LANES), 1)
    fold = jnp.where((along % 4 == across) & (along < 12), 1.0, 0.0)
    boxes = lax.dot_general(
        fold, shifted, (((1,), (1,)), ((), ())), precision=lax.Precision.HIGHEST,
        preferred_element_type=F32,
    )
    boxes = boxes[0:4] + head_bias[...]
    for r in range(rows):
        boxes_out[:, r, :] = boxes[:, r * width : r * width + cols]


def near():
    return pl.BlockSpec(memory_space=pltpu.VMEM)


def far():
    return pl.BlockSpec(memory_space=pltpu.HBM)


def digits(size, most):
    radices = []
    while size > 1:
        radix = next((r for r in range(min(most, size), 1, -1) if size % r == 0), size)
        radices.append(radix)
        size //= radix
    return radices


def partner(i, stride, radix, step):
    digit = (i // stride) % radix
    other = digit ^ step if radix & (radix - 1) == 0 else (digit + step) % radix
    return i + (other - digit) * stride


def sum_by_permutes(value):
    rounds = []
    for axis in ("row", "col"):
        stride = 1
        for radix in digits(lax.axis_size(axis), 4):
            rounds.append((axis, stride, radix))
            stride *= radix
    for axis, stride, radix in rounds:
        count = lax.axis_size(axis)
        others = [
            lax.ppermute(value, axis, [(i, partner(i, stride, radix, k)) for i in range(count)])
            for k in range(1, radix)
        ]
        if (axis, stride, radix) == rounds[-1] and radix == 2:
            return value, others[0]
        total = value.astype(F32)
        for other in others:
            total = total + other.astype(F32)
        value = total.astype(BF16)
    return value, jnp.zeros_like(value)


def digits(size, most):
    radices = []
    while size > 1:
        radix = next((r for r in range(min(most, size), 1, -1) if size % r == 0), size)
        radices.append(radix)
        size //= radix
    return radices


def pair_exchange(value, axis, first):
    count = lax.axis_size(axis)
    pairs = []
    for i in range(first, count - 1, 2):
        pairs += [(i, i + 1), (i + 1, i)]
    return lax.ppermute(value, axis, pairs)


def local(
    features,
    expand_weight,
    expand_bias,
    depth_weight,
    depth_bias,
    project_weight,
    project_bias,
    qkv_weight,
    aggregate_depth,
    aggregate_group,
    output_weight,
    output_bias,
    head_weight,
    head_bias,
):
    rows, cols, channels = features.shape
    head_dim = aggregate_group.shape[2]
    heads = channels // head_dim
    width = cols + 2 * SIDE
    tile = (rows, cols)
    wide = expand_weight.shape[2]

    def edges(value, dim, size, odd):
        far = value.shape[dim] - size
        return [
            lax.dynamic_slice_in_dim(value, jnp.where(odd == at, far, 0), size, dim) for at in (0, 1)
        ]

    odd_row = lax.axis_index("row") & 1
    odd_col = lax.axis_index("col") & 1
    low, high = edges(features, 1, SIDE, odd_col)
    col_1 = pair_exchange(high, "col", 1)
    col_0 = pair_exchange(low, "col", 0)
    low, high = edges(features, 0, REACH, odd_row)
    row_1 = pair_exchange(high, "row", 1)
    row_0 = pair_exchange(low, "row", 0)
    aggregate_depth = aggregate_depth.transpose(1, 2, 0, 3)
    depth_weight = depth_weight.transpose(1, 2, 0, 3)
    params = pltpu.CompilerParams(vmem_limit_bytes=24 * 2**20)
    made = [
        jax.ShapeDtypeStruct(qkv_weight.shape, BF16),
        jax.ShapeDtypeStruct((SECTIONS, 32, 3 * channels), F32),
        jax.ShapeDtypeStruct((SECTIONS, 3, channels, channels), BF16),
        jax.ShapeDtypeStruct((3, LANES, channels), BF16),
    ]
    biases = [jax.ShapeDtypeStruct(array.shape, F32) for array in (project_bias, output_bias)]
    qkv_weight, taps, group, head_weight, project_bias, output_bias = pl.pallas_call(
        functools.partial(prepare_kernel, head_dim),
        out_shape=made + biases,
        grid=(1,),
        in_specs=[near()] * 6,
        out_specs=[far()] * 6,
        scratch_shapes=[pltpu.VMEM(array.shape, array.dtype) for array in made]
        + [pltpu.VMEM((32 * SECTIONS, 3 * channels), F32), pltpu.SemaphoreType.DMA((6,))],
        compiler_params=params,
        cost_estimate=pl.CostEstimate(
            flops=2 * 10**9, bytes_accessed=4 * 10**6, transcendentals=0
        ),
        name="prepare",
    )(qkv_weight, aggregate_depth, aggregate_group, head_weight, project_bias, output_bias)

    col_0, col_1, taps = lax.optimization_barrier((col_0, col_1, taps))
    low, high = (
        jnp.concatenate(pieces, axis=0)
        for pieces in zip(edges(col_0, 0, REACH, odd_row), edges(col_1, 0, REACH, odd_row))
    )
    corner_1 = pair_exchange(high, "row", 1)
    corner_0 = pair_exchange(low, "row", 0)

    weights = [
        expand_weight, expand_bias, depth_weight, depth_bias, project_weight, project_bias,
        qkv_weight, taps, group,
    ]
    weight_specs = [near()] * 5 + [far()] * 4

    def outs_of(count):
        return [
            jax.ShapeDtypeStruct((count, width, channels), BF16),
            jax.ShapeDtypeStruct((LANES + KEY_ROWS, LANES), BF16),
        ]

    def front_scratch(count):
        return [
            pltpu.VMEM((count, width, 256), BF16),
            pltpu.VMEM((count, width, 256), BF16),
            pltpu.VMEM(((count - 2) * width, channels), F32),
            pltpu.VMEM((count - 2, width, channels), BF16),
            pltpu.VMEM((rows + 4, width, 2 * channels), BF16),
            pltpu.VMEM((9, TILE, expand_weight.shape[2]), BF16),
            pltpu.VMEM((25, TILE, 2 * channels), BF16),
            pltpu.VMEM(project_bias.shape, F32),
            pltpu.VMEM((channels, 2 * channels), BF16),
            pltpu.VMEM((32, 2 * channels), F32),
            pltpu.VMEM((2, channels, channels), BF16),
            pltpu.SemaphoreType.DMA((5,)),
        ]

    def attend_scratch(count):
        return [
            pltpu.VMEM((count, width, channels), BF16),
            pltpu.VMEM(output_bias.shape, F32),
            pltpu.SemaphoreType.DMA,
        ]

    def queries(mixed, section):
        count = mixed.shape[0]
        units = (count - 4) * width * channels
        return pl.pallas_call(
            functools.partial(query_kernel, tile, section),
            out_shape=[
                jax.ShapeDtypeStruct((count - 4, width, 2 * channels), BF16),
                jax.ShapeDtypeStruct((count - 4, width, channels), BF16),
            ],
            grid=(1,),
            in_specs=[far()] * 4,
            out_specs=[near()] * 2,
            scratch_shapes=[
                pltpu.VMEM((count, width, channels), BF16),
                pltpu.VMEM((count, width, channels), BF16),
                pltpu.VMEM((channels, channels), BF16),
                pltpu.VMEM((32, channels), F32),
                pltpu.VMEM((channels, channels), BF16),
                pltpu.VMEM((25, TILE, channels), BF16),
                pltpu.SemaphoreType.DMA((4,)),
            ],
            compiler_params=params,
            cost_estimate=pl.CostEstimate(
                flops=8 * units * channels, bytes_accessed=8 * units, transcendentals=0
            ),
            name="queries",
        )(mixed, qkv_weight, taps, group)

    first_rows = rows + 2 * REACH
    mixed, payload = pl.pallas_call(
        functools.partial(first_kernel, tile, head_dim),
        out_shape=outs_of(first_rows - 2),
        grid=(1,),
        in_specs=[near()] * 7 + weight_specs,
        out_specs=[far(), near()],
        scratch_shapes=[pltpu.VMEM((first_rows, width, channels), BF16)]
        + front_scratch(first_rows),
        compiler_params=params,
        name="first",
    )(features, row_0, row_1, col_0, col_1, corner_0, corner_1, *weights)
    query, mixed = queries(mixed, 0)
    payload, other = sum_by_permutes(payload)

    second_rows = first_rows - 6
    mixed, payload = pl.pallas_call(
        functools.partial(second_kernel, tile, head_dim),
        out_shape=outs_of(second_rows - 2),
        grid=(1,),
        in_specs=[near()] * 5 + [far()] + weight_specs,
        out_specs=[far(), near()],
        scratch_shapes=attend_scratch(second_rows) + front_scratch(second_rows),
        compiler_params=params,
        name="second",
    )(mixed, query, payload, other, output_weight, output_bias, *weights)
    query, mixed = queries(mixed, 1)
    payload, other = sum_by_permutes(payload)

    return pl.pallas_call(
        functools.partial(last_kernel, tile, head_dim),
        out_shape=[
            jax.ShapeDtypeStruct((rows, cols, channels), BF16),
            jax.ShapeDtypeStruct((4, rows, cols), F32),
        ],
        grid=(1,),
        in_specs=[near()] * 5 + [far()] + [near()] * 2,
        out_specs=[near()] * 2,
        scratch_shapes=attend_scratch(rows + 2),
        compiler_params=params,
        name="last",
    )(
        mixed, query, payload, other, output_weight, output_bias, head_weight,
        head_bias.reshape(4, 1),
    )


def solution(mesh):
    return jax.shard_map(
        local,
        mesh=mesh,
        in_specs=(P("row", "col", None),) + (P(),) * 13,
        out_specs=(P("row", "col", None), P(None, "row", "col")),
        check_vma=False,
    )
```

```python
import functools

import jax
import jax.numpy as jnp
from jax import lax
from jax.experimental import pallas as pl
from jax.experimental.pallas import tpu as pltpu
from jax.sharding import PartitionSpec as P

SECTIONS = 2
LANES = 128
SIDE = 8
REACH = 7
KEY_ROWS = 16
TILE = 16
PARTS = 2
F32 = jnp.float32
BF16 = jnp.bfloat16


def six_hard_swish(value):
    return value * jnp.minimum(jnp.maximum(value + 3.0, 0.0), 6.0)


def parted(count, parts):
    cuts = [count * k // parts for k in range(parts + 1)]
    return [(a, b - a) for a, b in zip(cuts, cuts[1:]) if b > a]


def group_size(count, most):
    return next(n for n in range(min(most, count), 0, -1) if count % n == 0)


def by_groups(count, most, body):
    size = group_size(count, most)

    def group(index, carry):
        body(index * size, size)
        return carry

    lax.fori_loop(0, count // size, group, 0)


def clear_outside(ref, halo, cols):
    rows = ref.shape[0]
    row, col = lax.axis_index("row"), lax.axis_index("col")

    @pl.when(row == 0)
    def _():
        ref[0:halo] = jnp.zeros((halo,) + ref.shape[1:], ref.dtype)

    @pl.when(row == lax.axis_size("row") - 1)
    def _():
        ref[rows - halo : rows] = jnp.zeros((halo,) + ref.shape[1:], ref.dtype)

    @pl.when(col == 0)
    def _():
        ref[:, cols + SIDE : cols + 2 * SIDE, :] = jnp.zeros((rows, SIDE, ref.shape[2]), ref.dtype)

    @pl.when(col == lax.axis_size("col") - 1)
    def _():
        ref[:, cols : cols + SIDE, :] = jnp.zeros((rows, SIDE, ref.shape[2]), ref.dtype)


def flat(value):
    return value.reshape(-1, value.shape[-1])


def same_head(head_dim):
    across = lax.broadcasted_iota(jnp.int32, (LANES, LANES), 0) // head_dim
    along = lax.broadcasted_iota(jnp.int32, (LANES, LANES), 1) // head_dim
    return across == along


def depthwise_row(rows, taps, size, width):
    rows = [row.reshape(width // TILE, TILE, LANES) for row in rows]
    total = None
    for b in range(size):
        part = None
        for a in range(size):
            term = rows[a] * taps(a, b)[None]
            part = term if part is None else part + term
        part = part.reshape(width, LANES).astype(F32)
        if b != size // 2:
            part = pltpu.roll(part, (size // 2 - b) % width, 0)
        total = part if total is None else total + part
    return total


def spread_taps(agg, wide_agg):
    for index in range(25):
        taps = agg[index : index + 1, :]
        wide_agg[index] = jnp.broadcast_to(taps, (TILE, taps.shape[1])).astype(BF16)


def aggregated(source, wide_agg, group, low, first, size, channels):
    width = source.shape[1]
    scaled = []
    for r in range(size):
        lanes = []
        for lane in range(low, low + channels, LANES):
            here = slice(lane, lane + LANES)
            value = depthwise_row(
                [source[first + r + a, :, here] for a in range(5)],
                lambda a, b: wide_agg[5 * a + b, :, here], 5, width,
            )
            lanes.append(value.astype(BF16))
        scaled.append(jnp.concatenate(lanes, axis=1))
    value = jnp.dot(jnp.concatenate(scaled, axis=0), group, preferred_element_type=F32)
    return value.astype(BF16).reshape(size, width, channels)


def front(x_ref, weights, outs, scratch, halo, tile, head_dim, section):
    expand, expand_bias, depth, depth_bias, project = weights[:5]
    mixed_out, payload_out = outs
    (
        hidden_0, hidden_1, total, mixed, pairs, wide_depth, wide_agg,
        project_bias, pair_weight, agg, group, sems,
    ) = scratch
    channels = x_ref.shape[2]
    tail = pl.ds(channels, 2 * channels)
    loads = [
        pltpu.make_async_copy(weights[5], project_bias, sems.at[0]),
        pltpu.make_async_copy(weights[6].at[section, :, tail], pair_weight, sems.at[1]),
        pltpu.make_async_copy(weights[7].at[section, :, tail], agg, sems.at[2]),
        pltpu.make_async_copy(weights[8].at[section, pl.ds(1, 2)], group, sems.at[3]),
    ]
    for load in loads:
        load.start()
    rows, width, channels = x_ref.shape
    tile_rows, tile_cols = tile
    inner = rows - 2
    chunk = hidden_0.shape[2]
    chunks = expand.shape[2] // chunk
    for index in range(9):
        taps = depth[index // 3, index % 3, section : section + 1, :] * (1.0 / 6.0)
        wide_depth[index] = jnp.broadcast_to(taps, (TILE, taps.shape[1])).astype(BF16)
    total[...] = 6.0 * flat(x_ref[1 : rows - 1]).astype(F32)

    def expand_rows(out, at, first, size):
        value = jnp.dot(
            flat(x_ref[first : first + size]), expand[section, :, pl.ds(at, chunk)],
            preferred_element_type=F32,
        )
        value = (value + expand_bias[section : section + 1, pl.ds(at, chunk)]).astype(BF16)
        out[first : first + size] = six_hard_swish(value).reshape(size, width, chunk)

    def spread_rows(hidden, at, first, size):
        spread = []
        for r in range(first, first + size):
            lanes = []
            for lane in range(0, chunk, LANES):
                here = pl.ds(pl.multiple_of(at + lane, LANES), LANES)
                value = depthwise_row(
                    [hidden[r + a, :, lane : lane + LANES] for a in range(3)],
                    lambda a, b: wide_depth[3 * a + b, :, here], 3, width,
                )
                value = (value + depth_bias[section : section + 1, here]).astype(BF16)
                lanes.append(six_hard_swish(value))
            spread.append(jnp.concatenate(lanes, axis=1))
        pixels = slice(first * width, (first + size) * width)
        total[pixels] += jnp.dot(
            jnp.concatenate(spread, axis=0), project[section, pl.ds(at, chunk), :],
            preferred_element_type=F32,
        )

    def stage(index, current, following):
        at = pl.multiple_of(index * chunk, chunk)
        ahead = pl.multiple_of(jnp.minimum(index + 1, chunks - 1) * chunk, chunk)
        for (first, size), (from_row, count) in zip(parted(inner, PARTS), parted(rows, PARTS)):
            expand_rows(following, ahead, from_row, count)
            spread_rows(current, at, first, size)
        clear_outside(following, halo, tile_cols)

    for first, size in parted(rows, PARTS):
        expand_rows(hidden_0, 0, first, size)
    clear_outside(hidden_0, halo, tile_cols)

    def two_stages(index, carry):
        stage(2 * index, hidden_0, hidden_1)
        stage(2 * index + 1, hidden_1, hidden_0)
        return carry

    lax.fori_loop(0, chunks // 2, two_stages, 0)
    loads[0].wait()
    value = total[...] * (1.0 / 6.0) + project_bias[section : section + 1, :]
    mixed[...] = value.astype(BF16).reshape(inner, width, channels)
    store = pltpu.make_async_copy(mixed, mixed_out, sems.at[4])
    store.start()
    for load in loads[1:]:
        load.wait()
    spread_taps(agg, wide_agg)
    around = halo - 1
    first_pair = around - 2
    count = tile_rows + 4
    for first, size in parted(count, PARTS - 1):
        at = first_pair + first
        value = jnp.dot(
            flat(mixed[at : at + size]), pair_weight[...], preferred_element_type=F32
        )
        pairs[first : first + size] = value.astype(BF16).reshape(size, width, 2 * channels)
    clear_outside(pairs, 2, tile_cols)
    size = group_size(tile_rows, 4)

    def summed(key, value):
        key = jnp.maximum(flat(key[:, 0:tile_cols]), 0.0)
        value = flat(value[:, 0:tile_cols])
        products = [
            lax.dot_general(
                key[:, lane : lane + LANES], value[:, lane : lane + LANES],
                (((0,), (0,)), ((), ())), preferred_element_type=F32,
            )
            for lane in range(0, channels, LANES)
        ]
        return products, jnp.sum(key.astype(F32), axis=0, keepdims=True)

    mine = slice(2, 2 + tile_rows)
    products, sums = summed(
        pairs[mine, :, 0:channels], pairs[mine, :, channels : 2 * channels]
    )

    def grouped_rows(index, carry):
        at = index * size
        more, sums = summed(
            aggregated(pairs, wide_agg, group[0], 0, at, size, channels),
            aggregated(pairs, wide_agg, group[1], channels, at, size, channels),
        )
        return [a + b for a, b in zip(carry[0], more)], carry[1] + sums

    more, more_sums = lax.fori_loop(
        0, tile_rows // size, grouped_rows,
        ([jnp.zeros((LANES, LANES), F32) for _ in products], jnp.zeros_like(sums)),
    )
    products = products + more
    sums = jnp.concatenate([sums, more_sums], axis=1)
    same = same_head(head_dim)
    summary = jnp.zeros((LANES, LANES), F32)
    key_sums = []
    for index, product in enumerate(products):
        product = jnp.where(same, product, 0.0)
        if index:
            product = pltpu.roll(product, index * head_dim, 1)
        summary = summary + product
        key_sums.append(sums[:, index * LANES : (index + 1) * LANES])
    key_sums.append(jnp.zeros((KEY_ROWS - len(products), LANES), F32))
    payload_out[0:LANES, :] = summary.astype(BF16)
    payload_out[LANES : LANES + KEY_ROWS, :] = jnp.concatenate(key_sums, axis=0).astype(BF16)
    store.wait()


def query_kernel(
    tile, section, mixed_in, qkv_weight, taps, groups, query, mixed_out,
    mixed, centre, weight, agg, group, wide_agg, sems,
):
    rows, width, channels = mixed.shape
    head = pl.ds(0, channels)
    loads = [
        pltpu.make_async_copy(mixed_in, mixed, sems.at[0]),
        pltpu.make_async_copy(qkv_weight.at[section, :, head], weight, sems.at[1]),
        pltpu.make_async_copy(taps.at[section, :, head], agg, sems.at[2]),
        pltpu.make_async_copy(groups.at[section, 0], group, sems.at[3]),
    ]
    for load in loads:
        load.start()
    for load in loads:
        load.wait()
    mixed_out[...] = mixed[2 : rows - 2]
    spread_taps(agg, wide_agg)
    for first, size in parted(rows, PARTS):
        value = jnp.dot(
            flat(mixed[first : first + size]), weight[...], preferred_element_type=F32
        )
        centre[first : first + size] = value.astype(BF16).reshape(size, width, channels)
    clear_outside(centre, (rows - tile[0]) // 2, tile[1])

    def query_rows(first, size):
        here = pl.ds(first, size)
        query[here, :, 0:channels] = jnp.maximum(centre[pl.ds(first + 2, size)], 0.0)
        grouped = aggregated(centre, wide_agg, group[...], 0, first, size, channels)
        query[here, :, channels : 2 * channels] = jnp.maximum(grouped, 0.0)

    by_groups(rows - 4, 5, query_rows)


def attend(
    mixed_ref, query_ref, payloads, weight, bias_in, held, head_dim, section, x_ref
):
    rows, width, channels = x_ref.shape
    bias, sem = held
    load = pltpu.make_async_copy(bias_in, bias, sem)
    load.start()
    same = same_head(head_dim)
    square = (LANES, LANES)
    diagonal = lax.broadcasted_iota(jnp.int32, square, 0) == lax.broadcasted_iota(
        jnp.int32, square, 1
    )
    ones = jnp.where(same, 1.0, 0.0).astype(BF16)
    nothing = jnp.zeros(square, BF16)
    payload = payloads[0][...].astype(F32)
    for part in payloads[1:]:
        payload = payload + part[...].astype(F32)
    packed = payload[0:LANES]
    count = 2 * channels // LANES
    summaries, sums = [], []
    for index in range(count):
        summary = packed if index == 0 else pltpu.roll(packed, LANES - index * head_dim, 1)
        summaries.append(jnp.where(same, summary, 0.0).astype(BF16))
        keys = payload[LANES + index : LANES + index + 1]
        keys = jnp.where(diagonal, keys, 0.0).astype(BF16)
        sums.append(jnp.dot(keys, ones, preferred_element_type=F32).astype(BF16))

    def paired(blocks, index):
        return jnp.concatenate(
            [
                jnp.concatenate([blocks[index], nothing], axis=1),
                jnp.concatenate([nothing, blocks[index + 1]], axis=1),
            ],
            axis=0,
        )

    summaries = [paired(summaries, index) for index in range(0, count, 2)]
    sums = [paired(sums, index) for index in range(0, count, 2)]
    step = 2 * LANES
    load.wait()

    def attend_rows(first, size):
        query = flat(query_ref[pl.ds(first, size)])
        parts = []
        for branch in range(count // 2):
            part = query[:, branch * step : (branch + 1) * step]
            numer = jnp.dot(part, summaries[branch], preferred_element_type=F32)
            denom = jnp.dot(part, sums[branch], preferred_element_type=F32) + 1e-6
            inverse = pl.reciprocal(denom, approx=True)
            inverse = inverse * (2.0 - denom * inverse)
            parts.append((numer * inverse).astype(BF16))
        value = jnp.dot(
            jnp.concatenate(parts, axis=1), weight[section], preferred_element_type=F32
        )
        value = value + bias[section : section + 1, :]
        value = value + flat(mixed_ref[pl.ds(first, size)]).astype(F32)
        x_ref[pl.ds(first, size)] = value.astype(BF16).reshape(size, width, channels)

    by_groups(rows, 5, attend_rows)


def tap(section, a, b):
    at = 32 * section + 5 * a + b
    return slice(at, at + 1)


def prepare_kernel(head_dim, qkv, agg, group, head, project_bias, output_bias, *refs):
    outs, made, taps, sems = refs[:6], refs[6:10], refs[10], refs[11]
    qkv_out, agg_out, group_out, head_out = made
    made = [*made, project_bias, output_bias]
    sections, channels, wide = qkv.shape
    half = 3 * LANES
    heads = LANES // head_dim
    src = lax.broadcasted_iota(jnp.int32, (half, LANES), 0)
    dst = lax.broadcasted_iota(jnp.int32, (half, LANES), 1)
    first = (dst // head_dim) * 3 * head_dim + dst % head_dim
    picks = [jnp.where(src == first + k * head_dim, 1.0, 0.0).astype(BF16) for k in range(3)]
    taps[...] = jnp.zeros(taps.shape, F32)
    for section in range(sections):
        for a in range(5):
            for b in range(5):
                taps[tap(section, a, b), :] = agg[a, b, section : section + 1, :]
    rest = taps[...]
    high = rest.astype(BF16)
    rest = rest - high.astype(F32)
    middle = rest.astype(BF16)
    low = (rest - middle.astype(F32)).astype(BF16)
    split = jnp.concatenate([high, middle, low], axis=0)
    count = taps.shape[0]
    weights = qkv[...].reshape(sections * channels, wide)
    for part in range(wide // half):
        here = slice(part * half, (part + 1) * half)
        for kind in range(3):
            to = kind * channels + part * LANES
            there = slice(to, to + LANES)
            value = jnp.dot(weights[:, here], picks[kind], preferred_element_type=F32)
            qkv_out[:, :, there] = value.astype(BF16).reshape(sections, channels, LANES)
            value = jnp.dot(split[:, here], picks[kind], preferred_element_type=F32)
            value = value[:count] + value[count : 2 * count] + value[2 * count :]
            agg_out[:, :, there] = value.reshape(sections, -1, LANES)
    row = lax.broadcasted_iota(jnp.int32, (head_dim, channels), 0)
    lane = lax.broadcasted_iota(jnp.int32, (head_dim, channels), 1)
    spread = jnp.where(lane % head_dim == row, 1.0, 0.0).astype(BF16)
    across = lax.broadcasted_iota(jnp.int32, (channels, channels), 0) // head_dim
    along = lax.broadcasted_iota(jnp.int32, (channels, channels), 1) // head_dim
    for section in range(sections):
        for kind in range(3):
            tall = [group[section, 3 * h + kind] for h in range(channels // head_dim)]
            value = jnp.dot(jnp.concatenate(tall, axis=0), spread, preferred_element_type=F32)
            group_out[section, kind] = jnp.where(across == along, value, 0.0).astype(BF16)
    head_out[...] = jnp.zeros(head_out.shape, BF16)
    for a in range(3):
        rows = [head[a, b] for b in range(3)] + [jnp.zeros((4, channels), BF16)]
        head_out[a, 0:16, :] = jnp.concatenate(rows, axis=0)
    stores = [pltpu.make_async_copy(made[i], outs[i], sems.at[i]) for i in range(6)]
    for store in stores:
        store.start()
    for store in stores:
        store.wait()


def first_kernel(
    tile, head_dim, own, col_1, col_0, row_1, row_0, corner_1, corner_0, *refs
):
    weights, outs, scratch = refs[:9], refs[9:11], refs[11:]
    x_ref = scratch[0]
    rows, cols = tile
    below = REACH + rows
    even_row = lax.axis_index("row") & 1 == 0
    even_col = lax.axis_index("col") & 1 == 0

    def sides(part_0, part_1):
        right = jnp.where(even_col, part_0, part_1)
        left = jnp.where(even_col, part_1, part_0)
        return jnp.concatenate([right, left], axis=1)

    x_ref[REACH:below, 0:cols, :] = own[...]
    x_ref[REACH:below, cols : cols + 2 * SIDE, :] = sides(col_0[...], col_1[...])
    for row, corner, first in (
        (row_0, corner_0, jnp.where(even_row, below, 0)),
        (row_1, corner_1, jnp.where(even_row, 0, below)),
    ):
        here = pl.ds(first, REACH)
        x_ref[here, 0:cols, :] = row[...]
        x_ref[here, cols : cols + 2 * SIDE, :] = sides(corner[0:REACH], corner[REACH:])
    front(x_ref, weights, outs, scratch[1:], REACH, tile, head_dim, 0)


def second_kernel(tile, head_dim, mixed, query, payload, other, out_weight, out_bias, *refs):
    weights, outs, scratch = refs[:9], refs[9:11], refs[11:]
    x_ref = scratch[0]
    attend(
        mixed, query, (payload, other), out_weight, out_bias, scratch[1:3], head_dim, 0, x_ref
    )
    front(x_ref, weights, outs, scratch[3:], REACH - 3, tile, head_dim, 1)


def last_kernel(
    tile, head_dim, mixed, query, payload, other, out_weight, out_bias, head_weight, head_bias,
    map_out, boxes_out, x_ref, *held,
):
    rows, cols = tile
    width = cols + 2 * SIDE
    attend(
        mixed, query, (payload, other), out_weight, out_bias, held, head_dim, 1, x_ref
    )
    clear_outside(x_ref, 1, cols)
    map_out[...] = x_ref[1 : 1 + rows, 0:cols, :]
    total = None
    for a in range(3):
        part = lax.dot_general(
            flat(x_ref[a : a + rows]), head_weight[a], (((1,), (1,)), ((), ())),
            preferred_element_type=F32,
        )
        total = part if total is None else total + part
    total = total.reshape(rows, width, LANES)
    lane = lax.broadcasted_iota(jnp.int32, (width, LANES), 1) // 4
    shifted = [
        jnp.where(
            lane == 0,
            pltpu.roll(total[r], 1, 0),
            jnp.where(lane == 2, pltpu.roll(total[r], width - 1, 0), total[r]),
        )
        for r in range(rows)
    ]
    shifted = jnp.concatenate(shifted, axis=0)
    across = lax.broadcasted_iota(jnp.int32, (8, LANES), 0)
    along = lax.broadcasted_iota(jnp.int32, (8, LANES), 1)
    fold = jnp.where((along % 4 == across) & (along < 12), 1.0, 0.0)
    boxes = lax.dot_general(
        fold, shifted, (((1,), (1,)), ((), ())), precision=lax.Precision.HIGHEST,
        preferred_element_type=F32,
    )
    boxes = boxes[0:4] + head_bias[...]
    for r in range(rows):
        boxes_out[:, r, :] = boxes[:, r * width : r * width + cols]


def near():
    return pl.BlockSpec(memory_space=pltpu.VMEM)


def far():
    return pl.BlockSpec(memory_space=pltpu.HBM)


def digits(size, most):
    radices = []
    while size > 1:
        radix = next((r for r in range(min(most, size), 1, -1) if size % r == 0), size)
        radices.append(radix)
        size //= radix
    return radices


def partner(i, stride, radix, step):
    digit = (i // stride) % radix
    other = digit ^ step if radix & (radix - 1) == 0 else (digit + step) % radix
    return i + (other - digit) * stride


def sum_by_permutes(value):
    rounds = []
    for axis in ("row", "col"):
        stride = 1
        for radix in digits(lax.axis_size(axis), 4):
            rounds.append((axis, stride, radix))
            stride *= radix
    for axis, stride, radix in rounds:
        count = lax.axis_size(axis)
        others = [
            lax.ppermute(value, axis, [(i, partner(i, stride, radix, k)) for i in range(count)])
            for k in range(1, radix)
        ]
        if (axis, stride, radix) == rounds[-1] and radix == 2:
            return value, others[0]
        total = value.astype(F32)
        for other in others:
            total = total + other.astype(F32)
        value = total.astype(BF16)
    return value, jnp.zeros_like(value)


def digits(size, most):
    radices = []
    while size > 1:
        radix = next((r for r in range(min(most, size), 1, -1) if size % r == 0), size)
        radices.append(radix)
        size //= radix
    return radices


def pair_exchange(value, axis, first):
    count = lax.axis_size(axis)
    pairs = []
    for i in range(first, count - 1, 2):
        pairs += [(i, i + 1), (i + 1, i)]
    return lax.ppermute(value, axis, pairs)


def local(
    features,
    expand_weight,
    expand_bias,
    depth_weight,
    depth_bias,
    project_weight,
    project_bias,
    qkv_weight,
    aggregate_depth,
    aggregate_group,
    output_weight,
    output_bias,
    head_weight,
    head_bias,
):
    rows, cols, channels = features.shape
    head_dim = aggregate_group.shape[2]
    heads = channels // head_dim
    width = cols + 2 * SIDE
    tile = (rows, cols)
    wide = expand_weight.shape[2]

    def edges(value, dim, size, odd):
        far = value.shape[dim] - size
        return [
            lax.dynamic_slice_in_dim(value, jnp.where(odd == at, far, 0), size, dim) for at in (0, 1)
        ]

    odd_row = lax.axis_index("row") & 1
    odd_col = lax.axis_index("col") & 1
    low, high = edges(features, 1, SIDE, odd_col)
    col_1 = pair_exchange(high, "col", 1)
    col_0 = pair_exchange(low, "col", 0)
    low, high = edges(features, 0, REACH, odd_row)
    row_1 = pair_exchange(high, "row", 1)
    row_0 = pair_exchange(low, "row", 0)
    low, high = (
        jnp.concatenate(pieces, axis=0)
        for pieces in zip(edges(col_0, 0, REACH, odd_row), edges(col_1, 0, REACH, odd_row))
    )
    corner_1 = pair_exchange(high, "row", 1)
    corner_0 = pair_exchange(low, "row", 0)

    aggregate_depth = aggregate_depth.transpose(1, 2, 0, 3)
    depth_weight = depth_weight.transpose(1, 2, 0, 3)
    params = pltpu.CompilerParams(vmem_limit_bytes=24 * 2**20)
    made = [
        jax.ShapeDtypeStruct(qkv_weight.shape, BF16),
        jax.ShapeDtypeStruct((SECTIONS, 32, 3 * channels), F32),
        jax.ShapeDtypeStruct((SECTIONS, 3, channels, channels), BF16),
        jax.ShapeDtypeStruct((3, LANES, channels), BF16),
    ]
    biases = [jax.ShapeDtypeStruct(array.shape, F32) for array in (project_bias, output_bias)]
    qkv_weight, taps, group, head_weight, project_bias, output_bias = pl.pallas_call(
        functools.partial(prepare_kernel, head_dim),
        out_shape=made + biases,
        grid=(1,),
        in_specs=[near()] * 6,
        out_specs=[far()] * 6,
        scratch_shapes=[pltpu.VMEM(array.shape, array.dtype) for array in made]
        + [pltpu.VMEM((32 * SECTIONS, 3 * channels), F32), pltpu.SemaphoreType.DMA((6,))],
        compiler_params=params,
        cost_estimate=pl.CostEstimate(
            flops=2 * 10**9, bytes_accessed=4 * 10**6, transcendentals=0
        ),
        name="prepare",
    )(qkv_weight, aggregate_depth, aggregate_group, head_weight, project_bias, output_bias)

    weights = [
        expand_weight, expand_bias, depth_weight, depth_bias, project_weight, project_bias,
        qkv_weight, taps, group,
    ]
    weight_specs = [near()] * 5 + [far()] * 4

    def outs_of(count):
        return [
            jax.ShapeDtypeStruct((count, width, channels), BF16),
            jax.ShapeDtypeStruct((LANES + KEY_ROWS, LANES), BF16),
        ]

    def front_scratch(count):
        return [
            pltpu.VMEM((count, width, 256), BF16),
            pltpu.VMEM((count, width, 256), BF16),
            pltpu.VMEM(((count - 2) * width, channels), F32),
            pltpu.VMEM((count - 2, width, channels), BF16),
            pltpu.VMEM((rows + 4, width, 2 * channels), BF16),
            pltpu.VMEM((9, TILE, expand_weight.shape[2]), BF16),
            pltpu.VMEM((25, TILE, 2 * channels), BF16),
            pltpu.VMEM(project_bias.shape, F32),
            pltpu.VMEM((channels, 2 * channels), BF16),
            pltpu.VMEM((32, 2 * channels), F32),
            pltpu.VMEM((2, channels, channels), BF16),
            pltpu.SemaphoreType.DMA((5,)),
        ]

    def attend_scratch(count):
        return [
            pltpu.VMEM((count, width, channels), BF16),
            pltpu.VMEM(output_bias.shape, F32),
            pltpu.SemaphoreType.DMA,
        ]

    def queries(mixed, section):
        count = mixed.shape[0]
        units = (count - 4) * width * channels
        return pl.pallas_call(
            functools.partial(query_kernel, tile, section),
            out_shape=[
                jax.ShapeDtypeStruct((count - 4, width, 2 * channels), BF16),
                jax.ShapeDtypeStruct((count - 4, width, channels), BF16),
            ],
            grid=(1,),
            in_specs=[far()] * 4,
            out_specs=[near()] * 2,
            scratch_shapes=[
                pltpu.VMEM((count, width, channels), BF16),
                pltpu.VMEM((count, width, channels), BF16),
                pltpu.VMEM((channels, channels), BF16),
                pltpu.VMEM((32, channels), F32),
                pltpu.VMEM((channels, channels), BF16),
                pltpu.VMEM((25, TILE, channels), BF16),
                pltpu.SemaphoreType.DMA((4,)),
            ],
            compiler_params=params,
            cost_estimate=pl.CostEstimate(
                flops=8 * units * channels, bytes_accessed=8 * units, transcendentals=0
            ),
            name="queries",
        )(mixed, qkv_weight, taps, group)

    first_rows = rows + 2 * REACH
    mixed, payload = pl.pallas_call(
        functools.partial(first_kernel, tile, head_dim),
        out_shape=outs_of(first_rows - 2),
        grid=(1,),
        in_specs=[near()] * 7 + weight_specs,
        out_specs=[far(), near()],
        scratch_shapes=[pltpu.VMEM((first_rows, width, channels), BF16)]
        + front_scratch(first_rows),
        compiler_params=params,
        name="first",
    )(features, col_1, col_0, row_1, row_0, corner_1, corner_0, *weights)
    query, mixed = queries(mixed, 0)
    payload, other = sum_by_permutes(payload)

    second_rows = first_rows - 6
    mixed, payload = pl.pallas_call(
        functools.partial(second_kernel, tile, head_dim),
        out_shape=outs_of(second_rows - 2),
        grid=(1,),
        in_specs=[near()] * 5 + [far()] + weight_specs,
        out_specs=[far(), near()],
        scratch_shapes=attend_scratch(second_rows) + front_scratch(second_rows),
        compiler_params=params,
        name="second",
    )(mixed, query, payload, other, output_weight, output_bias, *weights)
    query, mixed = queries(mixed, 1)
    payload, other = sum_by_permutes(payload)

    return pl.pallas_call(
        functools.partial(last_kernel, tile, head_dim),
        out_shape=[
            jax.ShapeDtypeStruct((rows, cols, channels), BF16),
            jax.ShapeDtypeStruct((4, rows, cols), F32),
        ],
        grid=(1,),
        in_specs=[near()] * 5 + [far()] + [near()] * 2,
        out_specs=[near()] * 2,
        scratch_shapes=attend_scratch(rows + 2),
        compiler_params=params,
        name="last",
    )(
        mixed, query, payload, other, output_weight, output_bias, head_weight,
        head_bias.reshape(4, 1),
    )


def solution(mesh):
    return jax.shard_map(
        local,
        mesh=mesh,
        in_specs=(P("row", "col", None),) + (P(),) * 13,
        out_specs=(P("row", "col", None), P(None, "row", "col")),
        check_vma=False,
    )
```

```python
import functools

import jax
import jax.numpy as jnp
from jax import lax
from jax.experimental import pallas as pl
from jax.experimental.pallas import tpu as pltpu
from jax.sharding import PartitionSpec as P

SECTIONS = 2
LANES = 128
SIDE = 8
REACH = 7
KEY_ROWS = 16
TILE = 16
PARTS = 2
F32 = jnp.float32
BF16 = jnp.bfloat16


def six_hard_swish(value, bound=6.0):
    return value * jnp.minimum(jnp.maximum(value + 3.0, 0.0), bound)


def parted(count, parts):
    cuts = [count * k // parts for k in range(parts + 1)]
    return [(a, b - a) for a, b in zip(cuts, cuts[1:]) if b > a]


def group_size(count, most):
    return next(n for n in range(min(most, count), 0, -1) if count % n == 0)


def by_groups(count, most, body):
    size = group_size(count, most)

    def group(index, carry):
        body(index * size, size)
        return carry

    lax.fori_loop(0, count // size, group, 0)


def clear_outside(ref, halo, cols):
    rows = ref.shape[0]
    row, col = lax.axis_index("row"), lax.axis_index("col")

    @pl.when(row == 0)
    def _():
        ref[0:halo] = jnp.zeros((halo,) + ref.shape[1:], ref.dtype)

    @pl.when(row == lax.axis_size("row") - 1)
    def _():
        ref[rows - halo : rows] = jnp.zeros((halo,) + ref.shape[1:], ref.dtype)

    @pl.when(col == 0)
    def _():
        ref[:, cols + SIDE : cols + 2 * SIDE, :] = jnp.zeros((rows, SIDE, ref.shape[2]), ref.dtype)

    @pl.when(col == lax.axis_size("col") - 1)
    def _():
        ref[:, cols : cols + SIDE, :] = jnp.zeros((rows, SIDE, ref.shape[2]), ref.dtype)


def set_bounds(bounds, cols):
    shape = bounds.shape[1:]
    column = lax.broadcasted_iota(jnp.int32, shape, 0)
    row, col = lax.axis_index("row"), lax.axis_index("col")
    start = jnp.where(col == lax.axis_size("col") - 1, cols, cols + SIDE)
    stop = jnp.where(col == 0, cols + 2 * SIDE, cols + SIDE)
    level = jnp.where((column >= start) & (column < stop), 0.0, 6.0)
    bounds[0] = jnp.where(row == 0, 0.0, level).astype(BF16)
    bounds[1] = level.astype(BF16)
    bounds[2] = jnp.where(row == lax.axis_size("row") - 1, 0.0, level).astype(BF16)


def flat(value):
    return value.reshape(-1, value.shape[-1])


def same_head(head_dim):
    across = lax.broadcasted_iota(jnp.int32, (LANES, LANES), 0) // head_dim
    along = lax.broadcasted_iota(jnp.int32, (LANES, LANES), 1) // head_dim
    return across == along


def depthwise_row(rows, taps, size, width):
    rows = [row.reshape(width // TILE, TILE, LANES) for row in rows]
    total = None
    for b in range(size):
        part = None
        for a in range(size):
            term = rows[a] * taps(a, b)[None]
            part = term if part is None else part + term
        part = part.reshape(width, LANES).astype(F32)
        if b != size // 2:
            part = pltpu.roll(part, (size // 2 - b) % width, 0)
        total = part if total is None else total + part
    return total


def spread_taps(agg, wide_agg):
    for index in range(25):
        taps = agg[index : index + 1, :]
        wide_agg[index] = jnp.broadcast_to(taps, (TILE, taps.shape[1])).astype(BF16)


def aggregated(source, wide_agg, group, low, first, size, channels):
    width = source.shape[1]
    scaled = []
    for r in range(size):
        lanes = []
        for lane in range(low, low + channels, LANES):
            here = slice(lane, lane + LANES)
            value = depthwise_row(
                [source[first + r + a, :, here] for a in range(5)],
                lambda a, b: wide_agg[5 * a + b, :, here], 5, width,
            )
            lanes.append(value.astype(BF16))
        scaled.append(jnp.concatenate(lanes, axis=1))
    value = jnp.dot(jnp.concatenate(scaled, axis=0), group, preferred_element_type=F32)
    return value.astype(BF16).reshape(size, width, channels)


def front(x_ref, weights, outs, scratch, halo, tile, head_dim, section):
    expand, expand_bias, depth, depth_bias, project = weights[:5]
    mixed_out, payload_out = outs
    (
        hidden_0, hidden_1, total, bounds, mixed, pairs, wide_depth, wide_agg,
        project_bias, pair_weight, agg, group, sems,
    ) = scratch
    channels = x_ref.shape[2]
    tail = pl.ds(channels, 2 * channels)
    loads = [
        pltpu.make_async_copy(weights[5], project_bias, sems.at[0]),
        pltpu.make_async_copy(weights[6].at[section, :, tail], pair_weight, sems.at[1]),
        pltpu.make_async_copy(weights[7].at[section, :, tail], agg, sems.at[2]),
        pltpu.make_async_copy(weights[8].at[section, pl.ds(1, 2)], group, sems.at[3]),
    ]
    for load in loads:
        load.start()
    rows, width, channels = x_ref.shape
    tile_rows, tile_cols = tile
    inner = rows - 2
    chunk = hidden_0.shape[2]
    chunks = expand.shape[2] // chunk
    for index in range(9):
        taps = depth[index // 3, index % 3, section : section + 1, :] * (1.0 / 6.0)
        wide_depth[index] = jnp.broadcast_to(taps, (TILE, taps.shape[1])).astype(BF16)
    set_bounds(bounds, tile_cols)
    total[...] = 6.0 * flat(x_ref[1 : rows - 1]).astype(F32)

    def expand_rows(out, at, first, size):
        value = jnp.dot(
            flat(x_ref[first : first + size]), expand[section, :, pl.ds(at, chunk)],
            preferred_element_type=F32,
        )
        value = (value + expand_bias[section : section + 1, pl.ds(at, chunk)]).astype(BF16)
        for r in range(size):
            which = 0 if first + r < halo else 2 if first + r >= rows - halo else 1
            part = value[r * width : (r + 1) * width]
            out[first + r] = six_hard_swish(part, bounds[which])

    def spread_rows(hidden, at, first, size):
        spread = []
        for r in range(first, first + size):
            lanes = []
            for lane in range(0, chunk, LANES):
                here = pl.ds(pl.multiple_of(at + lane, LANES), LANES)
                value = depthwise_row(
                    [hidden[r + a, :, lane : lane + LANES] for a in range(3)],
                    lambda a, b: wide_depth[3 * a + b, :, here], 3, width,
                )
                value = (value + depth_bias[section : section + 1, here]).astype(BF16)
                lanes.append(six_hard_swish(value))
            spread.append(jnp.concatenate(lanes, axis=1))
        pixels = slice(first * width, (first + size) * width)
        total[pixels] += jnp.dot(
            jnp.concatenate(spread, axis=0), project[section, pl.ds(at, chunk), :],
            preferred_element_type=F32,
        )

    def stage(index, current, following):
        at = pl.multiple_of(index * chunk, chunk)
        ahead = pl.multiple_of(jnp.minimum(index + 1, chunks - 1) * chunk, chunk)
        for (first, size), (from_row, count) in zip(parted(inner, PARTS), parted(rows, PARTS)):
            if following is not None:
                expand_rows(following, ahead, from_row, count)
            spread_rows(current, at, first, size)

    for first, size in parted(rows, PARTS):
        expand_rows(hidden_0, 0, first, size)

    def two_stages(index, carry):
        stage(2 * index, hidden_0, hidden_1)
        stage(2 * index + 1, hidden_1, hidden_0)
        return carry

    if section == 0:
        for index in range(0, chunks, 2):
            stage(index, hidden_0, hidden_1)
            stage(index + 1, hidden_1, hidden_0 if index + 2 < chunks else None)
    else:
        lax.fori_loop(0, chunks // 2, two_stages, 0)
    loads[0].wait()
    value = total[...] * (1.0 / 6.0) + project_bias[section : section + 1, :]
    mixed[...] = value.astype(BF16).reshape(inner, width, channels)
    store = pltpu.make_async_copy(mixed, mixed_out, sems.at[4])
    store.start()
    for load in loads[1:]:
        load.wait()
    spread_taps(agg, wide_agg)
    around = halo - 1
    first_pair = around - 2
    count = tile_rows + 4
    for first, size in parted(count, PARTS - 1):
        at = first_pair + first
        value = jnp.dot(
            flat(mixed[at : at + size]), pair_weight[...], preferred_element_type=F32
        )
        pairs[first : first + size] = value.astype(BF16).reshape(size, width, 2 * channels)
    clear_outside(pairs, 2, tile_cols)
    size = group_size(tile_rows, 4)

    def summed(key, value):
        key = jnp.maximum(flat(key[:, 0:tile_cols]), 0.0)
        value = flat(value[:, 0:tile_cols])
        products = [
            lax.dot_general(
                key[:, lane : lane + LANES], value[:, lane : lane + LANES],
                (((0,), (0,)), ((), ())), preferred_element_type=F32,
            )
            for lane in range(0, channels, LANES)
        ]
        return products, jnp.sum(key.astype(F32), axis=0, keepdims=True)

    mine = slice(2, 2 + tile_rows)
    products, sums = summed(
        pairs[mine, :, 0:channels], pairs[mine, :, channels : 2 * channels]
    )

    def grouped_rows(index, carry):
        at = index * size
        more, sums = summed(
            aggregated(pairs, wide_agg, group[0], 0, at, size, channels),
            aggregated(pairs, wide_agg, group[1], channels, at, size, channels),
        )
        return [a + b for a, b in zip(carry[0], more)], carry[1] + sums

    more, more_sums = lax.fori_loop(
        0, tile_rows // size, grouped_rows,
        ([jnp.zeros((LANES, LANES), F32) for _ in products], jnp.zeros_like(sums)),
    )
    products = products + more
    sums = jnp.concatenate([sums, more_sums], axis=1)
    same = same_head(head_dim)
    summary = jnp.zeros((LANES, LANES), F32)
    key_sums = []
    for index, product in enumerate(products):
        product = jnp.where(same, product, 0.0)
        if index:
            product = pltpu.roll(product, index * head_dim, 1)
        summary = summary + product
        key_sums.append(sums[:, index * LANES : (index + 1) * LANES])
    key_sums.append(jnp.zeros((KEY_ROWS - len(products), LANES), F32))
    payload_out[0:LANES, :] = summary.astype(BF16)
    payload_out[LANES : LANES + KEY_ROWS, :] = jnp.concatenate(key_sums, axis=0).astype(BF16)
    store.wait()


def query_kernel(
    tile, section, mixed_in, qkv_weight, taps, groups, query, mixed_out,
    mixed, centre, weight, agg, group, wide_agg, sems,
):
    rows, width, channels = mixed.shape
    head = pl.ds(0, channels)
    loads = [
        pltpu.make_async_copy(mixed_in, mixed, sems.at[0]),
        pltpu.make_async_copy(qkv_weight.at[section, :, head], weight, sems.at[1]),
        pltpu.make_async_copy(taps.at[section, :, head], agg, sems.at[2]),
        pltpu.make_async_copy(groups.at[section, 0], group, sems.at[3]),
    ]
    for load in loads:
        load.start()
    for load in loads:
        load.wait()
    mixed_out[...] = mixed[2 : rows - 2]
    spread_taps(agg, wide_agg)
    for first, size in parted(rows, PARTS):
        value = jnp.dot(
            flat(mixed[first : first + size]), weight[...], preferred_element_type=F32
        )
        centre[first : first + size] = value.astype(BF16).reshape(size, width, channels)
    clear_outside(centre, (rows - tile[0]) // 2, tile[1])

    def query_rows(first, size):
        here = pl.ds(first, size)
        query[here, :, 0:channels] = jnp.maximum(centre[pl.ds(first + 2, size)], 0.0)
        grouped = aggregated(centre, wide_agg, group[...], 0, first, size, channels)
        query[here, :, channels : 2 * channels] = jnp.maximum(grouped, 0.0)

    by_groups(rows - 4, 5, query_rows)


def attend(
    mixed_ref, query_ref, payloads, weight, bias_in, held, head_dim, section, x_ref
):
    rows, width, channels = x_ref.shape
    bias, sem = held
    load = pltpu.make_async_copy(bias_in, bias, sem)
    load.start()
    same = same_head(head_dim)
    square = (LANES, LANES)
    diagonal = lax.broadcasted_iota(jnp.int32, square, 0) == lax.broadcasted_iota(
        jnp.int32, square, 1
    )
    ones = jnp.where(same, 1.0, 0.0).astype(BF16)
    nothing = jnp.zeros(square, BF16)
    payload = payloads[0][...].astype(F32)
    for part in payloads[1:]:
        payload = payload + part[...].astype(F32)
    packed = payload[0:LANES]
    count = 2 * channels // LANES
    summaries, sums = [], []
    for index in range(count):
        summary = packed if index == 0 else pltpu.roll(packed, LANES - index * head_dim, 1)
        summaries.append(jnp.where(same, summary, 0.0).astype(BF16))
        keys = payload[LANES + index : LANES + index + 1]
        keys = jnp.where(diagonal, keys, 0.0).astype(BF16)
        sums.append(jnp.dot(keys, ones, preferred_element_type=F32).astype(BF16))

    def paired(blocks, index):
        return jnp.concatenate(
            [
                jnp.concatenate([blocks[index], nothing], axis=1),
                jnp.concatenate([nothing, blocks[index + 1]], axis=1),
            ],
            axis=0,
        )

    summaries = [paired(summaries, index) for index in range(0, count, 2)]
    sums = [paired(sums, index) for index in range(0, count, 2)]
    step = 2 * LANES
    load.wait()

    def attend_rows(first, size):
        query = flat(query_ref[pl.ds(first, size)])
        parts = []
        for branch in range(count // 2):
            part = query[:, branch * step : (branch + 1) * step]
            numer = jnp.dot(part, summaries[branch], preferred_element_type=F32)
            denom = jnp.dot(part, sums[branch], preferred_element_type=F32) + 1e-6
            inverse = pl.reciprocal(denom, approx=True)
            inverse = inverse * (2.0 - denom * inverse)
            parts.append((numer * inverse).astype(BF16))
        value = jnp.dot(
            jnp.concatenate(parts, axis=1), weight[section], preferred_element_type=F32
        )
        value = value + bias[section : section + 1, :]
        value = value + flat(mixed_ref[pl.ds(first, size)]).astype(F32)
        x_ref[pl.ds(first, size)] = value.astype(BF16).reshape(size, width, channels)

    by_groups(rows, 5, attend_rows)


def tap(section, a, b):
    at = 32 * section + 5 * a + b
    return slice(at, at + 1)


def prepare_kernel(head_dim, qkv, agg, group, head, project_bias, output_bias, *refs):
    outs, made, taps, sems = refs[:6], refs[6:10], refs[10], refs[11]
    qkv_out, agg_out, group_out, head_out = made
    made = [*made, project_bias, output_bias]
    sections, channels, wide = qkv.shape
    half = 3 * LANES
    heads = LANES // head_dim
    src = lax.broadcasted_iota(jnp.int32, (half, LANES), 0)
    dst = lax.broadcasted_iota(jnp.int32, (half, LANES), 1)
    first = (dst // head_dim) * 3 * head_dim + dst % head_dim
    picks = [jnp.where(src == first + k * head_dim, 1.0, 0.0).astype(BF16) for k in range(3)]
    taps[...] = jnp.zeros(taps.shape, F32)
    for section in range(sections):
        for a in range(5):
            for b in range(5):
                taps[tap(section, a, b), :] = agg[a, b, section : section + 1, :]
    rest = taps[...]
    high = rest.astype(BF16)
    rest = rest - high.astype(F32)
    middle = rest.astype(BF16)
    low = (rest - middle.astype(F32)).astype(BF16)
    split = jnp.concatenate([high, middle, low], axis=0)
    count = taps.shape[0]
    weights = qkv[...].reshape(sections * channels, wide)
    for part in range(wide // half):
        here = slice(part * half, (part + 1) * half)
        for kind in range(3):
            to = kind * channels + part * LANES
            there = slice(to, to + LANES)
            value = jnp.dot(weights[:, here], picks[kind], preferred_element_type=F32)
            qkv_out[:, :, there] = value.astype(BF16).reshape(sections, channels, LANES)
            value = jnp.dot(split[:, here], picks[kind], preferred_element_type=F32)
            value = value[:count] + value[count : 2 * count] + value[2 * count :]
            agg_out[:, :, there] = value.reshape(sections, -1, LANES)
    row = lax.broadcasted_iota(jnp.int32, (head_dim, channels), 0)
    lane = lax.broadcasted_iota(jnp.int32, (head_dim, channels), 1)
    spread = jnp.where(lane % head_dim == row, 1.0, 0.0).astype(BF16)
    across = lax.broadcasted_iota(jnp.int32, (channels, channels), 0) // head_dim
    along = lax.broadcasted_iota(jnp.int32, (channels, channels), 1) // head_dim
    for section in range(sections):
        for kind in range(3):
            tall = [group[section, 3 * h + kind] for h in range(channels // head_dim)]
            value = jnp.dot(jnp.concatenate(tall, axis=0), spread, preferred_element_type=F32)
            group_out[section, kind] = jnp.where(across == along, value, 0.0).astype(BF16)
    head_out[...] = jnp.zeros(head_out.shape, BF16)
    for a in range(3):
        rows = [head[a, b] for b in range(3)] + [jnp.zeros((4, channels), BF16)]
        head_out[a, 0:16, :] = jnp.concatenate(rows, axis=0)
    stores = [pltpu.make_async_copy(made[i], outs[i], sems.at[i]) for i in range(6)]
    for store in stores:
        store.start()
    for store in stores:
        store.wait()


def first_kernel(
    tile, head_dim, own, col_1, col_0, row_1, row_0, corner_1, corner_0, *refs
):
    weights, outs, scratch = refs[:9], refs[9:11], refs[11:]
    x_ref = scratch[0]
    rows, cols = tile
    below = REACH + rows
    even_row = lax.axis_index("row") & 1 == 0
    even_col = lax.axis_index("col") & 1 == 0

    def sides(part_0, part_1):
        right = jnp.where(even_col, part_0, part_1)
        left = jnp.where(even_col, part_1, part_0)
        return jnp.concatenate([right, left], axis=1)

    x_ref[REACH:below, 0:cols, :] = own[...]
    x_ref[REACH:below, cols : cols + 2 * SIDE, :] = sides(col_0[...], col_1[...])
    for row, corner, first in (
        (row_0, corner_0, jnp.where(even_row, below, 0)),
        (row_1, corner_1, jnp.where(even_row, 0, below)),
    ):
        here = pl.ds(first, REACH)
        x_ref[here, 0:cols, :] = row[...]
        x_ref[here, cols : cols + 2 * SIDE, :] = sides(corner[0:REACH], corner[REACH:])
    front(x_ref, weights, outs, scratch[1:], REACH, tile, head_dim, 0)


def second_kernel(tile, head_dim, mixed, query, payload, other, out_weight, out_bias, *refs):
    weights, outs, scratch = refs[:9], refs[9:11], refs[11:]
    x_ref = scratch[0]
    attend(
        mixed, query, (payload, other), out_weight, out_bias, scratch[1:3], head_dim, 0, x_ref
    )
    front(x_ref, weights, outs, scratch[3:], REACH - 3, tile, head_dim, 1)


def last_kernel(
    tile, head_dim, mixed, query, payload, other, out_weight, out_bias, head_weight, head_bias,
    map_out, boxes_out, x_ref, *held,
):
    rows, cols = tile
    width = cols + 2 * SIDE
    attend(
        mixed, query, (payload, other), out_weight, out_bias, held, head_dim, 1, x_ref
    )
    clear_outside(x_ref, 1, cols)
    map_out[...] = x_ref[1 : 1 + rows, 0:cols, :]
    total = None
    for a in range(3):
        part = lax.dot_general(
            flat(x_ref[a : a + rows]), head_weight[a], (((1,), (1,)), ((), ())),
            preferred_element_type=F32,
        )
        total = part if total is None else total + part
    total = total.reshape(rows, width, LANES)
    lane = lax.broadcasted_iota(jnp.int32, (width, LANES), 1) // 4
    shifted = [
        jnp.where(
            lane == 0,
            pltpu.roll(total[r], 1, 0),
            jnp.where(lane == 2, pltpu.roll(total[r], width - 1, 0), total[r]),
        )
        for r in range(rows)
    ]
    shifted = jnp.concatenate(shifted, axis=0)
    across = lax.broadcasted_iota(jnp.int32, (8, LANES), 0)
    along = lax.broadcasted_iota(jnp.int32, (8, LANES), 1)
    fold = jnp.where((along % 4 == across) & (along < 12), 1.0, 0.0)
    boxes = lax.dot_general(
        fold, shifted, (((1,), (1,)), ((), ())), precision=lax.Precision.HIGHEST,
        preferred_element_type=F32,
    )
    boxes = boxes[0:4] + head_bias[...]
    for r in range(rows):
        boxes_out[:, r, :] = boxes[:, r * width : r * width + cols]


def near():
    return pl.BlockSpec(memory_space=pltpu.VMEM)


def far():
    return pl.BlockSpec(memory_space=pltpu.HBM)


def digits(size, most):
    radices = []
    while size > 1:
        radix = next((r for r in range(min(most, size), 1, -1) if size % r == 0), size)
        radices.append(radix)
        size //= radix
    return radices


def partner(i, stride, radix, step):
    digit = (i // stride) % radix
    other = digit ^ step if radix & (radix - 1) == 0 else (digit + step) % radix
    return i + (other - digit) * stride


def sum_by_permutes(value):
    rounds = []
    for axis in ("row", "col"):
        stride = 1
        for radix in digits(lax.axis_size(axis), 4):
            rounds.append((axis, stride, radix))
            stride *= radix
    for axis, stride, radix in rounds:
        count = lax.axis_size(axis)
        others = [
            lax.ppermute(value, axis, [(i, partner(i, stride, radix, k)) for i in range(count)])
            for k in range(1, radix)
        ]
        if (axis, stride, radix) == rounds[-1] and radix == 2:
            return value, others[0]
        total = value.astype(F32)
        for other in others:
            total = total + other.astype(F32)
        value = total.astype(BF16)
    return value, jnp.zeros_like(value)


def digits(size, most):
    radices = []
    while size > 1:
        radix = next((r for r in range(min(most, size), 1, -1) if size % r == 0), size)
        radices.append(radix)
        size //= radix
    return radices


def pair_exchange(value, axis, first):
    count = lax.axis_size(axis)
    pairs = []
    for i in range(first, count - 1, 2):
        pairs += [(i, i + 1), (i + 1, i)]
    return lax.ppermute(value, axis, pairs)


def local(
    features,
    expand_weight,
    expand_bias,
    depth_weight,
    depth_bias,
    project_weight,
    project_bias,
    qkv_weight,
    aggregate_depth,
    aggregate_group,
    output_weight,
    output_bias,
    head_weight,
    head_bias,
):
    rows, cols, channels = features.shape
    head_dim = aggregate_group.shape[2]
    heads = channels // head_dim
    width = cols + 2 * SIDE
    tile = (rows, cols)
    wide = expand_weight.shape[2]

    def edges(value, dim, size, odd):
        far = value.shape[dim] - size
        return [
            lax.dynamic_slice_in_dim(value, jnp.where(odd == at, far, 0), size, dim) for at in (0, 1)
        ]

    odd_row = lax.axis_index("row") & 1
    odd_col = lax.axis_index("col") & 1
    low, high = edges(features, 1, SIDE, odd_col)
    col_1 = pair_exchange(high, "col", 1)
    col_0 = pair_exchange(low, "col", 0)
    low, high = edges(features, 0, REACH, odd_row)
    row_1 = pair_exchange(high, "row", 1)
    row_0 = pair_exchange(low, "row", 0)
    low, high = (
        jnp.concatenate(pieces, axis=0)
        for pieces in zip(edges(col_0, 0, REACH, odd_row), edges(col_1, 0, REACH, odd_row))
    )
    corner_1 = pair_exchange(high, "row", 1)
    corner_0 = pair_exchange(low, "row", 0)

    aggregate_depth = aggregate_depth.transpose(1, 2, 0, 3)
    depth_weight = depth_weight.transpose(1, 2, 0, 3)
    params = pltpu.CompilerParams(vmem_limit_bytes=24 * 2**20)
    made = [
        jax.ShapeDtypeStruct(qkv_weight.shape, BF16),
        jax.ShapeDtypeStruct((SECTIONS, 32, 3 * channels), F32),
        jax.ShapeDtypeStruct((SECTIONS, 3, channels, channels), BF16),
        jax.ShapeDtypeStruct((3, LANES, channels), BF16),
    ]
    biases = [jax.ShapeDtypeStruct(array.shape, F32) for array in (project_bias, output_bias)]
    qkv_weight, taps, group, head_weight, project_bias, output_bias = pl.pallas_call(
        functools.partial(prepare_kernel, head_dim),
        out_shape=made + biases,
        grid=(1,),
        in_specs=[near()] * 6,
        out_specs=[far()] * 6,
        scratch_shapes=[pltpu.VMEM(array.shape, array.dtype) for array in made]
        + [pltpu.VMEM((32 * SECTIONS, 3 * channels), F32), pltpu.SemaphoreType.DMA((6,))],
        compiler_params=params,
        cost_estimate=pl.CostEstimate(
            flops=2 * 10**9, bytes_accessed=4 * 10**6, transcendentals=0
        ),
        name="prepare",
    )(qkv_weight, aggregate_depth, aggregate_group, head_weight, project_bias, output_bias)

    weights = [
        expand_weight, expand_bias, depth_weight, depth_bias, project_weight, project_bias,
        qkv_weight, taps, group,
    ]
    weight_specs = [near()] * 5 + [far()] * 4

    def outs_of(count):
        return [
            jax.ShapeDtypeStruct((count, width, channels), BF16),
            jax.ShapeDtypeStruct((LANES + KEY_ROWS, LANES), BF16),
        ]

    def front_scratch(count):
        return [
            pltpu.VMEM((count, width, 256), BF16),
            pltpu.VMEM((count, width, 256), BF16),
            pltpu.VMEM(((count - 2) * width, channels), F32),
            pltpu.VMEM((3, width, 256), BF16),
            pltpu.VMEM((count - 2, width, channels), BF16),
            pltpu.VMEM((rows + 4, width, 2 * channels), BF16),
            pltpu.VMEM((9, TILE, expand_weight.shape[2]), BF16),
            pltpu.VMEM((25, TILE, 2 * channels), BF16),
            pltpu.VMEM(project_bias.shape, F32),
            pltpu.VMEM((channels, 2 * channels), BF16),
            pltpu.VMEM((32, 2 * channels), F32),
            pltpu.VMEM((2, channels, channels), BF16),
            pltpu.SemaphoreType.DMA((5,)),
        ]

    def attend_scratch(count):
        return [
            pltpu.VMEM((count, width, channels), BF16),
            pltpu.VMEM(output_bias.shape, F32),
            pltpu.SemaphoreType.DMA,
        ]

    def queries(mixed, section):
        count = mixed.shape[0]
        units = (count - 4) * width * channels
        return pl.pallas_call(
            functools.partial(query_kernel, tile, section),
            out_shape=[
                jax.ShapeDtypeStruct((count - 4, width, 2 * channels), BF16),
                jax.ShapeDtypeStruct((count - 4, width, channels), BF16),
            ],
            grid=(1,),
            in_specs=[far()] * 4,
            out_specs=[near()] * 2,
            scratch_shapes=[
                pltpu.VMEM((count, width, channels), BF16),
                pltpu.VMEM((count, width, channels), BF16),
                pltpu.VMEM((channels, channels), BF16),
                pltpu.VMEM((32, channels), F32),
                pltpu.VMEM((channels, channels), BF16),
                pltpu.VMEM((25, TILE, channels), BF16),
                pltpu.SemaphoreType.DMA((4,)),
            ],
            compiler_params=params,
            cost_estimate=pl.CostEstimate(
                flops=8 * units * channels, bytes_accessed=8 * units, transcendentals=0
            ),
            name="queries",
        )(mixed, qkv_weight, taps, group)

    first_rows = rows + 2 * REACH
    mixed, payload = pl.pallas_call(
        functools.partial(first_kernel, tile, head_dim),
        out_shape=outs_of(first_rows - 2),
        grid=(1,),
        in_specs=[near()] * 7 + weight_specs,
        out_specs=[far(), near()],
        scratch_shapes=[pltpu.VMEM((first_rows, width, channels), BF16)]
        + front_scratch(first_rows),
        compiler_params=params,
        name="first",
    )(features, col_1, col_0, row_1, row_0, corner_1, corner_0, *weights)
    query, mixed = queries(mixed, 0)
    payload, other = sum_by_permutes(payload)

    second_rows = first_rows - 6
    mixed, payload = pl.pallas_call(
        functools.partial(second_kernel, tile, head_dim),
        out_shape=outs_of(second_rows - 2),
        grid=(1,),
        in_specs=[near()] * 5 + [far()] + weight_specs,
        out_specs=[far(), near()],
        scratch_shapes=attend_scratch(second_rows) + front_scratch(second_rows),
        compiler_params=params,
        name="second",
    )(mixed, query, payload, other, output_weight, output_bias, *weights)
    query, mixed = queries(mixed, 1)
    payload, other = sum_by_permutes(payload)

    return pl.pallas_call(
        functools.partial(last_kernel, tile, head_dim),
        out_shape=[
            jax.ShapeDtypeStruct((rows, cols, channels), BF16),
            jax.ShapeDtypeStruct((4, rows, cols), F32),
        ],
        grid=(1,),
        in_specs=[near()] * 5 + [far()] + [near()] * 2,
        out_specs=[near()] * 2,
        scratch_shapes=attend_scratch(rows + 2),
        compiler_params=params,
        name="last",
    )(
        mixed, query, payload, other, output_weight, output_bias, head_weight,
        head_bias.reshape(4, 1),
    )


def solution(mesh):
    return jax.shard_map(
        local,
        mesh=mesh,
        in_specs=(P("row", "col", None),) + (P(),) * 13,
        out_specs=(P("row", "col", None), P(None, "row", "col")),
        check_vma=False,
    )
```

```python
import functools

import jax
import jax.numpy as jnp
from jax import lax
from jax.experimental import pallas as pl
from jax.experimental.pallas import tpu as pltpu
from jax.sharding import PartitionSpec as P

SECTIONS = 2
LANES = 128
SIDE = 8
REACH = 7
KEY_ROWS = 16
TILE = 16
PARTS = 2
F32 = jnp.float32
BF16 = jnp.bfloat16


def six_hard_swish(value, bound=6.0):
    return value * jnp.minimum(jnp.maximum(value + 3.0, 0.0), bound)


def parted(count, parts):
    cuts = [count * k // parts for k in range(parts + 1)]
    return [(a, b - a) for a, b in zip(cuts, cuts[1:]) if b > a]


def group_size(count, most):
    return next(n for n in range(min(most, count), 0, -1) if count % n == 0)


def by_groups(count, most, body):
    size = group_size(count, most)

    def group(index, carry):
        body(index * size, size)
        return carry

    lax.fori_loop(0, count // size, group, 0)


def clear_outside(ref, halo, cols):
    rows = ref.shape[0]
    row, col = lax.axis_index("row"), lax.axis_index("col")

    @pl.when(row == 0)
    def _():
        ref[0:halo] = jnp.zeros((halo,) + ref.shape[1:], ref.dtype)

    @pl.when(row == lax.axis_size("row") - 1)
    def _():
        ref[rows - halo : rows] = jnp.zeros((halo,) + ref.shape[1:], ref.dtype)

    @pl.when(col == 0)
    def _():
        ref[:, cols + SIDE : cols + 2 * SIDE, :] = jnp.zeros((rows, SIDE, ref.shape[2]), ref.dtype)

    @pl.when(col == lax.axis_size("col") - 1)
    def _():
        ref[:, cols : cols + SIDE, :] = jnp.zeros((rows, SIDE, ref.shape[2]), ref.dtype)


def set_bounds(bounds, cols):
    shape = bounds.shape[1:]
    column = lax.broadcasted_iota(jnp.int32, shape, 0)
    row, col = lax.axis_index("row"), lax.axis_index("col")
    start = jnp.where(col == lax.axis_size("col") - 1, cols, cols + SIDE)
    stop = jnp.where(col == 0, cols + 2 * SIDE, cols + SIDE)
    level = jnp.where((column >= start) & (column < stop), 0.0, 6.0)
    bounds[0] = jnp.where(row == 0, 0.0, level).astype(BF16)
    bounds[1] = level.astype(BF16)
    bounds[2] = jnp.where(row == lax.axis_size("row") - 1, 0.0, level).astype(BF16)


def flat(value):
    return value.reshape(-1, value.shape[-1])


def same_head(head_dim):
    across = lax.broadcasted_iota(jnp.int32, (LANES, LANES), 0) // head_dim
    along = lax.broadcasted_iota(jnp.int32, (LANES, LANES), 1) // head_dim
    return across == along


def depthwise_row(rows, taps, size, width):
    rows = [row.reshape(width // TILE, TILE, LANES) for row in rows]
    total = None
    for b in range(size):
        part = None
        for a in range(size):
            term = rows[a] * taps(a, b)[None]
            part = term if part is None else part + term
        part = part.reshape(width, LANES).astype(F32)
        if b != size // 2:
            part = pltpu.roll(part, (size // 2 - b) % width, 0)
        total = part if total is None else total + part
    return total


def spread_taps(agg, wide_agg):
    for index in range(25):
        taps = agg[index : index + 1, :]
        wide_agg[index] = jnp.broadcast_to(taps, (TILE, taps.shape[1])).astype(BF16)


def aggregated(source, wide_agg, group, low, first, size, channels):
    width = source.shape[1]
    scaled = []
    for r in range(size):
        lanes = []
        for lane in range(low, low + channels, LANES):
            here = slice(lane, lane + LANES)
            value = depthwise_row(
                [source[first + r + a, :, here] for a in range(5)],
                lambda a, b: wide_agg[5 * a + b, :, here], 5, width,
            )
            lanes.append(value.astype(BF16))
        scaled.append(jnp.concatenate(lanes, axis=1))
    value = jnp.dot(jnp.concatenate(scaled, axis=0), group, preferred_element_type=F32)
    return value.astype(BF16).reshape(size, width, channels)


def front(x_ref, weights, outs, scratch, halo, tile, head_dim, section):
    expand, expand_bias, depth, depth_bias, project = weights[:5]
    mixed_out, payload_out = outs
    (
        hidden_0, hidden_1, total, bounds, mixed, pairs, wide_depth, wide_agg,
        project_bias, pair_weight, agg, group, sems,
    ) = scratch
    channels = x_ref.shape[2]
    tail = pl.ds(channels, 2 * channels)
    loads = [
        pltpu.make_async_copy(weights[5], project_bias, sems.at[0]),
        pltpu.make_async_copy(weights[6].at[section, :, tail], pair_weight, sems.at[1]),
        pltpu.make_async_copy(weights[7].at[section, :, tail], agg, sems.at[2]),
        pltpu.make_async_copy(weights[8].at[section, pl.ds(1, 2)], group, sems.at[3]),
    ]
    for load in loads:
        load.start()
    rows, width, channels = x_ref.shape
    tile_rows, tile_cols = tile
    inner = rows - 2
    chunk = hidden_0.shape[2]
    chunks = expand.shape[2] // chunk
    for index in range(9):
        taps = depth[index // 3, index % 3, section : section + 1, :] * (1.0 / 6.0)
        wide_depth[index] = jnp.broadcast_to(taps, (TILE, taps.shape[1])).astype(BF16)
    set_bounds(bounds, tile_cols)
    total[...] = 6.0 * flat(x_ref[1 : rows - 1]).astype(F32)

    def expand_rows(out, at, first, size):
        value = jnp.dot(
            flat(x_ref[first : first + size]), expand[section, :, pl.ds(at, chunk)],
            preferred_element_type=F32,
        )
        value = (value + expand_bias[section : section + 1, pl.ds(at, chunk)]).astype(BF16)
        for r in range(size):
            which = 0 if first + r < halo else 2 if first + r >= rows - halo else 1
            part = value[r * width : (r + 1) * width]
            out[first + r] = six_hard_swish(part, bounds[which])

    def spread_rows(hidden, at, first, size):
        spread = []
        for r in range(first, first + size):
            lanes = []
            for lane in range(0, chunk, LANES):
                here = pl.ds(at + lane, LANES)
                value = depthwise_row(
                    [hidden[r + a, :, lane : lane + LANES] for a in range(3)],
                    lambda a, b: wide_depth[3 * a + b, :, here], 3, width,
                )
                value = (value + depth_bias[section : section + 1, here]).astype(BF16)
                lanes.append(six_hard_swish(value))
            spread.append(jnp.concatenate(lanes, axis=1))
        pixels = slice(first * width, (first + size) * width)
        total[pixels] += jnp.dot(
            jnp.concatenate(spread, axis=0), project[section, pl.ds(at, chunk), :],
            preferred_element_type=F32,
        )

    def stage(index, current, following):
        at = index * chunk
        ahead = at + chunk
        for (first, size), (from_row, count) in zip(parted(inner, PARTS), parted(rows, PARTS)):
            if following is not None:
                expand_rows(following, ahead, from_row, count)
            spread_rows(current, at, first, size)

    for first, size in parted(rows, PARTS):
        expand_rows(hidden_0, 0, first, size)

    for index in range(0, chunks, 2):
        stage(index, hidden_0, hidden_1)
        stage(index + 1, hidden_1, hidden_0 if index + 2 < chunks else None)
    loads[0].wait()
    value = total[...] * (1.0 / 6.0) + project_bias[section : section + 1, :]
    mixed[...] = value.astype(BF16).reshape(inner, width, channels)
    store = pltpu.make_async_copy(mixed, mixed_out, sems.at[4])
    store.start()
    for load in loads[1:]:
        load.wait()
    spread_taps(agg, wide_agg)
    around = halo - 1
    first_pair = around - 2
    count = tile_rows + 4
    for first, size in parted(count, PARTS - 1):
        at = first_pair + first
        value = jnp.dot(
            flat(mixed[at : at + size]), pair_weight[...], preferred_element_type=F32
        )
        pairs[first : first + size] = value.astype(BF16).reshape(size, width, 2 * channels)
    clear_outside(pairs, 2, tile_cols)
    size = group_size(tile_rows, 4)

    def summed(key, value):
        key = jnp.maximum(flat(key[:, 0:tile_cols]), 0.0)
        value = flat(value[:, 0:tile_cols])
        products = [
            lax.dot_general(
                key[:, lane : lane + LANES], value[:, lane : lane + LANES],
                (((0,), (0,)), ((), ())), preferred_element_type=F32,
            )
            for lane in range(0, channels, LANES)
        ]
        return products, jnp.sum(key.astype(F32), axis=0, keepdims=True)

    mine = slice(2, 2 + tile_rows)
    products, sums = summed(
        pairs[mine, :, 0:channels], pairs[mine, :, channels : 2 * channels]
    )

    for at in range(0, tile_rows, size):
        more, more_sums = summed(
            aggregated(pairs, wide_agg, group[0], 0, at, size, channels),
            aggregated(pairs, wide_agg, group[1], channels, at, size, channels),
        )
        if at:
            more = [a + b for a, b in zip(more, more_before)]
            more_sums = more_sums + sums_before
        more_before, sums_before = more, more_sums
    products = products + more
    sums = jnp.concatenate([sums, more_sums], axis=1)
    same = same_head(head_dim)
    summary = jnp.zeros((LANES, LANES), F32)
    key_sums = []
    for index, product in enumerate(products):
        product = jnp.where(same, product, 0.0)
        if index:
            product = pltpu.roll(product, index * head_dim, 1)
        summary = summary + product
        key_sums.append(sums[:, index * LANES : (index + 1) * LANES])
    key_sums.append(jnp.zeros((KEY_ROWS - len(products), LANES), F32))
    payload_out[0:LANES, :] = summary.astype(BF16)
    payload_out[LANES : LANES + KEY_ROWS, :] = jnp.concatenate(key_sums, axis=0).astype(BF16)
    store.wait()


def query_kernel(
    tile, section, mixed_in, qkv_weight, taps, groups, query, mixed_out,
    mixed, centre, weight, agg, group, wide_agg, sems,
):
    rows, width, channels = mixed.shape
    head = pl.ds(0, channels)
    loads = [
        pltpu.make_async_copy(mixed_in, mixed, sems.at[0]),
        pltpu.make_async_copy(qkv_weight.at[section, :, head], weight, sems.at[1]),
        pltpu.make_async_copy(taps.at[section, :, head], agg, sems.at[2]),
        pltpu.make_async_copy(groups.at[section, 0], group, sems.at[3]),
    ]
    for load in loads:
        load.start()
    for load in loads:
        load.wait()
    mixed_out[...] = mixed[2 : rows - 2]
    spread_taps(agg, wide_agg)
    for first, size in parted(rows, PARTS):
        value = jnp.dot(
            flat(mixed[first : first + size]), weight[...], preferred_element_type=F32
        )
        centre[first : first + size] = value.astype(BF16).reshape(size, width, channels)
    clear_outside(centre, (rows - tile[0]) // 2, tile[1])

    def query_rows(first, size):
        here = pl.ds(first, size)
        query[here, :, 0:channels] = jnp.maximum(centre[pl.ds(first + 2, size)], 0.0)
        grouped = aggregated(centre, wide_agg, group[...], 0, first, size, channels)
        query[here, :, channels : 2 * channels] = jnp.maximum(grouped, 0.0)

    by_groups(rows - 4, 8, query_rows)


def attend(
    mixed_ref, query_ref, payloads, weight, bias_in, held, head_dim, section, x_ref
):
    rows, width, channels = x_ref.shape
    bias, sem = held
    load = pltpu.make_async_copy(bias_in, bias, sem)
    load.start()
    same = same_head(head_dim)
    square = (LANES, LANES)
    diagonal = lax.broadcasted_iota(jnp.int32, square, 0) == lax.broadcasted_iota(
        jnp.int32, square, 1
    )
    ones = jnp.where(same, 1.0, 0.0).astype(BF16)
    nothing = jnp.zeros(square, BF16)
    payload = payloads[0][...].astype(F32)
    for part in payloads[1:]:
        payload = payload + part[...].astype(F32)
    packed = payload[0:LANES]
    count = 2 * channels // LANES
    summaries, sums = [], []
    for index in range(count):
        summary = packed if index == 0 else pltpu.roll(packed, LANES - index * head_dim, 1)
        summaries.append(jnp.where(same, summary, 0.0).astype(BF16))
        keys = payload[LANES + index : LANES + index + 1]
        keys = jnp.where(diagonal, keys, 0.0).astype(BF16)
        sums.append(jnp.dot(keys, ones, preferred_element_type=F32).astype(BF16))

    def paired(blocks, index):
        return jnp.concatenate(
            [
                jnp.concatenate([blocks[index], nothing], axis=1),
                jnp.concatenate([nothing, blocks[index + 1]], axis=1),
            ],
            axis=0,
        )

    summaries = [paired(summaries, index) for index in range(0, count, 2)]
    sums = [paired(sums, index) for index in range(0, count, 2)]
    step = 2 * LANES
    load.wait()

    def attend_rows(first, size):
        query = flat(query_ref[pl.ds(first, size)])
        parts = []
        for branch in range(count // 2):
            part = query[:, branch * step : (branch + 1) * step]
            numer = jnp.dot(part, summaries[branch], preferred_element_type=F32)
            denom = jnp.dot(part, sums[branch], preferred_element_type=F32) + 1e-6
            inverse = pl.reciprocal(denom, approx=True)
            inverse = inverse * (2.0 - denom * inverse)
            parts.append((numer * inverse).astype(BF16))
        value = jnp.dot(
            jnp.concatenate(parts, axis=1), weight[section], preferred_element_type=F32
        )
        value = value + bias[section : section + 1, :]
        value = value + flat(mixed_ref[pl.ds(first, size)]).astype(F32)
        x_ref[pl.ds(first, size)] = value.astype(BF16).reshape(size, width, channels)

    by_groups(rows, 10, attend_rows)


def tap(section, a, b):
    at = 32 * section + 5 * a + b
    return slice(at, at + 1)


def prepare_kernel(head_dim, qkv, agg, group, head, project_bias, output_bias, *refs):
    outs, made, taps, sems = refs[:6], refs[6:10], refs[10], refs[11]
    qkv_out, agg_out, group_out, head_out = made
    made = [*made, project_bias, output_bias]
    sections, channels, wide = qkv.shape
    half = 3 * LANES
    heads = LANES // head_dim
    src = lax.broadcasted_iota(jnp.int32, (half, LANES), 0)
    dst = lax.broadcasted_iota(jnp.int32, (half, LANES), 1)
    first = (dst // head_dim) * 3 * head_dim + dst % head_dim
    picks = [jnp.where(src == first + k * head_dim, 1.0, 0.0).astype(BF16) for k in range(3)]
    taps[...] = jnp.zeros(taps.shape, F32)
    for section in range(sections):
        for a in range(5):
            for b in range(5):
                taps[tap(section, a, b), :] = agg[a, b, section : section + 1, :]
    rest = taps[...]
    high = rest.astype(BF16)
    rest = rest - high.astype(F32)
    middle = rest.astype(BF16)
    low = (rest - middle.astype(F32)).astype(BF16)
    split = jnp.concatenate([high, middle, low], axis=0)
    count = taps.shape[0]
    weights = qkv[...].reshape(sections * channels, wide)
    for part in range(wide // half):
        here = slice(part * half, (part + 1) * half)
        for kind in range(3):
            to = kind * channels + part * LANES
            there = slice(to, to + LANES)
            value = jnp.dot(weights[:, here], picks[kind], preferred_element_type=F32)
            qkv_out[:, :, there] = value.astype(BF16).reshape(sections, channels, LANES)
            value = jnp.dot(split[:, here], picks[kind], preferred_element_type=F32)
            value = value[:count] + value[count : 2 * count] + value[2 * count :]
            agg_out[:, :, there] = value.reshape(sections, -1, LANES)
    row = lax.broadcasted_iota(jnp.int32, (head_dim, channels), 0)
    lane = lax.broadcasted_iota(jnp.int32, (head_dim, channels), 1)
    spread = jnp.where(lane % head_dim == row, 1.0, 0.0).astype(BF16)
    across = lax.broadcasted_iota(jnp.int32, (channels, channels), 0) // head_dim
    along = lax.broadcasted_iota(jnp.int32, (channels, channels), 1) // head_dim
    for section in range(sections):
        for kind in range(3):
            tall = [group[section, 3 * h + kind] for h in range(channels // head_dim)]
            value = jnp.dot(jnp.concatenate(tall, axis=0), spread, preferred_element_type=F32)
            group_out[section, kind] = jnp.where(across == along, value, 0.0).astype(BF16)
    head_out[...] = jnp.zeros(head_out.shape, BF16)
    for a in range(3):
        rows = [head[a, b] for b in range(3)] + [jnp.zeros((4, channels), BF16)]
        head_out[a, 0:16, :] = jnp.concatenate(rows, axis=0)
    stores = [pltpu.make_async_copy(made[i], outs[i], sems.at[i]) for i in range(6)]
    for store in stores:
        store.start()
    for store in stores:
        store.wait()


def first_kernel(
    tile, head_dim, own, col_1, col_0, row_1, row_0, corner_1, corner_0, *refs
):
    weights, outs, scratch = refs[:9], refs[9:11], refs[11:]
    x_ref = scratch[0]
    rows, cols = tile
    below = REACH + rows
    even_row = lax.axis_index("row") & 1 == 0
    even_col = lax.axis_index("col") & 1 == 0

    def sides(part_0, part_1):
        right = jnp.where(even_col, part_0, part_1)
        left = jnp.where(even_col, part_1, part_0)
        return jnp.concatenate([right, left], axis=1)

    x_ref[REACH:below, 0:cols, :] = own[...]
    x_ref[REACH:below, cols : cols + 2 * SIDE, :] = sides(col_0[...], col_1[...])
    for row, corner, first in (
        (row_0, corner_0, jnp.where(even_row, below, 0)),
        (row_1, corner_1, jnp.where(even_row, 0, below)),
    ):
        here = pl.ds(first, REACH)
        x_ref[here, 0:cols, :] = row[...]
        x_ref[here, cols : cols + 2 * SIDE, :] = sides(corner[0:REACH], corner[REACH:])
    front(x_ref, weights, outs, scratch[1:], REACH, tile, head_dim, 0)


def second_kernel(tile, head_dim, mixed, query, payload, other, out_weight, out_bias, *refs):
    weights, outs, scratch = refs[:9], refs[9:11], refs[11:]
    x_ref = scratch[0]
    attend(
        mixed, query, (payload, other), out_weight, out_bias, scratch[1:3], head_dim, 0, x_ref
    )
    front(x_ref, weights, outs, scratch[3:], REACH - 3, tile, head_dim, 1)


def last_kernel(
    tile, head_dim, mixed, query, payload, other, out_weight, out_bias, head_weight, head_bias,
    map_out, boxes_out, x_ref, *held,
):
    rows, cols = tile
    width = cols + 2 * SIDE
    attend(
        mixed, query, (payload, other), out_weight, out_bias, held, head_dim, 1, x_ref
    )
    clear_outside(x_ref, 1, cols)
    map_out[...] = x_ref[1 : 1 + rows, 0:cols, :]
    total = None
    for a in range(3):
        part = lax.dot_general(
            flat(x_ref[a : a + rows]), head_weight[a], (((1,), (1,)), ((), ())),
            preferred_element_type=F32,
        )
        total = part if total is None else total + part
    total = total.reshape(rows, width, LANES)
    lane = lax.broadcasted_iota(jnp.int32, (width, LANES), 1) // 4
    shifted = [
        jnp.where(
            lane == 0,
            pltpu.roll(total[r], 1, 0),
            jnp.where(lane == 2, pltpu.roll(total[r], width - 1, 0), total[r]),
        )
        for r in range(rows)
    ]
    shifted = jnp.concatenate(shifted, axis=0)
    across = lax.broadcasted_iota(jnp.int32, (8, LANES), 0)
    along = lax.broadcasted_iota(jnp.int32, (8, LANES), 1)
    fold = jnp.where((along % 4 == across) & (along < 12), 1.0, 0.0)
    boxes = lax.dot_general(
        fold, shifted, (((1,), (1,)), ((), ())), precision=lax.Precision.HIGHEST,
        preferred_element_type=F32,
    )
    boxes = boxes[0:4] + head_bias[...]
    for r in range(rows):
        boxes_out[:, r, :] = boxes[:, r * width : r * width + cols]


def near():
    return pl.BlockSpec(memory_space=pltpu.VMEM)


def far():
    return pl.BlockSpec(memory_space=pltpu.HBM)


def digits(size, most):
    radices = []
    while size > 1:
        radix = next((r for r in range(min(most, size), 1, -1) if size % r == 0), size)
        radices.append(radix)
        size //= radix
    return radices


def partner(i, stride, radix, step):
    digit = (i // stride) % radix
    other = digit ^ step if radix & (radix - 1) == 0 else (digit + step) % radix
    return i + (other - digit) * stride


def sum_by_permutes(value):
    rounds = []
    for axis in ("row", "col"):
        stride = 1
        for radix in digits(lax.axis_size(axis), 4):
            rounds.append((axis, stride, radix))
            stride *= radix
    for axis, stride, radix in rounds:
        count = lax.axis_size(axis)
        others = [
            lax.ppermute(value, axis, [(i, partner(i, stride, radix, k)) for i in range(count)])
            for k in range(1, radix)
        ]
        if (axis, stride, radix) == rounds[-1] and radix == 2:
            return value, others[0]
        total = value.astype(F32)
        for other in others:
            total = total + other.astype(F32)
        value = total.astype(BF16)
    return value, jnp.zeros_like(value)


def digits(size, most):
    radices = []
    while size > 1:
        radix = next((r for r in range(min(most, size), 1, -1) if size % r == 0), size)
        radices.append(radix)
        size //= radix
    return radices


def pair_exchange(value, axis, first):
    count = lax.axis_size(axis)
    pairs = []
    for i in range(first, count - 1, 2):
        pairs += [(i, i + 1), (i + 1, i)]
    return lax.ppermute(value, axis, pairs)


def local(
    features,
    expand_weight,
    expand_bias,
    depth_weight,
    depth_bias,
    project_weight,
    project_bias,
    qkv_weight,
    aggregate_depth,
    aggregate_group,
    output_weight,
    output_bias,
    head_weight,
    head_bias,
):
    rows, cols, channels = features.shape
    head_dim = aggregate_group.shape[2]
    heads = channels // head_dim
    width = cols + 2 * SIDE
    tile = (rows, cols)
    wide = expand_weight.shape[2]

    def edges(value, dim, size, odd):
        far = value.shape[dim] - size
        return [
            lax.dynamic_slice_in_dim(value, jnp.where(odd == at, far, 0), size, dim) for at in (0, 1)
        ]

    odd_row = lax.axis_index("row") & 1
    odd_col = lax.axis_index("col") & 1
    low, high = edges(features, 1, SIDE, odd_col)
    col_1 = pair_exchange(high, "col", 1)
    col_0 = pair_exchange(low, "col", 0)
    low, high = edges(features, 0, REACH, odd_row)
    row_1 = pair_exchange(high, "row", 1)
    row_0 = pair_exchange(low, "row", 0)
    low, high = (
        jnp.concatenate(pieces, axis=0)
        for pieces in zip(edges(col_0, 0, REACH, odd_row), edges(col_1, 0, REACH, odd_row))
    )
    corner_1 = pair_exchange(high, "row", 1)
    corner_0 = pair_exchange(low, "row", 0)

    aggregate_depth = aggregate_depth.transpose(1, 2, 0, 3)
    depth_weight = depth_weight.transpose(1, 2, 0, 3)
    params = pltpu.CompilerParams(vmem_limit_bytes=24 * 2**20)
    made = [
        jax.ShapeDtypeStruct(qkv_weight.shape, BF16),
        jax.ShapeDtypeStruct((SECTIONS, 32, 3 * channels), F32),
        jax.ShapeDtypeStruct((SECTIONS, 3, channels, channels), BF16),
        jax.ShapeDtypeStruct((3, LANES, channels), BF16),
    ]
    biases = [jax.ShapeDtypeStruct(array.shape, F32) for array in (project_bias, output_bias)]
    qkv_weight, taps, group, head_weight, project_bias, output_bias = pl.pallas_call(
        functools.partial(prepare_kernel, head_dim),
        out_shape=made + biases,
        grid=(1,),
        in_specs=[near()] * 6,
        out_specs=[far()] * 6,
        scratch_shapes=[pltpu.VMEM(array.shape, array.dtype) for array in made]
        + [pltpu.VMEM((32 * SECTIONS, 3 * channels), F32), pltpu.SemaphoreType.DMA((6,))],
        compiler_params=params,
        cost_estimate=pl.CostEstimate(
            flops=2 * 10**9, bytes_accessed=4 * 10**6, transcendentals=0
        ),
        name="prepare",
    )(qkv_weight, aggregate_depth, aggregate_group, head_weight, project_bias, output_bias)

    weights = [
        expand_weight, expand_bias, depth_weight, depth_bias, project_weight, project_bias,
        qkv_weight, taps, group,
    ]
    weight_specs = [near()] * 5 + [far()] * 4

    def outs_of(count):
        return [
            jax.ShapeDtypeStruct((count, width, channels), BF16),
            jax.ShapeDtypeStruct((LANES + KEY_ROWS, LANES), BF16),
        ]

    def front_scratch(count):
        return [
            pltpu.VMEM((count, width, 256), BF16),
            pltpu.VMEM((count, width, 256), BF16),
            pltpu.VMEM(((count - 2) * width, channels), F32),
            pltpu.VMEM((3, width, 256), BF16),
            pltpu.VMEM((count - 2, width, channels), BF16),
            pltpu.VMEM((rows + 4, width, 2 * channels), BF16),
            pltpu.VMEM((9, TILE, expand_weight.shape[2]), BF16),
            pltpu.VMEM((25, TILE, 2 * channels), BF16),
            pltpu.VMEM(project_bias.shape, F32),
            pltpu.VMEM((channels, 2 * channels), BF16),
            pltpu.VMEM((32, 2 * channels), F32),
            pltpu.VMEM((2, channels, channels), BF16),
            pltpu.SemaphoreType.DMA((5,)),
        ]

    def attend_scratch(count):
        return [
            pltpu.VMEM((count, width, channels), BF16),
            pltpu.VMEM(output_bias.shape, F32),
            pltpu.SemaphoreType.DMA,
        ]

    def queries(mixed, section):
        count = mixed.shape[0]
        units = (count - 4) * width * channels
        return pl.pallas_call(
            functools.partial(query_kernel, tile, section),
            out_shape=[
                jax.ShapeDtypeStruct((count - 4, width, 2 * channels), BF16),
                jax.ShapeDtypeStruct((count - 4, width, channels), BF16),
            ],
            grid=(1,),
            in_specs=[far()] * 4,
            out_specs=[near()] * 2,
            scratch_shapes=[
                pltpu.VMEM((count, width, channels), BF16),
                pltpu.VMEM((count, width, channels), BF16),
                pltpu.VMEM((channels, channels), BF16),
                pltpu.VMEM((32, channels), F32),
                pltpu.VMEM((channels, channels), BF16),
                pltpu.VMEM((25, TILE, channels), BF16),
                pltpu.SemaphoreType.DMA((4,)),
            ],
            compiler_params=params,
            cost_estimate=pl.CostEstimate(
                flops=8 * units * channels, bytes_accessed=8 * units, transcendentals=0
            ),
            name="queries",
        )(mixed, qkv_weight, taps, group)

    first_rows = rows + 2 * REACH
    mixed, payload = pl.pallas_call(
        functools.partial(first_kernel, tile, head_dim),
        out_shape=outs_of(first_rows - 2),
        grid=(1,),
        in_specs=[near()] * 7 + weight_specs,
        out_specs=[far(), near()],
        scratch_shapes=[pltpu.VMEM((first_rows, width, channels), BF16)]
        + front_scratch(first_rows),
        compiler_params=params,
        name="first",
    )(features, col_1, col_0, row_1, row_0, corner_1, corner_0, *weights)
    query, mixed = queries(mixed, 0)
    payload, other = sum_by_permutes(payload)

    second_rows = first_rows - 6
    mixed, payload = pl.pallas_call(
        functools.partial(second_kernel, tile, head_dim),
        out_shape=outs_of(second_rows - 2),
        grid=(1,),
        in_specs=[near()] * 5 + [far()] + weight_specs,
        out_specs=[far(), near()],
        scratch_shapes=attend_scratch(second_rows) + front_scratch(second_rows),
        compiler_params=params,
        name="second",
    )(mixed, query, payload, other, output_weight, output_bias, *weights)
    query, mixed = queries(mixed, 1)
    payload, other = sum_by_permutes(payload)

    return pl.pallas_call(
        functools.partial(last_kernel, tile, head_dim),
        out_shape=[
            jax.ShapeDtypeStruct((rows, cols, channels), BF16),
            jax.ShapeDtypeStruct((4, rows, cols), F32),
        ],
        grid=(1,),
        in_specs=[near()] * 5 + [far()] + [near()] * 2,
        out_specs=[near()] * 2,
        scratch_shapes=attend_scratch(rows + 2),
        compiler_params=params,
        name="last",
    )(
        mixed, query, payload, other, output_weight, output_bias, head_weight,
        head_bias.reshape(4, 1),
    )


def solution(mesh):
    return jax.shard_map(
        local,
        mesh=mesh,
        in_specs=(P("row", "col", None),) + (P(),) * 13,
        out_specs=(P("row", "col", None), P(None, "row", "col")),
        check_vma=False,
    )
```

```python
import functools

import jax
import jax.numpy as jnp
from jax import lax
from jax.experimental import pallas as pl
from jax.experimental.pallas import tpu as pltpu
from jax.sharding import PartitionSpec as P

SECTIONS = 2
LANES = 128
SIDE = 8
REACH = 7
KEY_ROWS = 16
TILE = 16
PARTS = 2
F32 = jnp.float32
BF16 = jnp.bfloat16


def six_hard_swish(value, bound=6.0):
    return value * jnp.minimum(jnp.maximum(value + 3.0, 0.0), bound)


def parted(count, parts):
    cuts = [count * k // parts for k in range(parts + 1)]
    return [(a, b - a) for a, b in zip(cuts, cuts[1:]) if b > a]


def group_size(count, most):
    return next(n for n in range(min(most, count), 0, -1) if count % n == 0)


def by_groups(count, most, body):
    size = group_size(count, most)

    def group(index, carry):
        body(index * size, size)
        return carry

    lax.fori_loop(0, count // size, group, 0)


def clear_outside(ref, halo, cols):
    rows = ref.shape[0]
    row, col = lax.axis_index("row"), lax.axis_index("col")

    @pl.when(row == 0)
    def _():
        ref[0:halo] = jnp.zeros((halo,) + ref.shape[1:], ref.dtype)

    @pl.when(row == lax.axis_size("row") - 1)
    def _():
        ref[rows - halo : rows] = jnp.zeros((halo,) + ref.shape[1:], ref.dtype)

    @pl.when(col == 0)
    def _():
        ref[:, cols + SIDE : cols + 2 * SIDE, :] = jnp.zeros((rows, SIDE, ref.shape[2]), ref.dtype)

    @pl.when(col == lax.axis_size("col") - 1)
    def _():
        ref[:, cols : cols + SIDE, :] = jnp.zeros((rows, SIDE, ref.shape[2]), ref.dtype)


def set_bounds(bounds, cols):
    shape = bounds.shape[1:]
    column = lax.broadcasted_iota(jnp.int32, shape, 0)
    row, col = lax.axis_index("row"), lax.axis_index("col")
    start = jnp.where(col == lax.axis_size("col") - 1, cols, cols + SIDE)
    stop = jnp.where(col == 0, cols + 2 * SIDE, cols + SIDE)
    level = jnp.where((column >= start) & (column < stop), 0.0, 6.0)
    bounds[0] = jnp.where(row == 0, 0.0, level).astype(BF16)
    bounds[1] = level.astype(BF16)
    bounds[2] = jnp.where(row == lax.axis_size("row") - 1, 0.0, level).astype(BF16)


def flat(value):
    return value.reshape(-1, value.shape[-1])


def same_head(head_dim):
    across = lax.broadcasted_iota(jnp.int32, (LANES, LANES), 0) // head_dim
    along = lax.broadcasted_iota(jnp.int32, (LANES, LANES), 1) // head_dim
    return across == along


def depthwise_row(rows, taps, size, width):
    rows = [row.reshape(width // TILE, TILE, LANES) for row in rows]
    total = None
    for b in range(size):
        part = None
        for a in range(size):
            term = rows[a] * taps(a, b)[None]
            part = term if part is None else part + term
        part = part.reshape(width, LANES).astype(F32)
        if b != size // 2:
            part = pltpu.roll(part, (size // 2 - b) % width, 0)
        total = part if total is None else total + part
    return total


def spread_taps(agg, wide_agg):
    for index in range(25):
        taps = agg[index : index + 1, :]
        wide_agg[index] = jnp.broadcast_to(taps, (TILE, taps.shape[1])).astype(BF16)


def aggregated(source, wide_agg, group, low, first, size, channels):
    width = source.shape[1]
    scaled = []
    for r in range(size):
        lanes = []
        for lane in range(low, low + channels, LANES):
            here = slice(lane, lane + LANES)
            value = depthwise_row(
                [source[first + r + a, :, here] for a in range(5)],
                lambda a, b: wide_agg[5 * a + b, :, here], 5, width,
            )
            lanes.append(value.astype(BF16))
        scaled.append(jnp.concatenate(lanes, axis=1))
    value = jnp.dot(jnp.concatenate(scaled, axis=0), group, preferred_element_type=F32)
    return value.astype(BF16).reshape(size, width, channels)


def front(x_ref, weights, outs, scratch, halo, tile, head_dim, section):
    expand, biases, depth, project = weights[:4]
    mixed_out, payload_out = outs
    (
        hidden_0, hidden_1, total, bounds, mixed, pairs, wide_depth, wide_agg,
        pair_weight, agg, group, sems,
    ) = scratch
    channels = x_ref.shape[2]
    tail = pl.ds(channels, 2 * channels)
    loads = [
        pltpu.make_async_copy(weights[4].at[section, :, tail], pair_weight, sems.at[0]),
        pltpu.make_async_copy(weights[5].at[section, :, tail], agg, sems.at[1]),
        pltpu.make_async_copy(weights[6].at[section, pl.ds(1, 2)], group, sems.at[2]),
    ]
    for load in loads:
        load.start()
    rows, width, channels = x_ref.shape
    tile_rows, tile_cols = tile
    inner = rows - 2
    chunk = hidden_0.shape[2]
    hidden_channels = expand.shape[2]
    chunks = hidden_channels // chunk
    for index in range(9):
        taps = depth[index // 3, index % 3, section : section + 1, :] * (1.0 / 6.0)
        wide_depth[index] = jnp.broadcast_to(taps, (TILE, taps.shape[1])).astype(BF16)
    set_bounds(bounds, tile_cols)
    total[...] = 6.0 * flat(x_ref[1 : rows - 1]).astype(F32)

    def expand_rows(out, at, first, size):
        value = jnp.dot(
            flat(x_ref[first : first + size]), expand[section, :, pl.ds(at, chunk)],
            preferred_element_type=F32,
        )
        value = (value + biases[section : section + 1, pl.ds(at, chunk)]).astype(BF16)
        for r in range(size):
            which = 0 if first + r < halo else 2 if first + r >= rows - halo else 1
            part = value[r * width : (r + 1) * width]
            out[first + r] = six_hard_swish(part, bounds[which])

    def spread_rows(hidden, at, first, size):
        spread = []
        for r in range(first, first + size):
            lanes = []
            for lane in range(0, chunk, LANES):
                here = pl.ds(at + lane, LANES)
                value = depthwise_row(
                    [hidden[r + a, :, lane : lane + LANES] for a in range(3)],
                    lambda a, b: wide_depth[3 * a + b, :, here], 3, width,
                )
                value = (value + biases[section : section + 1, pl.ds(hidden_channels + at + lane, LANES)]).astype(BF16)
                lanes.append(six_hard_swish(value))
            spread.append(jnp.concatenate(lanes, axis=1))
        pixels = slice(first * width, (first + size) * width)
        total[pixels] += jnp.dot(
            jnp.concatenate(spread, axis=0), project[section, pl.ds(at, chunk), :],
            preferred_element_type=F32,
        )

    def stage(index, current, following):
        at = index * chunk
        ahead = at + chunk
        for (first, size), (from_row, count) in zip(parted(inner, PARTS), parted(rows, PARTS)):
            if following is not None:
                expand_rows(following, ahead, from_row, count)
            spread_rows(current, at, first, size)

    for first, size in parted(rows, PARTS):
        expand_rows(hidden_0, 0, first, size)

    for index in range(0, chunks, 2):
        stage(index, hidden_0, hidden_1)
        stage(index + 1, hidden_1, hidden_0 if index + 2 < chunks else None)
    last = slice(2 * hidden_channels, 2 * hidden_channels + channels)
    value = total[...] * (1.0 / 6.0) + biases[section : section + 1, last]
    mixed[...] = value.astype(BF16).reshape(inner, width, channels)
    store = pltpu.make_async_copy(mixed, mixed_out, sems.at[3])
    store.start()
    for load in loads:
        load.wait()
    spread_taps(agg, wide_agg)
    around = halo - 1
    first_pair = around - 2
    count = tile_rows + 4
    for first, size in parted(count, PARTS - 1):
        at = first_pair + first
        value = jnp.dot(
            flat(mixed[at : at + size]), pair_weight[...], preferred_element_type=F32
        )
        pairs[first : first + size] = value.astype(BF16).reshape(size, width, 2 * channels)
    clear_outside(pairs, 2, tile_cols)
    size = group_size(tile_rows, 4)

    def summed(key, value):
        key = jnp.maximum(flat(key[:, 0:tile_cols]), 0.0)
        value = flat(value[:, 0:tile_cols])
        products = [
            lax.dot_general(
                key[:, lane : lane + LANES], value[:, lane : lane + LANES],
                (((0,), (0,)), ((), ())), preferred_element_type=F32,
            )
            for lane in range(0, channels, LANES)
        ]
        return products, jnp.sum(key.astype(F32), axis=0, keepdims=True)

    mine = slice(2, 2 + tile_rows)
    products, sums = summed(
        pairs[mine, :, 0:channels], pairs[mine, :, channels : 2 * channels]
    )

    for at in range(0, tile_rows, size):
        more, more_sums = summed(
            aggregated(pairs, wide_agg, group[0], 0, at, size, channels),
            aggregated(pairs, wide_agg, group[1], channels, at, size, channels),
        )
        if at:
            more = [a + b for a, b in zip(more, more_before)]
            more_sums = more_sums + sums_before
        more_before, sums_before = more, more_sums
    products = products + more
    sums = jnp.concatenate([sums, more_sums], axis=1)
    same = same_head(head_dim)
    summary = jnp.zeros((LANES, LANES), F32)
    key_sums = []
    for index, product in enumerate(products):
        product = jnp.where(same, product, 0.0)
        if index:
            product = pltpu.roll(product, index * head_dim, 1)
        summary = summary + product
        key_sums.append(sums[:, index * LANES : (index + 1) * LANES])
    key_sums.append(jnp.zeros((KEY_ROWS - len(products), LANES), F32))
    payload_out[0:LANES, :] = summary.astype(BF16)
    payload_out[LANES : LANES + KEY_ROWS, :] = jnp.concatenate(key_sums, axis=0).astype(BF16)
    store.wait()


def query_kernel(
    tile, section, mixed_in, qkv_weight, taps, groups, query, mixed_out,
    mixed, centre, weight, agg, group, wide_agg, sems,
):
    rows, width, channels = mixed.shape
    head = pl.ds(0, channels)
    loads = [
        pltpu.make_async_copy(mixed_in, mixed, sems.at[0]),
        pltpu.make_async_copy(qkv_weight.at[section, :, head], weight, sems.at[1]),
        pltpu.make_async_copy(taps.at[section, :, head], agg, sems.at[2]),
        pltpu.make_async_copy(groups.at[section, 0], group, sems.at[3]),
    ]
    for load in loads:
        load.start()
    for load in loads:
        load.wait()
    mixed_out[...] = mixed[2 : rows - 2]
    spread_taps(agg, wide_agg)
    for first, size in parted(rows, PARTS):
        value = jnp.dot(
            flat(mixed[first : first + size]), weight[...], preferred_element_type=F32
        )
        centre[first : first + size] = value.astype(BF16).reshape(size, width, channels)
    clear_outside(centre, (rows - tile[0]) // 2, tile[1])

    def query_rows(first, size):
        here = pl.ds(first, size)
        query[here, :, 0:channels] = jnp.maximum(centre[pl.ds(first + 2, size)], 0.0)
        grouped = aggregated(centre, wide_agg, group[...], 0, first, size, channels)
        query[here, :, channels : 2 * channels] = jnp.maximum(grouped, 0.0)

    size = group_size(rows - 4, 8)
    for first in range(0, rows - 4, size):
        query_rows(first, size)


def attend(
    mixed_ref, query_ref, payloads, weight, biases, head_dim, section, x_ref
):
    rows, width, channels = x_ref.shape
    bias = biases[section : section + 1, biases.shape[1] - channels :]
    same = same_head(head_dim)
    square = (LANES, LANES)
    diagonal = lax.broadcasted_iota(jnp.int32, square, 0) == lax.broadcasted_iota(
        jnp.int32, square, 1
    )
    ones = jnp.where(same, 1.0, 0.0).astype(BF16)
    nothing = jnp.zeros(square, BF16)
    payload = payloads[0][...].astype(F32)
    for part in payloads[1:]:
        payload = payload + part[...].astype(F32)
    packed = payload[0:LANES]
    count = 2 * channels // LANES
    summaries, sums = [], []
    for index in range(count):
        summary = packed if index == 0 else pltpu.roll(packed, LANES - index * head_dim, 1)
        summaries.append(jnp.where(same, summary, 0.0).astype(BF16))
        keys = payload[LANES + index : LANES + index + 1]
        keys = jnp.where(diagonal, keys, 0.0).astype(BF16)
        sums.append(jnp.dot(keys, ones, preferred_element_type=F32).astype(BF16))

    def paired(blocks, index):
        return jnp.concatenate(
            [
                jnp.concatenate([blocks[index], nothing], axis=1),
                jnp.concatenate([nothing, blocks[index + 1]], axis=1),
            ],
            axis=0,
        )

    summaries = [paired(summaries, index) for index in range(0, count, 2)]
    sums = [paired(sums, index) for index in range(0, count, 2)]
    step = 2 * LANES

    def attend_rows(first, size):
        query = flat(query_ref[pl.ds(first, size)])
        parts = []
        for branch in range(count // 2):
            part = query[:, branch * step : (branch + 1) * step]
            numer = jnp.dot(part, summaries[branch], preferred_element_type=F32)
            denom = jnp.dot(part, sums[branch], preferred_element_type=F32) + 1e-6
            inverse = pl.reciprocal(denom, approx=True)
            inverse = inverse * (2.0 - denom * inverse)
            parts.append((numer * inverse).astype(BF16))
        value = jnp.dot(
            jnp.concatenate(parts, axis=1), weight[section], preferred_element_type=F32
        )
        value = value + bias
        value = value + flat(mixed_ref[pl.ds(first, size)]).astype(F32)
        x_ref[pl.ds(first, size)] = value.astype(BF16).reshape(size, width, channels)

    size = group_size(rows, 10)
    for first in range(0, rows, size):
        attend_rows(first, size)


def tap(section, a, b):
    at = 32 * section + 5 * a + b
    return slice(at, at + 1)


def prepare_kernel(head_dim, qkv, agg, group, head, *refs):
    outs, made, taps, sems = refs[:4], refs[4:8], refs[8], refs[9]
    qkv_out, agg_out, group_out, head_out = made
    sections, channels, wide = qkv.shape
    half = 3 * LANES
    heads = LANES // head_dim
    src = lax.broadcasted_iota(jnp.int32, (half, LANES), 0)
    dst = lax.broadcasted_iota(jnp.int32, (half, LANES), 1)
    first = (dst // head_dim) * 3 * head_dim + dst % head_dim
    picks = [jnp.where(src == first + k * head_dim, 1.0, 0.0).astype(BF16) for k in range(3)]
    taps[...] = jnp.zeros(taps.shape, F32)
    for section in range(sections):
        for a in range(5):
            for b in range(5):
                taps[tap(section, a, b), :] = agg[a, b, section : section + 1, :]
    rest = taps[...]
    high = rest.astype(BF16)
    rest = rest - high.astype(F32)
    middle = rest.astype(BF16)
    low = (rest - middle.astype(F32)).astype(BF16)
    split = jnp.concatenate([high, middle, low], axis=0)
    count = taps.shape[0]
    weights = qkv[...].reshape(sections * channels, wide)
    for part in range(wide // half):
        here = slice(part * half, (part + 1) * half)
        for kind in range(3):
            to = kind * channels + part * LANES
            there = slice(to, to + LANES)
            value = jnp.dot(weights[:, here], picks[kind], preferred_element_type=F32)
            qkv_out[:, :, there] = value.astype(BF16).reshape(sections, channels, LANES)
            value = jnp.dot(split[:, here], picks[kind], preferred_element_type=F32)
            value = value[:count] + value[count : 2 * count] + value[2 * count :]
            agg_out[:, :, there] = value.reshape(sections, -1, LANES)
    row = lax.broadcasted_iota(jnp.int32, (head_dim, channels), 0)
    lane = lax.broadcasted_iota(jnp.int32, (head_dim, channels), 1)
    spread = jnp.where(lane % head_dim == row, 1.0, 0.0).astype(BF16)
    across = lax.broadcasted_iota(jnp.int32, (channels, channels), 0) // head_dim
    along = lax.broadcasted_iota(jnp.int32, (channels, channels), 1) // head_dim
    for section in range(sections):
        for kind in range(3):
            tall = [group[section, 3 * h + kind] for h in range(channels // head_dim)]
            value = jnp.dot(jnp.concatenate(tall, axis=0), spread, preferred_element_type=F32)
            group_out[section, kind] = jnp.where(across == along, value, 0.0).astype(BF16)
    head_out[...] = jnp.zeros(head_out.shape, BF16)
    for a in range(3):
        rows = [head[a, b] for b in range(3)] + [jnp.zeros((4, channels), BF16)]
        head_out[a, 0:16, :] = jnp.concatenate(rows, axis=0)
    stores = [pltpu.make_async_copy(made[i], outs[i], sems.at[i]) for i in range(4)]
    for store in stores:
        store.start()
    for store in stores:
        store.wait()


def first_kernel(
    tile, head_dim, own, col_1, col_0, row_1, row_0, corner_1, corner_0, *refs
):
    weights, outs, scratch = refs[:7], refs[7:9], refs[9:]
    x_ref = scratch[0]
    rows, cols = tile
    below = REACH + rows
    even_row = lax.axis_index("row") & 1 == 0
    even_col = lax.axis_index("col") & 1 == 0

    def sides(part_0, part_1):
        right = jnp.where(even_col, part_0, part_1)
        left = jnp.where(even_col, part_1, part_0)
        return jnp.concatenate([right, left], axis=1)

    x_ref[REACH:below, 0:cols, :] = own[...]
    x_ref[REACH:below, cols : cols + 2 * SIDE, :] = sides(col_0[...], col_1[...])
    for row, corner, first in (
        (row_0, corner_0, jnp.where(even_row, below, 0)),
        (row_1, corner_1, jnp.where(even_row, 0, below)),
    ):
        here = pl.ds(first, REACH)
        x_ref[here, 0:cols, :] = row[...]
        x_ref[here, cols : cols + 2 * SIDE, :] = sides(corner[0:REACH], corner[REACH:])
    front(x_ref, weights, outs, scratch[1:], REACH, tile, head_dim, 0)


def second_kernel(tile, head_dim, mixed, query, payload, other, out_weight, biases, *refs):
    weights, outs, scratch = refs[:7], refs[7:9], refs[9:]
    x_ref = scratch[0]
    attend(
        mixed, query, (payload, other), out_weight, biases, head_dim, 0, x_ref
    )
    front(x_ref, weights, outs, scratch[1:], REACH - 3, tile, head_dim, 1)


def last_kernel(
    tile, head_dim, mixed, query, payload, other, out_weight, biases, head_weight, head_bias,
    map_out, boxes_out, x_ref,
):
    rows, cols = tile
    width = cols + 2 * SIDE
    attend(
        mixed, query, (payload, other), out_weight, biases, head_dim, 1, x_ref
    )
    clear_outside(x_ref, 1, cols)
    map_out[...] = x_ref[1 : 1 + rows, 0:cols, :]
    total = None
    for a in range(3):
        part = lax.dot_general(
            flat(x_ref[a : a + rows]), head_weight[a], (((1,), (1,)), ((), ())),
            preferred_element_type=F32,
        )
        total = part if total is None else total + part
    total = total.reshape(rows, width, LANES)
    lane = lax.broadcasted_iota(jnp.int32, (width, LANES), 1) // 4
    shifted = [
        jnp.where(
            lane == 0,
            pltpu.roll(total[r], 1, 0),
            jnp.where(lane == 2, pltpu.roll(total[r], width - 1, 0), total[r]),
        )
        for r in range(rows)
    ]
    shifted = jnp.concatenate(shifted, axis=0)
    across = lax.broadcasted_iota(jnp.int32, (8, LANES), 0)
    along = lax.broadcasted_iota(jnp.int32, (8, LANES), 1)
    fold = jnp.where((along % 4 == across) & (along < 12), 1.0, 0.0)
    boxes = lax.dot_general(
        fold, shifted, (((1,), (1,)), ((), ())), precision=lax.Precision.HIGHEST,
        preferred_element_type=F32,
    )
    boxes = boxes[0:4] + head_bias[...]
    for r in range(rows):
        boxes_out[:, r, :] = boxes[:, r * width : r * width + cols]


def near():
    return pl.BlockSpec(memory_space=pltpu.VMEM)


def far():
    return pl.BlockSpec(memory_space=pltpu.HBM)


def digits(size, most):
    radices = []
    while size > 1:
        radix = next((r for r in range(min(most, size), 1, -1) if size % r == 0), size)
        radices.append(radix)
        size //= radix
    return radices


def partner(i, stride, radix, step):
    digit = (i // stride) % radix
    other = digit ^ step if radix & (radix - 1) == 0 else (digit + step) % radix
    return i + (other - digit) * stride


def sum_by_permutes(value):
    rounds = []
    for axis in ("row", "col"):
        stride = 1
        for radix in digits(lax.axis_size(axis), 4):
            rounds.append((axis, stride, radix))
            stride *= radix
    for axis, stride, radix in rounds:
        count = lax.axis_size(axis)
        others = [
            lax.ppermute(value, axis, [(i, partner(i, stride, radix, k)) for i in range(count)])
            for k in range(1, radix)
        ]
        if (axis, stride, radix) == rounds[-1] and radix == 2:
            return value, others[0]
        total = value.astype(F32)
        for other in others:
            total = total + other.astype(F32)
        value = total.astype(BF16)
    return value, jnp.zeros_like(value)


def digits(size, most):
    radices = []
    while size > 1:
        radix = next((r for r in range(min(most, size), 1, -1) if size % r == 0), size)
        radices.append(radix)
        size //= radix
    return radices


def pair_exchange(value, axis, first):
    count = lax.axis_size(axis)
    pairs = []
    for i in range(first, count - 1, 2):
        pairs += [(i, i + 1), (i + 1, i)]
    return lax.ppermute(value, axis, pairs)


def local(
    features,
    expand_weight,
    expand_bias,
    depth_weight,
    depth_bias,
    project_weight,
    project_bias,
    qkv_weight,
    aggregate_depth,
    aggregate_group,
    output_weight,
    output_bias,
    head_weight,
    head_bias,
):
    rows, cols, channels = features.shape
    head_dim = aggregate_group.shape[2]
    heads = channels // head_dim
    width = cols + 2 * SIDE
    tile = (rows, cols)
    wide = expand_weight.shape[2]

    def edges(value, dim, size, odd):
        far = value.shape[dim] - size
        return [
            lax.dynamic_slice_in_dim(value, jnp.where(odd == at, far, 0), size, dim) for at in (0, 1)
        ]

    odd_row = lax.axis_index("row") & 1
    odd_col = lax.axis_index("col") & 1
    low, high = edges(features, 1, SIDE, odd_col)
    col_1 = pair_exchange(high, "col", 1)
    col_0 = pair_exchange(low, "col", 0)
    low, high = edges(features, 0, REACH, odd_row)
    row_1 = pair_exchange(high, "row", 1)
    row_0 = pair_exchange(low, "row", 0)
    low, high = (
        jnp.concatenate(pieces, axis=0)
        for pieces in zip(edges(col_0, 0, REACH, odd_row), edges(col_1, 0, REACH, odd_row))
    )
    corner_1 = pair_exchange(high, "row", 1)
    corner_0 = pair_exchange(low, "row", 0)

    biases = jnp.concatenate([expand_bias, depth_bias, project_bias, output_bias], axis=1)
    aggregate_depth = aggregate_depth.transpose(1, 2, 0, 3)
    depth_weight = depth_weight.transpose(1, 2, 0, 3)
    params = pltpu.CompilerParams(vmem_limit_bytes=24 * 2**20)
    made = [
        jax.ShapeDtypeStruct(qkv_weight.shape, BF16),
        jax.ShapeDtypeStruct((SECTIONS, 32, 3 * channels), F32),
        jax.ShapeDtypeStruct((SECTIONS, 3, channels, channels), BF16),
        jax.ShapeDtypeStruct((3, LANES, channels), BF16),
    ]
    qkv_weight, taps, group, head_weight = pl.pallas_call(
        functools.partial(prepare_kernel, head_dim),
        out_shape=made,
        grid=(1,),
        in_specs=[near()] * 4,
        out_specs=[far()] * 4,
        scratch_shapes=[pltpu.VMEM(array.shape, array.dtype) for array in made]
        + [pltpu.VMEM((32 * SECTIONS, 3 * channels), F32), pltpu.SemaphoreType.DMA((4,))],
        compiler_params=params,
        cost_estimate=pl.CostEstimate(
            flops=2 * 10**9, bytes_accessed=4 * 10**6, transcendentals=0
        ),
        name="prepare",
    )(qkv_weight, aggregate_depth, aggregate_group, head_weight)

    weights = [
        expand_weight, biases, depth_weight, project_weight, qkv_weight, taps, group,
    ]
    weight_specs = [near()] * 4 + [far()] * 3

    def outs_of(count):
        return [
            jax.ShapeDtypeStruct((count, width, channels), BF16),
            jax.ShapeDtypeStruct((LANES + KEY_ROWS, LANES), BF16),
        ]

    def front_scratch(count):
        return [
            pltpu.VMEM((count, width, 256), BF16),
            pltpu.VMEM((count, width, 256), BF16),
            pltpu.VMEM(((count - 2) * width, channels), F32),
            pltpu.VMEM((3, width, 256), BF16),
            pltpu.VMEM((count - 2, width, channels), BF16),
            pltpu.VMEM((rows + 4, width, 2 * channels), BF16),
            pltpu.VMEM((9, TILE, expand_weight.shape[2]), BF16),
            pltpu.VMEM((25, TILE, 2 * channels), BF16),
            pltpu.VMEM((channels, 2 * channels), BF16),
            pltpu.VMEM((32, 2 * channels), F32),
            pltpu.VMEM((2, channels, channels), BF16),
            pltpu.SemaphoreType.DMA((4,)),
        ]

    def attend_scratch(count):
        return [
            pltpu.VMEM((count, width, channels), BF16),
        ]

    def queries(mixed, section):
        count = mixed.shape[0]
        units = (count - 4) * width * channels
        return pl.pallas_call(
            functools.partial(query_kernel, tile, section),
            out_shape=[
                jax.ShapeDtypeStruct((count - 4, width, 2 * channels), BF16),
                jax.ShapeDtypeStruct((count - 4, width, channels), BF16),
            ],
            grid=(1,),
            in_specs=[far()] * 4,
            out_specs=[near()] * 2,
            scratch_shapes=[
                pltpu.VMEM((count, width, channels), BF16),
                pltpu.VMEM((count, width, channels), BF16),
                pltpu.VMEM((channels, channels), BF16),
                pltpu.VMEM((32, channels), F32),
                pltpu.VMEM((channels, channels), BF16),
                pltpu.VMEM((25, TILE, channels), BF16),
                pltpu.SemaphoreType.DMA((4,)),
            ],
            compiler_params=params,
            cost_estimate=pl.CostEstimate(
                flops=8 * units * channels, bytes_accessed=8 * units, transcendentals=0
            ),
            name="queries",
        )(mixed, qkv_weight, taps, group)

    first_rows = rows + 2 * REACH
    mixed, payload = pl.pallas_call(
        functools.partial(first_kernel, tile, head_dim),
        out_shape=outs_of(first_rows - 2),
        grid=(1,),
        in_specs=[near()] * 7 + weight_specs,
        out_specs=[far(), near()],
        scratch_shapes=[pltpu.VMEM((first_rows, width, channels), BF16)]
        + front_scratch(first_rows),
        compiler_params=params,
        name="first",
    )(features, col_1, col_0, row_1, row_0, corner_1, corner_0, *weights)
    query, mixed = queries(mixed, 0)
    payload, other = sum_by_permutes(payload)

    second_rows = first_rows - 6
    mixed, payload = pl.pallas_call(
        functools.partial(second_kernel, tile, head_dim),
        out_shape=outs_of(second_rows - 2),
        grid=(1,),
        in_specs=[near()] * 6 + weight_specs,
        out_specs=[far(), near()],
        scratch_shapes=attend_scratch(second_rows) + front_scratch(second_rows),
        compiler_params=params,
        name="second",
    )(mixed, query, payload, other, output_weight, biases, *weights)
    query, mixed = queries(mixed, 1)
    payload, other = sum_by_permutes(payload)

    return pl.pallas_call(
        functools.partial(last_kernel, tile, head_dim),
        out_shape=[
            jax.ShapeDtypeStruct((rows, cols, channels), BF16),
            jax.ShapeDtypeStruct((4, rows, cols), F32),
        ],
        grid=(1,),
        in_specs=[near()] * 8,
        out_specs=[near()] * 2,
        scratch_shapes=attend_scratch(rows + 2),
        compiler_params=params,
        name="last",
    )(
        mixed, query, payload, other, output_weight, biases, head_weight,
        head_bias.reshape(4, 1),
    )


def solution(mesh):
    return jax.shard_map(
        local,
        mesh=mesh,
        in_specs=(P("row", "col", None),) + (P(),) * 13,
        out_specs=(P("row", "col", None), P(None, "row", "col")),
        check_vma=False,
    )
```

```python
import functools

import jax
import jax.numpy as jnp
from jax import lax
from jax.experimental import pallas as pl
from jax.experimental.pallas import tpu as pltpu
from jax.sharding import PartitionSpec as P

SECTIONS = 2
LANES = 128
SIDE = 8
REACH = 7
KEY_ROWS = 16
TILE = 16
PARTS = 2
F32 = jnp.float32
BF16 = jnp.bfloat16


def six_hard_swish(value, bound=6.0):
    return value * jnp.minimum(jnp.maximum(value + 3.0, 0.0), bound)


def parted(count, parts):
    cuts = [count * k // parts for k in range(parts + 1)]
    return [(a, b - a) for a, b in zip(cuts, cuts[1:]) if b > a]


def group_size(count, most):
    return next(n for n in range(min(most, count), 0, -1) if count % n == 0)


def clear_outside(ref, halo, cols):
    rows = ref.shape[0]
    row, col = lax.axis_index("row"), lax.axis_index("col")

    @pl.when(row == 0)
    def _():
        ref[0:halo] = jnp.zeros((halo,) + ref.shape[1:], ref.dtype)

    @pl.when(row == lax.axis_size("row") - 1)
    def _():
        ref[rows - halo : rows] = jnp.zeros((halo,) + ref.shape[1:], ref.dtype)

    @pl.when(col == 0)
    def _():
        ref[:, cols + SIDE : cols + 2 * SIDE, :] = jnp.zeros((rows, SIDE, ref.shape[2]), ref.dtype)

    @pl.when(col == lax.axis_size("col") - 1)
    def _():
        ref[:, cols : cols + SIDE, :] = jnp.zeros((rows, SIDE, ref.shape[2]), ref.dtype)


def set_bounds(bounds, cols):
    shape = bounds.shape[1:]
    column = lax.broadcasted_iota(jnp.int32, shape, 0)
    row, col = lax.axis_index("row"), lax.axis_index("col")
    start = jnp.where(col == lax.axis_size("col") - 1, cols, cols + SIDE)
    stop = jnp.where(col == 0, cols + 2 * SIDE, cols + SIDE)
    level = jnp.where((column >= start) & (column < stop), 0.0, 6.0)
    bounds[0] = jnp.where(row == 0, 0.0, level).astype(BF16)
    bounds[1] = level.astype(BF16)
    bounds[2] = jnp.where(row == lax.axis_size("row") - 1, 0.0, level).astype(BF16)


def flat(value):
    return value.reshape(-1, value.shape[-1])


def same_head(head_dim):
    across = lax.broadcasted_iota(jnp.int32, (LANES, LANES), 0) // head_dim
    along = lax.broadcasted_iota(jnp.int32, (LANES, LANES), 1) // head_dim
    return across == along


def depthwise_row(rows, taps, size, width):
    rows = [row.reshape(width // TILE, TILE, LANES) for row in rows]
    total = None
    for b in range(size):
        part = None
        for a in range(size):
            term = rows[a] * taps(a, b)[None]
            part = term if part is None else part + term
        part = part.reshape(width, LANES).astype(F32)
        if b != size // 2:
            part = pltpu.roll(part, (size // 2 - b) % width, 0)
        total = part if total is None else total + part
    return total


def spread_taps(agg, wide_agg):
    for index in range(25):
        taps = agg[index : index + 1, :]
        wide_agg[index] = jnp.broadcast_to(taps, (TILE, taps.shape[1])).astype(BF16)


def aggregated(source, wide_agg, group, low, first, size, channels):
    width = source.shape[1]
    scaled = []
    for r in range(size):
        lanes = []
        for lane in range(low, low + channels, LANES):
            here = slice(lane, lane + LANES)
            value = depthwise_row(
                [source[first + r + a, :, here] for a in range(5)],
                lambda a, b: wide_agg[5 * a + b, :, here], 5, width,
            )
            lanes.append(value.astype(BF16))
        scaled.append(jnp.concatenate(lanes, axis=1))
    value = jnp.dot(jnp.concatenate(scaled, axis=0), group, preferred_element_type=F32)
    return value.astype(BF16).reshape(size, width, channels)


def front(x_ref, weights, outs, scratch, halo, tile, head_dim, section):
    expand, expand_bias, depth, depth_bias, project = weights[:5]
    mixed_out, payload_out = outs
    (
        hidden_0, hidden_1, total, bounds, mixed, pairs, wide_depth, wide_agg,
        project_bias, pair_weight, agg, group, sems,
    ) = scratch
    channels = x_ref.shape[2]
    tail = pl.ds(channels, 2 * channels)
    loads = [
        pltpu.make_async_copy(weights[5], project_bias, sems.at[0]),
        pltpu.make_async_copy(weights[6].at[section, :, tail], pair_weight, sems.at[1]),
        pltpu.make_async_copy(weights[7].at[section, :, tail], agg, sems.at[2]),
        pltpu.make_async_copy(weights[8].at[section, pl.ds(1, 2)], group, sems.at[3]),
    ]
    for load in loads:
        load.start()
    rows, width, channels = x_ref.shape
    tile_rows, tile_cols = tile
    inner = rows - 2
    chunk = hidden_0.shape[2]
    chunks = expand.shape[2] // chunk
    for index in range(9):
        taps = depth[index // 3, index % 3, section : section + 1, :] * (1.0 / 6.0)
        wide_depth[index] = jnp.broadcast_to(taps, (TILE, taps.shape[1])).astype(BF16)
    set_bounds(bounds, tile_cols)
    total[...] = 6.0 * flat(x_ref[1 : rows - 1]).astype(F32)

    def expand_rows(out, at, first, size):
        value = jnp.dot(
            flat(x_ref[first : first + size]), expand[section, :, pl.ds(at, chunk)],
            preferred_element_type=F32,
        )
        value = (value + expand_bias[section : section + 1, pl.ds(at, chunk)]).astype(BF16)
        for r in range(size):
            which = 0 if first + r < halo else 2 if first + r >= rows - halo else 1
            part = value[r * width : (r + 1) * width]
            out[first + r] = six_hard_swish(part, bounds[which])

    def spread_rows(hidden, at, first, size):
        spread = []
        for r in range(first, first + size):
            lanes = []
            for lane in range(0, chunk, LANES):
                here = pl.ds(at + lane, LANES)
                value = depthwise_row(
                    [hidden[r + a, :, lane : lane + LANES] for a in range(3)],
                    lambda a, b: wide_depth[3 * a + b, :, here], 3, width,
                )
                value = (value + depth_bias[section : section + 1, here]).astype(BF16)
                lanes.append(six_hard_swish(value))
            spread.append(jnp.concatenate(lanes, axis=1))
        pixels = slice(first * width, (first + size) * width)
        total[pixels] += jnp.dot(
            jnp.concatenate(spread, axis=0), project[section, pl.ds(at, chunk), :],
            preferred_element_type=F32,
        )

    def stage(index, current, following):
        at = index * chunk
        ahead = at + chunk
        for (first, size), (from_row, count) in zip(parted(inner, PARTS), parted(rows, PARTS)):
            if following is not None:
                expand_rows(following, ahead, from_row, count)
            spread_rows(current, at, first, size)

    for first, size in parted(rows, PARTS):
        expand_rows(hidden_0, 0, first, size)

    for index in range(0, chunks, 2):
        stage(index, hidden_0, hidden_1)
        stage(index + 1, hidden_1, hidden_0 if index + 2 < chunks else None)
    loads[0].wait()
    value = total[...] * (1.0 / 6.0) + project_bias[section : section + 1, :]
    mixed[...] = value.astype(BF16).reshape(inner, width, channels)
    store = pltpu.make_async_copy(mixed, mixed_out, sems.at[4])
    store.start()
    for load in loads[1:]:
        load.wait()
    spread_taps(agg, wide_agg)
    around = halo - 1
    first_pair = around - 2
    count = tile_rows + 4
    for first, size in parted(count, PARTS - 1):
        at = first_pair + first
        value = jnp.dot(
            flat(mixed[at : at + size]), pair_weight[...], preferred_element_type=F32
        )
        pairs[first : first + size] = value.astype(BF16).reshape(size, width, 2 * channels)
    clear_outside(pairs, 2, tile_cols)
    size = group_size(tile_rows, 4)

    def summed(key, value):
        key = jnp.maximum(flat(key[:, 0:tile_cols]), 0.0)
        value = flat(value[:, 0:tile_cols])
        products = [
            lax.dot_general(
                key[:, lane : lane + LANES], value[:, lane : lane + LANES],
                (((0,), (0,)), ((), ())), preferred_element_type=F32,
            )
            for lane in range(0, channels, LANES)
        ]
        return products, jnp.sum(key.astype(F32), axis=0, keepdims=True)

    mine = slice(2, 2 + tile_rows)
    products, sums = summed(
        pairs[mine, :, 0:channels], pairs[mine, :, channels : 2 * channels]
    )

    for at in range(0, tile_rows, size):
        more, more_sums = summed(
            aggregated(pairs, wide_agg, group[0], 0, at, size, channels),
            aggregated(pairs, wide_agg, group[1], channels, at, size, channels),
        )
        if at:
            more = [a + b for a, b in zip(more, more_before)]
            more_sums = more_sums + sums_before
        more_before, sums_before = more, more_sums
    products = products + more
    sums = jnp.concatenate([sums, more_sums], axis=1)
    same = same_head(head_dim)
    summary = jnp.zeros((LANES, LANES), F32)
    key_sums = []
    for index, product in enumerate(products):
        product = jnp.where(same, product, 0.0)
        if index:
            product = pltpu.roll(product, index * head_dim, 1)
        summary = summary + product
        key_sums.append(sums[:, index * LANES : (index + 1) * LANES])
    key_sums.append(jnp.zeros((KEY_ROWS - len(products), LANES), F32))
    payload_out[0:LANES, :] = summary.astype(BF16)
    payload_out[LANES : LANES + KEY_ROWS, :] = jnp.concatenate(key_sums, axis=0).astype(BF16)
    store.wait()


def query_kernel(
    tile, section, mixed_in, qkv_weight, taps, groups, query, mixed_out,
    mixed, centre, weight, agg, group, wide_agg, sems,
):
    rows, width, channels = mixed.shape
    head = pl.ds(0, channels)
    loads = [
        pltpu.make_async_copy(mixed_in, mixed, sems.at[0]),
        pltpu.make_async_copy(qkv_weight.at[section, :, head], weight, sems.at[1]),
        pltpu.make_async_copy(taps.at[section, :, head], agg, sems.at[2]),
        pltpu.make_async_copy(groups.at[section, 0], group, sems.at[3]),
    ]
    for load in loads:
        load.start()
    for load in loads:
        load.wait()
    mixed_out[...] = mixed[2 : rows - 2]
    spread_taps(agg, wide_agg)
    for first, size in parted(rows, PARTS):
        value = jnp.dot(
            flat(mixed[first : first + size]), weight[...], preferred_element_type=F32
        )
        centre[first : first + size] = value.astype(BF16).reshape(size, width, channels)
    clear_outside(centre, (rows - tile[0]) // 2, tile[1])

    def query_rows(first, size):
        here = pl.ds(first, size)
        query[here, :, 0:channels] = jnp.maximum(centre[pl.ds(first + 2, size)], 0.0)
        grouped = aggregated(centre, wide_agg, group[...], 0, first, size, channels)
        query[here, :, channels : 2 * channels] = jnp.maximum(grouped, 0.0)

    size = group_size(rows - 4, 8)
    for first in range(0, rows - 4, size):
        query_rows(first, size)


def attend(
    mixed_ref, query_ref, payloads, weight, bias_in, held, head_dim, section, x_ref
):
    rows, width, channels = x_ref.shape
    bias, sem = held
    load = pltpu.make_async_copy(bias_in, bias, sem)
    load.start()
    same = same_head(head_dim)
    square = (LANES, LANES)
    diagonal = lax.broadcasted_iota(jnp.int32, square, 0) == lax.broadcasted_iota(
        jnp.int32, square, 1
    )
    ones = jnp.where(same, 1.0, 0.0).astype(BF16)
    nothing = jnp.zeros(square, BF16)
    payload = payloads[0][...].astype(F32)
    for part in payloads[1:]:
        payload = payload + part[...].astype(F32)
    packed = payload[0:LANES]
    count = 2 * channels // LANES
    summaries, sums = [], []
    for index in range(count):
        summary = packed if index == 0 else pltpu.roll(packed, LANES - index * head_dim, 1)
        summaries.append(jnp.where(same, summary, 0.0).astype(BF16))
        keys = payload[LANES + index : LANES + index + 1]
        keys = jnp.where(diagonal, keys, 0.0).astype(BF16)
        sums.append(jnp.dot(keys, ones, preferred_element_type=F32).astype(BF16))

    def paired(blocks, index):
        return jnp.concatenate(
            [
                jnp.concatenate([blocks[index], nothing], axis=1),
                jnp.concatenate([nothing, blocks[index + 1]], axis=1),
            ],
            axis=0,
        )

    summaries = [paired(summaries, index) for index in range(0, count, 2)]
    sums = [paired(sums, index) for index in range(0, count, 2)]
    step = 2 * LANES
    load.wait()

    def attend_rows(first, size):
        query = flat(query_ref[pl.ds(first, size)])
        parts = []
        for branch in range(count // 2):
            part = query[:, branch * step : (branch + 1) * step]
            numer = jnp.dot(part, summaries[branch], preferred_element_type=F32)
            denom = jnp.dot(part, sums[branch], preferred_element_type=F32) + 1e-6
            inverse = pl.reciprocal(denom, approx=True)
            inverse = inverse * (2.0 - denom * inverse)
            parts.append((numer * inverse).astype(BF16))
        value = jnp.dot(
            jnp.concatenate(parts, axis=1), weight[section], preferred_element_type=F32
        )
        value = value + bias[section : section + 1, :]
        value = value + flat(mixed_ref[pl.ds(first, size)]).astype(F32)
        x_ref[pl.ds(first, size)] = value.astype(BF16).reshape(size, width, channels)

    size = group_size(rows, 10)
    for first in range(0, rows, size):
        attend_rows(first, size)


def tap(section, a, b):
    at = 32 * section + 5 * a + b
    return slice(at, at + 1)


def prepare_kernel(head_dim, qkv, agg, group, head, project_bias, output_bias, *refs):
    outs, made, taps, sems = refs[:6], refs[6:10], refs[10], refs[11]
    qkv_out, agg_out, group_out, head_out = made
    made = [*made, project_bias, output_bias]
    sections, channels, wide = qkv.shape
    half = 3 * LANES
    heads = LANES // head_dim
    src = lax.broadcasted_iota(jnp.int32, (half, LANES), 0)
    dst = lax.broadcasted_iota(jnp.int32, (half, LANES), 1)
    first = (dst // head_dim) * 3 * head_dim + dst % head_dim
    picks = [jnp.where(src == first + k * head_dim, 1.0, 0.0).astype(BF16) for k in range(3)]
    taps[...] = jnp.zeros(taps.shape, F32)
    for section in range(sections):
        for a in range(5):
            for b in range(5):
                taps[tap(section, a, b), :] = agg[a, b, section : section + 1, :]
    rest = taps[...]
    high = rest.astype(BF16)
    rest = rest - high.astype(F32)
    middle = rest.astype(BF16)
    low = (rest - middle.astype(F32)).astype(BF16)
    split = jnp.concatenate([high, middle, low], axis=0)
    count = taps.shape[0]
    weights = qkv[...].reshape(sections * channels, wide)
    for part in range(wide // half):
        here = slice(part * half, (part + 1) * half)
        for kind in range(3):
            to = kind * channels + part * LANES
            there = slice(to, to + LANES)
            value = jnp.dot(weights[:, here], picks[kind], preferred_element_type=F32)
            qkv_out[:, :, there] = value.astype(BF16).reshape(sections, channels, LANES)
            value = jnp.dot(split[:, here], picks[kind], preferred_element_type=F32)
            value = value[:count] + value[count : 2 * count] + value[2 * count :]
            agg_out[:, :, there] = value.reshape(sections, -1, LANES)
    row = lax.broadcasted_iota(jnp.int32, (head_dim, channels), 0)
    lane = lax.broadcasted_iota(jnp.int32, (head_dim, channels), 1)
    spread = jnp.where(lane % head_dim == row, 1.0, 0.0).astype(BF16)
    across = lax.broadcasted_iota(jnp.int32, (channels, channels), 0) // head_dim
    along = lax.broadcasted_iota(jnp.int32, (channels, channels), 1) // head_dim
    for section in range(sections):
        for kind in range(3):
            tall = [group[section, 3 * h + kind] for h in range(channels // head_dim)]
            value = jnp.dot(jnp.concatenate(tall, axis=0), spread, preferred_element_type=F32)
            group_out[section, kind] = jnp.where(across == along, value, 0.0).astype(BF16)
    head_out[...] = jnp.zeros(head_out.shape, BF16)
    for a in range(3):
        rows = [head[a, b] for b in range(3)] + [jnp.zeros((4, channels), BF16)]
        head_out[a, 0:16, :] = jnp.concatenate(rows, axis=0)
    stores = [pltpu.make_async_copy(made[i], outs[i], sems.at[i]) for i in range(6)]
    for store in stores:
        store.start()
    for store in stores:
        store.wait()


def first_kernel(
    tile, head_dim, own, col_1, col_0, row_1, row_0, corner_1, corner_0, *refs
):
    weights, outs, scratch = refs[:9], refs[9:11], refs[11:]
    x_ref = scratch[0]
    rows, cols = tile
    below = REACH + rows
    even_row = lax.axis_index("row") & 1 == 0
    even_col = lax.axis_index("col") & 1 == 0

    def sides(part_0, part_1):
        right = jnp.where(even_col, part_0, part_1)
        left = jnp.where(even_col, part_1, part_0)
        return jnp.concatenate([right, left], axis=1)

    x_ref[REACH:below, 0:cols, :] = own[...]
    x_ref[REACH:below, cols : cols + 2 * SIDE, :] = sides(col_0[...], col_1[...])
    for row, corner, first in (
        (row_0, corner_0, jnp.where(even_row, below, 0)),
        (row_1, corner_1, jnp.where(even_row, 0, below)),
    ):
        here = pl.ds(first, REACH)
        x_ref[here, 0:cols, :] = row[...]
        x_ref[here, cols : cols + 2 * SIDE, :] = sides(corner[0:REACH], corner[REACH:])
    front(x_ref, weights, outs, scratch[1:], REACH, tile, head_dim, 0)


def second_kernel(tile, head_dim, mixed, query, payload, other, out_weight, out_bias, *refs):
    weights, outs, scratch = refs[:9], refs[9:11], refs[11:]
    x_ref = scratch[0]
    attend(
        mixed, query, (payload, other), out_weight, out_bias, scratch[1:3], head_dim, 0, x_ref
    )
    front(x_ref, weights, outs, scratch[3:], REACH - 3, tile, head_dim, 1)


def last_kernel(
    tile, head_dim, mixed, query, payload, other, out_weight, out_bias, head_weight, head_bias,
    map_out, boxes_out, x_ref, *held,
):
    rows, cols = tile
    width = cols + 2 * SIDE
    attend(
        mixed, query, (payload, other), out_weight, out_bias, held, head_dim, 1, x_ref
    )
    clear_outside(x_ref, 1, cols)
    map_out[...] = x_ref[1 : 1 + rows, 0:cols, :]
    total = None
    for a in range(3):
        part = lax.dot_general(
            flat(x_ref[a : a + rows]), head_weight[a], (((1,), (1,)), ((), ())),
            preferred_element_type=F32,
        )
        total = part if total is None else total + part
    total = total.reshape(rows, width, LANES)
    lane = lax.broadcasted_iota(jnp.int32, (width, LANES), 1) // 4
    shifted = [
        jnp.where(
            lane == 0,
            pltpu.roll(total[r], 1, 0),
            jnp.where(lane == 2, pltpu.roll(total[r], width - 1, 0), total[r]),
        )
        for r in range(rows)
    ]
    shifted = jnp.concatenate(shifted, axis=0)
    across = lax.broadcasted_iota(jnp.int32, (8, LANES), 0)
    along = lax.broadcasted_iota(jnp.int32, (8, LANES), 1)
    fold = jnp.where((along % 4 == across) & (along < 12), 1.0, 0.0)
    boxes = lax.dot_general(
        fold, shifted, (((1,), (1,)), ((), ())), precision=lax.Precision.HIGHEST,
        preferred_element_type=F32,
    )
    boxes = boxes[0:4] + head_bias[...]
    for r in range(rows):
        boxes_out[:, r, :] = boxes[:, r * width : r * width + cols]


def near():
    return pl.BlockSpec(memory_space=pltpu.VMEM)


def far():
    return pl.BlockSpec(memory_space=pltpu.HBM)


def digits(size, most):
    radices = []
    while size > 1:
        radix = next((r for r in range(min(most, size), 1, -1) if size % r == 0), size)
        radices.append(radix)
        size //= radix
    return radices


def partner(i, stride, radix, step):
    digit = (i // stride) % radix
    other = digit ^ step if radix & (radix - 1) == 0 else (digit + step) % radix
    return i + (other - digit) * stride


def sum_by_permutes(value):
    rounds = []
    for axis in ("row", "col"):
        stride = 1
        for radix in digits(lax.axis_size(axis), 4):
            rounds.append((axis, stride, radix))
            stride *= radix
    for axis, stride, radix in rounds:
        count = lax.axis_size(axis)
        others = [
            lax.ppermute(value, axis, [(i, partner(i, stride, radix, k)) for i in range(count)])
            for k in range(1, radix)
        ]
        if (axis, stride, radix) == rounds[-1] and radix == 2:
            return value, others[0]
        total = value.astype(F32)
        for other in others:
            total = total + other.astype(F32)
        value = total.astype(BF16)
    return value, jnp.zeros_like(value)


def digits(size, most):
    radices = []
    while size > 1:
        radix = next((r for r in range(min(most, size), 1, -1) if size % r == 0), size)
        radices.append(radix)
        size //= radix
    return radices


def pair_exchange(value, axis, first):
    count = lax.axis_size(axis)
    pairs = []
    for i in range(first, count - 1, 2):
        pairs += [(i, i + 1), (i + 1, i)]
    return lax.ppermute(value, axis, pairs)


def local(
    features,
    expand_weight,
    expand_bias,
    depth_weight,
    depth_bias,
    project_weight,
    project_bias,
    qkv_weight,
    aggregate_depth,
    aggregate_group,
    output_weight,
    output_bias,
    head_weight,
    head_bias,
):
    rows, cols, channels = features.shape
    head_dim = aggregate_group.shape[2]
    heads = channels // head_dim
    width = cols + 2 * SIDE
    tile = (rows, cols)
    wide = expand_weight.shape[2]

    def edges(value, dim, size, odd):
        far = value.shape[dim] - size
        return [
            lax.dynamic_slice_in_dim(value, jnp.where(odd == at, far, 0), size, dim) for at in (0, 1)
        ]

    odd_row = lax.axis_index("row") & 1
    odd_col = lax.axis_index("col") & 1
    low, high = edges(features, 1, SIDE, odd_col)
    col_1 = pair_exchange(high, "col", 1)
    col_0 = pair_exchange(low, "col", 0)
    low, high = edges(features, 0, REACH, odd_row)
    row_1 = pair_exchange(high, "row", 1)
    row_0 = pair_exchange(low, "row", 0)
    low, high = (
        jnp.concatenate(pieces, axis=0)
        for pieces in zip(edges(col_0, 0, REACH, odd_row), edges(col_1, 0, REACH, odd_row))
    )
    corner_1 = pair_exchange(high, "row", 1)
    corner_0 = pair_exchange(low, "row", 0)

    aggregate_depth = aggregate_depth.transpose(1, 2, 0, 3)
    depth_weight = depth_weight.transpose(1, 2, 0, 3)
    params = pltpu.CompilerParams(vmem_limit_bytes=24 * 2**20)
    made = [
        jax.ShapeDtypeStruct(qkv_weight.shape, BF16),
        jax.ShapeDtypeStruct((SECTIONS, 32, 3 * channels), F32),
        jax.ShapeDtypeStruct((SECTIONS, 3, channels, channels), BF16),
        jax.ShapeDtypeStruct((3, LANES, channels), BF16),
    ]
    biases = [jax.ShapeDtypeStruct(array.shape, F32) for array in (project_bias, output_bias)]
    qkv_weight, taps, group, head_weight, project_bias, output_bias = pl.pallas_call(
        functools.partial(prepare_kernel, head_dim),
        out_shape=made + biases,
        grid=(1,),
        in_specs=[near()] * 6,
        out_specs=[far()] * 6,
        scratch_shapes=[pltpu.VMEM(array.shape, array.dtype) for array in made]
        + [pltpu.VMEM((32 * SECTIONS, 3 * channels), F32), pltpu.SemaphoreType.DMA((6,))],
        compiler_params=params,
        cost_estimate=pl.CostEstimate(
            flops=2 * 10**9, bytes_accessed=4 * 10**6, transcendentals=0
        ),
        name="prepare",
    )(qkv_weight, aggregate_depth, aggregate_group, head_weight, project_bias, output_bias)

    weights = [
        expand_weight, expand_bias, depth_weight, depth_bias, project_weight, project_bias,
        qkv_weight, taps, group,
    ]
    weight_specs = [near()] * 5 + [far()] * 4

    def outs_of(count):
        return [
            jax.ShapeDtypeStruct((count, width, channels), BF16),
            jax.ShapeDtypeStruct((LANES + KEY_ROWS, LANES), BF16),
        ]

    def front_scratch(count):
        return [
            pltpu.VMEM((count, width, 256), BF16),
            pltpu.VMEM((count, width, 256), BF16),
            pltpu.VMEM(((count - 2) * width, channels), F32),
            pltpu.VMEM((3, width, 256), BF16),
            pltpu.VMEM((count - 2, width, channels), BF16),
            pltpu.VMEM((rows + 4, width, 2 * channels), BF16),
            pltpu.VMEM((9, TILE, expand_weight.shape[2]), BF16),
            pltpu.VMEM((25, TILE, 2 * channels), BF16),
            pltpu.VMEM(project_bias.shape, F32),
            pltpu.VMEM((channels, 2 * channels), BF16),
            pltpu.VMEM((32, 2 * channels), F32),
            pltpu.VMEM((2, channels, channels), BF16),
            pltpu.SemaphoreType.DMA((5,)),
        ]

    def attend_scratch(count):
        return [
            pltpu.VMEM((count, width, channels), BF16),
            pltpu.VMEM(output_bias.shape, F32),
            pltpu.SemaphoreType.DMA,
        ]

    def queries(mixed, section):
        count = mixed.shape[0]
        units = (count - 4) * width * channels
        return pl.pallas_call(
            functools.partial(query_kernel, tile, section),
            out_shape=[
                jax.ShapeDtypeStruct((count - 4, width, 2 * channels), BF16),
                jax.ShapeDtypeStruct((count - 4, width, channels), BF16),
            ],
            grid=(1,),
            in_specs=[far()] * 4,
            out_specs=[near()] * 2,
            scratch_shapes=[
                pltpu.VMEM((count, width, channels), BF16),
                pltpu.VMEM((count, width, channels), BF16),
                pltpu.VMEM((channels, channels), BF16),
                pltpu.VMEM((32, channels), F32),
                pltpu.VMEM((channels, channels), BF16),
                pltpu.VMEM((25, TILE, channels), BF16),
                pltpu.SemaphoreType.DMA((4,)),
            ],
            compiler_params=params,
            cost_estimate=pl.CostEstimate(
                flops=8 * units * channels, bytes_accessed=8 * units, transcendentals=0
            ),
            name="queries",
        )(mixed, qkv_weight, taps, group)

    first_rows = rows + 2 * REACH
    mixed, payload = pl.pallas_call(
        functools.partial(first_kernel, tile, head_dim),
        out_shape=outs_of(first_rows - 2),
        grid=(1,),
        in_specs=[near()] * 7 + weight_specs,
        out_specs=[far(), near()],
        scratch_shapes=[pltpu.VMEM((first_rows, width, channels), BF16)]
        + front_scratch(first_rows),
        compiler_params=params,
        name="first",
    )(features, col_1, col_0, row_1, row_0, corner_1, corner_0, *weights)
    query, mixed = queries(mixed, 0)
    payload, other = sum_by_permutes(payload)

    second_rows = first_rows - 6
    mixed, payload = pl.pallas_call(
        functools.partial(second_kernel, tile, head_dim),
        out_shape=outs_of(second_rows - 2),
        grid=(1,),
        in_specs=[near()] * 5 + [far()] + weight_specs,
        out_specs=[far(), near()],
        scratch_shapes=attend_scratch(second_rows) + front_scratch(second_rows),
        compiler_params=params,
        name="second",
    )(mixed, query, payload, other, output_weight, output_bias, *weights)
    query, mixed = queries(mixed, 1)
    payload, other = sum_by_permutes(payload)

    return pl.pallas_call(
        functools.partial(last_kernel, tile, head_dim),
        out_shape=[
            jax.ShapeDtypeStruct((rows, cols, channels), BF16),
            jax.ShapeDtypeStruct((4, rows, cols), F32),
        ],
        grid=(1,),
        in_specs=[near()] * 5 + [far()] + [near()] * 2,
        out_specs=[near()] * 2,
        scratch_shapes=attend_scratch(rows + 2),
        compiler_params=params,
        name="last",
    )(
        mixed, query, payload, other, output_weight, output_bias, head_weight,
        head_bias.reshape(4, 1),
    )


def solution(mesh):
    return jax.shard_map(
        local,
        mesh=mesh,
        in_specs=(P("row", "col", None),) + (P(),) * 13,
        out_specs=(P("row", "col", None), P(None, "row", "col")),
        check_vma=False,
    )
```
